32 devices in a mesh: row: 8 (over z, x), col: 4 (over y, core).
Axes of the slice: x: 2, y: 2, z: 4, core: 2. Of those that a mesh axis runs over, the one named last changes fastest.
Arguments:
- tokens: bfloat16 [8192, 2048], P('row', 'col'), may hold values from -5 to 5
- segment_ids: int32 [8192], P('row'), may hold values from 0 to 7, never falling along the last dimension, each value on 1 to 2048 neighbouring positions
- positions: int32 [8192], P('row'), may hold values from 0 to 4095
- attn_gain: float32 [2048], P('col'), may hold values from 0.5 to 1.5
- query_weight: bfloat16 [2048, 2048], P('row', 'col'), may hold values from -0.22097087 to 0.22097087
- query_bias: float32 [2048], P('col'), may hold values from -3 to 3
- key_weight: bfloat16 [2048, 2048], P('row', 'col'), may hold values from -0.22097087 to 0.22097087
- key_bias: float32 [2048], P('col'), may hold values from -3 to 3
- value_weight: bfloat16 [2048, 2048], P('row', 'col'), may hold values from -0.125 to 0.125
- value_bias: float32 [2048], P('col'), may hold values from -3 to 3
- out_weight: bfloat16 [2048, 2048], P('row', 'col'), may hold values from -1 to 1
- mlp_gain: float32 [2048], P('col'), may hold values from 0.5 to 1.5
- gate_weight: bfloat16 [2048, 5632], P('row', 'col'), may hold values from -0.13258252 to 0.176776695
- up_weight: bfloat16 [2048, 5632], P('row', 'col'), may hold values from -0.13258252 to 0.176776695
- down_weight: bfloat16 [5632, 2048], P('row', 'col'), may hold values from -0.15625 to 0.15625
- out_grad: bfloat16 [8192, 2048], P('row', 'col'), may hold values from -6 to 6
Outputs:
- mixed: bfloat16 [8192, 2048], P('row', 'col')
- tokens_grad: float32 [8192, 2048], P('row', 'col')
- attn_gain_grad: float32 [2048], P('col')
- query_weight_grad: float32 [2048, 2048], P('row', 'col')
- query_bias_grad: float32 [2048], P('col')
- key_weight_grad: float32 [2048, 2048], P('row', 'col')
- key_bias_grad: float32 [2048], P('col')
- value_weight_grad: float32 [2048, 2048], P('row', 'col')
- value_bias_grad: float32 [2048], P('col')
- out_weight_grad: float32 [2048, 2048], P('row', 'col')
- mlp_gain_grad: float32 [2048], P('col')
- gate_weight_grad: float32 [2048, 5632], P('row', 'col')
- up_weight_grad: float32 [2048, 5632], P('row', 'col')
- down_weight_grad: float32 [5632, 2048], P('row', 'col')
The draws below stay inside these ranges and needn't reach their ends.
Inputs may be any that keep to these rules, and one draw needn't show every extreme that they name: `segment_ids`: ids never fall along the tokens; each document has at most 2048 tokens and one has exactly that many.
All inputs are finite; a program needn't handle non-finite values.
Results may differ from the reference program's by a relative error of at most 0.023.
Values may be sent and summed in bfloat16 or wider, within the bound.
A program may use at most 320 MiB of HBM per device.

```python
import math
import jax
import jax.numpy as jnp
import numpy as np
from jax import lax

D = 2048
HEADS = 32
HEAD_DIM = 64
ROT = 16
FF = 5632
SEQ = 1024
TOKENS = 8192


def projection_pair(key):
    head_order = jax.random.permutation(jax.random.fold_in(key, 101), HEADS)
    column = jnp.arange(D, dtype=jnp.int32)
    head_of = column // HEAD_DIM
    dim_of = column % HEAD_DIM
    strength = jnp.where(head_of == head_order[0], 10.0, jnp.where(head_of == head_order[1], 8.0, jnp.where(head_of == head_order[2], 6.0, 0.0))).astype(jnp.float32)
    strong = (strength > 0.0) & (dim_of >= ROT)
    shared = jax.random.uniform(jax.random.fold_in(key, 102), (D, D), jnp.float32, -1.0, 1.0)
    key_noise = jax.random.uniform(jax.random.fold_in(key, 103), (D, D), jnp.float32, -1.0, 1.0)
    query_base = jnp.clip(jax.random.normal(jax.random.fold_in(key, 104), (D, D), jnp.float32), -6.0, 6.0)
    key_base = jnp.clip(jax.random.normal(jax.random.fold_in(key, 105), (D, D), jnp.float32), -6.0, 6.0)
    weight_scale = float(D) ** (-0.5)
    limit = 10.0 * weight_scale * 0.996
    query_cols = jnp.where(strong[None, :], strength[None, :] * shared, query_base) * weight_scale
    key_cols = jnp.where(strong[None, :], strength[None, :] * (0.9 * shared + 0.1 * key_noise), key_base) * weight_scale
    return (jnp.clip(query_cols, -limit, limit), jnp.clip(key_cols, -limit, limit))


def draw_query_weight(key, part):
    return projection_pair(key)[0].astype(jnp.bfloat16)


def draw_key_weight(key, part):
    return projection_pair(key)[1].astype(jnp.bfloat16)


def column_offset_weight(key, salt):
    weight_scale = float(D) ** (-0.5)
    base_part = jnp.clip(jax.random.normal(jax.random.fold_in(key, salt), (D, FF), jnp.float32), -6.0, 6.0)
    offset_part = jax.random.uniform(jax.random.fold_in(key, salt + 1), (1, FF), jnp.float32, 0.5, 1.5)
    return (base_part + offset_part) * weight_scale


def draw_gate_weight(key, part):
    return column_offset_weight(key, 301).astype(jnp.bfloat16)


def draw_up_weight(key, part):
    return column_offset_weight(key, 401).astype(jnp.bfloat16)


def draw_tokens(key, part):
    base_rows = jnp.clip(jax.random.normal(jax.random.fold_in(key, 201), (TOKENS, D), jnp.float32), -5.0, 5.0)
    shifted = jnp.concatenate([base_rows[:1], base_rows[:-1]], axis=0)
    row_index = jnp.arange(TOKENS, dtype=jnp.int32)
    copy_rows = (row_index % 2 == 1) & jax.random.bernoulli(jax.random.fold_in(key, 202), 0.25, (TOKENS,))
    jitter = 0.1 * jax.random.normal(jax.random.fold_in(key, 203), (TOKENS, D), jnp.float32)
    mixed_rows = jnp.where(copy_rows[:, None], jnp.clip(shifted + jitter, -5.0, 5.0), base_rows)
    return mixed_rows.astype(jnp.bfloat16)


def touch_ends(drawn, own_key, least, largest):
    spot = [jax.random.randint(jax.random.fold_in(own_key, axis), (), 0, length) for axis, length in enumerate(drawn.shape)]
    longest = drawn.shape.index(max(drawn.shape))
    next_to = spot[:longest] + [(spot[longest] + 1) % drawn.shape[longest]] + spot[longest + 1:]
    return drawn.at[tuple(spot)].set(least).at[tuple(next_to)].set(largest)


def level_of(rng, shape, cuts, smallest, high):
    factor_of, own = 1.0, jax.random.fold_in(rng, 6)
    for axis_at, blocks in cuts:
        draws = jnp.exp(jax.random.uniform(jax.random.fold_in(own, axis_at), (blocks,), jnp.float32, smallest / len(cuts), high / len(cuts)))
        factor_of = factor_of * jnp.repeat(draws, shape[axis_at] // blocks).reshape([-1 if axis == axis_at else 1 for axis in range(len(shape))])
    return factor_of


def split_up(amount, total, most, lean):
    portions = [(1 << 20) // math.isqrt(standing ** lean) + 1 for standing in range(2, amount + 1)]
    surplus, holding = total - most - (amount - 1), [1] * (amount - 1)
    while surplus > 0:
        movable = [i for i in range(amount - 1) if holding[i] < most]
        whole, left = sum([portions[i] for i in movable]), surplus
        for i in movable:
            extra = min(most - holding[i], max(1, left * portions[i] // whole), surplus)
            holding[i] = holding[i] + extra
            surplus = surplus - extra
    return np.array([most] + holding)


def ragged(stream_key, amount, total, most, slope):
    if amount == 2:
        one = jax.random.randint(stream_key, (), max(1, total - most), min(most, total - 1) + 1)
        return jnp.stack([one, total - one])
    lengths = jnp.asarray(split_up(amount, total, most, slope), jnp.int32)
    pairs = (amount - 1) // 2
    giver, taker = lengths[1:1 + 2 * pairs:2], lengths[2:2 + 2 * pairs:2]
    room = jnp.minimum(giver - 1, most - taker)
    moved = jax.random.randint(jax.random.fold_in(stream_key, 1), (pairs,), 0, 1 << 20) % (room + 1)
    lengths = lengths.at[1:1 + 2 * pairs:2].set(giver - moved).at[2:2 + 2 * pairs:2].set(taker + moved)
    return lengths[jax.random.permutation(jax.random.fold_in(stream_key, 2), amount)]


def centred(own_key, dims, scale, most, cuts=(), kind=jnp.bfloat16):
    values = scale * jax.random.normal(own_key, dims, jnp.float32)
    if cuts:
        values = values * level_of(own_key, dims, cuts, -0.22, 0.18)
    return jnp.clip(values, -most, most).astype(kind)


def setup_inputs(seed: int = 0) -> dict:
    arg_keys = jax.random.split(jax.random.key(seed), 17)
    return {
        "tokens": draw_tokens(jax.random.fold_in(arg_keys[16], 71), 0),
        "segment_ids": jnp.searchsorted(jnp.cumsum(ragged(arg_keys[1], TOKENS // SEQ, TOKENS, 2 * SEQ, 1)), jnp.arange(TOKENS), side="right").astype(jnp.int32),
        "positions": touch_ends(jax.random.randint(arg_keys[2], (TOKENS,), 0, 4 * SEQ), jax.random.fold_in(arg_keys[2], 1), 0, (4 * SEQ) - 1).astype(jnp.int32),
        "attn_gain": jnp.clip(1.0 + 0.1 * jax.random.normal(arg_keys[3], (D,), jnp.float32), 0.5, 1.5),
        "query_weight": draw_query_weight(jax.random.fold_in(arg_keys[16], 71), 0),
        "query_bias": centred(arg_keys[5], (D,), 0.5, 3.0, ((0, 4),), jnp.float32),
        "key_weight": draw_key_weight(jax.random.fold_in(arg_keys[16], 71), 0),
        "key_bias": centred(arg_keys[7], (D,), 0.5, 3.0, ((0, 4),), jnp.float32),
        "value_weight": centred(arg_keys[8], (D, D), D ** -0.5, 0.125, ((0, 8), (1, 4))),
        "value_bias": centred(arg_keys[9], (D,), 0.5, 3.0, ((0, 4),), jnp.float32),
        "out_weight": centred(arg_keys[10], (D, D), (D // 64) ** -0.5, 1.0, ((0, 8), (1, 4))),
        "mlp_gain": jnp.clip(1.0 + 0.1 * jax.random.normal(arg_keys[11], (D,), jnp.float32), 0.5, 1.5),
        "gate_weight": draw_gate_weight(jax.random.fold_in(arg_keys[16], 71), 0),
        "up_weight": draw_up_weight(jax.random.fold_in(arg_keys[16], 71), 0),
        "down_weight": centred(arg_keys[14], (FF, D), (FF // 4) ** -0.5, 0.15625, ((0, 8), (1, 4))),
        "out_grad": centred(arg_keys[15], (TOKENS, D), 1.0, 6.0, ((0, 8), (1, 4))),
    }


@jax.custom_vjp
def low(v):
    return lax.optimization_barrier(v.astype(jnp.bfloat16)).astype(jnp.float32)

@jax.custom_vjp
def low_back(v):
    return v

def low_keep(v):
    return (low(v), None)

def low_pass(kept, grad):
    return (grad,)

def back_keep(v):
    return (v, None)

def back_low(kept, grad):
    return (low(grad),)
low.defvjp(low_keep, low_pass)
low_back.defvjp(back_keep, back_low)
HIGH = lax.Precision.HIGHEST
BASE = 10000.0
NEG = -1e+30

def matmul(left, right):
    return jnp.dot(left, right, precision=HIGH)

def layer_norm(values, norm_gain):
    row_mean = lax.optimization_barrier(jnp.mean(values, axis=-1, keepdims=True))
    row_var = lax.optimization_barrier(jnp.mean(values * values, axis=-1, keepdims=True)) - row_mean * row_mean
    return (values - row_mean) * lax.rsqrt(row_var + 1e-05) * norm_gain

def rotate(values, positions, rot_dims, sign):
    half_dims = rot_dims // 2
    inv_freq = BASE ** (-(jnp.arange(half_dims, dtype=jnp.float32) * 2.0) / rot_dims)
    angles = positions.astype(jnp.float32)[:, None] * inv_freq[None, :]
    cosine = jnp.cos(angles)[:, None, :]
    sine_part = sign * jnp.sin(angles)[:, None, :]
    first_half = values[..., :half_dims]
    second = values[..., half_dims:rot_dims]
    return jnp.concatenate([first_half * cosine - second * sine_part, second * cosine + first_half * sine_part, values[..., rot_dims:]], axis=-1)

def visible(segment):
    length = segment.shape[0]
    query_pos = lax.broadcasted_iota(jnp.int32, (length, length), 0)
    key_pos = lax.broadcasted_iota(jnp.int32, (length, length), 1)
    return (segment[:, None] == segment[None, :]) & (query_pos >= key_pos)

def attend(pieces):
    queries, keys_rot, values, segment = pieces
    scale = queries.shape[-1] ** (-0.5)
    scores = low_back(jnp.einsum('qhe,khe->hqk', queries, keys_rot, precision=HIGH) * scale)
    scores = jnp.where(visible(segment)[None], scores, NEG)
    row_peak = lax.optimization_barrier(jnp.max(scores, axis=-1, keepdims=True))
    exp_scores = jnp.exp(scores - row_peak)
    soft_probs = low(exp_scores / lax.optimization_barrier(jnp.sum(exp_scores, axis=-1, keepdims=True)))
    return jnp.einsum('hqk,khe->qhe', soft_probs, values, precision=HIGH)

def group_forward(params, inputs, segments, positions):
    attn_gain, query_weight, query_bias, key_weight, key_bias, value_weight, value_bias, out_weight, mlp_gain, gate_weight, up_weight, down_weight = params
    row_count = inputs.shape[0]
    seq_count = row_count // SEQ
    normed_first = low(layer_norm(inputs, attn_gain))
    query_pre = low_back(matmul(normed_first, query_weight) + query_bias)
    key_pre = low_back(matmul(normed_first, key_weight) + key_bias)
    value_low = low(low_back(matmul(normed_first, value_weight) + value_bias))
    query_rot = low(rotate(query_pre.reshape(row_count, HEADS, HEAD_DIM), positions, ROT, 1.0))
    key_rot = low(rotate(key_pre.reshape(row_count, HEADS, HEAD_DIM), positions, ROT, 1.0))
    shape_seq = (seq_count, SEQ, HEADS, HEAD_DIM)
    attended = lax.map(jax.checkpoint(attend), (query_rot.reshape(shape_seq), key_rot.reshape(shape_seq), value_low.reshape(shape_seq), segments.reshape(seq_count, SEQ)))
    attn_low = low(low_back(attended.reshape(row_count, D)))
    resid = inputs + low_back(matmul(attn_low, out_weight))
    normed_second = low(layer_norm(resid, mlp_gain))
    gate_pre = low_back(matmul(normed_second, gate_weight))
    up_pre = low_back(matmul(normed_second, up_weight))
    hidden = low(jax.nn.silu(gate_pre) * up_pre)
    return resid + matmul(hidden, down_weight)

def whole(params, inputs, segments, positions):
    group_size = math.gcd(TOKENS // SEQ, max(1, 4096 // SEQ)) * SEQ
    blocks = TOKENS // group_size

    def one_group(pieces):
        return jax.checkpoint(group_forward)(params, pieces[0], pieces[1], pieces[2])
    result = lax.map(one_group, (inputs.reshape(blocks, group_size, D), segments.reshape(blocks, group_size), positions.reshape(blocks, group_size)))
    return result.reshape(TOKENS, D)

def reference(tokens, segment_ids, positions, attn_gain, query_weight, query_bias, key_weight, key_bias, value_weight, value_bias, out_weight, mlp_gain, gate_weight, up_weight, down_weight, out_grad):
    params = tuple((jnp.asarray(item).astype(jnp.float32) for item in (attn_gain, query_weight, query_bias, key_weight, key_bias, value_weight, value_bias, out_weight, mlp_gain, gate_weight, up_weight, down_weight)))
    inputs = tokens.astype(jnp.float32)

    def run_block(weights, values):
        return whole(weights, values, segment_ids, positions)
    result, pullback = jax.vjp(run_block, params, inputs)
    param_grads, input_grad = pullback(out_grad.astype(jnp.float32))
    return (result.astype(jnp.bfloat16), input_grad, param_grads[0], param_grads[1], param_grads[2], param_grads[3], param_grads[4], param_grads[5], param_grads[6], param_grads[7], param_grads[8], param_grads[9], param_grads[10], param_grads[11])
```

```python
import functools

import jax
import jax.numpy as jnp
from jax import lax
from jax.experimental import pallas as pl
from jax.experimental.pallas import tpu as pltpu
from jax.sharding import PartitionSpec as P

HEAD_DIM = 64
ROT = 16
SEQ = 1024
BASE = 10000.0
NEG = -1e30
F32 = jnp.float32
BF16 = jnp.bfloat16
SCALE = HEAD_DIM**-0.5
MESH = pl.DeviceIdType.MESH
QBLOCK = 256
PAIR = 2


def dot(left, right, left_dims=(1,), right_dims=(0,)):
    return lax.dot_general(
        left, right, ((left_dims, right_dims), ((), ())), preferred_element_type=F32
    )


def swap_pairs(values, lane):
    half = ROT // 2
    width = values.shape[1]
    ahead = pltpu.roll(values, width - half, 1)
    behind = pltpu.roll(values, half, 1)
    return jnp.where(lane < half, ahead, behind)


def attention_forward_kernel(
    q_ref, k_ref, v_ref, seg_col_ref, seg_row_ref, o_ref, lse_ref, acc_ref, lse_scratch
):
    width = q_ref.shape[1]
    heads = width // HEAD_DIM
    full_lane = lax.broadcasted_iota(jnp.int32, (1, width), 1)
    acc_ref[...] = jnp.zeros_like(acc_ref)
    lse_lane = lax.broadcasted_iota(jnp.int32, (1, lse_scratch.shape[1]), 1)

    @pl.loop(0, heads)
    def _(head):
        mask = full_lane // HEAD_DIM == head
        for start in range(0, SEQ, QBLOCK):
            keys = start + QBLOCK
            rows = slice(start, keys)
            queries = jnp.where(mask, q_ref[rows, :], jnp.zeros((), BF16))
            scores = dot(queries, k_ref[:keys, :], (1,), (1,))
            query_pos = start + lax.broadcasted_iota(jnp.int32, scores.shape, 0)
            key_pos = lax.broadcasted_iota(jnp.int32, scores.shape, 1)
            seen = (seg_col_ref[rows, :] == seg_row_ref[0, :, :keys]) & (key_pos <= query_pos)
            scores = jnp.where(seen, scores, NEG)
            peak = jnp.max(scores, axis=1, keepdims=True)
            weights = jnp.exp(scores - peak)
            total = jnp.sum(weights, axis=1, keepdims=True)
            probs = (weights * (1.0 / total)).astype(BF16)
            output = dot(probs, v_ref[:keys, :])
            acc_ref[rows, :] = jnp.where(mask, output, acc_ref[rows, :])
            lse_scratch[rows, :] = jnp.where(
                lse_lane == head, peak + jnp.log(total), lse_scratch[rows, :]
            )

    o_ref[...] = acc_ref[...].astype(BF16)
    lse_ref[0] = lse_scratch[...].T[: lse_ref.shape[1], :]


def attention_forward(queries, keys, values, segments):
    rows, width = queries.shape
    seqs = rows // SEQ
    block = lambda columns: pl.BlockSpec((SEQ, columns), lambda s: (s, 0))
    return pl.pallas_call(
        attention_forward_kernel,
        grid=(seqs,),
        in_specs=[block(width)] * 3 + [block(1), pl.BlockSpec((1, 1, SEQ), lambda s: (s, 0, 0))],
        out_specs=[block(width), pl.BlockSpec((1, 8, SEQ), lambda s: (s, 0, 0))],
        out_shape=[
            jax.ShapeDtypeStruct((rows, width), BF16),
            jax.ShapeDtypeStruct((seqs, 8, SEQ), F32),
        ],
        scratch_shapes=[pltpu.VMEM((SEQ, width), F32), pltpu.VMEM((SEQ, 128), F32)],
        compiler_params=pltpu.CompilerParams(vmem_limit_bytes=56 << 20),
        cost_estimate=pl.CostEstimate(
            flops=8 * rows * SEQ * width, bytes_accessed=10 * rows * width, transcendentals=0
        ),
        name="attention_forward",
    )(queries, keys, values, segments.reshape(rows, 1), segments.reshape(seqs, 1, SEQ))


def attention_backward_kernel(
    q_ref, k_ref, v_ref, do_ref, lse_ref, cos_ref, sin_ref, seg_col_ref, seg_row_ref,
    grad_ref, sums_ref, dq_ref, dk_ref, dv_ref,
):
    width = q_ref.shape[1]
    heads = width // HEAD_DIM
    full_lane = lax.broadcasted_iota(jnp.int32, (1, width), 1)
    in_head = full_lane % HEAD_DIM
    for ref in (dq_ref, dk_ref, dv_ref):
        ref[...] = jnp.zeros_like(ref)

    @pl.loop(0, heads)
    def _(head):
        mask = full_lane // HEAD_DIM == head
        nothing = jnp.zeros((), BF16)
        for start in range(0, SEQ, QBLOCK):
            keys = start + QBLOCK
            rows = slice(start, keys)
            queries = jnp.where(mask, q_ref[rows, :], nothing)
            grads = jnp.where(mask, do_ref[rows, :], nothing)
            scores = dot(k_ref[:keys, :], queries, (1,), (1,))
            key_pos = lax.broadcasted_iota(jnp.int32, scores.shape, 0)
            query_pos = start + lax.broadcasted_iota(jnp.int32, scores.shape, 1)
            seen = (seg_col_ref[:keys, :] == seg_row_ref[0, :, rows]) & (key_pos <= query_pos)
            probs = jnp.where(
                seen, jnp.exp(scores - lse_ref[0, pl.ds(head, 1), rows]), 0.0
            )
            dv_ref[:keys, :] += dot(probs.astype(BF16), grads)
            grad_probs = dot(v_ref[:keys, :], grads, (1,), (1,))
            delta = jnp.sum(probs * grad_probs, axis=0, keepdims=True)
            grad_scores = (probs * (grad_probs - delta)).astype(BF16)
            dk_ref[:keys, :] += dot(grad_scores, queries)
            masked_keys = jnp.where(mask, k_ref[:keys, :], nothing)
            dq_ref[rows, :] += dot(grad_scores, masked_keys, (0,), (0,))

    cosine = jnp.tile(cos_ref[...], (1, width // cos_ref.shape[1]))
    sine = jnp.tile(sin_ref[...], (1, width // sin_ref.shape[1]))
    for part, (ref, scale) in enumerate(((dq_ref, SCALE), (dk_ref, 1.0), (dv_ref, None))):
        grad = ref[...]
        if scale is not None:
            grad = grad * scale
            grad = grad * cosine - swap_pairs(grad, in_head) * sine
        low = grad.astype(BF16)
        columns = slice(part * width, (part + 1) * width)
        grad_ref[:, columns] = low
        sums_ref[0, :, columns] = jnp.sum(low.astype(F32), axis=0, keepdims=True)


def attention_backward(queries, keys, values, grad_out, lse, cosine, sine, segments):
    rows, width = queries.shape
    seqs = rows // SEQ
    block = lambda columns: pl.BlockSpec((SEQ, columns), lambda s: (s, 0))
    return pl.pallas_call(
        attention_backward_kernel,
        grid=(seqs,),
        in_specs=[block(width)] * 4
        + [
            pl.BlockSpec((1, 8, SEQ), lambda s: (s, 0, 0)),
            block(cosine.shape[1]),
            block(cosine.shape[1]),
            block(1),
            pl.BlockSpec((1, 1, SEQ), lambda s: (s, 0, 0)),
        ],
        out_specs=[block(3 * width), pl.BlockSpec((1, 1, 3 * width), lambda s: (s, 0, 0))],
        out_shape=[
            jax.ShapeDtypeStruct((rows, 3 * width), BF16),
            jax.ShapeDtypeStruct((seqs, 1, 3 * width), F32),
        ],
        scratch_shapes=[pltpu.VMEM((SEQ, width), F32)] * 3,
        compiler_params=pltpu.CompilerParams(vmem_limit_bytes=56 << 20),
        cost_estimate=pl.CostEstimate(
            flops=10 * rows * SEQ * width, bytes_accessed=20 * rows * width, transcendentals=0
        ),
        name="attention_backward",
    )(
        queries, keys, values, grad_out, lse, cosine, sine,
        segments.reshape(rows, 1), segments.reshape(seqs, 1, SEQ),
    )


def row_pairs():
    return [(r, r ^ 1) for r in range(lax.axis_size("row"))]


def row_lines():
    size = lax.axis_size("row")
    return [list(range(start, size, PAIR)) for start in range(PAIR)]


def neighbours():
    return [list(range(r, r + PAIR)) for r in range(0, lax.axis_size("row"), PAIR)]


def swap_rows(values):
    return lax.ppermute(values, "row", row_pairs())


def gather_line(values, axis=0):
    return lax.all_gather(values, "row", axis=axis, tiled=True, axis_index_groups=row_lines())


def scatter_line(values, axis=0):
    return lax.psum_scatter(
        values, "row", scatter_dimension=axis, tiled=True, axis_index_groups=row_lines()
    )


def pick(values, index, axis):
    size = values.shape[axis] // PAIR
    return lax.dynamic_slice_in_dim(values, index * size, size, axis)


def in_order(x, own, other, axis):
    return jnp.where(
        x == 0, jnp.concatenate([own, other], axis), jnp.concatenate([other, own], axis)
    )


def own_columns(weight, x):
    return in_order(x, pick(weight, x, 1), swap_rows(pick(weight, 1 - x, 1)), 0)


def own_units(weight, x):
    kept, sent = pick(weight, x, 1).T, pick(weight, 1 - x, 1).T
    return in_order(x, kept, swap_rows(sent), 1)


def own_inputs(grad, x):
    return in_order(x, pick(grad, x, 1), swap_rows(pick(grad, 1 - x, 1)), 0)


def own_rows(grad, x):
    return in_order(x, pick(grad, x, 0), swap_rows(pick(grad, 1 - x, 0)), 1)


def places():
    row, col = lax.axis_index("row"), lax.axis_index("col")
    return row % PAIR, col // 2, col % 2, row, col


def peers(row, col):
    x = row % PAIR
    over_x = (row + 1 - 2 * x, col)
    over_y = (row, (col + 2) % 4)
    over_core = (row, col + 1 - 2 * (col % 2))
    return over_x, over_y, over_core


def meet(devices):
    barrier = pltpu.get_barrier_semaphore()
    for device in devices:
        pl.semaphore_signal(barrier, inc=1, device_id=device, device_id_type=MESH)
    pl.semaphore_wait(barrier, len(devices))


def block_at(ref, a, col, rows, width, start, count):
    at = pl.multiple_of(a * rows + start, 128)
    return ref.at[pl.ds(at, count), pl.ds(pl.multiple_of(col * width, 128), width)]


CHUNKS = 4


def gather_plane_kernel(src_ref, out_ref, local_sem, send_sem, recv_sem):
    rows, width = src_ref.shape
    x, y, core, row, col = places()
    over_x, over_y, over_core = peers(row, col)
    meet((over_x, over_y, over_core))
    count = rows // CHUNKS
    col_y = (col + 2) % 4
    col_core = col + 1 - 2 * core
    first, second = list(range(CHUNKS // 2)), list(range(CHUNKS // 2, CHUNKS))

    def piece(a, c, s):
        return block_at(out_ref, a, c, rows, width, s * count, count)

    def copy(index, source, place, device):
        return pltpu.make_async_remote_copy(
            source, place, send_sem.at[index], recv_sem.at[index],
            device_id=device, device_id_type=MESH,
        )

    def own(s):
        return src_ref.at[pl.ds(s * count, count), :]

    sent = []

    def send(index, source, place, device):
        task = copy(index, source, place, device)
        task.start()
        sent.append(task)

    def wait(index, place):
        copy(index, place, place, over_core).wait_recv()

    local = pltpu.make_async_copy(
        src_ref, block_at(out_ref, x, col, rows, width, 0, rows), local_sem
    )
    local.start()
    for s, t in zip(first + second, second + first):
        send(s, own(s), piece(x, col, s), over_x)
        send(CHUNKS + t, own(t), piece(x, col, t), over_y)
    for s in range(CHUNKS):
        send(4 * CHUNKS + s, own(s), piece(x, col, s), over_core)
    for s, t in zip(first + second, second + first):
        wait(s, piece(1 - x, col, s))
        if s in first:
            send(2 * CHUNKS + s, piece(1 - x, col, s), piece(1 - x, col, s), over_y)
        send(5 * CHUNKS + s, piece(1 - x, col, s), piece(1 - x, col, s), over_core)
        wait(CHUNKS + t, piece(x, col_y, t))
        if t in second:
            send(2 * CHUNKS + t, piece(x, col_y, t), piece(x, col_y, t), over_x)
        send(6 * CHUNKS + t, piece(x, col_y, t), piece(x, col_y, t), over_core)
    for s, t in zip(first, second):
        for u in (s, t):
            wait(2 * CHUNKS + u, piece(1 - x, col_y, u))
            send(7 * CHUNKS + u, piece(1 - x, col_y, u), piece(1 - x, col_y, u), over_core)
    for group, (a, c) in enumerate(
        ((x, col_core), (1 - x, col_core), (x, (col_core + 2) % 4), (1 - x, (col_core + 2) % 4))
    ):
        for s in range(CHUNKS):
            wait((4 + group) * CHUNKS + s, piece(a, c, s))
    for task in sent:
        task.wait_send()
    local.wait()


def gather_plane(values, name, collective_id):
    cols = lax.axis_size("col")
    if cols != 4:
        across = lax.all_gather(values, "col", axis=1, tiled=True)
        return lax.all_gather(across, "row", axis=0, tiled=True, axis_index_groups=neighbours())
    rows, width = values.shape
    return pl.pallas_call(
        gather_plane_kernel,
        in_specs=[pl.BlockSpec(memory_space=pl.ANY)],
        out_specs=pl.BlockSpec(memory_space=pl.ANY),
        out_shape=jax.ShapeDtypeStruct((PAIR * rows, cols * width), values.dtype),
        scratch_shapes=[
            pltpu.SemaphoreType.DMA,
            pltpu.SemaphoreType.DMA((8 * CHUNKS,)),
            pltpu.SemaphoreType.DMA((8 * CHUNKS,)),
        ],
        compiler_params=pltpu.CompilerParams(collective_id=collective_id, has_side_effects=True),
        name=name,
    )(values)


def add_rows(out_ref, left_ref, right_ref, rows, step=64):
    @pl.loop(0, rows // step)
    def _(i):
        at = pl.ds(pl.multiple_of(i * step, step), step)
        total = left_ref[at, :].astype(F32) + right_ref[at, :].astype(F32)
        out_ref[at, :] = total.astype(out_ref.dtype)


def scatter_plane_kernel(
    part_ref, out_ref, own_ref, core_ref, x_ref, y_ref, last_ref,
    load_sem, send_sem, recv_sem,
):
    rows, width = own_ref.shape[1:]
    half = rows // 2
    x, y, core, row, col = places()
    over_x, over_y, over_core = peers(row, col)
    meet((over_x, over_y, over_core))
    top, bottom = pl.ds(0, half), pl.ds(half, half)

    def copy(index, source, place, device):
        return pltpu.make_async_remote_copy(
            source, place, send_sem.at[index], recv_sem.at[index],
            device_id=device, device_id_type=MESH,
        )

    sent = []

    def send(index, source, place, device):
        task = copy(index, source, place, device)
        task.start()
        sent.append(task)

    def wait(index, place):
        copy(index, place, place, over_core).wait_recv()

    order = ((1 - x, 1 - y), (1 - x, y), (x, 1 - y), (x, y))
    loads = []
    for i, (a, b) in enumerate(order):
        slot = 2 * a + b
        send(
            i, block_at(part_ref, a, 2 * b + 1 - core, rows, width, 0, rows),
            core_ref.at[slot], over_core,
        )
        load = pltpu.make_async_copy(
            block_at(part_ref, a, 2 * b + core, rows, width, 0, rows),
            own_ref.at[slot], load_sem.at[i],
        )
        load.start()
        loads.append(load)
    for i, (a, b) in enumerate(order):
        slot = 2 * a + b
        loads[i].wait()
        wait(i, core_ref.at[slot])
        add_rows(own_ref.at[slot], own_ref.at[slot], core_ref.at[slot], rows)
        if i in (0, 1):
            send(4 + i, own_ref.at[slot, top, :], x_ref.at[i], over_x)
        if i in (0, 2):
            send(6 + i // 2, own_ref.at[slot, bottom, :], y_ref.at[i // 2], over_y)
    wait(4, x_ref.at[0])
    slot = 2 * x + 1 - y
    add_rows(own_ref.at[slot, top, :], own_ref.at[slot, top, :], x_ref.at[0], half)
    send(8, own_ref.at[slot, top, :], last_ref.at[0], over_y)
    wait(6, y_ref.at[0])
    slot = 2 * (1 - x) + y
    add_rows(own_ref.at[slot, bottom, :], own_ref.at[slot, bottom, :], y_ref.at[0], half)
    send(9, own_ref.at[slot, bottom, :], last_ref.at[1], over_x)
    slot = 2 * x + y
    wait(5, x_ref.at[1])
    add_rows(own_ref.at[slot, top, :], own_ref.at[slot, top, :], x_ref.at[1], half)
    wait(7, y_ref.at[1])
    add_rows(own_ref.at[slot, bottom, :], own_ref.at[slot, bottom, :], y_ref.at[1], half)
    wait(8, last_ref.at[0])
    add_rows(out_ref.at[top, :], own_ref.at[slot, top, :], last_ref.at[0], half)
    wait(9, last_ref.at[1])
    add_rows(out_ref.at[bottom, :], own_ref.at[slot, bottom, :], last_ref.at[1], half)
    for task in sent:
        task.wait_send()


def scatter_plane(values, name, collective_id):
    cols = lax.axis_size("col")
    if cols != 4:
        mine = lax.psum_scatter(
            values, "row", scatter_dimension=0, tiled=True, axis_index_groups=neighbours()
        )
        return lax.psum_scatter(mine, "col", scatter_dimension=1, tiled=True).astype(F32)
    rows, width = values.shape[0] // PAIR, values.shape[1] // cols
    return pl.pallas_call(
        scatter_plane_kernel,
        in_specs=[pl.BlockSpec(memory_space=pl.ANY)],
        out_specs=pl.BlockSpec(memory_space=pltpu.VMEM),
        out_shape=jax.ShapeDtypeStruct((rows, width), F32),
        scratch_shapes=[
            pltpu.VMEM((4, rows, width), BF16),
            pltpu.VMEM((4, rows, width), BF16),
            pltpu.VMEM((2, rows // 2, width), BF16),
            pltpu.VMEM((2, rows // 2, width), BF16),
            pltpu.VMEM((2, rows // 2, width), BF16),
            pltpu.SemaphoreType.DMA((4,)),
            pltpu.SemaphoreType.DMA((10,)),
            pltpu.SemaphoreType.DMA((10,)),
        ],
        compiler_params=pltpu.CompilerParams(
            collective_id=collective_id, has_side_effects=True, vmem_limit_bytes=40 << 20
        ),
        name=name,
    )(values)


def gather_heads_kernel(src_ref, out_ref, local_sem, send_sem, recv_sem):
    rows, width = out_ref.shape[0], src_ref.shape[1]
    x, y, core, row, col = places()
    over_x, over_y, over_core = peers(row, col)
    meet((over_x, over_y, over_core))
    count = rows // 2
    col_y = (col + 2) % 4
    col_core = col + 1 - 2 * core

    def piece(c, a, s):
        at = pl.multiple_of((PAIR * c + a) * width, 128)
        return out_ref.at[pl.ds(s * count, count), pl.ds(at, width)]

    def mine(a, s):
        return src_ref.at[pl.ds(pl.multiple_of(a * rows + s * count, 128), count), :]

    def copy(index, source, place, device):
        return pltpu.make_async_remote_copy(
            source, place, send_sem.at[index], recv_sem.at[index],
            device_id=device, device_id_type=MESH,
        )

    sent = []

    def send(index, source, place, device):
        task = copy(index, source, place, device)
        task.start()
        sent.append(task)

    def wait(index, place):
        copy(index, place, place, over_core).wait_recv()

    local = []
    for s in range(2):
        send(s, mine(1 - x, s), piece(col, x, s), over_x)
        send(2 + s, mine(x, s), piece(col, x, s), over_y)
        task = pltpu.make_async_copy(mine(x, s), piece(col, x, s), local_sem.at[s])
        task.start()
        local.append(task)
    for s in range(2):
        send(4 + s, mine(x, s), piece(col, x, s), over_core)
    for s in range(2):
        wait(s, piece(col, 1 - x, s))
        send(6 + s, piece(col, 1 - x, s), piece(col, 1 - x, s), over_y)
        send(8 + s, piece(col, 1 - x, s), piece(col, 1 - x, s), over_core)
    for s in range(2):
        wait(2 + s, piece(col_y, x, s))
        send(10 + s, piece(col_y, x, s), piece(col_y, x, s), over_core)
    for s in range(2):
        wait(6 + s, piece(col_y, 1 - x, s))
        send(12 + s, piece(col_y, 1 - x, s), piece(col_y, 1 - x, s), over_core)
    far = (col_core + 2) % 4
    for s in range(2):
        wait(4 + s, piece(col_core, x, s))
        wait(8 + s, piece(col_core, 1 - x, s))
        wait(10 + s, piece(far, x, s))
        wait(12 + s, piece(far, 1 - x, s))
    for task in sent:
        task.wait_send()
    for task in local:
        task.wait()


def gather_heads(values, x, collective_id):
    cols = lax.axis_size("col")
    if cols != 4:
        here = in_order(x, pick(values, x, 0), swap_rows(pick(values, 1 - x, 0)), 1)
        return lax.all_gather(here, "col", axis=1, tiled=True)
    rows, width = values.shape[0] // PAIR, values.shape[1]
    return pl.pallas_call(
        gather_heads_kernel,
        in_specs=[pl.BlockSpec(memory_space=pl.ANY)],
        out_specs=pl.BlockSpec(memory_space=pl.ANY),
        out_shape=jax.ShapeDtypeStruct((rows, PAIR * cols * width), values.dtype),
        scratch_shapes=[
            pltpu.SemaphoreType.DMA((2,)),
            pltpu.SemaphoreType.DMA((14,)),
            pltpu.SemaphoreType.DMA((14,)),
        ],
        compiler_params=pltpu.CompilerParams(collective_id=collective_id, has_side_effects=True),
        name="gather_heads",
    )(values)


def scatter_heads_kernel(
    part_ref, out_ref, own_ref, core_ref, y_ref, load_sem, out_sem, send_sem, recv_sem
):
    rows, width = own_ref.shape[1:]
    half = width // PAIR
    count = rows // CHUNKS
    x, y, core, row, col = places()
    over_x, over_y, over_core = peers(row, col)
    meet((over_x, over_y, over_core))

    def copy(index, source, place, device):
        return pltpu.make_async_remote_copy(
            source, place, send_sem.at[index], recv_sem.at[index],
            device_id=device, device_id_type=MESH,
        )

    sent = []

    def send(index, source, place, device):
        task = copy(index, source, place, device)
        task.start()
        sent.append(task)

    def wait(index, place):
        copy(index, place, place, over_core).wait_recv()

    def part(c, s):
        return part_ref.at[
            pl.ds(s * count, count), pl.ds(pl.multiple_of(c * width, 128), width)
        ]

    loads = []
    for i, b in enumerate((1 - y, y)):
        for s in range(CHUNKS):
            at = pl.ds(s * count, count)
            index = i * CHUNKS + s
            send(index, part(2 * b + 1 - core, s), core_ref.at[i, at, :], over_core)
            load = pltpu.make_async_copy(
                part(2 * b + core, s), own_ref.at[i, at, :], load_sem.at[index]
            )
            load.start()
            loads.append(load)
    for i in range(2):
        for s in range(CHUNKS):
            at = pl.ds(s * count, count)
            index = i * CHUNKS + s
            loads[index].wait()
            wait(index, core_ref.at[i, at, :])
            add_rows(own_ref.at[i, at, :], own_ref.at[i, at, :], core_ref.at[i, at, :], count)
            if i == 0:
                send(2 * CHUNKS + s, own_ref.at[0, at, :], y_ref.at[at, :], over_y)
    left, right = pl.ds(0, half), pl.ds(half, half)
    kept = []
    for s in range(CHUNKS):
        at = pl.ds(s * count, count)
        wait(2 * CHUNKS + s, y_ref.at[at, :])
        add_rows(own_ref.at[1, at, :], own_ref.at[1, at, :], y_ref.at[at, :], count)
        place = out_ref.at[pl.ds(pl.multiple_of(x * rows + s * count, 128), count), :]
        theirs = own_ref.at[1, at, pl.ds(pl.multiple_of((1 - x) * half, 128), half)]
        ours = own_ref.at[1, at, pl.ds(pl.multiple_of(x * half, 128), half)]
        send(3 * CHUNKS + s, theirs, place, over_x)
        task = pltpu.make_async_copy(ours, place, out_sem.at[s])
        task.start()
        kept.append(task)
    for s in range(CHUNKS):
        wait(
            3 * CHUNKS + s,
            out_ref.at[pl.ds(pl.multiple_of((1 - x) * rows + s * count, 128), count), :],
        )
    for task in sent:
        task.wait_send()
    for task in kept:
        task.wait()


def scatter_heads(values, x, collective_id):
    cols = lax.axis_size("col")
    if cols != 4:
        mine = lax.psum_scatter(values, "col", scatter_dimension=1, tiled=True)
        return in_order(x, pick(mine, x, 1), swap_rows(pick(mine, 1 - x, 1)), 0)
    rows, width = values.shape[0], values.shape[1] // cols
    return pl.pallas_call(
        scatter_heads_kernel,
        in_specs=[pl.BlockSpec(memory_space=pl.ANY)],
        out_specs=pl.BlockSpec(memory_space=pl.ANY),
        out_shape=jax.ShapeDtypeStruct((PAIR * rows, width // PAIR), BF16),
        scratch_shapes=[
            pltpu.VMEM((2, rows, width), BF16),
            pltpu.VMEM((2, rows, width), BF16),
            pltpu.VMEM((rows, width), BF16),
            pltpu.SemaphoreType.DMA((2 * CHUNKS,)),
            pltpu.SemaphoreType.DMA((CHUNKS,)),
            pltpu.SemaphoreType.DMA((4 * CHUNKS,)),
            pltpu.SemaphoreType.DMA((4 * CHUNKS,)),
        ],
        compiler_params=pltpu.CompilerParams(
            collective_id=collective_id, has_side_effects=True, vmem_limit_bytes=32 << 20
        ),
        name="scatter_heads",
    )(values)


def row_stats(values):
    mean = jnp.mean(values, axis=1, keepdims=True)
    var = jnp.mean(values * values, axis=1, keepdims=True) - mean * mean
    return mean, lax.rsqrt(var + 1e-05)


def norm_backward(grad_norm, unit_values, inv_std, norm_gain):
    full_width = grad_norm.shape[1] * lax.axis_size("col")
    grad_unit = grad_norm * norm_gain
    row_sums = lax.psum(
        (jnp.sum(grad_unit, axis=1), jnp.sum(grad_unit * unit_values, axis=1)), "col"
    )
    grad_in = inv_std * (
        grad_unit
        - row_sums[0][:, None] / full_width
        - unit_values * row_sums[1][:, None] / full_width
    )
    return grad_in, jnp.sum(grad_norm * unit_values, axis=0)


def rotation_tables(positions):
    half = ROT // 2
    inv_freq = BASE ** (-(jnp.arange(half, dtype=F32) * 2.0) / ROT)
    angles = positions.astype(F32)[:, None] * inv_freq[None, :]
    cosine, sine = jnp.cos(angles), jnp.sin(angles)
    rest = HEAD_DIM - ROT
    ones = jnp.ones((positions.shape[0], rest), F32)
    cosine = jnp.concatenate([cosine, cosine, ones], axis=1)
    sine = jnp.concatenate([-sine, sine, 0.0 * ones], axis=1)
    return jnp.tile(cosine, (1, 2)), jnp.tile(sine, (1, 2))


TILE = 256


def norm_tile(values_ref, gain_ref, stats_ref):
    values = values_ref[...].astype(F32)
    mean, inv_std = row_stats(values)
    lane = lax.broadcasted_iota(jnp.int32, stats_ref.shape, 1)
    stats_ref[...] = jnp.where(lane == 0, mean, inv_std)
    return ((values - mean) * inv_std * gain_ref[...]).astype(BF16)


def project_heads_kernel(
    tokens_ref, gain_ref, weight_ref, bias_ref, cos_ref, sin_ref,
    normed_ref, q_ref, k_ref, v_ref, stats_ref,
):
    width = q_ref.shape[1]
    normed = norm_tile(tokens_ref, gain_ref, stats_ref)
    normed_ref[...] = normed
    in_head = lax.broadcasted_iota(jnp.int32, (1, width), 1) % HEAD_DIM
    cosine = jnp.tile(cos_ref[...], (1, width // cos_ref.shape[1]))
    sine = jnp.tile(sin_ref[...], (1, width // sin_ref.shape[1]))
    pre = dot(normed, weight_ref[...]) + bias_ref[...]
    for ref, at, scale in ((q_ref, 0, SCALE), (k_ref, width, 1.0)):
        part = pre[:, at : at + width]
        turned = part * cosine + swap_pairs(part, in_head) * sine
        ref[...] = turned.astype(BF16) * jnp.asarray(scale, BF16)
    v_ref[...] = pre[:, 2 * width :].astype(BF16)


def tiled(columns):
    return pl.BlockSpec((TILE, columns), lambda i: (i, 0))


def whole(shape):
    return pl.BlockSpec(shape, lambda i: (0,) * len(shape))


def project_heads(tokens, gain, weight, bias, cosine, sine):
    rows, depth = tokens.shape
    width = weight.shape[1] // 3
    return pl.pallas_call(
        project_heads_kernel,
        grid=(rows // TILE,),
        in_specs=[
            tiled(depth), whole((1, depth)), whole(weight.shape), whole((1, 3 * width)),
            tiled(cosine.shape[1]), tiled(cosine.shape[1]),
        ],
        out_specs=[tiled(depth)] + [tiled(width)] * 3 + [tiled(8)],
        out_shape=[jax.ShapeDtypeStruct((rows, depth), BF16)]
        + [jax.ShapeDtypeStruct((rows, width), BF16)] * 3
        + [jax.ShapeDtypeStruct((rows, 8), F32)],
        compiler_params=pltpu.CompilerParams(vmem_limit_bytes=48 << 20),
        cost_estimate=pl.CostEstimate(
            flops=6 * rows * depth * width,
            bytes_accessed=4 * rows * depth + 6 * depth * width, transcendentals=0,
        ),
        name="project_heads",
    )(tokens, gain.reshape(1, depth), weight, bias.reshape(1, 3 * width), cosine, sine)


def feed_forward_kernel(
    resid_ref, gain_ref, weight_ref, grad_ref, down_ref,
    normed_ref, hidden_ref, dgate_ref, dup_ref, stats_ref,
):
    lines, _, hidden, width = weight_ref.shape
    normed_ref[...] = norm_tile(resid_ref, gain_ref, stats_ref)
    gate = jnp.zeros((hidden, TILE), F32)
    up = jnp.zeros((hidden, TILE), F32)
    dhidden = jnp.zeros((hidden, TILE), F32)
    for z in range(lines):
        part = normed_ref[:, z * width : (z + 1) * width]
        gate += dot(weight_ref[z, 0], part, (1,), (1,))
        up += dot(weight_ref[z, 1], part, (1,), (1,))
    for c in range(down_ref.shape[0]):
        part = grad_ref[:, c * width : (c + 1) * width]
        dhidden += dot(down_ref[c], part, (1,), (1,))
    sigmoid = 1.0 / (1.0 + jnp.exp(-gate))
    silu = gate * sigmoid
    hidden_ref[...] = (silu * up).astype(BF16)
    dgate_ref[...] = (dhidden * up * sigmoid * (1.0 + gate * (1.0 - sigmoid))).astype(BF16)
    dup_ref[...] = (dhidden * silu).astype(BF16)


def feed_forward(resid, gain, weight, grad, down):
    rows, depth = resid.shape
    hidden = down.shape[1]
    across = pl.BlockSpec((hidden, TILE), lambda i: (0, i))
    return pl.pallas_call(
        feed_forward_kernel,
        grid=(rows // TILE,),
        in_specs=[
            tiled(depth), whole((1, depth)), whole(weight.shape), tiled(depth), whole(down.shape)
        ],
        out_specs=[tiled(depth)] + [across] * 3 + [tiled(8)],
        out_shape=[jax.ShapeDtypeStruct((rows, depth), BF16)]
        + [jax.ShapeDtypeStruct((hidden, rows), BF16)] * 3
        + [jax.ShapeDtypeStruct((rows, 8), F32)],
        compiler_params=pltpu.CompilerParams(vmem_limit_bytes=56 << 20),
        cost_estimate=pl.CostEstimate(
            flops=6 * rows * depth * hidden,
            bytes_accessed=6 * rows * depth + 6 * depth * hidden, transcendentals=0,
        ),
        name="feed_forward",
    )(resid, gain.reshape(1, depth), weight, grad, down)


def weight_grads_kernel(*refs):
    *left_refs, right_ref, out_ref = refs
    for i, left_ref in enumerate(left_refs):
        out_ref[0, i] = dot(left_ref[...], right_ref[...]).astype(BF16)


def weight_grads(lefts, right, width, name):
    hidden, rows = lefts[0].shape
    blocks = right.shape[1] // width
    return pl.pallas_call(
        weight_grads_kernel,
        grid=(blocks,),
        in_specs=[whole((hidden, rows))] * len(lefts)
        + [pl.BlockSpec((rows, width), lambda i: (0, i))],
        out_specs=pl.BlockSpec((1, len(lefts), hidden, width), lambda i: (i, 0, 0, 0)),
        out_shape=jax.ShapeDtypeStruct((blocks, len(lefts), hidden, width), BF16),
        compiler_params=pltpu.CompilerParams(vmem_limit_bytes=56 << 20),
        cost_estimate=pl.CostEstimate(
            flops=2 * len(lefts) * rows * hidden * right.shape[1],
            bytes_accessed=2 * rows * right.shape[1], transcendentals=0,
        ),
        name=name,
    )(*lefts, right)


def back_project_kernel(*refs):
    *left_refs, weight_ref, out_ref = refs
    width = weight_ref.shape[-1]
    lefts = [ref[...].T for ref in left_refs]
    for z in range(weight_ref.shape[0]):
        total = sum(dot(left, weight_ref[z, i]) for i, left in enumerate(lefts))
        out_ref[:, z * width : (z + 1) * width] = total.astype(BF16)


def back_project(lefts, weight, name):
    hidden, rows = lefts[0].shape
    depth = weight.shape[0] * weight.shape[-1]
    return pl.pallas_call(
        back_project_kernel,
        grid=(rows // TILE,),
        in_specs=[pl.BlockSpec((hidden, TILE), lambda i: (0, i))] * len(lefts)
        + [whole(weight.shape)],
        out_specs=tiled(depth),
        out_shape=jax.ShapeDtypeStruct((rows, depth), BF16),
        compiler_params=pltpu.CompilerParams(vmem_limit_bytes=48 << 20),
        cost_estimate=pl.CostEstimate(
            flops=2 * len(lefts) * rows * hidden * depth,
            bytes_accessed=2 * rows * depth, transcendentals=0,
        ),
        name=name,
    )(*lefts, weight)


def per_device(
    tokens, segment_ids, positions, attn_gain, query_weight, query_bias, key_weight, key_bias,
    value_weight, value_bias, out_weight, mlp_gain, gate_weight, up_weight, down_weight, out_grad,
):
    count, width = tokens.shape
    lines = lax.axis_size("row") // PAIR
    cols = lax.axis_size("col")
    row = lax.axis_index("row")
    col = lax.axis_index("col")
    x = row % PAIR
    half = width // PAIR

    qkv_weight = gather_line(
        jnp.concatenate(
            [own_columns(w, x) for w in (query_weight, key_weight, value_weight)], axis=1
        )
    )
    out_line = gather_line(out_weight)
    down_line = gather_line(down_weight)
    ffn_weight = gather_line(
        jnp.stack([own_units(w, x) for w in (gate_weight, up_weight)])[None]
    )
    out_other = swap_rows(out_line)
    depth = out_weight.shape[0]
    full = (lines, 1, depth, width)
    out_all = in_order(x, out_line.reshape(full), out_other.reshape(full), 1).reshape(-1, width)
    hidden = ffn_weight.shape[2]
    down_all = lax.all_to_all(
        down_line.reshape(lines, hidden, width), "col", split_axis=0, concat_axis=0, tiled=True
    )

    bias = jnp.concatenate(
        [pick(b, x, 0) for b in (query_bias, key_bias, value_bias)], axis=0
    )
    gains = lax.all_gather(jnp.stack([attn_gain, mlp_gain]), "col", axis=1, tiled=True)
    own_place = jnp.stack([positions, segment_ids])
    place = in_order(x, own_place, swap_rows(own_place), 1)
    cosine, sine = rotation_tables(place[0])
    plane_segments = place[1]

    tokens_all = gather_plane(tokens, "gather_tokens", 0)
    grad_all = gather_plane(out_grad, "gather_cotangent", 1)
    normed_first, queries, keys, values, stats_first = project_heads(
        tokens_all, gains[0], qkv_weight, bias, cosine, sine
    )
    attended, lse = attention_forward(queries, keys, values, plane_segments)
    attn_all = gather_heads(attended, x, 2)
    inputs = tokens.astype(F32)
    resid = inputs + dot(attn_all, out_all)

    resid_all = gather_plane(resid.astype(BF16), "gather_residual", 3)
    normed_second, hidden_low, grad_gate, grad_up, stats_second = feed_forward(
        resid_all, gains[1], ffn_weight, grad_all, down_all
    )
    grad_ffn = scatter_line(weight_grads((grad_gate, grad_up), normed_second, width, "ffn_grads"))
    grad_second = scatter_plane(
        back_project((grad_gate, grad_up), ffn_weight, "back_ffn"), "scatter_second", 4
    )
    grad_down = weight_grads((hidden_low,), grad_all, width, "down_grads")
    grad_down = lax.all_to_all(
        grad_down.reshape(cols, hidden, width), "col", split_axis=0, concat_axis=0, tiled=True
    )
    grad_down = scatter_line(grad_down.reshape(lines * hidden, width))
    own_stats = pick(stats_second, x, 0)
    mean_here, inv_here = own_stats[:, 0:1], own_stats[:, 1:2]
    grad_resid, mlp_gain_part = norm_backward(
        grad_second, (resid - mean_here) * inv_here, inv_here, mlp_gain
    )
    grad_resid = grad_resid + out_grad.astype(F32)
    grad_resid_low = grad_resid.astype(BF16)

    grad_attn = scatter_heads(dot(grad_resid_low, out_all, (1,), (1,)).astype(BF16), x, 5)
    grad_qkv, bias_sums = attention_backward(
        queries, keys, values, grad_attn, lse, cosine, sine, plane_segments
    )
    grad_out_weight = dot(attn_all, grad_resid_low, (0,), (0,)).astype(BF16)
    grad_out_weight = grad_out_weight.reshape(lines, PAIR, depth, width)
    grad_out_weight = pick(grad_out_weight, x, 1) + swap_rows(pick(grad_out_weight, 1 - x, 1))
    grad_out_weight = scatter_line(grad_out_weight.reshape(lines * depth, width))
    grad_qkv_weight = scatter_line(dot(normed_first, grad_qkv, (0,), (0,)).astype(BF16))
    grad_first = scatter_plane(
        dot(grad_qkv, qkv_weight, (1,), (1,)).astype(BF16), "scatter_first", 6
    )
    own_stats = pick(stats_first, x, 0)
    mean_here, inv_here = own_stats[:, 0:1], own_stats[:, 1:2]
    grad_input, attn_gain_part = norm_backward(
        grad_first, (inputs - mean_here) * inv_here, inv_here, attn_gain
    )
    tokens_grad = grad_input + grad_resid
    mixed = resid + scatter_plane(
        back_project((hidden_low,), down_all[:, None], "mix"), "scatter_mixed", 7
    )
    mixed = mixed.astype(BF16)

    bias_part = jnp.sum(bias_sums, axis=(0, 1)).reshape(3, half)
    bias_part = jnp.where(
        (jnp.arange(PAIR) == x)[None, :, None], bias_part[:, None, :], 0.0
    ).reshape(3, width)
    vectors = lax.psum(
        jnp.concatenate([bias_part, attn_gain_part[None], mlp_gain_part[None]], axis=0), "row"
    )
    wide = lambda grad: own_rows(grad, x).astype(F32)
    return (
        mixed,
        tokens_grad,
        vectors[3],
        wide(grad_qkv_weight[:, :half]),
        vectors[0],
        wide(grad_qkv_weight[:, half : 2 * half]),
        vectors[1],
        wide(grad_qkv_weight[:, 2 * half :]),
        vectors[2],
        grad_out_weight.astype(F32),
        vectors[4],
        own_inputs(grad_ffn[0, 0], x).T.astype(F32),
        own_inputs(grad_ffn[0, 1], x).T.astype(F32),
        grad_down.astype(F32),
    )


def solution(mesh):
    grid, rows, cols = P("row", "col"), P("row"), P("col")
    in_specs = (
        grid, rows, rows, cols, grid, cols, grid, cols, grid, cols, grid, cols, grid, grid, grid, grid,
    )
    out_specs = (
        grid, grid, cols, grid, cols, grid, cols, grid, cols, grid, cols, grid, grid, grid,
    )
    return jax.shard_map(
        per_device, mesh=mesh, in_specs=in_specs, out_specs=out_specs, check_vma=False
    )
```

```python
import functools

import jax
import jax.numpy as jnp
from jax import lax
from jax.experimental import pallas as pl
from jax.experimental.pallas import tpu as pltpu
from jax.sharding import PartitionSpec as P

HEAD_DIM = 64
ROT = 16
SEQ = 1024
BASE = 10000.0
NEG = -1e30
F32 = jnp.float32
BF16 = jnp.bfloat16
SCALE = HEAD_DIM**-0.5
MESH = pl.DeviceIdType.MESH
QBLOCK = 256
PAIR = 2


def dot(left, right, left_dims=(1,), right_dims=(0,)):
    return lax.dot_general(
        left, right, ((left_dims, right_dims), ((), ())), preferred_element_type=F32
    )


def taking(microseconds):
    return pl.CostEstimate(
        flops=microseconds * 10**9, bytes_accessed=microseconds * 10**6, transcendentals=0
    )


def swap_pairs(values, lane):
    half = ROT // 2
    width = values.shape[1]
    ahead = pltpu.roll(values, width - half, 1)
    behind = pltpu.roll(values, half, 1)
    return jnp.where(lane < half, ahead, behind)


def attention_forward_kernel(
    q_ref, k_ref, v_ref, seg_col_ref, seg_row_ref, o_ref, lse_ref, acc_ref, lse_scratch
):
    width = q_ref.shape[1]
    heads = width // HEAD_DIM
    full_lane = lax.broadcasted_iota(jnp.int32, (1, width), 1)
    acc_ref[...] = jnp.zeros_like(acc_ref)
    lse_lane = lax.broadcasted_iota(jnp.int32, (1, lse_scratch.shape[1]), 1)

    @pl.loop(0, heads)
    def _(head):
        mask = full_lane // HEAD_DIM == head
        for start in range(0, SEQ, QBLOCK):
            keys = start + QBLOCK
            rows = slice(start, keys)
            queries = jnp.where(mask, q_ref[rows, :], jnp.zeros((), BF16))
            scores = dot(queries, k_ref[:keys, :], (1,), (1,))
            query_pos = start + lax.broadcasted_iota(jnp.int32, scores.shape, 0)
            key_pos = lax.broadcasted_iota(jnp.int32, scores.shape, 1)
            seen = (seg_col_ref[rows, :] == seg_row_ref[0, :, :keys]) & (key_pos <= query_pos)
            scores = jnp.where(seen, scores, NEG)
            peak = jnp.max(scores, axis=1, keepdims=True)
            weights = jnp.exp(scores - peak)
            total = jnp.sum(weights, axis=1, keepdims=True)
            probs = (weights * (1.0 / total)).astype(BF16)
            output = dot(probs, v_ref[:keys, :])
            acc_ref[rows, :] = jnp.where(mask, output, acc_ref[rows, :])
            lse_scratch[rows, :] = jnp.where(
                lse_lane == head, peak + jnp.log(total), lse_scratch[rows, :]
            )

    o_ref[...] = acc_ref[...].astype(BF16)
    lse_ref[0] = lse_scratch[...].T[: lse_ref.shape[1], :]


def attention_forward_exchange_kernel(*refs):
    ins, (blocks_ref, _), outs, all_ref = refs[:5], refs[5:7], refs[7:9], refs[9]
    scratch, sems = refs[10:12], refs[12:]
    exchange_beside(
        lambda: attention_forward_kernel(*ins, *outs, *scratch),
        blocks_ref, all_ref, (1, 3), None, *sems,
    )


def attention_forward(queries, keys, values, segments, blocks=None, partly=None, collective_id=None):
    rows, width = queries.shape
    seqs = rows // SEQ
    block = lambda columns: pl.BlockSpec((SEQ, columns), lambda s: (s, 0))
    in_specs = [block(width)] * 3 + [block(1), pl.BlockSpec((1, 1, SEQ), lambda s: (s, 0, 0))]
    out_specs = [block(width), pl.BlockSpec((1, 8, SEQ), lambda s: (s, 0, 0))]
    out_shape = [
        jax.ShapeDtypeStruct((rows, width), BF16), jax.ShapeDtypeStruct((seqs, 8, SEQ), F32)
    ]
    operands = [queries, keys, values, segments.reshape(rows, 1), segments.reshape(seqs, 1, SEQ)]
    scratch = [pltpu.VMEM((SEQ, width), F32), pltpu.VMEM((SEQ, 128), F32)]
    params, aliases, kernel = {}, {}, attention_forward_kernel
    if blocks is not None:
        anywhere = pl.BlockSpec(memory_space=pl.ANY)
        in_specs, out_specs = in_specs + [anywhere] * 2, out_specs + [anywhere]
        out_shape = out_shape + [jax.ShapeDtypeStruct(blocks.shape, BF16)]
        operands = operands + [blocks, partly]
        scratch = scratch + [pltpu.SemaphoreType.DMA((2,))] * 2
        params = dict(collective_id=collective_id, has_side_effects=True)
        aliases, kernel = {6: 2}, attention_forward_exchange_kernel
    return pl.pallas_call(
        kernel,
        grid=(seqs,),
        in_specs=in_specs,
        out_specs=out_specs,
        out_shape=out_shape,
        scratch_shapes=scratch,
        input_output_aliases=aliases,
        compiler_params=pltpu.CompilerParams(vmem_limit_bytes=56 << 20, **params),
        cost_estimate=taking(21),
        name="attention_forward",
    )(*operands)


def attention_backward_kernel(
    q_ref, k_ref, v_ref, do_ref, lse_ref, cos_ref, sin_ref, seg_col_ref, seg_row_ref,
    grad_ref, sums_ref, dq_ref, dk_ref, dv_ref,
):
    width = q_ref.shape[1]
    heads = width // HEAD_DIM
    full_lane = lax.broadcasted_iota(jnp.int32, (1, width), 1)
    in_head = full_lane % HEAD_DIM
    for ref in (dq_ref, dk_ref, dv_ref):
        ref[...] = jnp.zeros_like(ref)

    @pl.loop(0, heads)
    def _(head):
        mask = full_lane // HEAD_DIM == head
        nothing = jnp.zeros((), BF16)
        for start in range(0, SEQ, QBLOCK):
            keys = start + QBLOCK
            rows = slice(start, keys)
            queries = jnp.where(mask, q_ref[rows, :], nothing)
            grads = jnp.where(mask, do_ref[rows, :], nothing)
            scores = dot(k_ref[:keys, :], queries, (1,), (1,))
            key_pos = lax.broadcasted_iota(jnp.int32, scores.shape, 0)
            query_pos = start + lax.broadcasted_iota(jnp.int32, scores.shape, 1)
            seen = (seg_col_ref[:keys, :] == seg_row_ref[0, :, rows]) & (key_pos <= query_pos)
            probs = jnp.where(
                seen, jnp.exp(scores - lse_ref[0, pl.ds(head, 1), rows]), 0.0
            )
            dv_ref[:keys, :] += dot(probs.astype(BF16), grads)
            grad_probs = dot(v_ref[:keys, :], grads, (1,), (1,))
            delta = jnp.sum(probs * grad_probs, axis=0, keepdims=True)
            grad_scores = (probs * (grad_probs - delta)).astype(BF16)
            dk_ref[:keys, :] += dot(grad_scores, queries)
            masked_keys = jnp.where(mask, k_ref[:keys, :], nothing)
            dq_ref[rows, :] += dot(grad_scores, masked_keys, (0,), (0,))

    cosine = jnp.tile(cos_ref[...], (1, width // cos_ref.shape[1]))
    sine = jnp.tile(sin_ref[...], (1, width // sin_ref.shape[1]))
    for part, (ref, scale) in enumerate(((dq_ref, SCALE), (dk_ref, 1.0), (dv_ref, None))):
        grad = ref[...]
        if scale is not None:
            grad = grad * scale
            grad = grad * cosine - swap_pairs(grad, in_head) * sine
        low = grad.astype(BF16)
        columns = slice(part * width, (part + 1) * width)
        grad_ref[:, columns] = low
        sums_ref[0, :, columns] = jnp.sum(low.astype(F32), axis=0, keepdims=True)


def attention_backward_exchange_kernel(*refs):
    ins, blocks_ref, outs, all_ref = refs[:9], refs[9], refs[10:12], refs[12]
    scratch, (stage, local_sem, *sems) = refs[13:16], refs[16:]
    exchange_beside(
        lambda: attention_backward_kernel(*ins, *outs, *scratch),
        blocks_ref, all_ref, (2, 3, 1), (stage, local_sem), *sems,
    )


def attention_backward(
    queries, keys, values, grad_out, lse, cosine, sine, segments, blocks=None, collective_id=None
):
    rows, width = queries.shape
    seqs = rows // SEQ
    block = lambda columns: pl.BlockSpec((SEQ, columns), lambda s: (s, 0))
    in_specs = [block(width)] * 4 + [
        pl.BlockSpec((1, 8, SEQ), lambda s: (s, 0, 0)),
        block(cosine.shape[1]),
        block(cosine.shape[1]),
        block(1),
        pl.BlockSpec((1, 1, SEQ), lambda s: (s, 0, 0)),
    ]
    out_specs = [block(3 * width), pl.BlockSpec((1, 1, 3 * width), lambda s: (s, 0, 0))]
    out_shape = [
        jax.ShapeDtypeStruct((rows, 3 * width), BF16),
        jax.ShapeDtypeStruct((seqs, 1, 3 * width), F32),
    ]
    operands = [
        queries, keys, values, grad_out, lse, cosine, sine,
        segments.reshape(rows, 1), segments.reshape(seqs, 1, SEQ),
    ]
    scratch = [pltpu.VMEM((SEQ, width), F32)] * 3
    params, kernel = {}, attention_backward_kernel
    if blocks is not None:
        anywhere = pl.BlockSpec(memory_space=pl.ANY)
        in_specs, out_specs = in_specs + [anywhere], out_specs + [anywhere]
        out_shape = out_shape + [jax.ShapeDtypeStruct(blocks.shape, BF16)]
        operands = operands + [blocks]
        scratch = scratch + [pltpu.VMEM(blocks.shape[1:], BF16), pltpu.SemaphoreType.DMA]
        scratch = scratch + [pltpu.SemaphoreType.DMA((3,))] * 2
        params = dict(collective_id=collective_id, has_side_effects=True)
        kernel = attention_backward_exchange_kernel
    return pl.pallas_call(
        kernel,
        grid=(seqs,),
        in_specs=in_specs,
        out_specs=out_specs,
        out_shape=out_shape,
        scratch_shapes=scratch,
        compiler_params=pltpu.CompilerParams(vmem_limit_bytes=56 << 20, **params),
        cost_estimate=taking(33),
        name="attention_backward",
    )(*operands)


def row_pairs():
    return [(r, r ^ 1) for r in range(lax.axis_size("row"))]


def row_lines():
    size = lax.axis_size("row")
    return [list(range(start, size, PAIR)) for start in range(PAIR)]


def neighbours():
    return [list(range(r, r + PAIR)) for r in range(0, lax.axis_size("row"), PAIR)]


def swap_rows(values):
    return lax.ppermute(values, "row", row_pairs())


def after(value, *others):
    return lax.optimization_barrier((value,) + others)[0]


def gather_line(values, axis=0):
    return lax.all_gather(values, "row", axis=axis, tiled=True, axis_index_groups=row_lines())


def scatter_line(values, axis=0):
    return lax.psum_scatter(
        values, "row", scatter_dimension=axis, tiled=True, axis_index_groups=row_lines()
    )


def pick(values, index, axis):
    size = values.shape[axis] // PAIR
    return lax.dynamic_slice_in_dim(values, index * size, size, axis)


def in_order(x, own, other, axis):
    return jnp.where(
        x == 0, jnp.concatenate([own, other], axis), jnp.concatenate([other, own], axis)
    )


def own_columns(weight, x):
    return in_order(x, pick(weight, x, 1), swap_rows(pick(weight, 1 - x, 1)), 0)


def own_units(weight, x):
    kept, sent = pick(weight, x, 1).T, pick(weight, 1 - x, 1).T
    return in_order(x, kept, swap_rows(sent), 1)


def own_rows(grad, x):
    return pick(grad, x, 0), swap_rows(pick(grad, 1 - x, 0))


def places():
    row, col = lax.axis_index("row"), lax.axis_index("col")
    return row % PAIR, col // 2, col % 2, row, col


def peers(row, col):
    x = row % PAIR
    over_x = (row + 1 - 2 * x, col)
    over_y = (row, (col + 2) % 4)
    over_core = (row, col + 1 - 2 * (col % 2))
    return over_x, over_y, over_core


def meet(devices):
    barrier = pltpu.get_barrier_semaphore()
    for device in devices:
        pl.semaphore_signal(barrier, inc=1, device_id=device, device_id_type=MESH)
    pl.semaphore_wait(barrier, len(devices))


def block_at(ref, a, col, rows, width, start, count):
    at = pl.multiple_of(a * rows + start, 128)
    return ref.at[pl.ds(at, count), pl.ds(pl.multiple_of(col * width, 128), width)]


CHUNKS = 4


class Copies:
    def __init__(self, send_sem, recv_sem, over_core):
        self.send_sem, self.recv_sem, self.any = send_sem, recv_sem, over_core
        self.sent = []

    def copy(self, index, source, place, device):
        return pltpu.make_async_remote_copy(
            source, place, self.send_sem.at[index], self.recv_sem.at[index],
            device_id=device, device_id_type=MESH,
        )

    def send(self, index, source, place, device):
        task = self.copy(index, source, place, device)
        task.start()
        self.sent.append(task)

    def wait(self, index, place):
        self.copy(index, place, place, self.any).wait_recv()

    def finish(self):
        for task in self.sent:
            task.wait_send()
        self.sent = []


class PlaneGather:
    def __init__(self, copies, base, src_ref, out_ref, local_sem, over_y=CHUNKS // 2):
        self.copies, self.base, self.src, self.out = copies, base, src_ref, out_ref
        self.local_sem = local_sem
        self.rows, self.width = src_ref.shape
        self.count = self.rows // CHUNKS
        self.x, self.y, self.core, self.row, self.col = places()
        self.over_x, self.over_y, self.over_core = peers(self.row, self.col)
        self.col_y = (self.col + 2) % 4
        self.col_core = self.col + 1 - 2 * self.core
        self.first = list(range(over_y))
        self.second = list(range(over_y, CHUNKS))

    def piece(self, a, c, s):
        return block_at(self.out, a, c, self.rows, self.width, s * self.count, self.count)

    def own(self, s):
        return self.src.at[pl.ds(s * self.count, self.count), :]

    def send(self, group, s, source, place, device):
        self.copies.send(self.base + group * CHUNKS + s, source, place, device)

    def pass_on(self, group, a, c, s, device):
        self.send(group, s, self.piece(a, c, s), self.piece(a, c, s), device)

    def wait(self, group, a, c, s):
        self.copies.wait(self.base + group * CHUNKS + s, self.piece(a, c, s))

    def start_x(self):
        for s in self.first + self.second:
            self.send(0, s, self.own(s), self.piece(self.x, self.col, s), self.over_x)

    def start_y(self):
        for s in self.second + self.first:
            self.send(1, s, self.own(s), self.piece(self.x, self.col, s), self.over_y)

    def start_core(self):
        self.local = pltpu.make_async_copy(
            self.src, block_at(self.out, self.x, self.col, self.rows, self.width, 0, self.rows),
            self.local_sem,
        )
        self.local.start()
        for s in range(CHUNKS):
            self.send(4, s, self.own(s), self.piece(self.x, self.col, s), self.over_core)

    def near(self, i):
        s, t = (self.first + self.second)[i], (self.second + self.first)[i]
        x, col, col_y = self.x, self.col, self.col_y
        self.wait(0, 1 - x, col, s)
        if s in self.first:
            self.pass_on(2, 1 - x, col, s, self.over_y)
        self.pass_on(5, 1 - x, col, s, self.over_core)
        self.wait(1, x, col_y, t)
        if t in self.second:
            self.pass_on(2, x, col_y, t, self.over_x)
        self.pass_on(6, x, col_y, t, self.over_core)

    def far(self):
        for u in range(CHUNKS):
            self.wait(2, 1 - self.x, self.col_y, u)
            self.pass_on(7, 1 - self.x, self.col_y, u, self.over_core)

    def finish(self):
        other, corner = self.col_core, (self.col_core + 2) % 4
        for group, (a, c) in enumerate(
            ((self.x, other), (1 - self.x, other), (self.x, corner), (1 - self.x, corner))
        ):
            for s in range(CHUNKS):
                self.wait(4 + group, a, c, s)
        self.local.wait()


def gather_plane_kernel(src_ref, out_ref, local_sem, send_sem, recv_sem):
    _, _, _, row, col = places()
    devices = peers(row, col)
    meet(devices)
    copies = Copies(send_sem, recv_sem, devices[2])
    gather = PlaneGather(copies, 0, src_ref, out_ref, local_sem)
    gather.start_x()
    gather.start_y()
    gather.start_core()
    for i in range(CHUNKS):
        gather.near(i)
    gather.far()
    gather.finish()
    copies.finish()


LINES = 4


class LineGather:
    def __init__(self, up_send, up_recv, down_send, down_recv, block):
        self.up, self.down, self.block = (up_send, up_recv), (down_send, down_recv), block
        self.row, self.col = lax.axis_index("row"), lax.axis_index("col")
        self.z = self.row // PAIR

    def task(self, sems, step, source, device):
        send, recv = sems
        place = self.block(source)
        return pltpu.make_async_remote_copy(
            place, place, send.at[step], recv.at[step],
            device_id=(device, self.col), device_id_type=MESH,
        )

    def upward(self, step):
        source = jnp.maximum(self.z - step, 0)
        return self.task(self.up, step, source, jnp.minimum(self.row + PAIR, PAIR * LINES - 1))

    def downward(self, step):
        source = jnp.minimum(self.z + step, LINES - 1)
        return self.task(self.down, step, source, jnp.maximum(self.row - PAIR, 0))

    def start(self, step):
        @pl.when((self.z >= step) & (self.z < LINES - 1))
        def _():
            self.upward(step).start()

        @pl.when((self.z + step < LINES) & (self.z > 0))
        def _():
            self.downward(step).start()

    def receive(self, step):
        @pl.when(self.z >= step)
        def _():
            source = jnp.maximum(self.z - step, 0)
            self.task(self.up, step - 1, source, self.row).wait_recv()

        @pl.when(self.z + step < LINES)
        def _():
            source = jnp.minimum(self.z + step, LINES - 1)
            self.task(self.down, step - 1, source, self.row).wait_recv()

    def hop(self, step):
        self.receive(step)
        if step < LINES - 1:
            self.start(step)

    def finish(self):
        for step in range(LINES - 1):

            @pl.when((self.z >= step) & (self.z < LINES - 1))
            def _():
                self.upward(step).wait_send()

            @pl.when((self.z + step < LINES) & (self.z > 0))
            def _():
                self.downward(step).wait_send()


def gather_first_kernel(
    tokens_ref, grad_ref, query_ref, key_ref, value_ref, out_weight_ref, gate_ref, up_ref,
    gains_ref, places_ref,
    tokens_all_ref, grad_all_ref, qkv_ref, out_all_ref, ffn_ref, gains_all_ref, places_all_ref,
    turned_ref, local_sem, send_sem, recv_sem, swap_send, swap_recv, *line_sems,
):
    x, y, core, row, col = places()
    z = row // PAIR
    over_x, over_y, over_core = peers(row, col)
    over_far = (row, 3 - col)
    size = PAIR * LINES
    meet(
        (
            over_x, over_y, over_core, over_far,
            ((row + PAIR) % size, col), ((row + size - PAIR) % size, col),
        )
    )
    copies = Copies(send_sem, recv_sem, over_core)
    depth, width = out_weight_ref.shape
    half = width // PAIR
    units = ffn_ref.shape[2]
    base = 16 * CHUNKS
    local = []

    def keep(source, place):
        task = pltpu.make_async_copy(source, place, local_sem.at[2 + len(local)])
        task.start()
        local.append(task)

    def part(r, w):
        return qkv_ref.at[
            pl.ds(pl.multiple_of(r * depth, 128), depth), pl.ds(w * half, half)
        ]

    def out_block(z, x):
        return out_all_ref.at[pl.ds(pl.multiple_of((PAIR * z + x) * depth, 128), depth), :]

    def ffn_block(w, x):
        return ffn_ref.at[0, w, :, pl.ds(pl.multiple_of(x * depth, 128), depth)]

    def gains_block(c):
        return gains_all_ref.at[:, pl.ds(pl.multiple_of(c * width, 128), width)]

    def places_block(a):
        rows = places_ref.shape[1]
        return places_all_ref.at[:, pl.ds(pl.multiple_of(a * rows, 128), rows)]

    for w, ref in enumerate((query_ref, key_ref, value_ref)):
        theirs = ref.at[:, pl.ds(pl.multiple_of((1 - x) * half, 128), half)]
        copies.send(base + w, theirs, part(row, w), over_x)
        keep(ref.at[:, pl.ds(pl.multiple_of(x * half, 128), half)], part(row, w))
    keep(out_weight_ref, out_block(z, x))
    keep(gains_ref, gains_block(col))
    keep(places_ref, places_block(x))
    tokens = PlaneGather(copies, 0, tokens_ref, tokens_all_ref, local_sem.at[0], CHUNKS)
    grad = PlaneGather(copies, 8 * CHUNKS, grad_ref, grad_all_ref, local_sem.at[1], CHUNKS)
    tokens.start_y()
    tokens.start_core()
    copies.send(base + 5, places_ref, places_block(x), over_x)
    for i, device in enumerate((over_core, over_y, over_far)):
        copies.send(base + 6 + i, gains_ref, gains_block(col), device)
    for w in range(3):
        local[w].wait()
        copies.wait(base + w, part(row + 1 - 2 * x, w))
    heads = LineGather(
        *line_sems[:4],
        lambda at: qkv_ref.at[pl.ds(pl.multiple_of(at * PAIR * depth, 128), PAIR * depth), :],
    )
    outs = LineGather(*line_sems[4:], lambda at: out_block(at, x))

    def swap_out(z, x):
        block = out_block(z, x)
        return pltpu.make_async_remote_copy(
            block, block, swap_send.at[z], swap_recv.at[z], device_id=over_x, device_id_type=MESH
        )

    def swap_outs(step):
        @pl.when(z >= step)
        def _():
            swap_out(jnp.maximum(z - step, 0), x).start()

        @pl.when(z + step < LINES)
        def _():
            swap_out(jnp.minimum(z + step, LINES - 1), x).start()

    heads.start(0)
    tokens.start_x()
    for w, ref in enumerate((gate_ref, up_ref)):
        for j in range(PAIR * units // 128):
            turned_ref[w, j * 128 : (j + 1) * 128, :] = ref[:, j * 128 : (j + 1) * 128].T
    for i in range(CHUNKS - 1):
        tokens.near(i)
    local[3].wait()
    outs.start(0)
    heads.hop(1)
    tokens.near(CHUNKS - 1)
    for w in range(2):
        theirs = turned_ref.at[w, pl.ds(pl.multiple_of((1 - x) * units, 16), units), :]
        copies.send(base + 3 + w, theirs, ffn_block(w, x), over_x)
        keep(turned_ref.at[w, pl.ds(pl.multiple_of(x * units, 16), units), :], ffn_block(w, x))
    swap_out(z, x).start()
    grad.start_x()
    grad.start_y()
    grad.start_core()
    tokens.far()
    heads.hop(2)
    outs.hop(1)
    swap_outs(1)
    for i in range(CHUNKS - 1):
        grad.near(i)
    heads.hop(3)
    outs.hop(2)
    swap_outs(2)
    grad.near(CHUNKS - 1)
    grad.far()
    outs.hop(3)
    swap_outs(3)
    for at in range(LINES):
        swap_out(at, 1 - x).wait_recv()
    for w in range(2):
        copies.wait(base + 3 + w, ffn_block(w, 1 - x))
    copies.wait(base + 5, places_block(1 - x))
    for i, c in enumerate((col + 1 - 2 * core, (col + 2) % 4, 3 - col)):
        copies.wait(base + 6 + i, gains_block(c))
    for at in range(LINES):
        swap_out(at, x).wait_send()
    for task in local[3 + 1 :]:
        task.wait()
    tokens.finish()
    grad.finish()
    heads.finish()
    outs.finish()
    copies.finish()


def gather_first(
    tokens, grad, query, key, value, out_weight, gate, up, gains, places, collective_id
):
    rows, width = tokens.shape
    depth = out_weight.shape[0]
    units = gate.shape[1] // PAIR
    shape = lambda *dims: jax.ShapeDtypeStruct(dims, BF16)
    sems = lambda n: pltpu.SemaphoreType.DMA((n,))
    return pl.pallas_call(
        gather_first_kernel,
        in_specs=[pl.BlockSpec(memory_space=pltpu.VMEM)] * 10,
        out_specs=[pl.BlockSpec(memory_space=pl.ANY)] * 7,
        out_shape=[
            shape(PAIR * rows, 4 * width), shape(PAIR * rows, 4 * width),
            shape(PAIR * LINES * depth, 3 * width // PAIR), shape(PAIR * LINES * depth, width),
            shape(1, 2, units, PAIR * depth),
            jax.ShapeDtypeStruct((gains.shape[0], 4 * width), F32),
            jax.ShapeDtypeStruct((places.shape[0], PAIR * rows), jnp.int32),
        ],
        scratch_shapes=[
            pltpu.VMEM((2, PAIR * units, depth), BF16),
            sems(10), sems(16 * CHUNKS + 9), sems(16 * CHUNKS + 9), sems(4), sems(4),
        ]
        + [sems(3)] * 8,
        compiler_params=pltpu.CompilerParams(
            collective_id=collective_id, has_side_effects=True, vmem_limit_bytes=60 << 20
        ),
        cost_estimate=taking(110),
        name="gather_first",
    )(tokens, grad, query, key, value, out_weight, gate, up, gains, places)


def gather_plane(values, name, collective_id):
    cols = lax.axis_size("col")
    if cols != 4:
        across = lax.all_gather(values, "col", axis=1, tiled=True)
        return lax.all_gather(across, "row", axis=0, tiled=True, axis_index_groups=neighbours())
    rows, width = values.shape
    return pl.pallas_call(
        gather_plane_kernel,
        in_specs=[pl.BlockSpec(memory_space=pltpu.VMEM)],
        out_specs=pl.BlockSpec(memory_space=pl.ANY),
        out_shape=jax.ShapeDtypeStruct((PAIR * rows, cols * width), values.dtype),
        scratch_shapes=[
            pltpu.SemaphoreType.DMA,
            pltpu.SemaphoreType.DMA((8 * CHUNKS,)),
            pltpu.SemaphoreType.DMA((8 * CHUNKS,)),
        ],
        cost_estimate=taking(40),
        compiler_params=pltpu.CompilerParams(collective_id=collective_id, has_side_effects=True),
        name=name,
    )(values)


def add_rows(out_ref, left_ref, right_ref, rows, step=64):
    @pl.loop(0, rows // step)
    def _(i):
        at = pl.ds(pl.multiple_of(i * step, step), step)
        total = left_ref[at, :].astype(F32) + right_ref[at, :].astype(F32)
        out_ref[at, :] = total.astype(out_ref.dtype)


def scatter_plane_kernel(
    part_ref, out_ref, own_ref, core_ref, x_ref, y_ref, last_ref,
    load_sem, send_sem, recv_sem,
):
    rows, width = own_ref.shape[1:]
    half = rows // 2
    x, y, core, row, col = places()
    over_x, over_y, over_core = peers(row, col)
    meet((over_x, over_y, over_core))
    top, bottom = pl.ds(0, half), pl.ds(half, half)

    def copy(index, source, place, device):
        return pltpu.make_async_remote_copy(
            source, place, send_sem.at[index], recv_sem.at[index],
            device_id=device, device_id_type=MESH,
        )

    sent = []

    def send(index, source, place, device):
        task = copy(index, source, place, device)
        task.start()
        sent.append(task)

    def wait(index, place):
        copy(index, place, place, over_core).wait_recv()

    order = ((1 - x, 1 - y), (1 - x, y), (x, 1 - y), (x, y))
    loads = []
    for i, (a, b) in enumerate(order):
        slot = 2 * a + b
        send(
            i, block_at(part_ref, a, 2 * b + 1 - core, rows, width, 0, rows),
            core_ref.at[slot], over_core,
        )
        load = pltpu.make_async_copy(
            block_at(part_ref, a, 2 * b + core, rows, width, 0, rows),
            own_ref.at[slot], load_sem.at[i],
        )
        load.start()
        loads.append(load)
    for i, (a, b) in enumerate(order):
        slot = 2 * a + b
        loads[i].wait()
        wait(i, core_ref.at[slot])
        add_rows(own_ref.at[slot], own_ref.at[slot], core_ref.at[slot], rows)
        if i in (0, 1):
            send(4 + i, own_ref.at[slot, top, :], x_ref.at[i], over_x)
        if i in (0, 2):
            send(6 + i // 2, own_ref.at[slot, bottom, :], y_ref.at[i // 2], over_y)
    wait(4, x_ref.at[0])
    slot = 2 * x + 1 - y
    add_rows(own_ref.at[slot, top, :], own_ref.at[slot, top, :], x_ref.at[0], half)
    send(8, own_ref.at[slot, top, :], last_ref.at[0], over_y)
    wait(6, y_ref.at[0])
    slot = 2 * (1 - x) + y
    add_rows(own_ref.at[slot, bottom, :], own_ref.at[slot, bottom, :], y_ref.at[0], half)
    send(9, own_ref.at[slot, bottom, :], last_ref.at[1], over_x)
    slot = 2 * x + y
    wait(5, x_ref.at[1])
    add_rows(own_ref.at[slot, top, :], own_ref.at[slot, top, :], x_ref.at[1], half)
    wait(7, y_ref.at[1])
    add_rows(own_ref.at[slot, bottom, :], own_ref.at[slot, bottom, :], y_ref.at[1], half)
    wait(8, last_ref.at[0])
    add_rows(out_ref.at[top, :], own_ref.at[slot, top, :], last_ref.at[0], half)
    wait(9, last_ref.at[1])
    add_rows(out_ref.at[bottom, :], own_ref.at[slot, bottom, :], last_ref.at[1], half)
    for task in sent:
        task.wait_send()


def scatter_plane(values, name, collective_id):
    cols = lax.axis_size("col")
    if cols != 4:
        mine = lax.psum_scatter(
            values, "row", scatter_dimension=0, tiled=True, axis_index_groups=neighbours()
        )
        return lax.psum_scatter(mine, "col", scatter_dimension=1, tiled=True).astype(F32)
    rows, width = values.shape[0] // PAIR, values.shape[1] // cols
    return pl.pallas_call(
        scatter_plane_kernel,
        in_specs=[pl.BlockSpec(memory_space=pl.ANY)],
        out_specs=pl.BlockSpec(memory_space=pltpu.VMEM),
        out_shape=jax.ShapeDtypeStruct((rows, width), F32),
        scratch_shapes=[
            pltpu.VMEM((4, rows, width), BF16),
            pltpu.VMEM((4, rows, width), BF16),
            pltpu.VMEM((2, rows // 2, width), BF16),
            pltpu.VMEM((2, rows // 2, width), BF16),
            pltpu.VMEM((2, rows // 2, width), BF16),
            pltpu.SemaphoreType.DMA((4,)),
            pltpu.SemaphoreType.DMA((10,)),
            pltpu.SemaphoreType.DMA((10,)),
        ],
        cost_estimate=taking(40),
        compiler_params=pltpu.CompilerParams(
            collective_id=collective_id, has_side_effects=True, vmem_limit_bytes=40 << 20
        ),
        name=name,
    )(values)


def gather_heads_kernel(src_ref, out_ref, local_sem, send_sem, recv_sem):
    rows, width = out_ref.shape[0], src_ref.shape[1]
    x, y, core, row, col = places()
    over_x, over_y, over_core = peers(row, col)
    meet((over_x, over_y, over_core))
    count = rows // 2
    col_y = (col + 2) % 4
    col_core = col + 1 - 2 * core

    def piece(c, a, s):
        at = pl.multiple_of((PAIR * c + a) * width, 128)
        return out_ref.at[pl.ds(s * count, count), pl.ds(at, width)]

    def mine(a, s):
        return src_ref.at[pl.ds(pl.multiple_of(a * rows + s * count, 128), count), :]

    def copy(index, source, place, device):
        return pltpu.make_async_remote_copy(
            source, place, send_sem.at[index], recv_sem.at[index],
            device_id=device, device_id_type=MESH,
        )

    sent = []

    def send(index, source, place, device):
        task = copy(index, source, place, device)
        task.start()
        sent.append(task)

    def wait(index, place):
        copy(index, place, place, over_core).wait_recv()

    local = []
    for s in range(2):
        send(s, mine(1 - x, s), piece(col, x, s), over_x)
        send(2 + s, mine(x, s), piece(col, x, s), over_y)
        task = pltpu.make_async_copy(mine(x, s), piece(col, x, s), local_sem.at[s])
        task.start()
        local.append(task)
    for s in range(2):
        send(4 + s, mine(x, s), piece(col, x, s), over_core)
    for s in range(2):
        wait(s, piece(col, 1 - x, s))
        send(6 + s, piece(col, 1 - x, s), piece(col, 1 - x, s), over_y)
        send(8 + s, piece(col, 1 - x, s), piece(col, 1 - x, s), over_core)
    for s in range(2):
        wait(2 + s, piece(col_y, x, s))
        send(10 + s, piece(col_y, x, s), piece(col_y, x, s), over_core)
    for s in range(2):
        wait(6 + s, piece(col_y, 1 - x, s))
        send(12 + s, piece(col_y, 1 - x, s), piece(col_y, 1 - x, s), over_core)
    far = (col_core + 2) % 4
    for s in range(2):
        wait(4 + s, piece(col_core, x, s))
        wait(8 + s, piece(col_core, 1 - x, s))
        wait(10 + s, piece(far, x, s))
        wait(12 + s, piece(far, 1 - x, s))
    for task in sent:
        task.wait_send()
    for task in local:
        task.wait()


def gather_heads(values, x, collective_id):
    cols = lax.axis_size("col")
    if cols != 4:
        here = in_order(x, pick(values, x, 0), swap_rows(pick(values, 1 - x, 0)), 1)
        return lax.all_gather(here, "col", axis=1, tiled=True)
    rows, width = values.shape[0] // PAIR, values.shape[1]
    return pl.pallas_call(
        gather_heads_kernel,
        in_specs=[pl.BlockSpec(memory_space=pltpu.VMEM)],
        out_specs=pl.BlockSpec(memory_space=pl.ANY),
        out_shape=jax.ShapeDtypeStruct((rows, PAIR * cols * width), values.dtype),
        scratch_shapes=[
            pltpu.SemaphoreType.DMA((2,)),
            pltpu.SemaphoreType.DMA((14,)),
            pltpu.SemaphoreType.DMA((14,)),
        ],
        cost_estimate=taking(28),
        compiler_params=pltpu.CompilerParams(collective_id=collective_id, has_side_effects=True),
        name="gather_heads",
    )(values)


def scatter_heads_kernel(
    part_ref, out_ref, own_ref, core_ref, y_ref, load_sem, out_sem, send_sem, recv_sem
):
    rows, width = own_ref.shape[1:]
    half = width // PAIR
    count = rows // CHUNKS
    x, y, core, row, col = places()
    over_x, over_y, over_core = peers(row, col)
    meet((over_x, over_y, over_core))

    def copy(index, source, place, device):
        return pltpu.make_async_remote_copy(
            source, place, send_sem.at[index], recv_sem.at[index],
            device_id=device, device_id_type=MESH,
        )

    sent = []

    def send(index, source, place, device):
        task = copy(index, source, place, device)
        task.start()
        sent.append(task)

    def wait(index, place):
        copy(index, place, place, over_core).wait_recv()

    def part(c, s):
        return part_ref.at[
            pl.ds(s * count, count), pl.ds(pl.multiple_of(c * width, 128), width)
        ]

    loads = []
    for i, b in enumerate((1 - y, y)):
        for s in range(CHUNKS):
            at = pl.ds(s * count, count)
            index = i * CHUNKS + s
            send(index, part(2 * b + 1 - core, s), core_ref.at[i, at, :], over_core)
            load = pltpu.make_async_copy(
                part(2 * b + core, s), own_ref.at[i, at, :], load_sem.at[index]
            )
            load.start()
            loads.append(load)
    for i in range(2):
        for s in range(CHUNKS):
            at = pl.ds(s * count, count)
            index = i * CHUNKS + s
            loads[index].wait()
            wait(index, core_ref.at[i, at, :])
            add_rows(own_ref.at[i, at, :], own_ref.at[i, at, :], core_ref.at[i, at, :], count)
            if i == 0:
                send(2 * CHUNKS + s, own_ref.at[0, at, :], y_ref.at[at, :], over_y)
    left, right = pl.ds(0, half), pl.ds(half, half)
    kept = []
    for s in range(CHUNKS):
        at = pl.ds(s * count, count)
        wait(2 * CHUNKS + s, y_ref.at[at, :])
        add_rows(own_ref.at[1, at, :], own_ref.at[1, at, :], y_ref.at[at, :], count)
        place = out_ref.at[pl.ds(pl.multiple_of(x * rows + s * count, 128), count), :]
        theirs = own_ref.at[1, at, pl.ds(pl.multiple_of((1 - x) * half, 128), half)]
        ours = own_ref.at[1, at, pl.ds(pl.multiple_of(x * half, 128), half)]
        send(3 * CHUNKS + s, theirs, place, over_x)
        task = pltpu.make_async_copy(ours, place, out_sem.at[s])
        task.start()
        kept.append(task)
    for s in range(CHUNKS):
        wait(
            3 * CHUNKS + s,
            out_ref.at[pl.ds(pl.multiple_of((1 - x) * rows + s * count, 128), count), :],
        )
    for task in sent:
        task.wait_send()
    for task in kept:
        task.wait()


def scatter_heads(values, x, collective_id):
    cols = lax.axis_size("col")
    if cols != 4:
        mine = lax.psum_scatter(values, "col", scatter_dimension=1, tiled=True)
        return in_order(x, pick(mine, x, 1), swap_rows(pick(mine, 1 - x, 1)), 0)
    rows, width = values.shape[0], values.shape[1] // cols
    return pl.pallas_call(
        scatter_heads_kernel,
        in_specs=[pl.BlockSpec(memory_space=pl.ANY)],
        out_specs=pl.BlockSpec(memory_space=pl.ANY),
        out_shape=jax.ShapeDtypeStruct((PAIR * rows, width // PAIR), BF16),
        scratch_shapes=[
            pltpu.VMEM((2, rows, width), BF16),
            pltpu.VMEM((2, rows, width), BF16),
            pltpu.VMEM((rows, width), BF16),
            pltpu.SemaphoreType.DMA((2 * CHUNKS,)),
            pltpu.SemaphoreType.DMA((CHUNKS,)),
            pltpu.SemaphoreType.DMA((4 * CHUNKS,)),
            pltpu.SemaphoreType.DMA((4 * CHUNKS,)),
        ],
        cost_estimate=taking(32),
        compiler_params=pltpu.CompilerParams(
            collective_id=collective_id, has_side_effects=True, vmem_limit_bytes=32 << 20
        ),
        name="scatter_heads",
    )(values)


def sum_rows_kernel(part_ref, out_ref, slots_ref, send_sem, recv_sem):
    size = slots_ref.shape[0]
    row, col = lax.axis_index("row"), lax.axis_index("col")
    others = [(lax.rem(row + step, size), col) for step in range(1, size)]
    meet(others)
    slots_ref[0] = part_ref[...]
    copies = [
        pltpu.make_async_remote_copy(
            slots_ref.at[0], slots_ref.at[step], send_sem.at[step], recv_sem.at[step],
            device_id=others[step - 1], device_id_type=MESH,
        )
        for step in range(1, size)
    ]
    for copy in copies:
        copy.start()
    for copy in copies:
        copy.wait_recv()
    total = jnp.zeros(part_ref.shape, F32)
    for r in range(size):
        total += slots_ref[lax.rem(row + size - r, size)]
    out_ref[...] = total
    for copy in copies:
        copy.wait_send()


def sum_rows(part, collective_id):
    size = lax.axis_size("row")
    if size != 8:
        return lax.psum(part, "row")
    return pl.pallas_call(
        sum_rows_kernel,
        in_specs=[pl.BlockSpec(memory_space=pltpu.VMEM)],
        out_specs=pl.BlockSpec(memory_space=pltpu.VMEM),
        out_shape=jax.ShapeDtypeStruct(part.shape, F32),
        scratch_shapes=[
            pltpu.VMEM((size,) + part.shape, F32),
            pltpu.SemaphoreType.DMA((size,)),
            pltpu.SemaphoreType.DMA((size,)),
        ],
        cost_estimate=taking(8),
        compiler_params=pltpu.CompilerParams(collective_id=collective_id, has_side_effects=True),
        name="sum_rows",
    )(part)


def row_stats(values):
    mean = jnp.mean(values, axis=1, keepdims=True)
    var = jnp.mean(values * values, axis=1, keepdims=True) - mean * mean
    return mean, lax.rsqrt(var + 1e-05)


def norm_backward(grad_norm, unit_values, inv_std, norm_gain):
    full_width = grad_norm.shape[1] * lax.axis_size("col")
    grad_unit = grad_norm * norm_gain
    row_sums = lax.psum(
        (jnp.sum(grad_unit, axis=1), jnp.sum(grad_unit * unit_values, axis=1)), "col"
    )
    grad_in = inv_std * (
        grad_unit
        - row_sums[0][:, None] / full_width
        - unit_values * row_sums[1][:, None] / full_width
    )
    return grad_in, jnp.sum(grad_norm * unit_values, axis=0)


def rotation_tables(positions):
    half = ROT // 2
    inv_freq = BASE ** (-(jnp.arange(half, dtype=F32) * 2.0) / ROT)
    angles = positions.astype(F32)[:, None] * inv_freq[None, :]
    cosine, sine = jnp.cos(angles), jnp.sin(angles)
    rest = HEAD_DIM - ROT
    ones = jnp.ones((positions.shape[0], rest), F32)
    cosine = jnp.concatenate([cosine, cosine, ones], axis=1)
    sine = jnp.concatenate([-sine, sine, 0.0 * ones], axis=1)
    return jnp.tile(cosine, (1, 2)), jnp.tile(sine, (1, 2))


TILE = 256


def norm_tile(values_ref, gain_ref, stats_ref):
    values = values_ref[...].astype(F32)
    mean, inv_std = row_stats(values)
    lane = lax.broadcasted_iota(jnp.int32, stats_ref.shape, 1)
    stats_ref[...] = jnp.where(lane == 0, mean, inv_std)
    return ((values - mean) * inv_std * gain_ref[...]).astype(BF16)


def project_heads_kernel(
    tokens_ref, gain_ref, weight_ref, bias_ref, cos_ref, sin_ref,
    normed_ref, q_ref, k_ref, v_ref, stats_ref,
):
    width = q_ref.shape[1]
    normed = norm_tile(tokens_ref, gain_ref, stats_ref)
    normed_ref[...] = normed
    in_head = lax.broadcasted_iota(jnp.int32, (1, width), 1) % HEAD_DIM
    cosine = jnp.tile(cos_ref[...], (1, width // cos_ref.shape[1]))
    sine = jnp.tile(sin_ref[...], (1, width // sin_ref.shape[1]))
    pre = dot(normed, weight_ref[...]) + bias_ref[...]
    for ref, at, scale in ((q_ref, 0, SCALE), (k_ref, width, 1.0)):
        part = pre[:, at : at + width]
        turned = part * cosine + swap_pairs(part, in_head) * sine
        ref[...] = turned.astype(BF16) * jnp.asarray(scale, BF16)
    v_ref[...] = pre[:, 2 * width :].astype(BF16)


def tiled(columns):
    return pl.BlockSpec((TILE, columns), lambda i: (i, 0))


def whole(shape):
    return pl.BlockSpec(shape, lambda i: (0,) * len(shape))


def column_block(blocks_ref, all_ref, other, sems, index):
    row, col = lax.axis_index("row"), lax.axis_index("col")
    send_sem, recv_sem = sems
    return pltpu.make_async_remote_copy(
        blocks_ref.at[other], all_ref.at[col], send_sem.at[index], recv_sem.at[index],
        device_id=(row, other), device_id_type=MESH,
    )


def exchange_beside(kernel, blocks_ref, all_ref, steps, local, *sems):
    row, col = lax.axis_index("row"), lax.axis_index("col")
    others = [col + d - 2 * d * ((col // d) % 2) if d < 3 else 3 - col for d in steps]

    @pl.when(pl.program_id(0) == 0)
    def _():
        meet([(row, other) for other in others])
        for i, other in enumerate(others):
            column_block(blocks_ref, all_ref, other, sems, i).start()
        if local is not None:
            pltpu.make_async_copy(blocks_ref.at[col], *local).start()

    kernel()

    @pl.when(pl.program_id(0) == pl.num_programs(0) - 1)
    def _():
        if local is not None:
            stage, local_sem = local
            pltpu.make_async_copy(blocks_ref.at[col], stage, local_sem).wait()
            task = pltpu.make_async_copy(stage, all_ref.at[col], local_sem)
            task.start()
            task.wait()
        for i, other in enumerate(others):
            task = column_block(blocks_ref, all_ref, other, sems, i)
            task.wait_send()
            send_sem, recv_sem = sems
            pltpu.make_async_remote_copy(
                blocks_ref.at[other], all_ref.at[other], send_sem.at[i], recv_sem.at[i],
                device_id=(row, other), device_id_type=MESH,
            ).wait_recv()


def project_heads_exchange_kernel(*refs):
    *ins, blocks_ref = refs[:7]
    outs, all_ref, (stage, local_sem, *sems) = refs[7:12], refs[12], refs[13:]
    exchange_beside(
        lambda: project_heads_kernel(*ins, *outs),
        blocks_ref, all_ref, (2,), (stage, local_sem), *sems,
    )


def project_heads(tokens, gain, weight, bias, cosine, sine, blocks=None, collective_id=None):
    rows, depth = tokens.shape
    width = weight.shape[1] // 3
    in_specs = [
        tiled(depth), whole((1, depth)), whole(weight.shape), whole((1, 3 * width)),
        tiled(cosine.shape[1]), tiled(cosine.shape[1]),
    ]
    out_specs = [tiled(depth)] + [tiled(width)] * 3 + [tiled(8)]
    out_shape = [
        jax.ShapeDtypeStruct((rows, depth), BF16),
        *[jax.ShapeDtypeStruct((rows, width), BF16)] * 3,
        jax.ShapeDtypeStruct((rows, 8), F32),
    ]
    operands = [tokens, gain.reshape(1, depth), weight, bias.reshape(1, 3 * width), cosine, sine]
    params, scratch, kernel = {}, [], project_heads_kernel
    if blocks is not None:
        anywhere = pl.BlockSpec(memory_space=pl.ANY)
        in_specs, out_specs = in_specs + [anywhere], out_specs + [anywhere]
        out_shape = out_shape + [jax.ShapeDtypeStruct(blocks.shape, BF16)]
        operands = operands + [blocks]
        scratch = [pltpu.VMEM(blocks.shape[1:], BF16), pltpu.SemaphoreType.DMA]
        scratch = scratch + [pltpu.SemaphoreType.DMA((1,))] * 2
        params = dict(collective_id=collective_id, has_side_effects=True)
        kernel = project_heads_exchange_kernel
    return pl.pallas_call(
        kernel,
        grid=(rows // TILE,),
        in_specs=in_specs,
        out_specs=out_specs,
        out_shape=out_shape,
        scratch_shapes=scratch,
        compiler_params=pltpu.CompilerParams(vmem_limit_bytes=48 << 20, **params),
        cost_estimate=taking(16),
        name="project_heads",
    )(*operands)


def feed_forward_kernel(
    resid_ref, gain_ref, weight_ref, grad_ref, down_ref,
    normed_ref, hidden_ref, dgate_ref, dup_ref, stats_ref,
):
    lines, _, hidden, width = weight_ref.shape
    normed_ref[...] = norm_tile(resid_ref, gain_ref, stats_ref)
    gate = jnp.zeros((hidden, TILE), F32)
    up = jnp.zeros((hidden, TILE), F32)
    dhidden = jnp.zeros((hidden, TILE), F32)
    for z in range(lines):
        part = normed_ref[:, z * width : (z + 1) * width]
        gate += dot(weight_ref[z, 0], part, (1,), (1,))
        up += dot(weight_ref[z, 1], part, (1,), (1,))
    for c in range(down_ref.shape[0]):
        part = grad_ref[:, c * width : (c + 1) * width]
        dhidden += dot(down_ref[c], part, (1,), (1,))
    sigmoid = 1.0 / (1.0 + jnp.exp(-gate))
    silu = gate * sigmoid
    hidden_ref[...] = (silu * up).astype(BF16)
    dgate_ref[...] = (dhidden * up * sigmoid * (1.0 + gate * (1.0 - sigmoid))).astype(BF16)
    dup_ref[...] = (dhidden * silu).astype(BF16)


def feed_forward(resid, gain, weight, grad, down):
    rows, depth = resid.shape
    hidden = down.shape[1]
    across = pl.BlockSpec((hidden, TILE), lambda i: (0, i))
    return pl.pallas_call(
        feed_forward_kernel,
        grid=(rows // TILE,),
        in_specs=[
            tiled(depth), whole((1, depth)), whole(weight.shape), tiled(depth), whole(down.shape)
        ],
        out_specs=[tiled(depth)] + [across] * 3 + [tiled(8)],
        out_shape=[jax.ShapeDtypeStruct((rows, depth), BF16)]
        + [jax.ShapeDtypeStruct((hidden, rows), BF16)] * 3
        + [jax.ShapeDtypeStruct((rows, 8), F32)],
        compiler_params=pltpu.CompilerParams(vmem_limit_bytes=56 << 20),
        cost_estimate=taking(28),
        name="feed_forward",
    )(resid, gain.reshape(1, depth), weight, grad, down)


def weight_grads_kernel(*refs):
    *left_refs, right_ref, out_ref = refs
    for i, left_ref in enumerate(left_refs):
        out_ref[0, i] = dot(left_ref[...], right_ref[...]).astype(BF16)


def weight_grads(lefts, right, width, name):
    hidden, rows = lefts[0].shape
    blocks = right.shape[1] // width
    return pl.pallas_call(
        weight_grads_kernel,
        grid=(blocks,),
        in_specs=[whole((hidden, rows))] * len(lefts)
        + [pl.BlockSpec((rows, width), lambda i: (0, i))],
        out_specs=pl.BlockSpec((1, len(lefts), hidden, width), lambda i: (i, 0, 0, 0)),
        out_shape=jax.ShapeDtypeStruct((blocks, len(lefts), hidden, width), BF16),
        compiler_params=pltpu.CompilerParams(vmem_limit_bytes=56 << 20),
        cost_estimate=taking(9 * len(lefts)),
        name=name,
    )(*lefts, right)


def back_project_kernel(*refs):
    *left_refs, weight_ref, out_ref = refs
    width = weight_ref.shape[-1]
    lefts = [ref[...].T for ref in left_refs]
    for z in range(weight_ref.shape[0]):
        total = sum(dot(left, weight_ref[z, i]) for i, left in enumerate(lefts))
        out_ref[:, z * width : (z + 1) * width] = total.astype(BF16)


def back_project(lefts, weight, name):
    hidden, rows = lefts[0].shape
    depth = weight.shape[0] * weight.shape[-1]
    return pl.pallas_call(
        back_project_kernel,
        grid=(rows // TILE,),
        in_specs=[pl.BlockSpec((hidden, TILE), lambda i: (0, i))] * len(lefts)
        + [whole(weight.shape)],
        out_specs=tiled(depth),
        out_shape=jax.ShapeDtypeStruct((rows, depth), BF16),
        compiler_params=pltpu.CompilerParams(vmem_limit_bytes=48 << 20),
        cost_estimate=taking(10 * len(lefts)),
        name=name,
    )(*lefts, weight)


class PlaneScatter:
    SEMS = 14

    def __init__(self, copies, base, fill, sent_ref, own_ref, core_ref, x_ref, y_ref, last_ref):
        self.copies, self.base, self.fill = copies, base, fill
        self.sent, self.own, self.core_part = sent_ref, own_ref, core_ref
        self.x_ref, self.y_ref, self.last = x_ref, y_ref, last_ref
        self.x, self.y, self.core, row, col = places()
        self.over_x, self.over_y, self.over_core = peers(row, col)
        x, y = self.x, self.y
        self.order = ((1 - x, 1 - y), (1 - x, y), (x, 1 - y), (x, y))
        self.half = sent_ref.shape[1] // 2
        self.rows = (pl.ds(0, self.half), pl.ds(self.half, self.half))

    def send(self, index, source, place, device):
        self.copies.send(self.base + index, source, place, device)

    def wait(self, index, place):
        self.copies.wait(self.base + index, place)

    def give(self, i, h):
        a, b = self.order[i]
        self.fill(self.sent.at[i], a, 2 * b + 1 - self.core, h, None)
        at = self.rows[h]
        self.send(2 * i + h, self.sent.at[i, at, :], self.core_part.at[i, at, :], self.over_core)

    def keep(self, i, h):
        a, b = self.order[i]
        at = self.rows[h]
        self.wait(2 * i + h, self.core_part.at[i, at, :])
        self.fill(self.own.at[i], a, 2 * b + self.core, h, self.core_part.at[i])
        if h == 0 and i in (0, 1):
            self.send(8 + i, self.own.at[i, at, :], self.x_ref.at[i], self.over_x)
        if h == 1 and i in (0, 2):
            self.send(10 + i // 2, self.own.at[i, at, :], self.y_ref.at[i // 2], self.over_y)

    def first(self):
        self.give(0, 0)
        self.give(0, 1)
        self.keep(0, 0)
        self.keep(0, 1)
        for h in range(2):
            self.give(1, h)
            self.give(2, h)
        self.keep(1, 0)
        self.keep(2, 1)
        self.keep(2, 0)
        self.keep(1, 1)
        for h in range(2):
            self.give(3, h)
        for h in range(2):
            self.keep(3, h)

    def add(self, i, h, ref):
        at = self.own.at[i, self.rows[h], :]
        add_rows(at, at, ref, self.half)

    def second(self):
        self.wait(8, self.x_ref.at[0])
        self.add(2, 0, self.x_ref.at[0])
        self.send(12, self.own.at[2, self.rows[0], :], self.last.at[0], self.over_y)
        self.wait(10, self.y_ref.at[0])
        self.add(1, 1, self.y_ref.at[0])
        self.send(13, self.own.at[1, self.rows[1], :], self.last.at[1], self.over_x)
        self.wait(9, self.x_ref.at[1])
        self.add(3, 0, self.x_ref.at[1])
        self.wait(11, self.y_ref.at[1])
        self.add(3, 1, self.y_ref.at[1])

    def third(self):
        self.wait(12, self.last.at[0])
        self.wait(13, self.last.at[1])

    def result(self, start, count):
        h, other = divmod(start, self.half)
        return self.own[3, pl.ds(start, count), :].astype(F32) + self.last[
            h, pl.ds(other, count), :
        ].astype(F32)


STEP = 128


class NormBack:
    def __init__(
        self, copies, base, values_ref, stats_ref, gain_ref, base_ref, out_ref, low_ref, dgain_ref,
        sums_ref,
    ):
        self.copies, self.base = copies, base
        self.values, self.stats, self.gain, self.more = values_ref, stats_ref, gain_ref, base_ref
        self.out, self.low, self.dgain, self.sums = out_ref, low_ref, dgain_ref, sums_ref

    def unit_of(self, at):
        stats = self.stats[at, :]
        return (self.values[at, :].astype(F32) - stats[:, 0:1]) * stats[:, 1:2]

    def start(self, result, devices):
        lane = lax.broadcasted_iota(jnp.int32, (1, 128), 1)
        self.dgain[...] = jnp.zeros_like(self.dgain)
        for start in range(0, self.out.shape[0], STEP):
            at = pl.ds(start, STEP)
            grad = result(start, STEP)
            self.out[at, :] = grad
            unit = self.unit_of(at)
            self.dgain[...] += jnp.sum(grad * unit, axis=0, keepdims=True)
            grad = grad * self.gain[...]
            first = jnp.sum(grad, axis=1, keepdims=True)
            second = jnp.sum(grad * unit, axis=1, keepdims=True)
            both = jnp.where(lane == 0, first, jnp.where(lane == 1, second, 0.0))
            self.sums[0, :, start : start + STEP] = both.T[:8]
        for i, device in enumerate(devices):
            self.copies.send(self.base + i, self.sums.at[0], self.sums.at[1 + i], device)

    def finish(self):
        rows, width = self.out.shape
        for i in range(3):
            self.copies.wait(self.base + i, self.sums.at[1 + i])
        for start in range(0, rows, STEP):
            at = pl.ds(start, STEP)
            columns = slice(start, start + STEP)
            total = (self.sums[0, :, columns] + self.sums[1, :, columns]) + (
                self.sums[2, :, columns] + self.sums[3, :, columns]
            )
            total = jnp.concatenate([total, jnp.zeros((STEP - 8, STEP), F32)], axis=0).T
            total = total * (1.0 / (4 * width))
            unit = self.unit_of(at)
            grad = self.out[at, :] * self.gain[...]
            grad = self.stats[at, 1:2] * (grad - total[:, 0:1] - unit * total[:, 1:2])
            grad = grad + self.more[at, :].astype(F32)
            self.out[at, :] = grad
            if self.low is not None:
                self.low[at, :] = grad.astype(BF16)


def scatter_scratch(rows, width):
    block = lambda n, r: pltpu.VMEM((n, r, width), BF16)
    return [
        block(4, rows), block(4, rows), block(4, rows),
        block(2, rows // 2), block(2, rows // 2), block(2, rows // 2),
    ]


def around():
    _, _, _, row, col = places()
    over_x, over_y, over_core = peers(row, col)
    return over_x, over_y, over_core, (row, 3 - col)


def filling(rows, product):
    half = rows // 2

    def fill(ref, a, c, h, more):
        @pl.loop(0, half // TILE)
        def _(i):
            start = h * half + i * TILE
            total = product(pl.ds(pl.multiple_of(a * rows + start, TILE), TILE), c)
            at = pl.ds(pl.multiple_of(start, TILE), TILE)
            if more is not None:
                total = total + more[at, :].astype(F32)
            ref[at, :] = total.astype(BF16)

    return fill


def turn_rows(left_ref, source_ref, a, rows):
    @pl.loop(0, rows // TILE)
    def _(i):
        at = pl.ds(pl.multiple_of(a * rows + i * TILE, TILE), TILE)
        left_ref[at, :] = source_ref[:, at].T


def back_second_kernel(
    gate_ref, up_ref, weight_ref, values_ref, stats_ref, gain_ref, base_ref,
    out_ref, low_ref, dgain_ref,
    gate_vmem, up_vmem, weight_vmem, left_ref, sums_ref, load_sem, send_sem, recv_sem, *scratch,
):
    rows, width = out_ref.shape
    x, y, core, _, _ = places()
    devices = around()

    def load_left(i, a):
        at = pl.ds(pl.multiple_of(a * rows, TILE), rows)
        return [
            pltpu.make_async_copy(ref.at[:, at], vmem.at[:, at], load_sem.at[2 * i + j])
            for j, (ref, vmem) in enumerate(((gate_ref, gate_vmem), (up_ref, up_vmem)))
        ]

    def load_weight(i, c):
        return pltpu.make_async_copy(weight_ref.at[c], weight_vmem.at[c], load_sem.at[4 + i])

    lefts = [load_left(0, 1 - x), load_left(1, x)]
    columns = (2 * (1 - y) + 1 - core, 2 * (1 - y) + core, 2 * y + 1 - core, 2 * y + core)
    weights = [load_weight(i, c) for i, c in enumerate(columns)]
    for task in (*lefts[0], *weights, *lefts[1]):
        task.start()
    meet(devices)
    copies = Copies(send_sem, recv_sem, devices[2])

    def turn(i, a):
        for j, (task, vmem) in enumerate(zip(lefts[i], (gate_vmem, up_vmem))):
            task.wait()
            turn_rows(left_ref.at[j], vmem, a, rows)

    def product(at, c):
        return dot(left_ref[0, at, :], weight_vmem[c, 0]) + dot(
            left_ref[1, at, :], weight_vmem[c, 1]
        )

    scatter = PlaneScatter(copies, 0, filling(rows, product), *scratch)
    turn(0, 1 - x)
    weights[0].wait()
    scatter.give(0, 0)
    scatter.give(0, 1)
    weights[1].wait()
    scatter.keep(0, 0)
    scatter.keep(0, 1)
    weights[2].wait()
    scatter.give(1, 0)
    scatter.give(1, 1)
    weights[3].wait()
    scatter.keep(1, 0)
    turn(1, x)
    scatter.give(2, 1)
    scatter.give(2, 0)
    scatter.keep(2, 1)
    scatter.keep(2, 0)
    scatter.keep(1, 1)
    scatter.give(3, 0)
    scatter.give(3, 1)
    scatter.keep(3, 0)
    scatter.keep(3, 1)
    scatter.second()
    scatter.third()
    norm = NormBack(
        copies, PlaneScatter.SEMS, values_ref, stats_ref, gain_ref, base_ref, out_ref, low_ref,
        dgain_ref, sums_ref,
    )
    norm.start(scatter.result, devices[1:])
    norm.finish()
    copies.finish()


def back_second(gate, up, weight, values, stats, gain, base, collective_id):
    rows, width = values.shape
    hidden, tokens = gate.shape
    vmem, anywhere = pl.BlockSpec(memory_space=pltpu.VMEM), pl.BlockSpec(memory_space=pl.ANY)
    sems = lambda n: pltpu.SemaphoreType.DMA((n,))
    return pl.pallas_call(
        back_second_kernel,
        in_specs=[anywhere] * 3 + [vmem] * 4,
        out_specs=[vmem] * 3,
        out_shape=[
            jax.ShapeDtypeStruct((rows, width), F32),
            jax.ShapeDtypeStruct((rows, width), BF16),
            jax.ShapeDtypeStruct((1, width), F32),
        ],
        scratch_shapes=[
            pltpu.VMEM(gate.shape, BF16), pltpu.VMEM(up.shape, BF16),
            pltpu.VMEM(weight.shape, BF16), pltpu.VMEM((2, tokens, hidden), BF16),
            pltpu.VMEM((4, 8, rows), F32),
            sems(8), sems(PlaneScatter.SEMS + 3), sems(PlaneScatter.SEMS + 3),
            *scatter_scratch(rows, width),
        ],
        compiler_params=pltpu.CompilerParams(
            collective_id=collective_id, has_side_effects=True, vmem_limit_bytes=60 << 20
        ),
        cost_estimate=taking(50),
        name="back_second",
    )(gate, up, weight, values, stats, gain.reshape(1, width), base)


def back_first_kernel(
    grad_ref, weight_ref, hidden_ref, down_ref, values_ref, stats_ref, gain_ref, base_ref, resid_ref,
    out_ref, dgain_ref, mixed_ref,
    left_ref, sums_ref, send_sem, recv_sem, *scratch,
):
    rows, width = out_ref.shape
    x, _, _, _, _ = places()
    devices = around()
    meet(devices)
    copies = Copies(send_sem, recv_sem, devices[2])

    def product(at, c):
        weight = weight_ref[pl.ds(pl.multiple_of(c * width, 128), width), :]
        return dot(grad_ref[at, :], weight, (1,), (1,))

    def mix(at, c):
        return dot(left_ref[at, :], down_ref[c])

    scatter = PlaneScatter(copies, 0, filling(rows, product), *scratch[:6])
    mixing = PlaneScatter(copies, PlaneScatter.SEMS + 3, filling(rows, mix), *scratch[6:])
    norm = NormBack(
        copies, PlaneScatter.SEMS, values_ref, stats_ref, gain_ref, base_ref, out_ref, None,
        dgain_ref, sums_ref,
    )
    scatter.first()
    for a in range(PAIR):
        turn_rows(left_ref, hidden_ref, a, rows)
    mixing.first()
    scatter.second()
    scatter.third()
    norm.start(scatter.result, devices[1:])
    mixing.second()
    norm.finish()
    mixing.third()
    for start in range(0, rows, STEP):
        at = pl.ds(start, STEP)
        mixed_ref[at, :] = (resid_ref[at, :] + mixing.result(start, STEP)).astype(BF16)
    copies.finish()


def back_first(grad, weight, hidden, down, values, stats, gain, base, resid, collective_id):
    rows, width = values.shape
    vmem = pl.BlockSpec(memory_space=pltpu.VMEM)
    sems = lambda n: pltpu.SemaphoreType.DMA((n,))
    return pl.pallas_call(
        back_first_kernel,
        in_specs=[vmem] * 9,
        out_specs=[vmem] * 3,
        out_shape=[
            jax.ShapeDtypeStruct((rows, width), F32),
            jax.ShapeDtypeStruct((1, width), F32),
            jax.ShapeDtypeStruct((rows, width), BF16),
        ],
        scratch_shapes=[
            pltpu.VMEM(hidden.shape[::-1], BF16), pltpu.VMEM((4, 8, rows), F32),
            sems(2 * PlaneScatter.SEMS + 3), sems(2 * PlaneScatter.SEMS + 3),
            *scatter_scratch(rows, width), *scatter_scratch(rows, width),
        ],
        compiler_params=pltpu.CompilerParams(
            collective_id=collective_id, has_side_effects=True, vmem_limit_bytes=62 << 20
        ),
        cost_estimate=taking(80),
        name="back_first",
    )(grad, weight, hidden, down, values, stats, gain.reshape(1, width), base, resid)


def per_device(
    tokens, segment_ids, positions, attn_gain, query_weight, query_bias, key_weight, key_bias,
    value_weight, value_bias, out_weight, mlp_gain, gate_weight, up_weight, down_weight, out_grad,
):
    count, width = tokens.shape
    lines = lax.axis_size("row") // PAIR
    cols = lax.axis_size("col")
    row = lax.axis_index("row")
    col = lax.axis_index("col")
    x = row % PAIR
    half = width // PAIR

    fast = cols == 4 and lines == LINES
    bias = jnp.concatenate(
        [pick(b, x, 0) for b in (query_bias, key_bias, value_bias)], axis=0
    )
    depth = out_weight.shape[0]
    hidden = down_weight.shape[0]
    down_line = gather_line(down_weight)
    if fast:
        tokens_all, grad_all, qkv_weight, out_all, ffn_part, gains, places_all = gather_first(
            tokens, out_grad, query_weight, key_weight, value_weight, out_weight,
            gate_weight, up_weight,
            jnp.pad(jnp.stack([attn_gain, mlp_gain]), ((0, 6), (0, 0))),
            jnp.pad(jnp.stack([positions, segment_ids]), ((0, 6), (0, 0))), 0,
        )
    else:
        qkv_weight = gather_line(
            jnp.concatenate(
                [own_columns(w, x) for w in (query_weight, key_weight, value_weight)], axis=1
            )
        )
        tokens_all = gather_plane(tokens, "gather_tokens", 0)
        grad_all = gather_plane(out_grad, "gather_cotangent", 1)
        out_line = gather_line(out_weight)
        full = (lines, 1, depth, width)
        out_all = in_order(
            x, out_line.reshape(full), swap_rows(out_line).reshape(full), 1
        ).reshape(-1, width)
        ffn_part = jnp.stack([own_units(w, x) for w in (gate_weight, up_weight)])[None]
        gains = lax.all_gather(jnp.stack([attn_gain, mlp_gain]), "col", axis=1, tiled=True)
        own_place = jnp.stack([positions, segment_ids])
        places_all = in_order(x, own_place, swap_rows(own_place), 1)
    cosine, sine = rotation_tables(places_all[0])
    plane_segments = places_all[1]
    down_blocks = after(down_line, tokens_all).reshape(lines, hidden, width)
    ffn_weight = gather_line(after(ffn_part, down_blocks))

    projections = (tokens_all, gains[0], qkv_weight, bias, cosine, sine)
    if fast:
        normed_first, queries, keys, values, stats_first, down_partly = project_heads(
            *projections, down_blocks, 1
        )
        attended, lse, down_all = attention_forward(
            queries, keys, values, plane_segments, down_blocks, down_partly, 8
        )
    else:
        normed_first, queries, keys, values, stats_first = project_heads(*projections)
        attended, lse = attention_forward(queries, keys, values, plane_segments)
        down_all = lax.all_to_all(down_blocks, "col", split_axis=0, concat_axis=0, tiled=True)
    attn_all = gather_heads(attended, x, 2)
    inputs = tokens.astype(F32)
    resid = inputs + dot(attn_all, out_all)

    resid_all = gather_plane(resid.astype(BF16), "gather_residual", 3)
    normed_second, hidden_low, grad_gate, grad_up, stats_second = feed_forward(
        resid_all, gains[1], ffn_weight, grad_all, down_all
    )
    grad_ffn = weight_grads((grad_gate, grad_up), normed_second, width, "ffn_grads")
    own_stats = pick(stats_second, x, 0)
    if fast:
        grad_resid, grad_resid_low, mlp_gain_part = back_second(
            after(grad_gate, grad_ffn), grad_up, ffn_weight,
            resid, own_stats, mlp_gain, out_grad, 4,
        )
        mlp_gain_part = mlp_gain_part[0]
    else:
        grad_second = scatter_plane(
            back_project((grad_gate, grad_up), ffn_weight, "back_ffn"), "scatter_second", 4
        )
        mean_here, inv_here = own_stats[:, 0:1], own_stats[:, 1:2]
        grad_resid, mlp_gain_part = norm_backward(
            grad_second, (resid - mean_here) * inv_here, inv_here, mlp_gain
        )
        grad_resid = grad_resid + out_grad.astype(F32)
        grad_resid_low = grad_resid.astype(BF16)
    grad_ffn = scatter_line(grad_ffn)

    grad_out_weight = dot(attn_all, grad_resid_low, (0,), (0,)).astype(BF16)
    grad_out_weight = grad_out_weight.reshape(lines, PAIR, depth, width)
    grad_out_other = swap_rows(pick(grad_out_weight, 1 - x, 1))
    grad_attn = scatter_heads(dot(grad_resid_low, out_all, (1,), (1,)).astype(BF16), x, 5)
    grad_out_weight = pick(grad_out_weight, x, 1) + grad_out_other
    grad_attn = after(grad_attn, grad_out_weight)
    grad_down = weight_grads((after(hidden_low, grad_attn),), grad_all, width, "down_grads")
    grad_down = grad_down.reshape(cols, hidden, width)
    backward = (queries, keys, values, grad_attn, lse, cosine, sine, plane_segments)
    if fast:
        grad_qkv, bias_sums, grad_down = attention_backward(*backward, grad_down, 9)
    else:
        grad_qkv, bias_sums = attention_backward(*backward)
        grad_down = lax.all_to_all(grad_down, "col", split_axis=0, concat_axis=0, tiled=True)
    grad_qkv_weight = dot(normed_first, grad_qkv, (0,), (0,)).astype(BF16)
    grad_out_weight = scatter_line(
        after(grad_out_weight, grad_ffn).reshape(lines * depth, width)
    )
    grad_down = scatter_line(
        after(grad_down, grad_out_weight).reshape(lines * hidden, width)
    )
    grad_qkv_later = after(grad_qkv, grad_qkv_weight)
    grad_qkv_weight = scatter_line(grad_qkv_weight)
    own_stats = pick(stats_first, x, 0)
    if fast:
        tokens_grad, attn_gain_part, mixed = back_first(
            grad_qkv_later, qkv_weight, hidden_low, down_all,
            tokens, own_stats, attn_gain, grad_resid, resid, 6,
        )
        attn_gain_part = attn_gain_part[0]
    else:
        grad_first = scatter_plane(
            dot(grad_qkv_later, qkv_weight, (1,), (1,)).astype(BF16), "scatter_first", 6
        )
        mean_here, inv_here = own_stats[:, 0:1], own_stats[:, 1:2]
        grad_input, attn_gain_part = norm_backward(
            grad_first, (inputs - mean_here) * inv_here, inv_here, attn_gain
        )
        tokens_grad = grad_input + grad_resid
        mixed = resid + scatter_plane(
            back_project((hidden_low,), down_all[:, None], "mix"), "scatter_mixed", 10
        )
        mixed = mixed.astype(BF16)
    kept, other = pick(grad_ffn[0], x, 2), swap_rows(pick(grad_ffn[0], 1 - x, 2))
    gate_grad, up_grad = (
        in_order(x, kept[i], other[i], 0).T.astype(F32) for i in range(2)
    )

    bias_part = jnp.sum(bias_sums, axis=(0, 1)).reshape(3, half)
    bias_part = jnp.where(
        (jnp.arange(PAIR) == x)[None, :, None], bias_part[:, None, :], 0.0
    ).reshape(3, width)
    vectors = sum_rows(
        jnp.concatenate(
            [bias_part, attn_gain_part[None], mlp_gain_part[None], jnp.zeros((3, width), F32)]
        ),
        7,
    )
    grad_qkv_weight = own_rows(grad_qkv_weight, x)
    wide = lambda w: jnp.where(
        x == 0,
        jnp.concatenate([grad_qkv_weight[0][:, w], grad_qkv_weight[1][:, w]], axis=1),
        jnp.concatenate([grad_qkv_weight[1][:, w], grad_qkv_weight[0][:, w]], axis=1),
    ).astype(F32)
    return (
        mixed,
        tokens_grad,
        vectors[3],
        wide(slice(0, half)),
        vectors[0],
        wide(slice(half, 2 * half)),
        vectors[1],
        wide(slice(2 * half, 3 * half)),
        vectors[2],
        grad_out_weight.astype(F32),
        vectors[4],
        gate_grad,
        up_grad,
        grad_down.astype(F32),
    )


def solution(mesh):
    grid, rows, cols = P("row", "col"), P("row"), P("col")
    in_specs = (
        grid, rows, rows, cols, grid, cols, grid, cols, grid, cols, grid, cols, grid, grid, grid, grid,
    )
    out_specs = (
        grid, grid, cols, grid, cols, grid, cols, grid, cols, grid, cols, grid, grid, grid,
    )
    return jax.shard_map(
        per_device, mesh=mesh, in_specs=in_specs, out_specs=out_specs, check_vma=False
    )
```

```python
import functools

import jax
import jax.numpy as jnp
from jax import lax
from jax.experimental import pallas as pl
from jax.experimental.pallas import tpu as pltpu
from jax.sharding import PartitionSpec as P

HEAD_DIM = 64
ROT = 16
SEQ = 1024
BASE = 10000.0
NEG = -1e30
F32 = jnp.float32
BF16 = jnp.bfloat16
SCALE = HEAD_DIM**-0.5
MESH = pl.DeviceIdType.MESH
QBLOCK = 256
PAIR = 2


def dot(left, right, left_dims=(1,), right_dims=(0,)):
    return lax.dot_general(
        left, right, ((left_dims, right_dims), ((), ())), preferred_element_type=F32
    )


def taking(microseconds):
    return pl.CostEstimate(
        flops=microseconds * 10**9, bytes_accessed=microseconds * 10**6, transcendentals=0
    )


def swap_pairs(values, lane):
    half = ROT // 2
    width = values.shape[1]
    ahead = pltpu.roll(values, width - half, 1)
    behind = pltpu.roll(values, half, 1)
    return jnp.where(lane < half, ahead, behind)


def attention_forward_kernel(
    q_ref, k_ref, v_ref, seg_col_ref, seg_row_ref, o_ref, lse_ref, acc_ref, lse_scratch
):
    width = q_ref.shape[1]
    heads = width // HEAD_DIM
    full_lane = lax.broadcasted_iota(jnp.int32, (1, width), 1)
    acc_ref[...] = jnp.zeros_like(acc_ref)
    lse_lane = lax.broadcasted_iota(jnp.int32, (1, lse_scratch.shape[1]), 1)

    @pl.loop(0, heads)
    def _(head):
        mask = full_lane // HEAD_DIM == head
        for start in range(0, SEQ, QBLOCK):
            keys = start + QBLOCK
            rows = slice(start, keys)
            queries = jnp.where(mask, q_ref[rows, :], jnp.zeros((), BF16))
            scores = dot(queries, k_ref[:keys, :], (1,), (1,))
            query_pos = start + lax.broadcasted_iota(jnp.int32, scores.shape, 0)
            key_pos = lax.broadcasted_iota(jnp.int32, scores.shape, 1)
            seen = (seg_col_ref[rows, :] == seg_row_ref[0, :, :keys]) & (key_pos <= query_pos)
            scores = jnp.where(seen, scores, NEG)
            peak = jnp.max(scores, axis=1, keepdims=True)
            weights = jnp.exp(scores - peak)
            total = jnp.sum(weights, axis=1, keepdims=True)
            probs = (weights * (1.0 / total)).astype(BF16)
            output = dot(probs, v_ref[:keys, :])
            acc_ref[rows, :] = jnp.where(mask, output, acc_ref[rows, :])
            lse_scratch[rows, :] = jnp.where(
                lse_lane == head, peak + jnp.log(total), lse_scratch[rows, :]
            )

    o_ref[...] = acc_ref[...].astype(BF16)
    lse_ref[0] = lse_scratch[...].T[: lse_ref.shape[1], :]


def attention_forward_exchange_kernel(*refs):
    ins, (blocks_ref, _), outs, all_ref = refs[:5], refs[5:7], refs[7:9], refs[9]
    scratch, sems = refs[10:12], refs[12:]
    exchange_beside(
        lambda: attention_forward_kernel(*ins, *outs, *scratch),
        blocks_ref, all_ref, (1, 3), None, *sems,
    )


def attention_forward(queries, keys, values, segments, blocks=None, partly=None, collective_id=None):
    rows, width = queries.shape
    seqs = rows // SEQ
    block = lambda columns: pl.BlockSpec((SEQ, columns), lambda s: (s, 0))
    in_specs = [block(width)] * 3 + [block(1), pl.BlockSpec((1, 1, SEQ), lambda s: (s, 0, 0))]
    out_specs = [block(width), pl.BlockSpec((1, 8, SEQ), lambda s: (s, 0, 0))]
    out_shape = [
        jax.ShapeDtypeStruct((rows, width), BF16), jax.ShapeDtypeStruct((seqs, 8, SEQ), F32)
    ]
    operands = [queries, keys, values, segments.reshape(rows, 1), segments.reshape(seqs, 1, SEQ)]
    scratch = [pltpu.VMEM((SEQ, width), F32), pltpu.VMEM((SEQ, 128), F32)]
    params, aliases, kernel = {}, {}, attention_forward_kernel
    if blocks is not None:
        anywhere = pl.BlockSpec(memory_space=pl.ANY)
        in_specs, out_specs = in_specs + [anywhere] * 2, out_specs + [anywhere]
        out_shape = out_shape + [jax.ShapeDtypeStruct(blocks.shape, BF16)]
        operands = operands + [blocks, partly]
        scratch = scratch + [pltpu.SemaphoreType.DMA((2,))] * 2
        params = dict(collective_id=collective_id, has_side_effects=True)
        aliases, kernel = {6: 2}, attention_forward_exchange_kernel
    return pl.pallas_call(
        kernel,
        grid=(seqs,),
        in_specs=in_specs,
        out_specs=out_specs,
        out_shape=out_shape,
        scratch_shapes=scratch,
        input_output_aliases=aliases,
        compiler_params=pltpu.CompilerParams(vmem_limit_bytes=56 << 20, **params),
        cost_estimate=taking(21),
        name="attention_forward",
    )(*operands)


def attention_backward_kernel(
    q_ref, k_ref, v_ref, do_ref, lse_ref, cos_ref, sin_ref, seg_col_ref, seg_row_ref,
    grad_ref, sums_ref, dq_ref, dk_ref, dv_ref, halfway=None,
):
    width = q_ref.shape[1]
    heads = width // HEAD_DIM
    full_lane = lax.broadcasted_iota(jnp.int32, (1, width), 1)
    in_head = full_lane % HEAD_DIM
    for ref in (dq_ref, dk_ref, dv_ref):
        ref[...] = jnp.zeros_like(ref)

    def one_head(head):
        mask = full_lane // HEAD_DIM == head
        nothing = jnp.zeros((), BF16)
        for start in range(0, SEQ, 2 * QBLOCK):
            keys = start + 2 * QBLOCK
            rows = slice(start, keys)
            queries = jnp.where(mask, q_ref[rows, :], nothing)
            grads = jnp.where(mask, do_ref[rows, :], nothing)
            scores = dot(k_ref[:keys, :], queries, (1,), (1,))
            key_pos = lax.broadcasted_iota(jnp.int32, scores.shape, 0)
            query_pos = start + lax.broadcasted_iota(jnp.int32, scores.shape, 1)
            seen = (seg_col_ref[:keys, :] == seg_row_ref[0, :, rows]) & (key_pos <= query_pos)
            probs = jnp.where(
                seen, jnp.exp(scores - lse_ref[0, pl.ds(head, 1), rows]), 0.0
            )
            dv_ref[:keys, :] += dot(probs.astype(BF16), grads)
            grad_probs = dot(v_ref[:keys, :], grads, (1,), (1,))
            delta = jnp.sum(probs * grad_probs, axis=0, keepdims=True)
            grad_scores = (probs * (grad_probs - delta)).astype(BF16)
            dk_ref[:keys, :] += dot(grad_scores, queries)
            masked_keys = jnp.where(mask, k_ref[:keys, :], nothing)
            dq_ref[rows, :] += dot(grad_scores, masked_keys, (0,), (0,))

    pl.loop(0, heads // 2)(one_head)
    if halfway is not None:
        halfway()
    pl.loop(heads // 2, heads)(one_head)

    cosine = jnp.tile(cos_ref[...], (1, width // cos_ref.shape[1]))
    sine = jnp.tile(sin_ref[...], (1, width // sin_ref.shape[1]))
    for part, (ref, scale) in enumerate(((dq_ref, SCALE), (dk_ref, 1.0), (dv_ref, None))):
        grad = ref[...]
        if scale is not None:
            grad = grad * scale
            grad = grad * cosine - swap_pairs(grad, in_head) * sine
        low = grad.astype(BF16)
        columns = slice(part * width, (part + 1) * width)
        grad_ref[:, columns] = low
        sums_ref[0, :, columns] = jnp.sum(low.astype(F32), axis=0, keepdims=True)


def attention_backward_sums_kernel(*refs):
    ins, parts_ref, resid_ref = refs[:9], refs[9], refs[10]
    outs, mixed_ref, scratch = refs[11:13], refs[13], refs[14:17]
    load_sem, send_sem, recv_sem, *blocks = refs[17:]
    devices = peers(lax.axis_index("row"), lax.axis_index("col"))
    copies = Copies(send_sem, recv_sem, devices[2])
    mixing = PartsScatter(copies, 0, parts_ref, load_sem, *blocks)
    step = pl.program_id(0)

    @pl.when(step == 0)
    def _():
        meet(devices)
        mixing.start()
        mixing.keep(0, 0)
        mixing.keep(0, 1)

    def halfway():
        @pl.when(step == 0)
        def _():
            for i, h in ((1, 0), (2, 0), (2, 1), (1, 1), (3, 0), (3, 1)):
                mixing.keep(i, h)

        @pl.when(step == 1)
        def _():
            mixing.second()

    attention_backward_kernel(*ins, *outs, *scratch, halfway=halfway)

    @pl.when(step == 1)
    def _():
        mixing.third()
        for start in range(0, mixed_ref.shape[0], STEP):
            at = pl.ds(start, STEP)
            mixed_ref[at, :] = (resid_ref[at, :] + mixing.result(start, STEP)).astype(BF16)
        mixing.drain()


def attention_backward(
    queries, keys, values, grad_out, lse, cosine, sine, segments,
    parts=None, resid=None, collective_id=None,
):
    rows, width = queries.shape
    seqs = rows // SEQ
    block = lambda columns: pl.BlockSpec((SEQ, columns), lambda s: (s, 0))
    in_specs = [block(width)] * 4 + [
        pl.BlockSpec((1, 8, SEQ), lambda s: (s, 0, 0)),
        block(cosine.shape[1]),
        block(cosine.shape[1]),
        block(1),
        pl.BlockSpec((1, 1, SEQ), lambda s: (s, 0, 0)),
    ]
    out_specs = [block(3 * width), pl.BlockSpec((1, 1, 3 * width), lambda s: (s, 0, 0))]
    out_shape = [
        jax.ShapeDtypeStruct((rows, 3 * width), BF16),
        jax.ShapeDtypeStruct((seqs, 1, 3 * width), F32),
    ]
    operands = [
        queries, keys, values, grad_out, lse, cosine, sine,
        segments.reshape(rows, 1), segments.reshape(seqs, 1, SEQ),
    ]
    scratch = [pltpu.VMEM((SEQ, width), F32)] * 3
    params, kernel = {}, attention_backward_kernel
    if parts is not None:
        in_specs = in_specs + [pl.BlockSpec(memory_space=pl.ANY), whole(resid.shape)]
        out_specs = out_specs + [whole(resid.shape)]
        out_shape = out_shape + [jax.ShapeDtypeStruct(resid.shape, BF16)]
        operands = operands + [parts, resid]
        sems = lambda n: pltpu.SemaphoreType.DMA((n,))
        scratch = scratch + [sems(4), sems(PlaneScatter.SEMS), sems(PlaneScatter.SEMS)]
        scratch = scratch + scatter_scratch(*resid.shape)[1:]
        params = dict(collective_id=collective_id, has_side_effects=True)
        kernel = attention_backward_sums_kernel
    return pl.pallas_call(
        kernel,
        grid=(seqs,),
        in_specs=in_specs,
        out_specs=out_specs,
        out_shape=out_shape,
        scratch_shapes=scratch,
        compiler_params=pltpu.CompilerParams(vmem_limit_bytes=60 << 20, **params),
        cost_estimate=taking(42),
        name="attention_backward",
    )(*operands)


def row_pairs():
    return [(r, r ^ 1) for r in range(lax.axis_size("row"))]


def row_lines():
    size = lax.axis_size("row")
    return [list(range(start, size, PAIR)) for start in range(PAIR)]


def neighbours():
    return [list(range(r, r + PAIR)) for r in range(0, lax.axis_size("row"), PAIR)]


def swap_rows(values):
    return lax.ppermute(values, "row", row_pairs())


def after(value, *others):
    return lax.optimization_barrier((value,) + others)[0]


def gather_line(values, axis=0):
    return lax.all_gather(values, "row", axis=axis, tiled=True, axis_index_groups=row_lines())


def scatter_line(values, axis=0):
    return lax.psum_scatter(
        values, "row", scatter_dimension=axis, tiled=True, axis_index_groups=row_lines()
    )


def pick(values, index, axis):
    size = values.shape[axis] // PAIR
    return lax.dynamic_slice_in_dim(values, index * size, size, axis)


def in_order(x, own, other, axis):
    return jnp.where(
        x == 0, jnp.concatenate([own, other], axis), jnp.concatenate([other, own], axis)
    )


def own_columns(weight, x):
    return in_order(x, pick(weight, x, 1), swap_rows(pick(weight, 1 - x, 1)), 0)


def own_units(weight, x):
    kept, sent = pick(weight, x, 1).T, pick(weight, 1 - x, 1).T
    return in_order(x, kept, swap_rows(sent), 1)


def own_rows(grad, x):
    return pick(grad, x, 0), swap_rows(pick(grad, 1 - x, 0))


def places():
    row, col = lax.axis_index("row"), lax.axis_index("col")
    return row % PAIR, col // 2, col % 2, row, col


def peers(row, col):
    x = row % PAIR
    over_x = (row + 1 - 2 * x, col)
    over_y = (row, (col + 2) % 4)
    over_core = (row, col + 1 - 2 * (col % 2))
    return over_x, over_y, over_core


def meet(devices):
    barrier = pltpu.get_barrier_semaphore()
    for device in devices:
        pl.semaphore_signal(barrier, inc=1, device_id=device, device_id_type=MESH)
    pl.semaphore_wait(barrier, len(devices))


def block_at(ref, a, col, rows, width, start, count):
    at = pl.multiple_of(a * rows + start, 128)
    return ref.at[pl.ds(at, count), pl.ds(pl.multiple_of(col * width, 128), width)]


CHUNKS = 4


class Copies:
    def __init__(self, send_sem, recv_sem, over_core):
        self.send_sem, self.recv_sem, self.any = send_sem, recv_sem, over_core
        self.sent = []

    def copy(self, index, source, place, device):
        return pltpu.make_async_remote_copy(
            source, place, self.send_sem.at[index], self.recv_sem.at[index],
            device_id=device, device_id_type=MESH,
        )

    def send(self, index, source, place, device):
        task = self.copy(index, source, place, device)
        task.start()
        self.sent.append(task)

    def wait(self, index, place):
        self.copy(index, place, place, self.any).wait_recv()

    def finish(self):
        for task in self.sent:
            task.wait_send()
        self.sent = []


class PlaneGather:
    def __init__(self, copies, base, src_ref, out_ref, local_sem, over_y=CHUNKS // 2):
        self.copies, self.base, self.src, self.out = copies, base, src_ref, out_ref
        self.local_sem = local_sem
        self.rows, self.width = src_ref.shape
        self.count = self.rows // CHUNKS
        self.x, self.y, self.core, self.row, self.col = places()
        self.over_x, self.over_y, self.over_core = peers(self.row, self.col)
        self.col_y = (self.col + 2) % 4
        self.col_core = self.col + 1 - 2 * self.core
        self.first = list(range(over_y))
        self.second = list(range(over_y, CHUNKS))

    def piece(self, a, c, s):
        return block_at(self.out, a, c, self.rows, self.width, s * self.count, self.count)

    def own(self, s):
        return self.src.at[pl.ds(s * self.count, self.count), :]

    def send(self, group, s, source, place, device):
        self.copies.send(self.base + group * CHUNKS + s, source, place, device)

    def pass_on(self, group, a, c, s, device):
        self.send(group, s, self.piece(a, c, s), self.piece(a, c, s), device)

    def wait(self, group, a, c, s):
        self.copies.wait(self.base + group * CHUNKS + s, self.piece(a, c, s))

    def start_x(self):
        for s in self.first + self.second:
            self.send(0, s, self.own(s), self.piece(self.x, self.col, s), self.over_x)

    def start_y(self):
        for s in self.second + self.first:
            self.send(1, s, self.own(s), self.piece(self.x, self.col, s), self.over_y)

    def start_core(self):
        self.local = pltpu.make_async_copy(
            self.src, block_at(self.out, self.x, self.col, self.rows, self.width, 0, self.rows),
            self.local_sem,
        )
        self.local.start()
        for s in range(CHUNKS):
            self.send(4, s, self.own(s), self.piece(self.x, self.col, s), self.over_core)

    def near(self, i):
        s, t = (self.first + self.second)[i], (self.second + self.first)[i]
        x, col, col_y = self.x, self.col, self.col_y
        self.wait(0, 1 - x, col, s)
        if s in self.first:
            self.pass_on(2, 1 - x, col, s, self.over_y)
        self.pass_on(5, 1 - x, col, s, self.over_core)
        self.wait(1, x, col_y, t)
        if t in self.second:
            self.pass_on(2, x, col_y, t, self.over_x)
        self.pass_on(6, x, col_y, t, self.over_core)

    def far(self):
        for u in range(CHUNKS):
            self.wait(2, 1 - self.x, self.col_y, u)
            self.pass_on(7, 1 - self.x, self.col_y, u, self.over_core)

    def finish(self):
        other, corner = self.col_core, (self.col_core + 2) % 4
        for group, (a, c) in enumerate(
            ((self.x, other), (1 - self.x, other), (self.x, corner), (1 - self.x, corner))
        ):
            for s in range(CHUNKS):
                self.wait(4 + group, a, c, s)
        self.local.wait()


def gather_plane_kernel(src_ref, out_ref, local_sem, send_sem, recv_sem):
    _, _, _, row, col = places()
    devices = peers(row, col)
    meet(devices)
    copies = Copies(send_sem, recv_sem, devices[2])
    gather = PlaneGather(copies, 0, src_ref, out_ref, local_sem)
    gather.start_x()
    gather.start_y()
    gather.start_core()
    for i in range(CHUNKS):
        gather.near(i)
    gather.far()
    gather.finish()
    copies.finish()


LINES = 4


class LineGather:
    def __init__(self, up_send, up_recv, down_send, down_recv, block):
        self.up, self.down, self.block = (up_send, up_recv), (down_send, down_recv), block
        self.row, self.col = lax.axis_index("row"), lax.axis_index("col")
        self.z = self.row // PAIR

    def task(self, sems, step, source, device):
        send, recv = sems
        place = self.block(source)
        return pltpu.make_async_remote_copy(
            place, place, send.at[step], recv.at[step],
            device_id=(device, self.col), device_id_type=MESH,
        )

    def upward(self, step):
        source = jnp.maximum(self.z - step, 0)
        return self.task(self.up, step, source, jnp.minimum(self.row + PAIR, PAIR * LINES - 1))

    def downward(self, step):
        source = jnp.minimum(self.z + step, LINES - 1)
        return self.task(self.down, step, source, jnp.maximum(self.row - PAIR, 0))

    def start(self, step):
        @pl.when((self.z >= step) & (self.z < LINES - 1))
        def _():
            self.upward(step).start()

        @pl.when((self.z + step < LINES) & (self.z > 0))
        def _():
            self.downward(step).start()

    def receive(self, step):
        @pl.when(self.z >= step)
        def _():
            source = jnp.maximum(self.z - step, 0)
            self.task(self.up, step - 1, source, self.row).wait_recv()

        @pl.when(self.z + step < LINES)
        def _():
            source = jnp.minimum(self.z + step, LINES - 1)
            self.task(self.down, step - 1, source, self.row).wait_recv()

    def hop(self, step):
        self.receive(step)
        if step < LINES - 1:
            self.start(step)

    def finish(self):
        for step in range(LINES - 1):

            @pl.when((self.z >= step) & (self.z < LINES - 1))
            def _():
                self.upward(step).wait_send()

            @pl.when((self.z + step < LINES) & (self.z > 0))
            def _():
                self.downward(step).wait_send()


def gather_first_kernel(
    tokens_ref, grad_ref, query_ref, key_ref, value_ref, out_weight_ref, gate_ref, up_ref,
    gains_ref, places_ref,
    tokens_all_ref, grad_all_ref, qkv_ref, out_all_ref, ffn_ref, gains_all_ref, places_all_ref,
    turned_ref, local_sem, send_sem, recv_sem, swap_send, swap_recv, *line_sems,
):
    x, y, core, row, col = places()
    z = row // PAIR
    over_x, over_y, over_core = peers(row, col)
    over_far = (row, 3 - col)
    size = PAIR * LINES
    meet(
        (
            over_x, over_y, over_core, over_far,
            ((row + PAIR) % size, col), ((row + size - PAIR) % size, col),
        )
    )
    copies = Copies(send_sem, recv_sem, over_core)
    depth, width = out_weight_ref.shape
    half = width // PAIR
    units = ffn_ref.shape[2]
    base = 16 * CHUNKS
    local = []

    def keep(source, place):
        task = pltpu.make_async_copy(source, place, local_sem.at[2 + len(local)])
        task.start()
        local.append(task)

    def part(r, w):
        return qkv_ref.at[
            pl.ds(pl.multiple_of(r * depth, 128), depth), pl.ds(w * half, half)
        ]

    def out_block(z, x):
        return out_all_ref.at[pl.ds(pl.multiple_of((PAIR * z + x) * depth, 128), depth), :]

    def ffn_block(w, x):
        return ffn_ref.at[0, w, :, pl.ds(pl.multiple_of(x * depth, 128), depth)]

    def gains_block(c):
        return gains_all_ref.at[:, pl.ds(pl.multiple_of(c * width, 128), width)]

    def places_block(a):
        rows = places_ref.shape[1]
        return places_all_ref.at[:, pl.ds(pl.multiple_of(a * rows, 128), rows)]

    for w, ref in enumerate((query_ref, key_ref, value_ref)):
        theirs = ref.at[:, pl.ds(pl.multiple_of((1 - x) * half, 128), half)]
        copies.send(base + w, theirs, part(row, w), over_x)
        keep(ref.at[:, pl.ds(pl.multiple_of(x * half, 128), half)], part(row, w))
    keep(out_weight_ref, out_block(z, x))
    keep(gains_ref, gains_block(col))
    keep(places_ref, places_block(x))
    tokens = PlaneGather(copies, 0, tokens_ref, tokens_all_ref, local_sem.at[0], CHUNKS)
    grad = PlaneGather(copies, 8 * CHUNKS, grad_ref, grad_all_ref, local_sem.at[1], CHUNKS)
    tokens.start_y()
    tokens.start_core()
    copies.send(base + 5, places_ref, places_block(x), over_x)
    for i, device in enumerate((over_core, over_y, over_far)):
        copies.send(base + 6 + i, gains_ref, gains_block(col), device)
    for w in range(3):
        local[w].wait()
        copies.wait(base + w, part(row + 1 - 2 * x, w))
    heads = LineGather(
        *line_sems[:4],
        lambda at: qkv_ref.at[pl.ds(pl.multiple_of(at * PAIR * depth, 128), PAIR * depth), :],
    )
    outs = LineGather(*line_sems[4:], lambda at: out_block(at, x))

    def swap_out(z, x):
        block = out_block(z, x)
        return pltpu.make_async_remote_copy(
            block, block, swap_send.at[z], swap_recv.at[z], device_id=over_x, device_id_type=MESH
        )

    def swap_outs(step):
        @pl.when(z >= step)
        def _():
            swap_out(jnp.maximum(z - step, 0), x).start()

        @pl.when(z + step < LINES)
        def _():
            swap_out(jnp.minimum(z + step, LINES - 1), x).start()

    heads.start(0)
    tokens.start_x()
    for w, ref in enumerate((gate_ref, up_ref)):
        for j in range(PAIR * units // 128):
            turned_ref[w, j * 128 : (j + 1) * 128, :] = ref[:, j * 128 : (j + 1) * 128].T
    for i in range(CHUNKS - 1):
        tokens.near(i)
    local[3].wait()
    outs.start(0)
    heads.hop(1)
    tokens.near(CHUNKS - 1)
    for w in range(2):
        theirs = turned_ref.at[w, pl.ds(pl.multiple_of((1 - x) * units, 16), units), :]
        copies.send(base + 3 + w, theirs, ffn_block(w, x), over_x)
        keep(turned_ref.at[w, pl.ds(pl.multiple_of(x * units, 16), units), :], ffn_block(w, x))
    swap_out(z, x).start()
    grad.start_x()
    grad.start_y()
    grad.start_core()
    tokens.far()
    heads.hop(2)
    outs.hop(1)
    swap_outs(1)
    for i in range(CHUNKS - 1):
        grad.near(i)
    heads.hop(3)
    outs.hop(2)
    swap_outs(2)
    grad.near(CHUNKS - 1)
    grad.far()
    outs.hop(3)
    swap_outs(3)
    for at in range(LINES):
        swap_out(at, 1 - x).wait_recv()
    for w in range(2):
        copies.wait(base + 3 + w, ffn_block(w, 1 - x))
    copies.wait(base + 5, places_block(1 - x))
    for i, c in enumerate((col + 1 - 2 * core, (col + 2) % 4, 3 - col)):
        copies.wait(base + 6 + i, gains_block(c))
    for at in range(LINES):
        swap_out(at, x).wait_send()
    for task in local[3 + 1 :]:
        task.wait()
    tokens.finish()
    grad.finish()
    heads.finish()
    outs.finish()
    copies.finish()


def gather_first(
    tokens, grad, query, key, value, out_weight, gate, up, gains, places, collective_id
):
    rows, width = tokens.shape
    depth = out_weight.shape[0]
    units = gate.shape[1] // PAIR
    shape = lambda *dims: jax.ShapeDtypeStruct(dims, BF16)
    sems = lambda n: pltpu.SemaphoreType.DMA((n,))
    return pl.pallas_call(
        gather_first_kernel,
        in_specs=[pl.BlockSpec(memory_space=pltpu.VMEM)] * 10,
        out_specs=[pl.BlockSpec(memory_space=pl.ANY)] * 7,
        out_shape=[
            shape(PAIR * rows, 4 * width), shape(PAIR * rows, 4 * width),
            shape(PAIR * LINES * depth, 3 * width // PAIR), shape(PAIR * LINES * depth, width),
            shape(1, 2, units, PAIR * depth),
            jax.ShapeDtypeStruct((gains.shape[0], 4 * width), F32),
            jax.ShapeDtypeStruct((places.shape[0], PAIR * rows), jnp.int32),
        ],
        scratch_shapes=[
            pltpu.VMEM((2, PAIR * units, depth), BF16),
            sems(10), sems(16 * CHUNKS + 9), sems(16 * CHUNKS + 9), sems(4), sems(4),
        ]
        + [sems(3)] * 8,
        compiler_params=pltpu.CompilerParams(
            collective_id=collective_id, has_side_effects=True, vmem_limit_bytes=60 << 20
        ),
        cost_estimate=taking(110),
        name="gather_first",
    )(tokens, grad, query, key, value, out_weight, gate, up, gains, places)


def gather_plane(values, name, collective_id):
    cols = lax.axis_size("col")
    if cols != 4:
        across = lax.all_gather(values, "col", axis=1, tiled=True)
        return lax.all_gather(across, "row", axis=0, tiled=True, axis_index_groups=neighbours())
    rows, width = values.shape
    return pl.pallas_call(
        gather_plane_kernel,
        in_specs=[pl.BlockSpec(memory_space=pltpu.VMEM)],
        out_specs=pl.BlockSpec(memory_space=pl.ANY),
        out_shape=jax.ShapeDtypeStruct((PAIR * rows, cols * width), values.dtype),
        scratch_shapes=[
            pltpu.SemaphoreType.DMA,
            pltpu.SemaphoreType.DMA((8 * CHUNKS,)),
            pltpu.SemaphoreType.DMA((8 * CHUNKS,)),
        ],
        cost_estimate=taking(40),
        compiler_params=pltpu.CompilerParams(collective_id=collective_id, has_side_effects=True),
        name=name,
    )(values)


def add_rows(out_ref, left_ref, right_ref, rows, step=64):
    @pl.loop(0, rows // step)
    def _(i):
        at = pl.ds(pl.multiple_of(i * step, step), step)
        total = left_ref[at, :].astype(F32) + right_ref[at, :].astype(F32)
        out_ref[at, :] = total.astype(out_ref.dtype)


def scatter_plane_kernel(
    part_ref, out_ref, own_ref, core_ref, x_ref, y_ref, last_ref,
    load_sem, send_sem, recv_sem,
):
    rows, width = own_ref.shape[1:]
    half = rows // 2
    x, y, core, row, col = places()
    over_x, over_y, over_core = peers(row, col)
    meet((over_x, over_y, over_core))
    top, bottom = pl.ds(0, half), pl.ds(half, half)

    def copy(index, source, place, device):
        return pltpu.make_async_remote_copy(
            source, place, send_sem.at[index], recv_sem.at[index],
            device_id=device, device_id_type=MESH,
        )

    sent = []

    def send(index, source, place, device):
        task = copy(index, source, place, device)
        task.start()
        sent.append(task)

    def wait(index, place):
        copy(index, place, place, over_core).wait_recv()

    order = ((1 - x, 1 - y), (1 - x, y), (x, 1 - y), (x, y))
    loads = []
    for i, (a, b) in enumerate(order):
        slot = 2 * a + b
        send(
            i, block_at(part_ref, a, 2 * b + 1 - core, rows, width, 0, rows),
            core_ref.at[slot], over_core,
        )
        load = pltpu.make_async_copy(
            block_at(part_ref, a, 2 * b + core, rows, width, 0, rows),
            own_ref.at[slot], load_sem.at[i],
        )
        load.start()
        loads.append(load)
    for i, (a, b) in enumerate(order):
        slot = 2 * a + b
        loads[i].wait()
        wait(i, core_ref.at[slot])
        add_rows(own_ref.at[slot], own_ref.at[slot], core_ref.at[slot], rows)
        if i in (0, 1):
            send(4 + i, own_ref.at[slot, top, :], x_ref.at[i], over_x)
        if i in (0, 2):
            send(6 + i // 2, own_ref.at[slot, bottom, :], y_ref.at[i // 2], over_y)
    wait(4, x_ref.at[0])
    slot = 2 * x + 1 - y
    add_rows(own_ref.at[slot, top, :], own_ref.at[slot, top, :], x_ref.at[0], half)
    send(8, own_ref.at[slot, top, :], last_ref.at[0], over_y)
    wait(6, y_ref.at[0])
    slot = 2 * (1 - x) + y
    add_rows(own_ref.at[slot, bottom, :], own_ref.at[slot, bottom, :], y_ref.at[0], half)
    send(9, own_ref.at[slot, bottom, :], last_ref.at[1], over_x)
    slot = 2 * x + y
    wait(5, x_ref.at[1])
    add_rows(own_ref.at[slot, top, :], own_ref.at[slot, top, :], x_ref.at[1], half)
    wait(7, y_ref.at[1])
    add_rows(own_ref.at[slot, bottom, :], own_ref.at[slot, bottom, :], y_ref.at[1], half)
    wait(8, last_ref.at[0])
    add_rows(out_ref.at[top, :], own_ref.at[slot, top, :], last_ref.at[0], half)
    wait(9, last_ref.at[1])
    add_rows(out_ref.at[bottom, :], own_ref.at[slot, bottom, :], last_ref.at[1], half)
    for task in sent:
        task.wait_send()


def scatter_plane(values, name, collective_id):
    cols = lax.axis_size("col")
    if cols != 4:
        mine = lax.psum_scatter(
            values, "row", scatter_dimension=0, tiled=True, axis_index_groups=neighbours()
        )
        return lax.psum_scatter(mine, "col", scatter_dimension=1, tiled=True).astype(F32)
    rows, width = values.shape[0] // PAIR, values.shape[1] // cols
    return pl.pallas_call(
        scatter_plane_kernel,
        in_specs=[pl.BlockSpec(memory_space=pl.ANY)],
        out_specs=pl.BlockSpec(memory_space=pltpu.VMEM),
        out_shape=jax.ShapeDtypeStruct((rows, width), F32),
        scratch_shapes=[
            pltpu.VMEM((4, rows, width), BF16),
            pltpu.VMEM((4, rows, width), BF16),
            pltpu.VMEM((2, rows // 2, width), BF16),
            pltpu.VMEM((2, rows // 2, width), BF16),
            pltpu.VMEM((2, rows // 2, width), BF16),
            pltpu.SemaphoreType.DMA((4,)),
            pltpu.SemaphoreType.DMA((10,)),
            pltpu.SemaphoreType.DMA((10,)),
        ],
        cost_estimate=taking(40),
        compiler_params=pltpu.CompilerParams(
            collective_id=collective_id, has_side_effects=True, vmem_limit_bytes=40 << 20
        ),
        name=name,
    )(values)


def gather_heads_kernel(src_ref, out_ref, local_sem, send_sem, recv_sem):
    rows, width = out_ref.shape[0], src_ref.shape[1]
    x, y, core, row, col = places()
    over_x, over_y, over_core = peers(row, col)
    meet((over_x, over_y, over_core))
    count = rows // 2
    col_y = (col + 2) % 4
    col_core = col + 1 - 2 * core

    def piece(c, a, s):
        at = pl.multiple_of((PAIR * c + a) * width, 128)
        return out_ref.at[pl.ds(s * count, count), pl.ds(at, width)]

    def mine(a, s):
        return src_ref.at[pl.ds(pl.multiple_of(a * rows + s * count, 128), count), :]

    def copy(index, source, place, device):
        return pltpu.make_async_remote_copy(
            source, place, send_sem.at[index], recv_sem.at[index],
            device_id=device, device_id_type=MESH,
        )

    sent = []

    def send(index, source, place, device):
        task = copy(index, source, place, device)
        task.start()
        sent.append(task)

    def wait(index, place):
        copy(index, place, place, over_core).wait_recv()

    local = []
    for s in range(2):
        send(s, mine(1 - x, s), piece(col, x, s), over_x)
        send(2 + s, mine(x, s), piece(col, x, s), over_y)
        task = pltpu.make_async_copy(mine(x, s), piece(col, x, s), local_sem.at[s])
        task.start()
        local.append(task)
    for s in range(2):
        send(4 + s, mine(x, s), piece(col, x, s), over_core)
    for s in range(2):
        wait(s, piece(col, 1 - x, s))
        send(6 + s, piece(col, 1 - x, s), piece(col, 1 - x, s), over_y)
        send(8 + s, piece(col, 1 - x, s), piece(col, 1 - x, s), over_core)
    for s in range(2):
        wait(2 + s, piece(col_y, x, s))
        send(10 + s, piece(col_y, x, s), piece(col_y, x, s), over_core)
    for s in range(2):
        wait(6 + s, piece(col_y, 1 - x, s))
        send(12 + s, piece(col_y, 1 - x, s), piece(col_y, 1 - x, s), over_core)
    far = (col_core + 2) % 4
    for s in range(2):
        wait(4 + s, piece(col_core, x, s))
        wait(8 + s, piece(col_core, 1 - x, s))
        wait(10 + s, piece(far, x, s))
        wait(12 + s, piece(far, 1 - x, s))
    for task in sent:
        task.wait_send()
    for task in local:
        task.wait()


def gather_heads(values, x, collective_id):
    cols = lax.axis_size("col")
    if cols != 4:
        here = in_order(x, pick(values, x, 0), swap_rows(pick(values, 1 - x, 0)), 1)
        return lax.all_gather(here, "col", axis=1, tiled=True)
    rows, width = values.shape[0] // PAIR, values.shape[1]
    return pl.pallas_call(
        gather_heads_kernel,
        in_specs=[pl.BlockSpec(memory_space=pltpu.VMEM)],
        out_specs=pl.BlockSpec(memory_space=pl.ANY),
        out_shape=jax.ShapeDtypeStruct((rows, PAIR * cols * width), values.dtype),
        scratch_shapes=[
            pltpu.SemaphoreType.DMA((2,)),
            pltpu.SemaphoreType.DMA((14,)),
            pltpu.SemaphoreType.DMA((14,)),
        ],
        cost_estimate=taking(28),
        compiler_params=pltpu.CompilerParams(collective_id=collective_id, has_side_effects=True),
        name="gather_heads",
    )(values)


def scatter_heads(values, x):
    mine = lax.psum_scatter(values, "col", scatter_dimension=1, tiled=True)
    return in_order(x, pick(mine, x, 1), swap_rows(pick(mine, 1 - x, 1)), 0)


def sum_rows_kernel(part_ref, out_ref, slots_ref, send_sem, recv_sem):
    size = slots_ref.shape[0]
    row, col = lax.axis_index("row"), lax.axis_index("col")
    others = [(lax.rem(row + step, size), col) for step in range(1, size)]
    meet(others)
    slots_ref[0] = part_ref[...]
    copies = [
        pltpu.make_async_remote_copy(
            slots_ref.at[0], slots_ref.at[step], send_sem.at[step], recv_sem.at[step],
            device_id=others[step - 1], device_id_type=MESH,
        )
        for step in range(1, size)
    ]
    for copy in copies:
        copy.start()
    for copy in copies:
        copy.wait_recv()
    total = jnp.zeros(part_ref.shape, F32)
    for r in range(size):
        total += slots_ref[lax.rem(row + size - r, size)]
    out_ref[...] = total
    for copy in copies:
        copy.wait_send()


def sum_rows(part, collective_id):
    size = lax.axis_size("row")
    if size != 8:
        return lax.psum(part, "row")
    return pl.pallas_call(
        sum_rows_kernel,
        in_specs=[pl.BlockSpec(memory_space=pltpu.VMEM)],
        out_specs=pl.BlockSpec(memory_space=pltpu.VMEM),
        out_shape=jax.ShapeDtypeStruct(part.shape, F32),
        scratch_shapes=[
            pltpu.VMEM((size,) + part.shape, F32),
            pltpu.SemaphoreType.DMA((size,)),
            pltpu.SemaphoreType.DMA((size,)),
        ],
        cost_estimate=taking(8),
        compiler_params=pltpu.CompilerParams(collective_id=collective_id, has_side_effects=True),
        name="sum_rows",
    )(part)


def row_stats(values):
    mean = jnp.mean(values, axis=1, keepdims=True)
    var = jnp.mean(values * values, axis=1, keepdims=True) - mean * mean
    return mean, lax.rsqrt(var + 1e-05)


def norm_backward(grad_norm, unit_values, inv_std, norm_gain):
    full_width = grad_norm.shape[1] * lax.axis_size("col")
    grad_unit = grad_norm * norm_gain
    row_sums = lax.psum(
        (jnp.sum(grad_unit, axis=1), jnp.sum(grad_unit * unit_values, axis=1)), "col"
    )
    grad_in = inv_std * (
        grad_unit
        - row_sums[0][:, None] / full_width
        - unit_values * row_sums[1][:, None] / full_width
    )
    return grad_in, jnp.sum(grad_norm * unit_values, axis=0)


def rotation_tables(positions):
    half = ROT // 2
    inv_freq = BASE ** (-(jnp.arange(half, dtype=F32) * 2.0) / ROT)
    angles = positions.astype(F32)[:, None] * inv_freq[None, :]
    cosine, sine = jnp.cos(angles), jnp.sin(angles)
    rest = HEAD_DIM - ROT
    ones = jnp.ones((positions.shape[0], rest), F32)
    cosine = jnp.concatenate([cosine, cosine, ones], axis=1)
    sine = jnp.concatenate([-sine, sine, 0.0 * ones], axis=1)
    return jnp.tile(cosine, (1, 2)), jnp.tile(sine, (1, 2))


TILE = 256


def norm_tile(values_ref, gain_ref, stats_ref):
    values = values_ref[...].astype(F32)
    mean, inv_std = row_stats(values)
    lane = lax.broadcasted_iota(jnp.int32, stats_ref.shape, 1)
    stats_ref[...] = jnp.where(lane == 0, mean, inv_std)
    return ((values - mean) * inv_std * gain_ref[...]).astype(BF16)


def project_heads_kernel(
    tokens_ref, gain_ref, weight_ref, bias_ref, cos_ref, sin_ref,
    normed_ref, q_ref, k_ref, v_ref, stats_ref,
):
    width = q_ref.shape[1]
    normed = norm_tile(tokens_ref, gain_ref, stats_ref)
    normed_ref[...] = normed
    in_head = lax.broadcasted_iota(jnp.int32, (1, width), 1) % HEAD_DIM
    cosine = jnp.tile(cos_ref[...], (1, width // cos_ref.shape[1]))
    sine = jnp.tile(sin_ref[...], (1, width // sin_ref.shape[1]))
    pre = dot(normed, weight_ref[...]) + bias_ref[...]
    for ref, at, scale in ((q_ref, 0, SCALE), (k_ref, width, 1.0)):
        part = pre[:, at : at + width]
        turned = part * cosine + swap_pairs(part, in_head) * sine
        ref[...] = turned.astype(BF16) * jnp.asarray(scale, BF16)
    v_ref[...] = pre[:, 2 * width :].astype(BF16)


def tiled(columns):
    return pl.BlockSpec((TILE, columns), lambda i: (i, 0))


def whole(shape):
    return pl.BlockSpec(shape, lambda i: (0,) * len(shape))


def column_block(blocks_ref, all_ref, other, sems, index):
    row, col = lax.axis_index("row"), lax.axis_index("col")
    send_sem, recv_sem = sems
    return pltpu.make_async_remote_copy(
        blocks_ref.at[other], all_ref.at[col], send_sem.at[index], recv_sem.at[index],
        device_id=(row, other), device_id_type=MESH,
    )


def exchange_beside(kernel, blocks_ref, all_ref, steps, local, *sems, more=()):
    row, col = lax.axis_index("row"), lax.axis_index("col")
    others = [col + d - 2 * d * ((col // d) % 2) if d < 3 else 3 - col for d in steps]

    @pl.when(pl.program_id(0) == 0)
    def _():
        meet([(row, other) for other in others] + list(more))
        for i, other in enumerate(others):
            column_block(blocks_ref, all_ref, other, sems, i).start()
        if local is not None:
            pltpu.make_async_copy(blocks_ref.at[col], *local).start()

    kernel()

    @pl.when(pl.program_id(0) == pl.num_programs(0) - 1)
    def _():
        if local is not None:
            stage, local_sem = local
            pltpu.make_async_copy(blocks_ref.at[col], stage, local_sem).wait()
            task = pltpu.make_async_copy(stage, all_ref.at[col], local_sem)
            task.start()
            task.wait()
        for i, other in enumerate(others):
            task = column_block(blocks_ref, all_ref, other, sems, i)
            task.wait_send()
            send_sem, recv_sem = sems
            pltpu.make_async_remote_copy(
                blocks_ref.at[other], all_ref.at[other], send_sem.at[i], recv_sem.at[i],
                device_id=(row, other), device_id_type=MESH,
            ).wait_recv()


def project_heads_exchange_kernel(*refs):
    *ins, blocks_ref = refs[:7]
    outs, all_ref, (stage, local_sem, *sems) = refs[7:12], refs[12], refs[13:]
    exchange_beside(
        lambda: project_heads_kernel(*ins, *outs),
        blocks_ref, all_ref, (2,), (stage, local_sem), *sems,
    )


def project_heads(tokens, gain, weight, bias, cosine, sine, blocks=None, collective_id=None):
    rows, depth = tokens.shape
    width = weight.shape[1] // 3
    in_specs = [
        tiled(depth), whole((1, depth)), whole(weight.shape), whole((1, 3 * width)),
        tiled(cosine.shape[1]), tiled(cosine.shape[1]),
    ]
    out_specs = [tiled(depth)] + [tiled(width)] * 3 + [tiled(8)]
    out_shape = [
        jax.ShapeDtypeStruct((rows, depth), BF16),
        *[jax.ShapeDtypeStruct((rows, width), BF16)] * 3,
        jax.ShapeDtypeStruct((rows, 8), F32),
    ]
    operands = [tokens, gain.reshape(1, depth), weight, bias.reshape(1, 3 * width), cosine, sine]
    params, scratch, kernel = {}, [], project_heads_kernel
    if blocks is not None:
        anywhere = pl.BlockSpec(memory_space=pl.ANY)
        in_specs, out_specs = in_specs + [anywhere], out_specs + [anywhere]
        out_shape = out_shape + [jax.ShapeDtypeStruct(blocks.shape, BF16)]
        operands = operands + [blocks]
        scratch = [pltpu.VMEM(blocks.shape[1:], BF16), pltpu.SemaphoreType.DMA]
        scratch = scratch + [pltpu.SemaphoreType.DMA((1,))] * 2
        params = dict(collective_id=collective_id, has_side_effects=True)
        kernel = project_heads_exchange_kernel
    return pl.pallas_call(
        kernel,
        grid=(rows // TILE,),
        in_specs=in_specs,
        out_specs=out_specs,
        out_shape=out_shape,
        scratch_shapes=scratch,
        compiler_params=pltpu.CompilerParams(vmem_limit_bytes=48 << 20, **params),
        cost_estimate=taking(16),
        name="project_heads",
    )(*operands)


def feed_forward_kernel(
    resid_ref, gain_ref, weight_ref, grad_ref, down_ref,
    normed_ref, hidden_ref, dgate_ref, dup_ref, stats_ref,
):
    lines, _, hidden, width = weight_ref.shape
    normed_ref[...] = norm_tile(resid_ref, gain_ref, stats_ref)
    gate = jnp.zeros((hidden, TILE), F32)
    up = jnp.zeros((hidden, TILE), F32)
    dhidden = jnp.zeros((hidden, TILE), F32)
    for z in range(lines):
        part = normed_ref[:, z * width : (z + 1) * width]
        gate += dot(weight_ref[z, 0], part, (1,), (1,))
        up += dot(weight_ref[z, 1], part, (1,), (1,))
    for c in range(down_ref.shape[0]):
        part = grad_ref[:, c * width : (c + 1) * width]
        dhidden += dot(down_ref[c], part, (1,), (1,))
    sigmoid = 1.0 / (1.0 + jnp.exp(-gate))
    silu = gate * sigmoid
    hidden_ref[...] = (silu * up).astype(BF16)
    dgate_ref[...] = (dhidden * up * sigmoid * (1.0 + gate * (1.0 - sigmoid))).astype(BF16)
    dup_ref[...] = (dhidden * silu).astype(BF16)


def feed_forward(resid, gain, weight, grad, down):
    rows, depth = resid.shape
    hidden = down.shape[1]
    across = pl.BlockSpec((hidden, TILE), lambda i: (0, i))
    return pl.pallas_call(
        feed_forward_kernel,
        grid=(rows // TILE,),
        in_specs=[
            tiled(depth), whole((1, depth)), whole(weight.shape), tiled(depth), whole(down.shape)
        ],
        out_specs=[tiled(depth)] + [across] * 3 + [tiled(8)],
        out_shape=[jax.ShapeDtypeStruct((rows, depth), BF16)]
        + [jax.ShapeDtypeStruct((hidden, rows), BF16)] * 3
        + [jax.ShapeDtypeStruct((rows, 8), F32)],
        compiler_params=pltpu.CompilerParams(vmem_limit_bytes=56 << 20),
        cost_estimate=taking(28),
        name="feed_forward",
    )(resid, gain.reshape(1, depth), weight, grad, down)


def weight_grads_kernel(*refs):
    *left_refs, right_ref, out_ref = refs
    for i, left_ref in enumerate(left_refs):
        out_ref[0, i] = dot(left_ref[...], right_ref[...]).astype(BF16)


def weight_grads(lefts, right, width, name):
    hidden, rows = lefts[0].shape
    blocks = right.shape[1] // width
    return pl.pallas_call(
        weight_grads_kernel,
        grid=(blocks,),
        in_specs=[whole((hidden, rows))] * len(lefts)
        + [pl.BlockSpec((rows, width), lambda i: (0, i))],
        out_specs=pl.BlockSpec((1, len(lefts), hidden, width), lambda i: (i, 0, 0, 0)),
        out_shape=jax.ShapeDtypeStruct((blocks, len(lefts), hidden, width), BF16),
        compiler_params=pltpu.CompilerParams(vmem_limit_bytes=56 << 20),
        cost_estimate=taking(9 * len(lefts)),
        name=name,
    )(*lefts, right)


def back_project_kernel(*refs):
    *left_refs, weight_ref, out_ref = refs
    width = weight_ref.shape[-1]
    lefts = [ref[...].T for ref in left_refs]
    for z in range(weight_ref.shape[0]):
        total = sum(dot(left, weight_ref[z, i]) for i, left in enumerate(lefts))
        out_ref[:, z * width : (z + 1) * width] = total.astype(BF16)


def back_project(lefts, weight, name):
    hidden, rows = lefts[0].shape
    depth = weight.shape[0] * weight.shape[-1]
    return pl.pallas_call(
        back_project_kernel,
        grid=(rows // TILE,),
        in_specs=[pl.BlockSpec((hidden, TILE), lambda i: (0, i))] * len(lefts)
        + [whole(weight.shape)],
        out_specs=tiled(depth),
        out_shape=jax.ShapeDtypeStruct((rows, depth), BF16),
        compiler_params=pltpu.CompilerParams(vmem_limit_bytes=48 << 20),
        cost_estimate=taking(10 * len(lefts)),
        name=name,
    )(*lefts, weight)


class PlaneScatter:
    SEMS = 14

    def __init__(self, copies, base, fill, sent_ref, own_ref, core_ref, x_ref, y_ref, last_ref):
        self.copies, self.base, self.fill = copies, base, fill
        self.sent, self.own, self.core_part = sent_ref, own_ref, core_ref
        self.x_ref, self.y_ref, self.last = x_ref, y_ref, last_ref
        self.x, self.y, self.core, row, col = places()
        self.over_x, self.over_y, self.over_core = peers(row, col)
        x, y = self.x, self.y
        self.order = ((1 - x, 1 - y), (1 - x, y), (x, 1 - y), (x, y))
        self.theirs = [2 * b + 1 - self.core for _, b in self.order]
        self.ours = [2 * b + self.core for _, b in self.order]
        self.half = own_ref.shape[1] // 2
        self.rows = (pl.ds(0, self.half), pl.ds(self.half, self.half))
        self.given = Copies(copies.send_sem, copies.recv_sem, self.over_core)

    def send(self, index, source, place, device):
        self.copies.send(self.base + index, source, place, device)

    def wait(self, index, place):
        self.copies.wait(self.base + index, place)

    def give(self, i, h):
        a, _ = self.order[i]
        self.fill(self.sent.at[i], a, self.theirs[i], h, None)
        at = self.rows[h]
        self.given.send(
            self.base + 2 * i + h, self.sent.at[i, at, :], self.core_part.at[i, at, :], self.over_core
        )

    def keep(self, i, h):
        a, _ = self.order[i]
        at = self.rows[h]
        self.wait(2 * i + h, self.core_part.at[i, at, :])
        self.fill(self.own.at[i], a, self.ours[i], h, self.core_part.at[i])
        self.part_done(i, h)

    def part_done(self, i, h):
        at = self.rows[h]
        if h == 0 and i in (0, 1):
            self.send(8 + i, self.own.at[i, at, :], self.x_ref.at[i], self.over_x)
        if h == 1 and i in (0, 2):
            self.send(10 + i // 2, self.own.at[i, at, :], self.y_ref.at[i // 2], self.over_y)

    def first(self):
        self.give(0, 0)
        self.give(0, 1)
        self.keep(0, 0)
        self.keep(0, 1)
        for h in range(2):
            self.give(1, h)
            self.give(2, h)
        self.keep(1, 0)
        self.keep(2, 1)
        self.keep(2, 0)
        self.keep(1, 1)
        for h in range(2):
            self.give(3, h)
        for h in range(2):
            self.keep(3, h)

    def settle(self):
        self.given.finish()

    def drain(self):
        view = self.own.at[0, self.rows[0], :]
        for index in range(self.SEMS):
            self.copies.copy(self.base + index, view, view, self.over_core).wait_send()

    def add(self, i, h, ref):
        at = self.own.at[i, self.rows[h], :]
        add_rows(at, at, ref, self.half)

    def second(self):
        self.wait(8, self.x_ref.at[0])
        self.add(2, 0, self.x_ref.at[0])
        self.send(12, self.own.at[2, self.rows[0], :], self.last.at[0], self.over_y)
        self.wait(10, self.y_ref.at[0])
        self.add(1, 1, self.y_ref.at[0])
        self.send(13, self.own.at[1, self.rows[1], :], self.last.at[1], self.over_x)
        self.wait(9, self.x_ref.at[1])
        self.add(3, 0, self.x_ref.at[1])
        self.wait(11, self.y_ref.at[1])
        self.add(3, 1, self.y_ref.at[1])

    def third(self):
        self.wait(12, self.last.at[0])
        self.wait(13, self.last.at[1])

    def result(self, start, count):
        h, other = divmod(start, self.half)
        return self.own[3, pl.ds(start, count), :].astype(F32) + self.last[
            h, pl.ds(other, count), :
        ].astype(F32)


class PartsScatter(PlaneScatter):
    def __init__(self, copies, base, parts_ref, load_sem, *scratch):
        super().__init__(copies, base, None, None, *scratch)
        blocks = [a * 4 for a, _ in self.order]
        self.parts, self.load_sem = parts_ref, load_sem
        self.sources = [parts_ref.at[at + c] for at, c in zip(blocks, self.theirs)]
        self.loads = [
            pltpu.make_async_copy(parts_ref.at[at + c], self.own.at[i], load_sem.at[i])
            for i, (at, c) in enumerate(zip(blocks, self.ours))
        ]

    def start(self):
        for i, load in enumerate(self.loads):
            load.start()
            for h, at in enumerate(self.rows):
                self.given.send(
                    self.base + 2 * i + h, self.sources[i].at[at, :],
                    self.core_part.at[i, at, :], self.over_core,
                )

    def keep(self, i, h):
        if h == 0:
            self.loads[i].wait()
        at = self.rows[h]
        self.wait(2 * i + h, self.core_part.at[i, at, :])
        self.add(i, h, self.core_part.at[i, at, :])
        self.part_done(i, h)


class LineScatter:
    def __init__(self, up_send, up_recv, down_send, down_recv, part, up_ref, down_ref):
        self.part, self.row, self.col = part, lax.axis_index("row"), lax.axis_index("col")
        self.z = self.row // PAIR
        last = LINES - 1
        self.ways = (
            (self.z, lambda n: n, up_ref, up_send, up_recv, jnp.minimum(self.row + PAIR, PAIR * last + PAIR - 1)),
            (last - self.z, lambda n: last - n, down_ref, down_send, down_recv, jnp.maximum(self.row - PAIR, 0)),
        )

    def clear(self):
        for n, _, slots, _, _, _ in self.ways:

            @pl.when(n == 0)
            def _():
                slots[LINES - 2] = jnp.zeros(slots.shape[1:], slots.dtype)

    def task(self, way, step, source):
        _, _, slots, send, recv, device = way
        return pltpu.make_async_remote_copy(
            source, slots.at[step], send.at[step], recv.at[step],
            device_id=(device, self.col), device_id_type=MESH,
        )

    def sends(self, way, step, act):
        n, place, slots, _, _, _ = way

        @pl.when(n == 0)
        def _():
            act(self.task(way, step, self.part(place(LINES - 1 - step))))

        if step > 0:

            @pl.when((n > 0) & (n <= step))
            def _():
                act(self.task(way, step, slots.at[step - 1]))

    def start(self):
        for way in self.ways:
            self.sends(way, 0, lambda task: task.start())

    def hop(self, step):
        for way in self.ways:
            n, place, slots, _, _, _ = way

            @pl.when((n >= 1) & (n <= step + 1))
            def _():
                self.task(way, step, slots.at[step]).wait_recv()
                add_rows(
                    slots.at[step], slots.at[step], self.part(place(LINES - 2 - step + n)),
                    slots.shape[1],
                )

            self.sends(way, step + 1, lambda task: task.start())

    def receive(self):
        last = LINES - 2
        for way in self.ways:
            n, _, slots, _, _, _ = way

            @pl.when(n >= 1)
            def _():
                self.task(way, last, slots.at[last]).wait_recv()

    def total(self, at):
        last = LINES - 2
        result = self.part(self.z)[at, :].astype(F32)
        for _, _, slots, _, _, _ in self.ways:
            result = result + slots[last, at, :].astype(F32)
        return result

    def finish(self):
        for way in self.ways:
            for step in range(LINES - 1):
                self.sends(way, step, lambda task: task.wait_send())


STEP = 128


class NormBack:
    def __init__(
        self, copies, base, values_ref, stats_ref, gain_ref, base_ref, out_ref, low_ref, dgain_ref,
        sums_ref,
    ):
        self.copies, self.base = copies, base
        self.values, self.stats, self.gain, self.more = values_ref, stats_ref, gain_ref, base_ref
        self.out, self.low, self.dgain, self.sums = out_ref, low_ref, dgain_ref, sums_ref

    def unit_of(self, at):
        stats = self.stats[at, :]
        return (self.values[at, :].astype(F32) - stats[:, 0:1]) * stats[:, 1:2]

    def start(self, result, devices):
        lane = lax.broadcasted_iota(jnp.int32, (1, 128), 1)
        self.dgain[...] = jnp.zeros_like(self.dgain)
        for start in range(0, self.out.shape[0], STEP):
            at = pl.ds(start, STEP)
            grad = result(start, STEP)
            self.out[at, :] = grad
            unit = self.unit_of(at)
            self.dgain[...] += jnp.sum(grad * unit, axis=0, keepdims=True)
            grad = grad * self.gain[...]
            first = jnp.sum(grad, axis=1, keepdims=True)
            second = jnp.sum(grad * unit, axis=1, keepdims=True)
            both = jnp.where(lane == 0, first, jnp.where(lane == 1, second, 0.0))
            self.sums[0, :, start : start + STEP] = both.T[:8]
        for i, device in enumerate(devices):
            self.copies.send(self.base + i, self.sums.at[0], self.sums.at[1 + i], device)

    def finish(self):
        rows, width = self.out.shape
        for i in range(3):
            self.copies.wait(self.base + i, self.sums.at[1 + i])
        for start in range(0, rows, STEP):
            at = pl.ds(start, STEP)
            columns = slice(start, start + STEP)
            total = (self.sums[0, :, columns] + self.sums[1, :, columns]) + (
                self.sums[2, :, columns] + self.sums[3, :, columns]
            )
            total = jnp.concatenate([total, jnp.zeros((STEP - 8, STEP), F32)], axis=0).T
            total = total * (1.0 / (4 * width))
            unit = self.unit_of(at)
            grad = self.out[at, :] * self.gain[...]
            grad = self.stats[at, 1:2] * (grad - total[:, 0:1] - unit * total[:, 1:2])
            grad = grad + self.more[at, :].astype(F32)
            self.out[at, :] = grad
            if self.low is not None:
                self.low[at, :] = grad.astype(BF16)


def scatter_scratch(rows, width):
    block = lambda n, r: pltpu.VMEM((n, r, width), BF16)
    return [
        block(4, rows), block(4, rows), block(4, rows),
        block(2, rows // 2), block(2, rows // 2), block(2, rows // 2),
    ]


def around():
    _, _, _, row, col = places()
    over_x, over_y, over_core = peers(row, col)
    return over_x, over_y, over_core, (row, 3 - col)


def filling(rows, product):
    half = rows // 2

    def fill(ref, a, c, h, more):
        @pl.loop(0, half // TILE)
        def _(i):
            start = h * half + i * TILE
            total = product(pl.ds(pl.multiple_of(a * rows + start, TILE), TILE), c)
            at = pl.ds(pl.multiple_of(start, TILE), TILE)
            if more is not None:
                total = total + more[at, :].astype(F32)
            ref[at, :] = total.astype(BF16)

    return fill


def turn_rows(left_ref, source_ref, a, rows):
    @pl.loop(0, rows // TILE)
    def _(i):
        at = pl.ds(pl.multiple_of(a * rows + i * TILE, TILE), TILE)
        left_ref[at, :] = source_ref[:, at].T


def back_second_kernel(
    gate_ref, up_ref, weight_ref, hidden_hbm, grad_hbm, values_ref, stats_ref, gain_ref, base_ref,
    out_ref, low_ref, dgain_ref, down_ref,
    hidden_ref, grad_ref, gate_vmem, up_vmem, weight_vmem, left_ref, sums_ref, load_sem, send_sem, recv_sem, *scratch,
):
    rows, width = out_ref.shape
    x, y, core, _, _ = places()
    devices = around()

    def load_left(i, a):
        at = pl.ds(pl.multiple_of(a * rows, TILE), rows)
        return [
            pltpu.make_async_copy(ref.at[:, at], vmem.at[:, at], load_sem.at[2 * i + j])
            for j, (ref, vmem) in enumerate(((gate_ref, gate_vmem), (up_ref, up_vmem)))
        ]

    def load_weight(i, c):
        return pltpu.make_async_copy(weight_ref.at[c], weight_vmem.at[c], load_sem.at[4 + i])

    lefts = [load_left(0, 1 - x), load_left(1, x)]
    columns = (2 * (1 - y) + 1 - core, 2 * (1 - y) + core, 2 * y + 1 - core, 2 * y + core)
    weights = [load_weight(i, c) for i, c in enumerate(columns)]
    others = [
        pltpu.make_async_copy(hidden_hbm, hidden_ref, load_sem.at[8]),
        pltpu.make_async_copy(grad_hbm, grad_ref, load_sem.at[9]),
    ]
    for task in (*lefts[0], *weights, *lefts[1], *others):
        task.start()
    meet(devices)
    copies = Copies(send_sem, recv_sem, devices[2])

    def turn(i, a):
        for j, (task, vmem) in enumerate(zip(lefts[i], (gate_vmem, up_vmem))):
            task.wait()
            turn_rows(left_ref.at[j], vmem, a, rows)

    def product(at, c):
        return dot(left_ref[0, at, :], weight_vmem[c, 0]) + dot(
            left_ref[1, at, :], weight_vmem[c, 1]
        )

    scatter = PlaneScatter(copies, 0, filling(rows, product), *scratch)
    turn(0, 1 - x)
    weights[0].wait()
    scatter.give(0, 0)
    scatter.give(0, 1)
    weights[1].wait()
    scatter.keep(0, 0)
    scatter.keep(0, 1)
    weights[2].wait()
    scatter.give(1, 0)
    scatter.give(1, 1)
    weights[3].wait()
    scatter.keep(1, 0)
    turn(1, x)
    scatter.give(2, 1)
    scatter.give(2, 0)
    scatter.keep(2, 1)
    scatter.keep(2, 0)
    scatter.keep(1, 1)
    scatter.give(3, 0)
    scatter.give(3, 1)
    scatter.keep(3, 0)
    scatter.keep(3, 1)
    scatter.settle()
    scatter.second()
    for task in others:
        task.wait()
    for c in range(down_ref.shape[0]):
        right = grad_ref[:, c * width : (c + 1) * width]
        down_ref[c] = dot(hidden_ref[...], right).astype(BF16)
    scatter.third()
    norm = NormBack(
        copies, PlaneScatter.SEMS, values_ref, stats_ref, gain_ref, base_ref, out_ref, low_ref,
        dgain_ref, sums_ref,
    )
    norm.start(scatter.result, devices[1:])
    norm.finish()
    copies.finish()


def back_second(gate, up, weight, hidden, grad, values, stats, gain, base, collective_id):
    rows, width = values.shape
    units, tokens = gate.shape
    vmem, anywhere = pl.BlockSpec(memory_space=pltpu.VMEM), pl.BlockSpec(memory_space=pl.ANY)
    sems = lambda n: pltpu.SemaphoreType.DMA((n,))
    return pl.pallas_call(
        back_second_kernel,
        in_specs=[anywhere] * 5 + [vmem] * 4,
        out_specs=[vmem] * 4,
        out_shape=[
            jax.ShapeDtypeStruct((rows, width), F32),
            jax.ShapeDtypeStruct((rows, width), BF16),
            jax.ShapeDtypeStruct((1, width), F32),
            jax.ShapeDtypeStruct((grad.shape[1] // width, units, width), BF16),
        ],
        scratch_shapes=[
            pltpu.VMEM(hidden.shape, BF16), pltpu.VMEM(grad.shape, BF16),
            pltpu.VMEM(gate.shape, BF16), pltpu.VMEM(up.shape, BF16),
            pltpu.VMEM(weight.shape, BF16), pltpu.VMEM((2, tokens, units), BF16),
            pltpu.VMEM((4, 8, rows), F32),
            sems(10), sems(PlaneScatter.SEMS + 3), sems(PlaneScatter.SEMS + 3),
            *scatter_scratch(rows, width),
        ],
        compiler_params=pltpu.CompilerParams(
            collective_id=collective_id, has_side_effects=True, vmem_limit_bytes=63 << 20
        ),
        cost_estimate=taking(50),
        name="back_second",
    )(gate, up, weight, hidden, grad, values, stats, gain.reshape(1, width), base)


def back_first_kernel(
    grad_ref, weight_ref, values_ref, stats_ref, gain_ref, base_ref, part_ref, ffn_ref, heads_ref,
    out_ref, dgain_ref, query_ref, key_ref, value_ref, gate_ref, up_grad_ref, out_grad_ref,
    sums_ref, up_ref, down_line_ref, heads_up_ref, heads_down_ref, swap_ref, swapped_ref, turn_ref,
    send_sem, recv_sem, *scratch,
):
    line_sems, scratch = scratch[:12], scratch[12:]
    rows, width = out_ref.shape
    x, _, _, row, col = places()
    devices = around()
    size = PAIR * LINES
    meet((*devices, ((row + PAIR) % size, col), ((row + size - PAIR) % size, col)))
    copies = Copies(send_sem, recv_sem, devices[2])
    depth, columns = up_ref.shape[2:]

    def line_of(k):
        at = pl.ds(k * columns, columns)
        return LineScatter(
            *line_sems[4 * k : 4 * k + 4],
            lambda b: part_ref.at[pl.ds(pl.multiple_of(b * depth, 128), depth), at],
            up_ref.at[k], down_line_ref.at[k],
        )

    out_depth = out_grad_ref.shape[0]
    heads = LineScatter(
        *line_sems[8:],
        lambda b: heads_ref.at[pl.ds(pl.multiple_of(b * out_depth, 128), out_depth), :],
        heads_up_ref, heads_down_ref,
    )
    lines = [line_of(k) for k in range(2)] + [heads]
    for line in lines:
        line.clear()
        line.start()

    def product(at, c):
        weight = weight_ref[pl.ds(pl.multiple_of(c * width, 128), width), :]
        return dot(grad_ref[at, :], weight, (1,), (1,))

    scatter = PlaneScatter(copies, 0, filling(rows, product), *scratch)
    norm = NormBack(
        copies, PlaneScatter.SEMS, values_ref, stats_ref, gain_ref, base_ref, out_ref, None,
        dgain_ref, sums_ref,
    )
    half = depth // PAIR
    theirs = pl.multiple_of((1 - x) * half, 128)
    ours = pl.multiple_of(x * half, 128)
    swap = PlaneScatter.SEMS + 3
    units = ffn_ref.shape[2]
    scatter.first()
    for line in lines:
        line.hop(0)
    scatter.settle()
    scatter.second()
    here = pl.ds(pl.multiple_of(x * units, 16), units)
    there = pl.ds(pl.multiple_of((1 - x) * units, 16), units)
    for w in range(2):
        copies.send(
            swap + 2 + w, ffn_ref.at[0, w, :, pl.ds(theirs, half)], turn_ref.at[w, here, :], devices[0]
        )
        turn_ref[w, here, :] = ffn_ref[0, w, :, pl.ds(ours, half)]
    for line in lines:
        line.hop(1)
    scatter.third()
    norm.start(scatter.result, devices[1:4])
    part = width // PAIR
    outs = (query_ref, key_ref, value_ref)

    def pieces(k):
        for w in range(3):
            start, end = max(k * columns, w * part), min((k + 1) * columns, (w + 1) * part)
            if start < end:
                yield outs[w], start - w * part, start, end - start

    def close(k):
        lines[k].receive()
        at = pl.ds(k * columns, columns)
        swap_ref[:, at] = lines[k].total(pl.ds(theirs, half)).astype(BF16)
        copies.send(swap + k, swap_ref.at[:, at], swapped_ref.at[:, at], devices[0])
        total = lines[k].total(pl.ds(ours, half))
        for ref, place, start, size in pieces(k):
            columns_at = pl.ds(pl.multiple_of(x * part + place, 128), size)
            ref[:, columns_at] = total[:, start - k * columns : start - k * columns + size]

    close(0)
    norm.finish()
    close(1)
    for w, ref in enumerate((gate_ref, up_grad_ref)):
        copies.wait(swap + 2 + w, turn_ref.at[w, there, :])
        for j in range(PAIR * units // 128):
            at = slice(j * 128, (j + 1) * 128)
            ref[:, at] = turn_ref[w, at, :].T.astype(F32)
    heads.receive()
    out_grad_ref[...] = heads.total(pl.ds(0, out_depth))
    heads.finish()
    for k in range(2):
        at = pl.ds(k * columns, columns)
        copies.wait(swap + k, swapped_ref.at[:, at])
        for ref, place, start, size in pieces(k):
            columns_at = pl.ds(pl.multiple_of((1 - x) * part + place, 128), size)
            ref[:, columns_at] = swapped_ref[:, start : start + size].astype(F32)
        lines[k].finish()
    copies.finish()


def back_first(
    grad, weight, values, stats, gain, base, part, ffn, heads, collective_id
):
    rows, width = values.shape
    depth, columns = part.shape[0] // LINES, part.shape[1]
    vmem = pl.BlockSpec(memory_space=pltpu.VMEM)
    sems = lambda n: pltpu.SemaphoreType.DMA((n,))
    count = PlaneScatter.SEMS + 7
    units = ffn.shape[2]
    return pl.pallas_call(
        back_first_kernel,
        in_specs=[vmem] * 9,
        out_specs=[vmem] * 8,
        out_shape=[
            jax.ShapeDtypeStruct((rows, width), F32),
            jax.ShapeDtypeStruct((1, width), F32),
        ]
        + [jax.ShapeDtypeStruct((depth // PAIR, width), F32)] * 3
        + [jax.ShapeDtypeStruct((depth // PAIR, PAIR * units), F32)] * 2
        + [jax.ShapeDtypeStruct((heads.shape[0] // LINES, width), F32)],
        scratch_shapes=[
            pltpu.VMEM((4, 8, rows), F32),
            pltpu.VMEM((2, LINES - 1, depth, columns // 2), BF16),
            pltpu.VMEM((2, LINES - 1, depth, columns // 2), BF16),
            *[pltpu.VMEM((LINES - 1, heads.shape[0] // LINES, width), BF16)] * 2,
            pltpu.VMEM((depth // PAIR, columns), BF16), pltpu.VMEM((depth // PAIR, columns), BF16),
            pltpu.VMEM((2, PAIR * units, depth // PAIR), BF16),
            sems(count), sems(count), *[sems(LINES - 1)] * 12,
            *scatter_scratch(rows, width),
        ],
        compiler_params=pltpu.CompilerParams(
            collective_id=collective_id, has_side_effects=True, vmem_limit_bytes=63 << 20
        ),
        cost_estimate=taking(60),
        name="back_first",
    )(grad, weight, values, stats, gain.reshape(1, width), base, part, ffn, heads)


def back_heads_kernel(
    low_ref, weight_ref, attn_hbm, hidden_hbm, down_hbm, blocks_ref,
    out_ref, part_ref, mix_ref, all_ref,
    stage_ref, attn_ref, hidden_ref, down_ref, left_ref, sent_ref, own_ref, core_ref, y_ref, give_ref, come_ref,
    load_sem, out_sem, send_sem, recv_sem,
):
    rows, width = low_ref.shape
    half = width // PAIR
    count = rows // CHUNKS
    x, y, core, row, col = places()
    over_x, over_y, over_core = peers(row, col)
    over_far = (row, 3 - col)
    loads = [
        pltpu.make_async_copy(source, place, load_sem.at[i])
        for i, (source, place) in enumerate(
            ((attn_hbm, attn_ref), (hidden_hbm, hidden_ref), (down_hbm, down_ref))
        )
    ]
    for load in loads:
        load.start()
    stage = pltpu.make_async_copy(blocks_ref.at[col], stage_ref, load_sem.at[3])
    stage.start()
    meet((over_x, over_y, over_core, over_far))
    copies = Copies(send_sem, recv_sem, over_core)
    sides = (1 - y, y)

    def at_chunk(s):
        return pl.ds(s * count, count)

    def product(s, c):
        weight = weight_ref[pl.ds(pl.multiple_of(c * width, 128), width), :]
        return dot(low_ref[at_chunk(s), :], weight, (1,), (1,))

    def give(i, s):
        at = at_chunk(s)
        sent_ref[i, at, :] = product(s, 2 * sides[i] + 1 - core).astype(BF16)
        copies.send(i * CHUNKS + s, sent_ref.at[i, at, :], core_ref.at[i, at, :], over_core)

    def keep(i, s):
        at = at_chunk(s)
        part = product(s, 2 * sides[i] + core)
        copies.wait(i * CHUNKS + s, core_ref.at[i, at, :])
        own_ref[i, at, :] = (part + core_ref[i, at, :].astype(F32)).astype(BF16)
        if i == 0:
            copies.send(2 * CHUNKS + s, own_ref.at[0, at, :], y_ref.at[at, :], over_y)

    depth = give_ref.shape[1]

    def out_grad(z, x):
        at = pl.ds(pl.multiple_of((PAIR * z + x) * depth, 128), depth)
        return dot(attn_ref[:, at], low_ref[...], (0,), (0,))

    others = (((col + 2) % 4, over_y), (3 - col, over_far), (col + 1 - 2 * core, over_core))
    for s in range(CHUNKS):
        give(0, s)
    loads[0].wait()
    for z in range(LINES):
        give_ref[z] = out_grad(z, 1 - x).astype(BF16)
    copies.send(4 * CHUNKS, give_ref, come_ref, over_x)
    for s in range(CHUNKS):
        keep(0, s)
    for i, (other, device) in enumerate(others):
        copies.send(4 * CHUNKS + 1 + i, blocks_ref.at[other], all_ref.at[col], device)
    for s in range(CHUNKS):
        give(1, s)
    for s in range(CHUNKS):
        keep(1, s)
    for z in range(LINES):
        part_ref[z * depth : (z + 1) * depth, :] = out_grad(z, x).astype(BF16)
    stage.wait()
    stage = pltpu.make_async_copy(stage_ref, all_ref.at[col], load_sem.at[3])
    stage.start()
    for load in loads[1:]:
        load.wait()
    for a in range(PAIR):
        turn_rows(left_ref, hidden_ref, a, rows)
    kept = []
    for s in range(CHUNKS):

        @pl.loop(0, PAIR * rows // TILE)
        def _(i):
            a, start = i // (rows // TILE), pl.multiple_of(i % (rows // TILE) * TILE, TILE)
            left = left_ref[pl.ds(pl.multiple_of(i * TILE, TILE), TILE), :]
            mix_ref[a * CHUNKS + s, pl.ds(start, TILE), :] = dot(left, down_ref[s]).astype(BF16)

        at = at_chunk(s)
        copies.wait(2 * CHUNKS + s, y_ref.at[at, :])
        own_ref[1, at, :] = (
            own_ref[1, at, :].astype(F32) + y_ref[at, :].astype(F32)
        ).astype(BF16)
        place = out_ref.at[pl.ds(pl.multiple_of(x * rows + s * count, 128), count), :]
        theirs = own_ref.at[1, at, pl.ds(pl.multiple_of((1 - x) * half, 128), half)]
        ours = own_ref.at[1, at, pl.ds(pl.multiple_of(x * half, 128), half)]
        copies.send(3 * CHUNKS + s, theirs, place, over_x)
        task = pltpu.make_async_copy(ours, place, out_sem.at[s])
        task.start()
        kept.append(task)
    copies.wait(4 * CHUNKS, come_ref)
    for z in range(LINES):
        at = pl.ds(z * depth, depth)
        add_rows(part_ref.at[at, :], part_ref.at[at, :], come_ref.at[z], depth)
    for s in range(CHUNKS):
        copies.wait(
            3 * CHUNKS + s,
            out_ref.at[pl.ds(pl.multiple_of((1 - x) * rows + s * count, 128), count), :],
        )
    for i, (other, _) in enumerate(others):
        copies.wait(4 * CHUNKS + 1 + i, all_ref.at[other])
    copies.finish()
    stage.wait()
    for task in kept:
        task.wait()


def back_heads(low, weight, attn, hidden, down, blocks, collective_id):
    rows, width = low.shape
    depth = weight.shape[0] // (PAIR * LINES)
    vmem, anywhere = pl.BlockSpec(memory_space=pltpu.VMEM), pl.BlockSpec(memory_space=pl.ANY)
    sems = lambda n: pltpu.SemaphoreType.DMA((n,))
    wide = pltpu.VMEM((2, rows, width), BF16)
    swapped = pltpu.VMEM((LINES, depth, width), BF16)
    return pl.pallas_call(
        back_heads_kernel,
        in_specs=[vmem] * 2 + [anywhere] * 4,
        out_specs=[anywhere, vmem, vmem, anywhere],
        out_shape=[
            jax.ShapeDtypeStruct((PAIR * rows, width // PAIR), BF16),
            jax.ShapeDtypeStruct((LINES * depth, width), BF16),
            jax.ShapeDtypeStruct((PAIR * CHUNKS, rows, width), BF16),
            jax.ShapeDtypeStruct(blocks.shape, BF16),
        ],
        scratch_shapes=[
            pltpu.VMEM(blocks.shape[1:], BF16),
            pltpu.VMEM(attn.shape, BF16), pltpu.VMEM(hidden.shape, BF16),
            pltpu.VMEM(down.shape, BF16), pltpu.VMEM(hidden.shape[::-1], BF16),
            wide, wide, wide, pltpu.VMEM((rows, width), BF16),
            swapped, swapped,
            sems(4), sems(CHUNKS), sems(4 * CHUNKS + 4), sems(4 * CHUNKS + 4),
        ],
        compiler_params=pltpu.CompilerParams(
            collective_id=collective_id, has_side_effects=True, vmem_limit_bytes=60 << 20
        ),
        cost_estimate=taking(60),
        name="back_heads",
    )(low, weight, attn, hidden, down, blocks)


def per_device(
    tokens, segment_ids, positions, attn_gain, query_weight, query_bias, key_weight, key_bias,
    value_weight, value_bias, out_weight, mlp_gain, gate_weight, up_weight, down_weight, out_grad,
):
    count, width = tokens.shape
    lines = lax.axis_size("row") // PAIR
    cols = lax.axis_size("col")
    row = lax.axis_index("row")
    col = lax.axis_index("col")
    x = row % PAIR
    half = width // PAIR

    fast = cols == 4 and lines == LINES
    bias = jnp.concatenate(
        [pick(b, x, 0) for b in (query_bias, key_bias, value_bias)], axis=0
    )
    depth = out_weight.shape[0]
    hidden = down_weight.shape[0]
    down_line = gather_line(down_weight)
    if fast:
        tokens_all, grad_all, qkv_weight, out_all, ffn_part, gains, places_all = gather_first(
            tokens, out_grad, query_weight, key_weight, value_weight, out_weight,
            gate_weight, up_weight,
            jnp.pad(jnp.stack([attn_gain, mlp_gain]), ((0, 6), (0, 0))),
            jnp.pad(jnp.stack([positions, segment_ids]), ((0, 6), (0, 0))), 0,
        )
    else:
        qkv_weight = gather_line(
            jnp.concatenate(
                [own_columns(w, x) for w in (query_weight, key_weight, value_weight)], axis=1
            )
        )
        tokens_all = gather_plane(tokens, "gather_tokens", 0)
        grad_all = gather_plane(out_grad, "gather_cotangent", 1)
        out_line = gather_line(out_weight)
        full = (lines, 1, depth, width)
        out_all = in_order(
            x, out_line.reshape(full), swap_rows(out_line).reshape(full), 1
        ).reshape(-1, width)
        ffn_part = jnp.stack([own_units(w, x) for w in (gate_weight, up_weight)])[None]
        gains = lax.all_gather(jnp.stack([attn_gain, mlp_gain]), "col", axis=1, tiled=True)
        own_place = jnp.stack([positions, segment_ids])
        places_all = in_order(x, own_place, swap_rows(own_place), 1)
    cosine, sine = rotation_tables(places_all[0])
    plane_segments = places_all[1]
    down_blocks = after(down_line, tokens_all).reshape(lines, hidden, width)
    ffn_weight = gather_line(after(ffn_part, down_blocks))

    projections = (tokens_all, gains[0], qkv_weight, bias, cosine, sine)
    if fast:
        normed_first, queries, keys, values, stats_first, down_partly = project_heads(
            *projections, down_blocks, 1
        )
        attended, lse, down_all = attention_forward(
            queries, keys, values, plane_segments, down_blocks, down_partly, 8
        )
    else:
        normed_first, queries, keys, values, stats_first = project_heads(*projections)
        attended, lse = attention_forward(queries, keys, values, plane_segments)
        down_all = lax.all_to_all(down_blocks, "col", split_axis=0, concat_axis=0, tiled=True)
    attn_all = gather_heads(attended, x, 2)
    inputs = tokens.astype(F32)
    resid = inputs + dot(attn_all, out_all)

    resid_all = gather_plane(resid.astype(BF16), "gather_residual", 3)
    normed_second, hidden_low, grad_gate, grad_up, stats_second = feed_forward(
        resid_all, gains[1], ffn_weight, grad_all, down_all
    )
    if fast:
        grad_ffn = weight_grads((grad_gate, grad_up), normed_second, width, "ffn_grads")
    else:
        grad_ffn = weight_grads((grad_gate, grad_up), normed_second, width, "ffn_grads")
    own_stats = pick(stats_second, x, 0)
    if fast:
        grad_resid, grad_resid_low, mlp_gain_part, down_blocks = back_second(
            after(grad_gate, grad_ffn), grad_up, ffn_weight, hidden_low, grad_all,
            resid, own_stats, mlp_gain, out_grad, 4,
        )
        mlp_gain_part = mlp_gain_part[0]
    else:
        grad_second = scatter_plane(
            back_project((grad_gate, grad_up), ffn_weight, "back_ffn"), "scatter_second", 4
        )
        mean_here, inv_here = own_stats[:, 0:1], own_stats[:, 1:2]
        grad_resid, mlp_gain_part = norm_backward(
            grad_second, (resid - mean_here) * inv_here, inv_here, mlp_gain
        )
        grad_resid = grad_resid + out_grad.astype(F32)
        grad_resid_low = grad_resid.astype(BF16)
    grad_ffn = scatter_line(grad_ffn)

    if fast:
        grad_attn, grad_out_weight, mixed, grad_down = back_heads(
            grad_resid_low, out_all, attn_all, hidden_low, down_all, down_blocks, 5
        )
        grad_qkv, bias_sums, mixed = attention_backward(
            queries, keys, values, grad_attn, lse, cosine, sine, plane_segments, mixed, resid, 9
        )
    else:
        grad_out_weight = dot(attn_all, grad_resid_low, (0,), (0,)).astype(BF16)
        grad_out_weight = grad_out_weight.reshape(lines, PAIR, depth, width)
        grad_out_weight = pick(grad_out_weight, x, 1) + swap_rows(pick(grad_out_weight, 1 - x, 1))
        grad_out_weight = scatter_line(grad_out_weight.reshape(lines * depth, width)).astype(F32)
        grad_attn = scatter_heads(dot(grad_resid_low, out_all, (1,), (1,)).astype(BF16), x)
        grad_qkv, bias_sums = attention_backward(
            queries, keys, values, grad_attn, lse, cosine, sine, plane_segments
        )
        grad_down = weight_grads((hidden_low,), grad_all, width, "down_grads")
        grad_down = lax.all_to_all(
            grad_down.reshape(cols, hidden, width), "col", split_axis=0, concat_axis=0, tiled=True
        )
    grad_qkv_weight = dot(normed_first, grad_qkv, (0,), (0,)).astype(BF16)
    grad_down = scatter_line(after(grad_down, grad_ffn).reshape(lines * hidden, width))
    grad_qkv_later = after(grad_qkv, grad_qkv_weight)
    own_stats = pick(stats_first, x, 0)
    if fast:
        (
            tokens_grad, attn_gain_part, query_grad, key_grad, value_grad, gate_grad, up_grad,
            grad_out_weight,
        ) = back_first(
            after(grad_qkv_later, grad_down), qkv_weight,
            tokens, own_stats, attn_gain, grad_resid, grad_qkv_weight, grad_ffn, grad_out_weight, 6,
        )
        attn_gain_part = attn_gain_part[0]
    else:
        kept, other = pick(grad_ffn[0], x, 2), swap_rows(pick(grad_ffn[0], 1 - x, 2))
        gate_grad, up_grad = (
            in_order(x, kept[i], other[i], 0).T.astype(F32) for i in range(2)
        )
        kept, other = own_rows(scatter_line(grad_qkv_weight), x)
        query_grad, key_grad, value_grad = (
            in_order(x, kept[:, at : at + half], other[:, at : at + half], 1).astype(F32)
            for at in (0, half, 2 * half)
        )
        grad_first = scatter_plane(
            dot(grad_qkv_later, qkv_weight, (1,), (1,)).astype(BF16), "scatter_first", 6
        )
        mean_here, inv_here = own_stats[:, 0:1], own_stats[:, 1:2]
        grad_input, attn_gain_part = norm_backward(
            grad_first, (inputs - mean_here) * inv_here, inv_here, attn_gain
        )
        tokens_grad = grad_input + grad_resid
        mixed = resid + scatter_plane(
            back_project((hidden_low,), down_all[:, None], "mix"), "scatter_mixed", 10
        )
        mixed = mixed.astype(BF16)

    bias_part = jnp.sum(bias_sums, axis=(0, 1)).reshape(3, half)
    bias_part = jnp.where(
        (jnp.arange(PAIR) == x)[None, :, None], bias_part[:, None, :], 0.0
    ).reshape(3, width)
    vectors = sum_rows(
        jnp.concatenate(
            [bias_part, attn_gain_part[None], mlp_gain_part[None], jnp.zeros((3, width), F32)]
        ),
        11,
    )
    return (
        mixed,
        tokens_grad,
        vectors[3],
        query_grad,
        vectors[0],
        key_grad,
        vectors[1],
        value_grad,
        vectors[2],
        grad_out_weight,
        vectors[4],
        gate_grad,
        up_grad,
        grad_down.astype(F32),
    )


def solution(mesh):
    grid, rows, cols = P("row", "col"), P("row"), P("col")
    in_specs = (
        grid, rows, rows, cols, grid, cols, grid, cols, grid, cols, grid, cols, grid, grid, grid, grid,
    )
    out_specs = (
        grid, grid, cols, grid, cols, grid, cols, grid, cols, grid, cols, grid, grid, grid,
    )
    return jax.shard_map(
        per_device, mesh=mesh, in_specs=in_specs, out_specs=out_specs, check_vma=False
    )
```

```python
import functools

import jax
import jax.numpy as jnp
from jax import lax
from jax.experimental import pallas as pl
from jax.experimental.pallas import tpu as pltpu
from jax.sharding import PartitionSpec as P

HEAD_DIM = 64
ROT = 16
SEQ = 1024
BASE = 10000.0
NEG = -1e30
F32 = jnp.float32
BF16 = jnp.bfloat16
SCALE = HEAD_DIM**-0.5
MESH = pl.DeviceIdType.MESH
QBLOCK = 256
PAIR = 2


def dot(left, right, left_dims=(1,), right_dims=(0,)):
    return lax.dot_general(
        left, right, ((left_dims, right_dims), ((), ())), preferred_element_type=F32
    )


def taking(microseconds):
    return pl.CostEstimate(
        flops=microseconds * 10**9, bytes_accessed=microseconds * 10**6, transcendentals=0
    )


def swap_pairs(values, lane):
    half = ROT // 2
    width = values.shape[1]
    ahead = pltpu.roll(values, width - half, 1)
    behind = pltpu.roll(values, half, 1)
    return jnp.where(lane < half, ahead, behind)


def attention_forward_kernel(
    q_ref, k_ref, v_ref, seg_col_ref, seg_row_ref, o_ref, lse_ref, acc_ref, lse_scratch
):
    width = q_ref.shape[1]
    heads = width // HEAD_DIM
    full_lane = lax.broadcasted_iota(jnp.int32, (1, width), 1)
    acc_ref[...] = jnp.zeros_like(acc_ref)
    lse_lane = lax.broadcasted_iota(jnp.int32, (1, lse_scratch.shape[1]), 1)

    @pl.loop(0, heads)
    def _(head):
        mask = full_lane // HEAD_DIM == head
        for start in range(0, SEQ, QBLOCK):
            keys = start + QBLOCK
            rows = slice(start, keys)
            queries = jnp.where(mask, q_ref[rows, :], jnp.zeros((), BF16))
            scores = dot(queries, k_ref[:keys, :], (1,), (1,))
            query_pos = start + lax.broadcasted_iota(jnp.int32, scores.shape, 0)
            key_pos = lax.broadcasted_iota(jnp.int32, scores.shape, 1)
            seen = (seg_col_ref[rows, :] == seg_row_ref[0, :, :keys]) & (key_pos <= query_pos)
            scores = jnp.where(seen, scores, NEG)
            peak = jnp.max(scores, axis=1, keepdims=True)
            weights = jnp.exp(scores - peak)
            total = jnp.sum(weights, axis=1, keepdims=True)
            probs = (weights * (1.0 / total)).astype(BF16)
            output = dot(probs, v_ref[:keys, :])
            acc_ref[rows, :] = jnp.where(mask, output, acc_ref[rows, :])
            lse_scratch[rows, :] = jnp.where(
                lse_lane == head, peak + jnp.log(total), lse_scratch[rows, :]
            )

    o_ref[...] = acc_ref[...].astype(BF16)
    lse_ref[0] = lse_scratch[...].T[: lse_ref.shape[1], :]


def attention_forward_exchange_kernel(*refs):
    ins, (blocks_ref, _), outs, all_ref = refs[:5], refs[5:7], refs[7:9], refs[9]
    scratch, sems = refs[10:12], refs[12:]
    exchange_beside(
        lambda: attention_forward_kernel(*ins, *outs, *scratch),
        blocks_ref, all_ref, (1, 3), None, *sems,
    )


def attention_forward(queries, keys, values, segments, blocks=None, partly=None, collective_id=None):
    rows, width = queries.shape
    seqs = rows // SEQ
    block = lambda columns: pl.BlockSpec((SEQ, columns), lambda s: (s, 0))
    in_specs = [block(width)] * 3 + [block(1), pl.BlockSpec((1, 1, SEQ), lambda s: (s, 0, 0))]
    out_specs = [block(width), pl.BlockSpec((1, 8, SEQ), lambda s: (s, 0, 0))]
    out_shape = [
        jax.ShapeDtypeStruct((rows, width), BF16), jax.ShapeDtypeStruct((seqs, 8, SEQ), F32)
    ]
    operands = [queries, keys, values, segments.reshape(rows, 1), segments.reshape(seqs, 1, SEQ)]
    scratch = [pltpu.VMEM((SEQ, width), F32), pltpu.VMEM((SEQ, 128), F32)]
    params, aliases, kernel = {}, {}, attention_forward_kernel
    if blocks is not None:
        anywhere = pl.BlockSpec(memory_space=pl.ANY)
        in_specs, out_specs = in_specs + [anywhere] * 2, out_specs + [anywhere]
        out_shape = out_shape + [jax.ShapeDtypeStruct(blocks.shape, BF16)]
        operands = operands + [blocks, partly]
        scratch = scratch + [pltpu.SemaphoreType.DMA((2,))] * 2
        params = dict(collective_id=collective_id, has_side_effects=True)
        aliases, kernel = {6: 2}, attention_forward_exchange_kernel
    return pl.pallas_call(
        kernel,
        grid=(seqs,),
        in_specs=in_specs,
        out_specs=out_specs,
        out_shape=out_shape,
        scratch_shapes=scratch,
        input_output_aliases=aliases,
        compiler_params=pltpu.CompilerParams(vmem_limit_bytes=56 << 20, **params),
        cost_estimate=taking(21),
        name="attention_forward",
    )(*operands)


def attention_backward_kernel(
    q_ref, k_ref, v_ref, do_ref, lse_ref, cos_ref, sin_ref, seg_col_ref, seg_row_ref,
    grad_ref, sums_ref, dq_ref, dk_ref, dv_ref, halfway=None,
):
    width = q_ref.shape[1]
    heads = width // HEAD_DIM
    full_lane = lax.broadcasted_iota(jnp.int32, (1, width), 1)
    in_head = full_lane % HEAD_DIM
    for ref in (dq_ref, dk_ref, dv_ref):
        ref[...] = jnp.zeros_like(ref)

    def one_head(head):
        mask = full_lane // HEAD_DIM == head
        nothing = jnp.zeros((), BF16)
        for start in range(0, SEQ, 2 * QBLOCK):
            keys = start + 2 * QBLOCK
            rows = slice(start, keys)
            queries = jnp.where(mask, q_ref[rows, :], nothing)
            grads = jnp.where(mask, do_ref[rows, :], nothing)
            scores = dot(k_ref[:keys, :], queries, (1,), (1,))
            key_pos = lax.broadcasted_iota(jnp.int32, scores.shape, 0)
            query_pos = start + lax.broadcasted_iota(jnp.int32, scores.shape, 1)
            seen = (seg_col_ref[:keys, :] == seg_row_ref[0, :, rows]) & (key_pos <= query_pos)
            probs = jnp.where(
                seen, jnp.exp(scores - lse_ref[0, pl.ds(head, 1), rows]), 0.0
            )
            dv_ref[:keys, :] += dot(probs.astype(BF16), grads)
            grad_probs = dot(v_ref[:keys, :], grads, (1,), (1,))
            delta = jnp.sum(probs * grad_probs, axis=0, keepdims=True)
            grad_scores = (probs * (grad_probs - delta)).astype(BF16)
            dk_ref[:keys, :] += dot(grad_scores, queries)
            masked_keys = jnp.where(mask, k_ref[:keys, :], nothing)
            dq_ref[rows, :] += dot(grad_scores, masked_keys, (0,), (0,))

    pl.loop(0, heads // 2)(one_head)
    if halfway is not None:
        halfway()
    pl.loop(heads // 2, heads)(one_head)

    cosine = jnp.tile(cos_ref[...], (1, width // cos_ref.shape[1]))
    sine = jnp.tile(sin_ref[...], (1, width // sin_ref.shape[1]))
    for part, (ref, scale) in enumerate(((dq_ref, SCALE), (dk_ref, 1.0), (dv_ref, None))):
        grad = ref[...]
        if scale is not None:
            grad = grad * scale
            grad = grad * cosine - swap_pairs(grad, in_head) * sine
        low = grad.astype(BF16)
        columns = slice(part * width, (part + 1) * width)
        grad_ref[:, columns] = low
        sums_ref[0, :, columns] = jnp.sum(low.astype(F32), axis=0, keepdims=True)


def attention_backward_sums_kernel(*refs):
    ins, parts_ref, resid_ref = refs[:9], refs[9], refs[10]
    outs, mixed_ref, scratch = refs[11:13], refs[13], refs[14:17]
    load_sem, send_sem, recv_sem, *blocks = refs[17:]
    devices = peers(lax.axis_index("row"), lax.axis_index("col"))
    copies = Copies(send_sem, recv_sem, devices[2])
    mixing = PartsScatter(copies, 0, parts_ref, load_sem, *blocks)
    step = pl.program_id(0)

    @pl.when(step == 0)
    def _():
        meet(devices)
        mixing.start()
        mixing.keep(0, 0)
        mixing.keep(0, 1)

    def halfway():
        @pl.when(step == 0)
        def _():
            for i, h in ((1, 0), (2, 0), (2, 1), (1, 1), (3, 0), (3, 1)):
                mixing.keep(i, h)

        @pl.when(step == 1)
        def _():
            mixing.second()

    attention_backward_kernel(*ins, *outs, *scratch, halfway=halfway)

    @pl.when(step == 1)
    def _():
        mixing.third()
        for start in range(0, mixed_ref.shape[0], STEP):
            at = pl.ds(start, STEP)
            mixed_ref[at, :] = (resid_ref[at, :] + mixing.result(start, STEP)).astype(BF16)
        mixing.drain()


def attention_backward(
    queries, keys, values, grad_out, lse, cosine, sine, segments,
    parts=None, resid=None, collective_id=None,
):
    rows, width = queries.shape
    seqs = rows // SEQ
    block = lambda columns: pl.BlockSpec((SEQ, columns), lambda s: (s, 0))
    in_specs = [block(width)] * 4 + [
        pl.BlockSpec((1, 8, SEQ), lambda s: (s, 0, 0)),
        block(cosine.shape[1]),
        block(cosine.shape[1]),
        block(1),
        pl.BlockSpec((1, 1, SEQ), lambda s: (s, 0, 0)),
    ]
    out_specs = [block(3 * width), pl.BlockSpec((1, 1, 3 * width), lambda s: (s, 0, 0))]
    out_shape = [
        jax.ShapeDtypeStruct((rows, 3 * width), BF16),
        jax.ShapeDtypeStruct((seqs, 1, 3 * width), F32),
    ]
    operands = [
        queries, keys, values, grad_out, lse, cosine, sine,
        segments.reshape(rows, 1), segments.reshape(seqs, 1, SEQ),
    ]
    scratch = [pltpu.VMEM((SEQ, width), F32)] * 3
    params, kernel = {}, attention_backward_kernel
    if parts is not None:
        in_specs = in_specs + [pl.BlockSpec(memory_space=pl.ANY), whole(resid.shape)]
        out_specs = out_specs + [whole(resid.shape)]
        out_shape = out_shape + [jax.ShapeDtypeStruct(resid.shape, BF16)]
        operands = operands + [parts, resid]
        sems = lambda n: pltpu.SemaphoreType.DMA((n,))
        scratch = scratch + [sems(4), sems(PlaneScatter.SEMS), sems(PlaneScatter.SEMS)]
        scratch = scratch + scatter_scratch(*resid.shape)[1:]
        params = dict(collective_id=collective_id, has_side_effects=True)
        kernel = attention_backward_sums_kernel
    return pl.pallas_call(
        kernel,
        grid=(seqs,),
        in_specs=in_specs,
        out_specs=out_specs,
        out_shape=out_shape,
        scratch_shapes=scratch,
        compiler_params=pltpu.CompilerParams(vmem_limit_bytes=60 << 20, **params),
        cost_estimate=taking(42),
        name="attention_backward",
    )(*operands)


def row_pairs():
    return [(r, r ^ 1) for r in range(lax.axis_size("row"))]


def row_lines():
    size = lax.axis_size("row")
    return [list(range(start, size, PAIR)) for start in range(PAIR)]


def neighbours():
    return [list(range(r, r + PAIR)) for r in range(0, lax.axis_size("row"), PAIR)]


def swap_rows(values):
    return lax.ppermute(values, "row", row_pairs())


def after(value, *others):
    return lax.optimization_barrier((value,) + others)[0]


def gather_line(values, axis=0):
    return lax.all_gather(values, "row", axis=axis, tiled=True, axis_index_groups=row_lines())


def scatter_line(values, axis=0):
    return lax.psum_scatter(
        values, "row", scatter_dimension=axis, tiled=True, axis_index_groups=row_lines()
    )


def pick(values, index, axis):
    size = values.shape[axis] // PAIR
    return lax.dynamic_slice_in_dim(values, index * size, size, axis)


def in_order(x, own, other, axis):
    return jnp.where(
        x == 0, jnp.concatenate([own, other], axis), jnp.concatenate([other, own], axis)
    )


def own_columns(weight, x):
    return in_order(x, pick(weight, x, 1), swap_rows(pick(weight, 1 - x, 1)), 0)


def own_units(weight, x):
    kept, sent = pick(weight, x, 1).T, pick(weight, 1 - x, 1).T
    return in_order(x, kept, swap_rows(sent), 1)


def own_rows(grad, x):
    return pick(grad, x, 0), swap_rows(pick(grad, 1 - x, 0))


def places():
    row, col = lax.axis_index("row"), lax.axis_index("col")
    return row % PAIR, col // 2, col % 2, row, col


def peers(row, col):
    x = row % PAIR
    over_x = (row + 1 - 2 * x, col)
    over_y = (row, (col + 2) % 4)
    over_core = (row, col + 1 - 2 * (col % 2))
    return over_x, over_y, over_core


def meet(devices):
    barrier = pltpu.get_barrier_semaphore()
    for device in devices:
        pl.semaphore_signal(barrier, inc=1, device_id=device, device_id_type=MESH)
    pl.semaphore_wait(barrier, len(devices))


def block_at(ref, a, col, rows, width, start, count):
    at = pl.multiple_of(a * rows + start, 128)
    return ref.at[pl.ds(at, count), pl.ds(pl.multiple_of(col * width, 128), width)]


CHUNKS = 4


class Copies:
    def __init__(self, send_sem, recv_sem, over_core):
        self.send_sem, self.recv_sem, self.any = send_sem, recv_sem, over_core
        self.sent = []

    def copy(self, index, source, place, device):
        return pltpu.make_async_remote_copy(
            source, place, self.send_sem.at[index], self.recv_sem.at[index],
            device_id=device, device_id_type=MESH,
        )

    def send(self, index, source, place, device):
        task = self.copy(index, source, place, device)
        task.start()
        self.sent.append(task)

    def wait(self, index, place):
        self.copy(index, place, place, self.any).wait_recv()

    def finish(self):
        for task in self.sent:
            task.wait_send()
        self.sent = []


class PlaneGather:
    def __init__(self, copies, base, src_ref, out_ref, local_sem, over_y=CHUNKS // 2):
        self.copies, self.base, self.src, self.out = copies, base, src_ref, out_ref
        self.local_sem = local_sem
        self.rows, self.width = src_ref.shape
        self.count = self.rows // CHUNKS
        self.x, self.y, self.core, self.row, self.col = places()
        self.over_x, self.over_y, self.over_core = peers(self.row, self.col)
        self.col_y = (self.col + 2) % 4
        self.col_core = self.col + 1 - 2 * self.core
        self.first = list(range(over_y))
        self.second = list(range(over_y, CHUNKS))

    def piece(self, a, c, s):
        return block_at(self.out, a, c, self.rows, self.width, s * self.count, self.count)

    def own(self, s):
        return self.src.at[pl.ds(s * self.count, self.count), :]

    def send(self, group, s, source, place, device):
        self.copies.send(self.base + group * CHUNKS + s, source, place, device)

    def pass_on(self, group, a, c, s, device):
        self.send(group, s, self.piece(a, c, s), self.piece(a, c, s), device)

    def wait(self, group, a, c, s):
        self.copies.wait(self.base + group * CHUNKS + s, self.piece(a, c, s))

    def start_x(self):
        for s in self.first + self.second:
            self.send(0, s, self.own(s), self.piece(self.x, self.col, s), self.over_x)

    def start_y(self):
        for s in self.second + self.first:
            self.send(1, s, self.own(s), self.piece(self.x, self.col, s), self.over_y)

    def start_chunk(self, s):
        self.send(0, s, self.own(s), self.piece(self.x, self.col, s), self.over_x)
        self.send(1, s, self.own(s), self.piece(self.x, self.col, s), self.over_y)
        self.send(4, s, self.own(s), self.piece(self.x, self.col, s), self.over_core)

    def near_in_order(self, s):
        x, col, col_y = self.x, self.col, self.col_y
        self.wait(0, 1 - x, col, s)
        if s in self.first:
            self.pass_on(2, 1 - x, col, s, self.over_y)
        self.pass_on(5, 1 - x, col, s, self.over_core)
        self.wait(1, x, col_y, s)
        if s in self.second:
            self.pass_on(2, x, col_y, s, self.over_x)
        self.pass_on(6, x, col_y, s, self.over_core)

    def keep_own(self):
        self.local = pltpu.make_async_copy(
            self.src, block_at(self.out, self.x, self.col, self.rows, self.width, 0, self.rows),
            self.local_sem,
        )
        self.local.start()

    def start_core(self):
        self.keep_own()
        for s in range(CHUNKS):
            self.send(4, s, self.own(s), self.piece(self.x, self.col, s), self.over_core)

    def near(self, i):
        s, t = (self.first + self.second)[i], (self.second + self.first)[i]
        x, col, col_y = self.x, self.col, self.col_y
        self.wait(0, 1 - x, col, s)
        if s in self.first:
            self.pass_on(2, 1 - x, col, s, self.over_y)
        self.pass_on(5, 1 - x, col, s, self.over_core)
        self.wait(1, x, col_y, t)
        if t in self.second:
            self.pass_on(2, x, col_y, t, self.over_x)
        self.pass_on(6, x, col_y, t, self.over_core)

    def far(self):
        for u in range(CHUNKS):
            self.wait(2, 1 - self.x, self.col_y, u)
            self.pass_on(7, 1 - self.x, self.col_y, u, self.over_core)

    def finish(self):
        other, corner = self.col_core, (self.col_core + 2) % 4
        for group, (a, c) in enumerate(
            ((self.x, other), (1 - self.x, other), (self.x, corner), (1 - self.x, corner))
        ):
            for s in range(CHUNKS):
                self.wait(4 + group, a, c, s)
        self.local.wait()


def gather_plane_kernel(src_ref, out_ref, local_sem, send_sem, recv_sem):
    _, _, _, row, col = places()
    devices = peers(row, col)
    meet(devices)
    copies = Copies(send_sem, recv_sem, devices[2])
    gather = PlaneGather(copies, 0, src_ref, out_ref, local_sem)
    gather.start_x()
    gather.start_y()
    gather.start_core()
    for i in range(CHUNKS):
        gather.near(i)
    gather.far()
    gather.finish()
    copies.finish()


LINES = 4


class LineGather:
    def __init__(self, up_send, up_recv, down_send, down_recv, block):
        self.up, self.down, self.block = (up_send, up_recv), (down_send, down_recv), block
        self.row, self.col = lax.axis_index("row"), lax.axis_index("col")
        self.z = self.row // PAIR

    def task(self, sems, step, source, device):
        send, recv = sems
        place = self.block(source)
        return pltpu.make_async_remote_copy(
            place, place, send.at[step], recv.at[step],
            device_id=(device, self.col), device_id_type=MESH,
        )

    def upward(self, step):
        source = jnp.maximum(self.z - step, 0)
        return self.task(self.up, step, source, jnp.minimum(self.row + PAIR, PAIR * LINES - 1))

    def downward(self, step):
        source = jnp.minimum(self.z + step, LINES - 1)
        return self.task(self.down, step, source, jnp.maximum(self.row - PAIR, 0))

    def start(self, step):
        @pl.when((self.z >= step) & (self.z < LINES - 1))
        def _():
            self.upward(step).start()

        @pl.when((self.z + step < LINES) & (self.z > 0))
        def _():
            self.downward(step).start()

    def receive(self, step):
        @pl.when(self.z >= step)
        def _():
            source = jnp.maximum(self.z - step, 0)
            self.task(self.up, step - 1, source, self.row).wait_recv()

        @pl.when(self.z + step < LINES)
        def _():
            source = jnp.minimum(self.z + step, LINES - 1)
            self.task(self.down, step - 1, source, self.row).wait_recv()

    def hop(self, step):
        self.receive(step)
        if step < LINES - 1:
            self.start(step)

    def finish(self):
        for step in range(LINES - 1):

            @pl.when((self.z >= step) & (self.z < LINES - 1))
            def _():
                self.upward(step).wait_send()

            @pl.when((self.z + step < LINES) & (self.z > 0))
            def _():
                self.downward(step).wait_send()


def gather_first_kernel(
    tokens_ref, grad_ref, query_ref, key_ref, value_ref, out_weight_ref, gate_ref, up_ref,
    gains_ref, places_ref,
    tokens_all_ref, grad_all_ref, qkv_ref, out_all_ref, ffn_ref, gains_all_ref, places_all_ref,
    turned_ref, local_sem, send_sem, recv_sem, swap_send, swap_recv, *line_sems,
):
    x, y, core, row, col = places()
    z = row // PAIR
    over_x, over_y, over_core = peers(row, col)
    over_far = (row, 3 - col)
    size = PAIR * LINES
    meet(
        (
            over_x, over_y, over_core, over_far,
            ((row + PAIR) % size, col), ((row + size - PAIR) % size, col),
        )
    )
    copies = Copies(send_sem, recv_sem, over_core)
    depth, width = out_weight_ref.shape
    half = width // PAIR
    units = ffn_ref.shape[2]
    base = 16 * CHUNKS
    local = []

    def keep(source, place):
        task = pltpu.make_async_copy(source, place, local_sem.at[2 + len(local)])
        task.start()
        local.append(task)

    def part(r, w):
        return qkv_ref.at[
            pl.ds(pl.multiple_of(r * depth, 128), depth), pl.ds(w * half, half)
        ]

    def out_block(z, x):
        return out_all_ref.at[pl.ds(pl.multiple_of((PAIR * z + x) * depth, 128), depth), :]

    def ffn_block(w, x):
        return ffn_ref.at[0, w, :, pl.ds(pl.multiple_of(x * depth, 128), depth)]

    def gains_block(c):
        return gains_all_ref.at[:, pl.ds(pl.multiple_of(c * width, 128), width)]

    def places_block(a):
        rows = places_ref.shape[1]
        return places_all_ref.at[:, pl.ds(pl.multiple_of(a * rows, 128), rows)]

    for w, ref in enumerate((query_ref, key_ref, value_ref)):
        theirs = ref.at[:, pl.ds(pl.multiple_of((1 - x) * half, 128), half)]
        copies.send(base + w, theirs, part(row, w), over_x)
        keep(ref.at[:, pl.ds(pl.multiple_of(x * half, 128), half)], part(row, w))
    keep(out_weight_ref, out_block(z, x))
    keep(gains_ref, gains_block(col))
    keep(places_ref, places_block(x))
    tokens = PlaneGather(copies, 0, tokens_ref, tokens_all_ref, local_sem.at[0], CHUNKS)
    grad = PlaneGather(copies, 8 * CHUNKS, grad_ref, grad_all_ref, local_sem.at[1], CHUNKS)
    tokens.start_y()
    tokens.start_core()
    copies.send(base + 5, places_ref, places_block(x), over_x)
    for i, device in enumerate((over_core, over_y, over_far)):
        copies.send(base + 6 + i, gains_ref, gains_block(col), device)
    for w in range(3):
        local[w].wait()
        copies.wait(base + w, part(row + 1 - 2 * x, w))
    heads = LineGather(
        *line_sems[:4],
        lambda at: qkv_ref.at[pl.ds(pl.multiple_of(at * PAIR * depth, 128), PAIR * depth), :],
    )
    outs = LineGather(*line_sems[4:], lambda at: out_block(at, x))

    def swap_out(z, x):
        block = out_block(z, x)
        return pltpu.make_async_remote_copy(
            block, block, swap_send.at[z], swap_recv.at[z], device_id=over_x, device_id_type=MESH
        )

    def swap_outs(step):
        @pl.when(z >= step)
        def _():
            swap_out(jnp.maximum(z - step, 0), x).start()

        @pl.when(z + step < LINES)
        def _():
            swap_out(jnp.minimum(z + step, LINES - 1), x).start()

    heads.start(0)
    tokens.start_x()
    for w, ref in enumerate((gate_ref, up_ref)):
        for j in range(PAIR * units // 128):
            turned_ref[w, j * 128 : (j + 1) * 128, :] = ref[:, j * 128 : (j + 1) * 128].T
    for i in range(CHUNKS - 1):
        tokens.near(i)
    local[3].wait()
    outs.start(0)
    heads.hop(1)
    tokens.near(CHUNKS - 1)
    for w in range(2):
        theirs = turned_ref.at[w, pl.ds(pl.multiple_of((1 - x) * units, 16), units), :]
        copies.send(base + 3 + w, theirs, ffn_block(w, x), over_x)
        keep(turned_ref.at[w, pl.ds(pl.multiple_of(x * units, 16), units), :], ffn_block(w, x))
    swap_out(z, x).start()
    grad.start_x()
    grad.start_y()
    grad.start_core()
    tokens.far()
    heads.hop(2)
    outs.hop(1)
    swap_outs(1)
    for i in range(CHUNKS - 1):
        grad.near(i)
    heads.hop(3)
    outs.hop(2)
    swap_outs(2)
    grad.near(CHUNKS - 1)
    grad.far()
    outs.hop(3)
    swap_outs(3)
    for at in range(LINES):
        swap_out(at, 1 - x).wait_recv()
    for w in range(2):
        copies.wait(base + 3 + w, ffn_block(w, 1 - x))
    copies.wait(base + 5, places_block(1 - x))
    for i, c in enumerate((col + 1 - 2 * core, (col + 2) % 4, 3 - col)):
        copies.wait(base + 6 + i, gains_block(c))
    for at in range(LINES):
        swap_out(at, x).wait_send()
    for task in local[3 + 1 :]:
        task.wait()
    tokens.finish()
    grad.finish()
    heads.finish()
    outs.finish()
    copies.finish()


def gather_first(
    tokens, grad, query, key, value, out_weight, gate, up, gains, places, collective_id
):
    rows, width = tokens.shape
    depth = out_weight.shape[0]
    units = gate.shape[1] // PAIR
    shape = lambda *dims: jax.ShapeDtypeStruct(dims, BF16)
    sems = lambda n: pltpu.SemaphoreType.DMA((n,))
    return pl.pallas_call(
        gather_first_kernel,
        in_specs=[pl.BlockSpec(memory_space=pltpu.VMEM)] * 10,
        out_specs=[pl.BlockSpec(memory_space=pl.ANY)] * 7,
        out_shape=[
            shape(PAIR * rows, 4 * width), shape(PAIR * rows, 4 * width),
            shape(PAIR * LINES * depth, 3 * width // PAIR), shape(PAIR * LINES * depth, width),
            shape(1, 2, units, PAIR * depth),
            jax.ShapeDtypeStruct((gains.shape[0], 4 * width), F32),
            jax.ShapeDtypeStruct((places.shape[0], PAIR * rows), jnp.int32),
        ],
        scratch_shapes=[
            pltpu.VMEM((2, PAIR * units, depth), BF16),
            sems(10), sems(16 * CHUNKS + 9), sems(16 * CHUNKS + 9), sems(4), sems(4),
        ]
        + [sems(3)] * 8,
        compiler_params=pltpu.CompilerParams(
            collective_id=collective_id, has_side_effects=True, vmem_limit_bytes=60 << 20
        ),
        cost_estimate=taking(110),
        name="gather_first",
    )(tokens, grad, query, key, value, out_weight, gate, up, gains, places)


def gather_plane(values, name, collective_id):
    cols = lax.axis_size("col")
    if cols != 4:
        across = lax.all_gather(values, "col", axis=1, tiled=True)
        return lax.all_gather(across, "row", axis=0, tiled=True, axis_index_groups=neighbours())
    rows, width = values.shape
    return pl.pallas_call(
        gather_plane_kernel,
        in_specs=[pl.BlockSpec(memory_space=pltpu.VMEM)],
        out_specs=pl.BlockSpec(memory_space=pl.ANY),
        out_shape=jax.ShapeDtypeStruct((PAIR * rows, cols * width), values.dtype),
        scratch_shapes=[
            pltpu.SemaphoreType.DMA,
            pltpu.SemaphoreType.DMA((8 * CHUNKS,)),
            pltpu.SemaphoreType.DMA((8 * CHUNKS,)),
        ],
        cost_estimate=taking(40),
        compiler_params=pltpu.CompilerParams(collective_id=collective_id, has_side_effects=True),
        name=name,
    )(values)


def add_rows(out_ref, left_ref, right_ref, rows, step=64):
    @pl.loop(0, rows // step)
    def _(i):
        at = pl.ds(pl.multiple_of(i * step, step), step)
        total = left_ref[at, :].astype(F32) + right_ref[at, :].astype(F32)
        out_ref[at, :] = total.astype(out_ref.dtype)


def scatter_plane_kernel(
    part_ref, out_ref, own_ref, core_ref, x_ref, y_ref, last_ref,
    load_sem, send_sem, recv_sem,
):
    rows, width = own_ref.shape[1:]
    half = rows // 2
    x, y, core, row, col = places()
    over_x, over_y, over_core = peers(row, col)
    meet((over_x, over_y, over_core))
    top, bottom = pl.ds(0, half), pl.ds(half, half)

    def copy(index, source, place, device):
        return pltpu.make_async_remote_copy(
            source, place, send_sem.at[index], recv_sem.at[index],
            device_id=device, device_id_type=MESH,
        )

    sent = []

    def send(index, source, place, device):
        task = copy(index, source, place, device)
        task.start()
        sent.append(task)

    def wait(index, place):
        copy(index, place, place, over_core).wait_recv()

    order = ((1 - x, 1 - y), (1 - x, y), (x, 1 - y), (x, y))
    loads = []
    for i, (a, b) in enumerate(order):
        slot = 2 * a + b
        send(
            i, block_at(part_ref, a, 2 * b + 1 - core, rows, width, 0, rows),
            core_ref.at[slot], over_core,
        )
        load = pltpu.make_async_copy(
            block_at(part_ref, a, 2 * b + core, rows, width, 0, rows),
            own_ref.at[slot], load_sem.at[i],
        )
        load.start()
        loads.append(load)
    for i, (a, b) in enumerate(order):
        slot = 2 * a + b
        loads[i].wait()
        wait(i, core_ref.at[slot])
        add_rows(own_ref.at[slot], own_ref.at[slot], core_ref.at[slot], rows)
        if i in (0, 1):
            send(4 + i, own_ref.at[slot, top, :], x_ref.at[i], over_x)
        if i in (0, 2):
            send(6 + i // 2, own_ref.at[slot, bottom, :], y_ref.at[i // 2], over_y)
    wait(4, x_ref.at[0])
    slot = 2 * x + 1 - y
    add_rows(own_ref.at[slot, top, :], own_ref.at[slot, top, :], x_ref.at[0], half)
    send(8, own_ref.at[slot, top, :], last_ref.at[0], over_y)
    wait(6, y_ref.at[0])
    slot = 2 * (1 - x) + y
    add_rows(own_ref.at[slot, bottom, :], own_ref.at[slot, bottom, :], y_ref.at[0], half)
    send(9, own_ref.at[slot, bottom, :], last_ref.at[1], over_x)
    slot = 2 * x + y
    wait(5, x_ref.at[1])
    add_rows(own_ref.at[slot, top, :], own_ref.at[slot, top, :], x_ref.at[1], half)
    wait(7, y_ref.at[1])
    add_rows(own_ref.at[slot, bottom, :], own_ref.at[slot, bottom, :], y_ref.at[1], half)
    wait(8, last_ref.at[0])
    add_rows(out_ref.at[top, :], own_ref.at[slot, top, :], last_ref.at[0], half)
    wait(9, last_ref.at[1])
    add_rows(out_ref.at[bottom, :], own_ref.at[slot, bottom, :], last_ref.at[1], half)
    for task in sent:
        task.wait_send()


def scatter_plane(values, name, collective_id):
    cols = lax.axis_size("col")
    if cols != 4:
        mine = lax.psum_scatter(
            values, "row", scatter_dimension=0, tiled=True, axis_index_groups=neighbours()
        )
        return lax.psum_scatter(mine, "col", scatter_dimension=1, tiled=True).astype(F32)
    rows, width = values.shape[0] // PAIR, values.shape[1] // cols
    return pl.pallas_call(
        scatter_plane_kernel,
        in_specs=[pl.BlockSpec(memory_space=pl.ANY)],
        out_specs=pl.BlockSpec(memory_space=pltpu.VMEM),
        out_shape=jax.ShapeDtypeStruct((rows, width), F32),
        scratch_shapes=[
            pltpu.VMEM((4, rows, width), BF16),
            pltpu.VMEM((4, rows, width), BF16),
            pltpu.VMEM((2, rows // 2, width), BF16),
            pltpu.VMEM((2, rows // 2, width), BF16),
            pltpu.VMEM((2, rows // 2, width), BF16),
            pltpu.SemaphoreType.DMA((4,)),
            pltpu.SemaphoreType.DMA((10,)),
            pltpu.SemaphoreType.DMA((10,)),
        ],
        cost_estimate=taking(40),
        compiler_params=pltpu.CompilerParams(
            collective_id=collective_id, has_side_effects=True, vmem_limit_bytes=40 << 20
        ),
        name=name,
    )(values)


def gather_heads(values, x):
    here = in_order(x, pick(values, x, 0), swap_rows(pick(values, 1 - x, 0)), 1)
    return lax.all_gather(here, "col", axis=1, tiled=True)


def scatter_heads(values, x):
    mine = lax.psum_scatter(values, "col", scatter_dimension=1, tiled=True)
    return in_order(x, pick(mine, x, 1), swap_rows(pick(mine, 1 - x, 1)), 0)


def project_out_kernel(
    heads_ref, weight_ref, tokens_ref, all_ref, resid_ref, resid_all_ref,
    joined_ref, low_ref, local_sem, send_sem, recv_sem,
):
    rows, width = resid_ref.shape
    part = heads_ref.shape[1]
    x, y, core, row, col = places()
    over_x, over_y, over_core = peers(row, col)
    count = rows // CHUNKS
    col_y, col_core = (col + 2) % 4, col + 1 - 2 * core
    corner = (col_core + 2) % 4
    meet((over_x, over_y, over_core))
    copies = Copies(send_sem, recv_sem, over_core)
    base = 8 * CHUNKS

    def piece(c, a, s):
        at = pl.multiple_of((PAIR * c + a) * part, 128)
        return joined_ref.at[pl.ds(s * count, count), pl.ds(at, part)]

    def mine(a, s):
        return heads_ref.at[pl.ds(pl.multiple_of(a * rows + s * count, 128), count), :]

    def send(group, s, source, place, device):
        copies.send(base + group * CHUNKS + s, source, place, device)

    def pass_on(group, s, place, device):
        send(group, s, place, place, device)

    def wait(group, s, place):
        copies.wait(base + group * CHUNKS + s, place)

    local = []
    for s in range(CHUNKS):
        send(0, s, mine(1 - x, s), piece(col, x, s), over_x)
        send(1, s, mine(x, s), piece(col, x, s), over_y)
        send(2, s, mine(x, s), piece(col, x, s), over_core)
        task = pltpu.make_async_copy(mine(x, s), piece(col, x, s), local_sem.at[s])
        task.start()
        local.append(task)
    gather = PlaneGather(copies, 0, low_ref, resid_all_ref, local_sem.at[CHUNKS])

    def relay(s):
        wait(0, s, piece(col, 1 - x, s))
        pass_on(3, s, piece(col, 1 - x, s), over_y)
        pass_on(4, s, piece(col, 1 - x, s), over_core)

    relay(0)
    for s in range(CHUNKS):
        if s + 1 < CHUNKS:
            relay(s + 1)
        wait(1, s, piece(col_y, x, s))
        pass_on(5, s, piece(col_y, x, s), over_core)
        wait(3, s, piece(col_y, 1 - x, s))
        pass_on(6, s, piece(col_y, 1 - x, s), over_core)
        wait(2, s, piece(col_core, x, s))
        wait(4, s, piece(col_core, 1 - x, s))
        wait(5, s, piece(corner, x, s))
        wait(6, s, piece(corner, 1 - x, s))
        local[s].wait()
        at = pl.ds(s * count, count)
        result = tokens_ref[at, :].astype(F32) + dot(joined_ref[at, :], weight_ref[...])
        resid_ref[at, :] = result
        low_ref[at, :] = result.astype(BF16)
        gather.start_chunk(s)
    store = pltpu.make_async_copy(joined_ref, all_ref, local_sem.at[CHUNKS + 1])
    store.start()
    gather.keep_own()
    for s in range(CHUNKS):
        gather.near_in_order(s)
    gather.far()
    gather.finish()
    copies.finish()
    store.wait()


def project_out(heads, weight, tokens, collective_id):
    rows, width = tokens.shape
    vmem, anywhere = pl.BlockSpec(memory_space=pltpu.VMEM), pl.BlockSpec(memory_space=pl.ANY)
    sems = lambda n: pltpu.SemaphoreType.DMA((n,))
    return pl.pallas_call(
        project_out_kernel,
        in_specs=[vmem] * 3,
        out_specs=[anywhere, vmem, anywhere],
        out_shape=[
            jax.ShapeDtypeStruct((rows, 4 * width), BF16),
            jax.ShapeDtypeStruct((rows, width), F32),
            jax.ShapeDtypeStruct((PAIR * rows, 4 * width), BF16),
        ],
        scratch_shapes=[
            pltpu.VMEM((rows, 4 * width), BF16), pltpu.VMEM((rows, width), BF16),
            sems(CHUNKS + 2), sems(15 * CHUNKS), sems(15 * CHUNKS),
        ],
        compiler_params=pltpu.CompilerParams(
            collective_id=collective_id, has_side_effects=True, vmem_limit_bytes=60 << 20
        ),
        cost_estimate=taking(66),
        name="project_out",
    )(heads, weight, tokens)


class RowSum:
    def __init__(self, copies, base, slots_ref):
        self.copies, self.base, self.slots = copies, base, slots_ref
        self.row, self.col = lax.axis_index("row"), lax.axis_index("col")
        self.size = slots_ref.shape[0]
        self.others = [((self.row + step) % self.size, self.col) for step in range(1, self.size)]

    def start(self):
        for step, device in enumerate(self.others, 1):
            self.copies.send(self.base + step - 1, self.slots.at[0], self.slots.at[step], device)

    def finish(self):
        for step in range(1, self.size):
            self.copies.wait(self.base + step - 1, self.slots.at[step])
        total = jnp.zeros(self.slots.shape[1:], F32)
        for r in range(self.size):
            total += self.slots[(self.row + self.size - r) % self.size]
        return total


def row_stats(values):
    mean = jnp.mean(values, axis=1, keepdims=True)
    var = jnp.mean(values * values, axis=1, keepdims=True) - mean * mean
    return mean, lax.rsqrt(var + 1e-05)


def norm_backward(grad_norm, unit_values, inv_std, norm_gain):
    full_width = grad_norm.shape[1] * lax.axis_size("col")
    grad_unit = grad_norm * norm_gain
    row_sums = lax.psum(
        (jnp.sum(grad_unit, axis=1), jnp.sum(grad_unit * unit_values, axis=1)), "col"
    )
    grad_in = inv_std * (
        grad_unit
        - row_sums[0][:, None] / full_width
        - unit_values * row_sums[1][:, None] / full_width
    )
    return grad_in, jnp.sum(grad_norm * unit_values, axis=0)


def rotation_tables(positions):
    half = ROT // 2
    inv_freq = BASE ** (-(jnp.arange(half, dtype=F32) * 2.0) / ROT)
    angles = positions.astype(F32)[:, None] * inv_freq[None, :]
    cosine, sine = jnp.cos(angles), jnp.sin(angles)
    rest = HEAD_DIM - ROT
    ones = jnp.ones((positions.shape[0], rest), F32)
    cosine = jnp.concatenate([cosine, cosine, ones], axis=1)
    sine = jnp.concatenate([-sine, sine, 0.0 * ones], axis=1)
    return jnp.tile(cosine, (1, 2)), jnp.tile(sine, (1, 2))


TILE = 256


def norm_tile(values_ref, gain_ref, stats_ref):
    values = values_ref[...].astype(F32)
    mean, inv_std = row_stats(values)
    lane = lax.broadcasted_iota(jnp.int32, stats_ref.shape, 1)
    stats_ref[...] = jnp.where(lane == 0, mean, inv_std)
    return ((values - mean) * inv_std * gain_ref[...]).astype(BF16)


def project_heads_kernel(
    tokens_ref, gain_ref, weight_ref, bias_ref, cos_ref, sin_ref,
    normed_ref, q_ref, k_ref, v_ref, stats_ref,
):
    width = q_ref.shape[1]
    normed = norm_tile(tokens_ref, gain_ref, stats_ref)
    normed_ref[...] = normed
    in_head = lax.broadcasted_iota(jnp.int32, (1, width), 1) % HEAD_DIM
    cosine = jnp.tile(cos_ref[...], (1, width // cos_ref.shape[1]))
    sine = jnp.tile(sin_ref[...], (1, width // sin_ref.shape[1]))
    pre = dot(normed, weight_ref[...]) + bias_ref[...]
    for ref, at, scale in ((q_ref, 0, SCALE), (k_ref, width, 1.0)):
        part = pre[:, at : at + width]
        turned = part * cosine + swap_pairs(part, in_head) * sine
        ref[...] = turned.astype(BF16) * jnp.asarray(scale, BF16)
    v_ref[...] = pre[:, 2 * width :].astype(BF16)


def tiled(columns):
    return pl.BlockSpec((TILE, columns), lambda i: (i, 0))


def whole(shape):
    return pl.BlockSpec(shape, lambda i: (0,) * len(shape))


def column_block(blocks_ref, all_ref, other, sems, index):
    row, col = lax.axis_index("row"), lax.axis_index("col")
    send_sem, recv_sem = sems
    return pltpu.make_async_remote_copy(
        blocks_ref.at[other], all_ref.at[col], send_sem.at[index], recv_sem.at[index],
        device_id=(row, other), device_id_type=MESH,
    )


def exchange_beside(kernel, blocks_ref, all_ref, steps, local, *sems, more=()):
    row, col = lax.axis_index("row"), lax.axis_index("col")
    others = [col + d - 2 * d * ((col // d) % 2) if d < 3 else 3 - col for d in steps]

    @pl.when(pl.program_id(0) == 0)
    def _():
        meet([(row, other) for other in others] + list(more))
        for i, other in enumerate(others):
            column_block(blocks_ref, all_ref, other, sems, i).start()
        if local is not None:
            pltpu.make_async_copy(blocks_ref.at[col], *local).start()

    kernel()

    @pl.when(pl.program_id(0) == pl.num_programs(0) - 1)
    def _():
        if local is not None:
            stage, local_sem = local
            pltpu.make_async_copy(blocks_ref.at[col], stage, local_sem).wait()
            task = pltpu.make_async_copy(stage, all_ref.at[col], local_sem)
            task.start()
            task.wait()
        for i, other in enumerate(others):
            task = column_block(blocks_ref, all_ref, other, sems, i)
            task.wait_send()
            send_sem, recv_sem = sems
            pltpu.make_async_remote_copy(
                blocks_ref.at[other], all_ref.at[other], send_sem.at[i], recv_sem.at[i],
                device_id=(row, other), device_id_type=MESH,
            ).wait_recv()


def project_heads_exchange_kernel(*refs):
    *ins, blocks_ref = refs[:7]
    outs, all_ref, (stage, local_sem, *sems) = refs[7:12], refs[12], refs[13:]
    exchange_beside(
        lambda: project_heads_kernel(*ins, *outs),
        blocks_ref, all_ref, (2,), (stage, local_sem), *sems,
    )


def project_heads(tokens, gain, weight, bias, cosine, sine, blocks=None, collective_id=None):
    rows, depth = tokens.shape
    width = weight.shape[1] // 3
    in_specs = [
        tiled(depth), whole((1, depth)), whole(weight.shape), whole((1, 3 * width)),
        tiled(cosine.shape[1]), tiled(cosine.shape[1]),
    ]
    out_specs = [tiled(depth)] + [tiled(width)] * 3 + [tiled(8)]
    out_shape = [
        jax.ShapeDtypeStruct((rows, depth), BF16),
        *[jax.ShapeDtypeStruct((rows, width), BF16)] * 3,
        jax.ShapeDtypeStruct((rows, 8), F32),
    ]
    operands = [tokens, gain.reshape(1, depth), weight, bias.reshape(1, 3 * width), cosine, sine]
    params, scratch, kernel = {}, [], project_heads_kernel
    if blocks is not None:
        anywhere = pl.BlockSpec(memory_space=pl.ANY)
        in_specs, out_specs = in_specs + [anywhere], out_specs + [anywhere]
        out_shape = out_shape + [jax.ShapeDtypeStruct(blocks.shape, BF16)]
        operands = operands + [blocks]
        scratch = [pltpu.VMEM(blocks.shape[1:], BF16), pltpu.SemaphoreType.DMA]
        scratch = scratch + [pltpu.SemaphoreType.DMA((1,))] * 2
        params = dict(collective_id=collective_id, has_side_effects=True)
        kernel = project_heads_exchange_kernel
    return pl.pallas_call(
        kernel,
        grid=(rows // TILE,),
        in_specs=in_specs,
        out_specs=out_specs,
        out_shape=out_shape,
        scratch_shapes=scratch,
        compiler_params=pltpu.CompilerParams(vmem_limit_bytes=60 << 20, **params),
        cost_estimate=taking(16),
        name="project_heads",
    )(*operands)


def feed_forward_kernel(
    resid_ref, gain_ref, weight_ref, grad_ref, down_ref,
    normed_ref, hidden_ref, dgate_ref, dup_ref, stats_ref,
):
    lines, _, hidden, width = weight_ref.shape
    normed_ref[...] = norm_tile(resid_ref, gain_ref, stats_ref)
    gate = jnp.zeros((hidden, TILE), F32)
    up = jnp.zeros((hidden, TILE), F32)
    dhidden = jnp.zeros((hidden, TILE), F32)
    for z in range(lines):
        part = normed_ref[:, z * width : (z + 1) * width]
        gate += dot(weight_ref[z, 0], part, (1,), (1,))
        up += dot(weight_ref[z, 1], part, (1,), (1,))
    for c in range(down_ref.shape[0]):
        part = grad_ref[:, c * width : (c + 1) * width]
        dhidden += dot(down_ref[c], part, (1,), (1,))
    sigmoid = 1.0 / (1.0 + jnp.exp(-gate))
    silu = gate * sigmoid
    hidden_ref[...] = (silu * up).astype(BF16)
    dgate_ref[...] = (dhidden * up * sigmoid * (1.0 + gate * (1.0 - sigmoid))).astype(BF16)
    dup_ref[...] = (dhidden * silu).astype(BF16)


def feed_forward(resid, gain, weight, grad, down):
    rows, depth = resid.shape
    hidden = down.shape[1]
    across = pl.BlockSpec((hidden, TILE), lambda i: (0, i))
    return pl.pallas_call(
        feed_forward_kernel,
        grid=(rows // TILE,),
        in_specs=[
            tiled(depth), whole((1, depth)), whole(weight.shape), tiled(depth), whole(down.shape)
        ],
        out_specs=[tiled(depth)] + [across] * 3 + [tiled(8)],
        out_shape=[jax.ShapeDtypeStruct((rows, depth), BF16)]
        + [jax.ShapeDtypeStruct((hidden, rows), BF16)] * 3
        + [jax.ShapeDtypeStruct((rows, 8), F32)],
        compiler_params=pltpu.CompilerParams(vmem_limit_bytes=56 << 20),
        cost_estimate=taking(28),
        name="feed_forward",
    )(resid, gain.reshape(1, depth), weight, grad, down)


def weight_grads_kernel(*refs):
    *left_refs, right_ref, out_ref = refs
    for i, left_ref in enumerate(left_refs):
        out_ref[0, i] = dot(left_ref[...], right_ref[...]).astype(BF16)


def weight_grads(lefts, right, width, name):
    hidden, rows = lefts[0].shape
    blocks = right.shape[1] // width
    return pl.pallas_call(
        weight_grads_kernel,
        grid=(blocks,),
        in_specs=[whole((hidden, rows))] * len(lefts)
        + [pl.BlockSpec((rows, width), lambda i: (0, i))],
        out_specs=pl.BlockSpec((1, len(lefts), hidden, width), lambda i: (i, 0, 0, 0)),
        out_shape=jax.ShapeDtypeStruct((blocks, len(lefts), hidden, width), BF16),
        compiler_params=pltpu.CompilerParams(vmem_limit_bytes=56 << 20),
        cost_estimate=taking(9 * len(lefts)),
        name=name,
    )(*lefts, right)


def back_project_kernel(*refs):
    *left_refs, weight_ref, out_ref = refs
    width = weight_ref.shape[-1]
    lefts = [ref[...].T for ref in left_refs]
    for z in range(weight_ref.shape[0]):
        total = sum(dot(left, weight_ref[z, i]) for i, left in enumerate(lefts))
        out_ref[:, z * width : (z + 1) * width] = total.astype(BF16)


def back_project(lefts, weight, name):
    hidden, rows = lefts[0].shape
    depth = weight.shape[0] * weight.shape[-1]
    return pl.pallas_call(
        back_project_kernel,
        grid=(rows // TILE,),
        in_specs=[pl.BlockSpec((hidden, TILE), lambda i: (0, i))] * len(lefts)
        + [whole(weight.shape)],
        out_specs=tiled(depth),
        out_shape=jax.ShapeDtypeStruct((rows, depth), BF16),
        compiler_params=pltpu.CompilerParams(vmem_limit_bytes=48 << 20),
        cost_estimate=taking(10 * len(lefts)),
        name=name,
    )(*lefts, weight)


class PlaneScatter:
    SEMS = 14

    def __init__(self, copies, base, fill, sent_ref, own_ref, core_ref, x_ref, y_ref, last_ref):
        self.copies, self.base, self.fill = copies, base, fill
        self.sent, self.own, self.core_part = sent_ref, own_ref, core_ref
        self.x_ref, self.y_ref, self.last = x_ref, y_ref, last_ref
        self.x, self.y, self.core, row, col = places()
        self.over_x, self.over_y, self.over_core = peers(row, col)
        x, y = self.x, self.y
        self.order = ((1 - x, 1 - y), (1 - x, y), (x, 1 - y), (x, y))
        self.theirs = [2 * b + 1 - self.core for _, b in self.order]
        self.ours = [2 * b + self.core for _, b in self.order]
        self.half = own_ref.shape[1] // 2
        self.rows = (pl.ds(0, self.half), pl.ds(self.half, self.half))
        self.given = Copies(copies.send_sem, copies.recv_sem, self.over_core)

    def send(self, index, source, place, device):
        self.copies.send(self.base + index, source, place, device)

    def wait(self, index, place):
        self.copies.wait(self.base + index, place)

    def give(self, i, h):
        a, _ = self.order[i]
        self.fill(self.sent.at[i], a, self.theirs[i], h, None)
        at = self.rows[h]
        self.given.send(
            self.base + 2 * i + h, self.sent.at[i, at, :], self.core_part.at[i, at, :], self.over_core
        )

    def keep(self, i, h):
        a, _ = self.order[i]
        at = self.rows[h]
        self.wait(2 * i + h, self.core_part.at[i, at, :])
        self.fill(self.own.at[i], a, self.ours[i], h, self.core_part.at[i])
        self.part_done(i, h)

    def part_done(self, i, h):
        at = self.rows[h]
        if h == 0 and i in (0, 1):
            self.send(8 + i, self.own.at[i, at, :], self.x_ref.at[i], self.over_x)
        if h == 1 and i in (0, 2):
            self.send(10 + i // 2, self.own.at[i, at, :], self.y_ref.at[i // 2], self.over_y)

    def begin(self):
        self.give(0, 0)
        self.give(0, 1)
        self.keep(0, 0)
        self.keep(0, 1)

    def proceed(self):
        for h in range(2):
            self.give(1, h)
            self.give(2, h)
        self.keep(1, 0)
        self.keep(2, 1)

    def complete(self):
        self.keep(2, 0)
        self.keep(1, 1)
        for h in range(2):
            self.give(3, h)
        for h in range(2):
            self.keep(3, h)

    def settle(self):
        self.given.finish()

    def drain(self):
        view = self.own.at[0, self.rows[0], :]
        for index in range(self.SEMS):
            self.copies.copy(self.base + index, view, view, self.over_core).wait_send()

    def add(self, i, h, ref):
        at = self.own.at[i, self.rows[h], :]
        add_rows(at, at, ref, self.half)

    def second(self):
        self.wait(8, self.x_ref.at[0])
        self.add(2, 0, self.x_ref.at[0])
        self.send(12, self.own.at[2, self.rows[0], :], self.last.at[0], self.over_y)
        self.wait(10, self.y_ref.at[0])
        self.add(1, 1, self.y_ref.at[0])
        self.send(13, self.own.at[1, self.rows[1], :], self.last.at[1], self.over_x)
        self.wait(9, self.x_ref.at[1])
        self.add(3, 0, self.x_ref.at[1])
        self.wait(11, self.y_ref.at[1])
        self.add(3, 1, self.y_ref.at[1])

    def third(self):
        self.wait(12, self.last.at[0])
        self.wait(13, self.last.at[1])

    def result(self, start, count):
        h, other = divmod(start, self.half)
        return self.own[3, pl.ds(start, count), :].astype(F32) + self.last[
            h, pl.ds(other, count), :
        ].astype(F32)


class PartsScatter(PlaneScatter):
    def __init__(self, copies, base, parts_ref, load_sem, *scratch):
        super().__init__(copies, base, None, None, *scratch)
        blocks = [a * 4 for a, _ in self.order]
        self.parts, self.load_sem = parts_ref, load_sem
        self.sources = [parts_ref.at[at + c] for at, c in zip(blocks, self.theirs)]
        self.loads = [
            pltpu.make_async_copy(parts_ref.at[at + c], self.own.at[i], load_sem.at[i])
            for i, (at, c) in enumerate(zip(blocks, self.ours))
        ]

    def start(self):
        for i, load in enumerate(self.loads):
            load.start()
            for h, at in enumerate(self.rows):
                self.given.send(
                    self.base + 2 * i + h, self.sources[i].at[at, :],
                    self.core_part.at[i, at, :], self.over_core,
                )

    def keep(self, i, h):
        if h == 0:
            self.loads[i].wait()
        at = self.rows[h]
        self.wait(2 * i + h, self.core_part.at[i, at, :])
        self.add(i, h, self.core_part.at[i, at, :])
        self.part_done(i, h)


class LineScatter:
    def __init__(self, up_send, up_recv, down_send, down_recv, part, up_ref, down_ref):
        self.part, self.row, self.col = part, lax.axis_index("row"), lax.axis_index("col")
        self.z = self.row // PAIR
        last = LINES - 1
        self.ways = (
            (self.z, lambda n: n, up_ref, up_send, up_recv, jnp.minimum(self.row + PAIR, PAIR * last + PAIR - 1)),
            (last - self.z, lambda n: last - n, down_ref, down_send, down_recv, jnp.maximum(self.row - PAIR, 0)),
        )

    def clear(self):
        for n, _, slots, _, _, _ in self.ways:

            @pl.when(n == 0)
            def _():
                slots[LINES - 2] = jnp.zeros(slots.shape[1:], slots.dtype)

    def task(self, way, step, source):
        _, _, slots, send, recv, device = way
        return pltpu.make_async_remote_copy(
            source, slots.at[step], send.at[step], recv.at[step],
            device_id=(device, self.col), device_id_type=MESH,
        )

    def sends(self, way, step, act):
        n, place, slots, _, _, _ = way

        @pl.when(n == 0)
        def _():
            act(self.task(way, step, self.part(place(LINES - 1 - step))))

        if step > 0:

            @pl.when((n > 0) & (n <= step))
            def _():
                act(self.task(way, step, slots.at[step - 1]))

    def start(self):
        for way in self.ways:
            self.sends(way, 0, lambda task: task.start())

    def hop(self, step):
        for way in self.ways:
            n, place, slots, _, _, _ = way

            @pl.when((n >= 1) & (n <= step + 1))
            def _():
                self.task(way, step, slots.at[step]).wait_recv()
                add_rows(
                    slots.at[step], slots.at[step], self.part(place(LINES - 2 - step + n)),
                    slots.shape[1],
                )

            self.sends(way, step + 1, lambda task: task.start())

    def receive(self):
        last = LINES - 2
        for way in self.ways:
            n, _, slots, _, _, _ = way

            @pl.when(n >= 1)
            def _():
                self.task(way, last, slots.at[last]).wait_recv()

    def total(self, at):
        last = LINES - 2
        result = self.part(self.z)[at, :].astype(F32)
        for _, _, slots, _, _, _ in self.ways:
            result = result + slots[last, at, :].astype(F32)
        return result

    def finish(self):
        for way in self.ways:
            for step in range(LINES - 1):
                self.sends(way, step, lambda task: task.wait_send())


STEP = 128


class NormBack:
    def __init__(
        self, copies, base, values_ref, stats_ref, gain_ref, base_ref, out_ref, low_ref, dgain_ref,
        sums_ref,
    ):
        self.copies, self.base = copies, base
        self.values, self.stats, self.gain, self.more = values_ref, stats_ref, gain_ref, base_ref
        self.out, self.low, self.dgain, self.sums = out_ref, low_ref, dgain_ref, sums_ref

    def unit_of(self, at):
        stats = self.stats[at, :]
        return (self.values[at, :].astype(F32) - stats[:, 0:1]) * stats[:, 1:2]

    def start(self, result, devices):
        lane = lax.broadcasted_iota(jnp.int32, (1, 128), 1)
        self.dgain[...] = jnp.zeros_like(self.dgain)
        for start in range(0, self.out.shape[0], STEP):
            at = pl.ds(start, STEP)
            grad = result(start, STEP)
            self.out[at, :] = grad
            unit = self.unit_of(at)
            self.dgain[...] += jnp.sum(grad * unit, axis=0, keepdims=True)
            grad = grad * self.gain[...]
            first = jnp.sum(grad, axis=1, keepdims=True)
            second = jnp.sum(grad * unit, axis=1, keepdims=True)
            both = jnp.where(lane == 0, first, jnp.where(lane == 1, second, 0.0))
            self.sums[0, :, start : start + STEP] = both.T[:8]
        for i, device in enumerate(devices):
            self.copies.send(self.base + i, self.sums.at[0], self.sums.at[1 + i], device)

    def finish(self):
        rows, width = self.out.shape
        for i in range(3):
            self.copies.wait(self.base + i, self.sums.at[1 + i])
        for start in range(0, rows, STEP):
            at = pl.ds(start, STEP)
            columns = slice(start, start + STEP)
            total = (self.sums[0, :, columns] + self.sums[1, :, columns]) + (
                self.sums[2, :, columns] + self.sums[3, :, columns]
            )
            total = jnp.concatenate([total, jnp.zeros((STEP - 8, STEP), F32)], axis=0).T
            total = total * (1.0 / (4 * width))
            unit = self.unit_of(at)
            grad = self.out[at, :] * self.gain[...]
            grad = self.stats[at, 1:2] * (grad - total[:, 0:1] - unit * total[:, 1:2])
            grad = grad + self.more[at, :].astype(F32)
            self.out[at, :] = grad
            if self.low is not None:
                self.low[at, :] = grad.astype(BF16)


def scatter_scratch(rows, width):
    block = lambda n, r: pltpu.VMEM((n, r, width), BF16)
    return [
        block(4, rows), block(4, rows), block(4, rows),
        block(2, rows // 2), block(2, rows // 2), block(2, rows // 2),
    ]


def around():
    _, _, _, row, col = places()
    over_x, over_y, over_core = peers(row, col)
    return over_x, over_y, over_core, (row, 3 - col)


def filling(rows, product):
    half = rows // 2

    def fill(ref, a, c, h, more):
        @pl.loop(0, half // TILE)
        def _(i):
            start = h * half + i * TILE
            total = product(pl.ds(pl.multiple_of(a * rows + start, TILE), TILE), c)
            at = pl.ds(pl.multiple_of(start, TILE), TILE)
            if more is not None:
                total = total + more[at, :].astype(F32)
            ref[at, :] = total.astype(BF16)

    return fill


def turn_rows(left_ref, source_ref, a, rows):
    @pl.loop(0, rows // TILE)
    def _(i):
        at = pl.ds(pl.multiple_of(a * rows + i * TILE, TILE), TILE)
        left_ref[at, :] = source_ref[:, at].T


def back_second_kernel(
    gate_ref, up_ref, weight_ref, hidden_hbm, grad_hbm, values_ref, stats_ref, gain_ref, base_ref,
    out_ref, low_ref, dgain_ref, down_ref,
    hidden_ref, grad_ref, gate_vmem, up_vmem, weight_vmem, left_ref, sums_ref, load_sem, send_sem, recv_sem, *scratch,
):
    rows, width = out_ref.shape
    x, y, core, _, _ = places()
    devices = around()

    def load_left(i, a):
        at = pl.ds(pl.multiple_of(a * rows, TILE), rows)
        return [
            pltpu.make_async_copy(ref.at[:, at], vmem.at[:, at], load_sem.at[2 * i + j])
            for j, (ref, vmem) in enumerate(((gate_ref, gate_vmem), (up_ref, up_vmem)))
        ]

    def load_weight(i, c):
        return pltpu.make_async_copy(weight_ref.at[c], weight_vmem.at[c], load_sem.at[4 + i])

    lefts = [load_left(0, 1 - x), load_left(1, x)]
    columns = (2 * (1 - y) + 1 - core, 2 * (1 - y) + core, 2 * y + 1 - core, 2 * y + core)
    weights = [load_weight(i, c) for i, c in enumerate(columns)]
    others = [
        pltpu.make_async_copy(hidden_hbm, hidden_ref, load_sem.at[8]),
        pltpu.make_async_copy(grad_hbm, grad_ref, load_sem.at[9]),
    ]
    for task in (*lefts[0], *weights, *lefts[1], *others):
        task.start()
    meet(devices)
    copies = Copies(send_sem, recv_sem, devices[2])

    def turn(i, a):
        for j, (task, vmem) in enumerate(zip(lefts[i], (gate_vmem, up_vmem))):
            task.wait()
            turn_rows(left_ref.at[j], vmem, a, rows)

    def product(at, c):
        return dot(left_ref[0, at, :], weight_vmem[c, 0]) + dot(
            left_ref[1, at, :], weight_vmem[c, 1]
        )

    scatter = PlaneScatter(copies, 0, filling(rows, product), *scratch)
    turn(0, 1 - x)
    weights[0].wait()
    scatter.give(0, 0)
    scatter.give(0, 1)
    weights[1].wait()
    scatter.keep(0, 0)
    scatter.keep(0, 1)
    weights[2].wait()
    scatter.give(1, 0)
    scatter.give(1, 1)
    weights[3].wait()
    scatter.keep(1, 0)
    turn(1, x)
    scatter.give(2, 1)
    scatter.give(2, 0)
    scatter.keep(2, 1)
    scatter.keep(2, 0)
    scatter.keep(1, 1)
    scatter.give(3, 0)
    scatter.give(3, 1)
    scatter.keep(3, 0)
    scatter.keep(3, 1)
    scatter.settle()
    scatter.second()
    for task in others:
        task.wait()
    for c in range(down_ref.shape[0]):
        right = grad_ref[:, c * width : (c + 1) * width]
        down_ref[c] = dot(hidden_ref[...], right).astype(BF16)
    scatter.third()
    norm = NormBack(
        copies, PlaneScatter.SEMS, values_ref, stats_ref, gain_ref, base_ref, out_ref, low_ref,
        dgain_ref, sums_ref,
    )
    norm.start(scatter.result, devices[1:])
    norm.finish()
    copies.finish()


def back_second(gate, up, weight, hidden, grad, values, stats, gain, base, collective_id):
    rows, width = values.shape
    units, tokens = gate.shape
    vmem, anywhere = pl.BlockSpec(memory_space=pltpu.VMEM), pl.BlockSpec(memory_space=pl.ANY)
    sems = lambda n: pltpu.SemaphoreType.DMA((n,))
    return pl.pallas_call(
        back_second_kernel,
        in_specs=[anywhere] * 5 + [vmem] * 4,
        out_specs=[vmem] * 4,
        out_shape=[
            jax.ShapeDtypeStruct((rows, width), F32),
            jax.ShapeDtypeStruct((rows, width), BF16),
            jax.ShapeDtypeStruct((1, width), F32),
            jax.ShapeDtypeStruct((grad.shape[1] // width, units, width), BF16),
        ],
        scratch_shapes=[
            pltpu.VMEM(hidden.shape, BF16), pltpu.VMEM(grad.shape, BF16),
            pltpu.VMEM(gate.shape, BF16), pltpu.VMEM(up.shape, BF16),
            pltpu.VMEM(weight.shape, BF16), pltpu.VMEM((2, tokens, units), BF16),
            pltpu.VMEM((4, 8, rows), F32),
            sems(10), sems(PlaneScatter.SEMS + 3), sems(PlaneScatter.SEMS + 3),
            *scatter_scratch(rows, width),
        ],
        compiler_params=pltpu.CompilerParams(
            collective_id=collective_id, has_side_effects=True, vmem_limit_bytes=63 << 20
        ),
        cost_estimate=taking(50),
        name="back_second",
    )(gate, up, weight, hidden, grad, values, stats, gain.reshape(1, width), base)


def back_first_kernel(
    grad_ref, weight_ref, values_ref, stats_ref, gain_ref, base_ref, part_ref, ffn_ref, heads_ref,
    vectors_ref,
    out_ref, vector_sums_ref, query_ref, key_ref, value_ref, gate_ref, up_grad_ref, out_grad_ref,
    dgain_ref, slots_ref, sums_ref, up_ref, down_line_ref, heads_up_ref, heads_down_ref, swap_ref, swapped_ref, turn_ref,
    send_sem, recv_sem, *scratch,
):
    line_sems, scratch = scratch[:12], scratch[12:]
    rows, width = out_ref.shape
    x, _, _, row, col = places()
    devices = around()
    copies = Copies(send_sem, recv_sem, devices[2])
    vectors = RowSum(copies, PlaneScatter.SEMS + 7, slots_ref)
    meet((*devices[1:], *vectors.others))
    depth, columns = up_ref.shape[2:]

    def line_of(k):
        at = pl.ds(k * columns, columns)
        return LineScatter(
            *line_sems[4 * k : 4 * k + 4],
            lambda b: part_ref.at[pl.ds(pl.multiple_of(b * depth, 128), depth), at],
            up_ref.at[k], down_line_ref.at[k],
        )

    out_depth = out_grad_ref.shape[0]
    heads = LineScatter(
        *line_sems[8:],
        lambda b: heads_ref.at[pl.ds(pl.multiple_of(b * out_depth, 128), out_depth), :],
        heads_up_ref, heads_down_ref,
    )
    lines = [line_of(k) for k in range(2)] + [heads]
    for line in lines:
        line.clear()
    lines[0].start()

    def product(at, c):
        weight = weight_ref[pl.ds(pl.multiple_of(c * width, 128), width), :]
        return dot(grad_ref[at, :], weight, (1,), (1,))

    scatter = PlaneScatter(copies, 0, filling(rows, product), *scratch)
    norm = NormBack(
        copies, PlaneScatter.SEMS, values_ref, stats_ref, gain_ref, base_ref, out_ref, None,
        dgain_ref, sums_ref,
    )
    half = depth // PAIR
    theirs = pl.multiple_of((1 - x) * half, 128)
    ours = pl.multiple_of(x * half, 128)
    swap = PlaneScatter.SEMS + 3
    units = ffn_ref.shape[2]
    scatter.begin()
    lines[1].start()
    scatter.proceed()
    lines[0].hop(0)
    heads.start()
    scatter.complete()
    lines[1].hop(0)
    scatter.settle()
    heads.hop(0)
    scatter.second()
    lines[0].hop(1)
    here = pl.ds(pl.multiple_of(x * units, 16), units)
    there = pl.ds(pl.multiple_of((1 - x) * units, 16), units)
    for w in range(2):
        copies.send(
            swap + 2 + w, ffn_ref.at[0, w, :, pl.ds(theirs, half)], turn_ref.at[w, here, :], devices[0]
        )
        turn_ref[w, here, :] = ffn_ref[0, w, :, pl.ds(ours, half)]
    lines[1].hop(1)
    scatter.third()
    heads.hop(1)
    norm.start(scatter.result, devices[1:4])
    slots_ref[0] = vectors_ref[...]
    slots_ref[0, 3:4, :] = dgain_ref[...]
    vectors.start()
    part = width // PAIR
    outs = (query_ref, key_ref, value_ref)

    def pieces(k):
        for w in range(3):
            start, end = max(k * columns, w * part), min((k + 1) * columns, (w + 1) * part)
            if start < end:
                yield outs[w], start - w * part, start, end - start

    def close(k):
        lines[k].receive()
        at = pl.ds(k * columns, columns)
        swap_ref[:, at] = lines[k].total(pl.ds(theirs, half)).astype(BF16)
        copies.send(swap + k, swap_ref.at[:, at], swapped_ref.at[:, at], devices[0])
        total = lines[k].total(pl.ds(ours, half))
        for ref, place, start, size in pieces(k):
            columns_at = pl.ds(pl.multiple_of(x * part + place, 128), size)
            ref[:, columns_at] = total[:, start - k * columns : start - k * columns + size]

    close(0)
    norm.finish()
    close(1)
    for w, ref in enumerate((gate_ref, up_grad_ref)):
        copies.wait(swap + 2 + w, turn_ref.at[w, there, :])
        for j in range(PAIR * units // 128):
            at = slice(j * 128, (j + 1) * 128)
            ref[:, at] = turn_ref[w, at, :].T.astype(F32)
    heads.receive()
    out_grad_ref[...] = heads.total(pl.ds(0, out_depth))
    heads.finish()
    vector_sums_ref[...] = vectors.finish()
    for k in range(2):
        at = pl.ds(k * columns, columns)
        copies.wait(swap + k, swapped_ref.at[:, at])
        for ref, place, start, size in pieces(k):
            columns_at = pl.ds(pl.multiple_of((1 - x) * part + place, 128), size)
            ref[:, columns_at] = swapped_ref[:, start : start + size].astype(F32)
        lines[k].finish()
    copies.finish()


def back_first(
    grad, weight, values, stats, gain, base, part, ffn, heads, vectors, collective_id
):
    rows, width = values.shape
    depth, columns = part.shape[0] // LINES, part.shape[1]
    vmem = pl.BlockSpec(memory_space=pltpu.VMEM)
    sems = lambda n: pltpu.SemaphoreType.DMA((n,))
    count = PlaneScatter.SEMS + 7 + PAIR * LINES - 1
    units = ffn.shape[2]
    return pl.pallas_call(
        back_first_kernel,
        in_specs=[vmem] * 10,
        out_specs=[vmem] * 8,
        out_shape=[
            jax.ShapeDtypeStruct((rows, width), F32),
            jax.ShapeDtypeStruct(vectors.shape, F32),
        ]
        + [jax.ShapeDtypeStruct((depth // PAIR, width), F32)] * 3
        + [jax.ShapeDtypeStruct((depth // PAIR, PAIR * units), F32)] * 2
        + [jax.ShapeDtypeStruct((heads.shape[0] // LINES, width), F32)],
        scratch_shapes=[
            pltpu.VMEM((1, width), F32), pltpu.VMEM((PAIR * LINES,) + vectors.shape, F32),
            pltpu.VMEM((4, 8, rows), F32),
            pltpu.VMEM((2, LINES - 1, depth, columns // 2), BF16),
            pltpu.VMEM((2, LINES - 1, depth, columns // 2), BF16),
            *[pltpu.VMEM((LINES - 1, heads.shape[0] // LINES, width), BF16)] * 2,
            pltpu.VMEM((depth // PAIR, columns), BF16), pltpu.VMEM((depth // PAIR, columns), BF16),
            pltpu.VMEM((2, PAIR * units, depth // PAIR), BF16),
            sems(count), sems(count), *[sems(LINES - 1)] * 12,
            *scatter_scratch(rows, width),
        ],
        compiler_params=pltpu.CompilerParams(
            collective_id=collective_id, has_side_effects=True, vmem_limit_bytes=63 << 20
        ),
        cost_estimate=taking(10),
        name="back_first",
    )(grad, weight, values, stats, gain.reshape(1, width), base, part, ffn, heads, vectors)


def back_heads_kernel(
    low_ref, weight_ref, attn_hbm, hidden_hbm, down_hbm, blocks_ref,
    out_ref, part_ref, mix_ref, all_ref,
    stage_ref, attn_ref, hidden_ref, down_ref, left_ref, sent_ref, own_ref, core_ref, y_ref, give_ref, come_ref,
    load_sem, out_sem, send_sem, recv_sem,
):
    rows, width = low_ref.shape
    half = width // PAIR
    count = rows // CHUNKS
    x, y, core, row, col = places()
    over_x, over_y, over_core = peers(row, col)
    over_far = (row, 3 - col)
    loads = [
        pltpu.make_async_copy(source, place, load_sem.at[i])
        for i, (source, place) in enumerate(
            ((attn_hbm, attn_ref), (hidden_hbm, hidden_ref), (down_hbm, down_ref))
        )
    ]
    for load in loads:
        load.start()
    stage = pltpu.make_async_copy(blocks_ref.at[col], stage_ref, load_sem.at[3])
    stage.start()
    meet((over_x, over_y, over_core, over_far))
    copies = Copies(send_sem, recv_sem, over_core)
    sides = (1 - y, y)

    def at_chunk(s):
        return pl.ds(s * count, count)

    def product(s, c):
        weight = weight_ref[pl.ds(pl.multiple_of(c * width, 128), width), :]
        return dot(low_ref[at_chunk(s), :], weight, (1,), (1,))

    def give(i, s):
        at = at_chunk(s)
        sent_ref[i, at, :] = product(s, 2 * sides[i] + 1 - core).astype(BF16)
        copies.send(i * CHUNKS + s, sent_ref.at[i, at, :], core_ref.at[i, at, :], over_core)

    def keep(i, s):
        at = at_chunk(s)
        part = product(s, 2 * sides[i] + core)
        copies.wait(i * CHUNKS + s, core_ref.at[i, at, :])
        own_ref[i, at, :] = (part + core_ref[i, at, :].astype(F32)).astype(BF16)
        if i == 0:
            copies.send(2 * CHUNKS + s, own_ref.at[0, at, :], y_ref.at[at, :], over_y)

    depth = give_ref.shape[1]

    def out_grad(z, x):
        at = pl.ds(pl.multiple_of((PAIR * z + x) * depth, 128), depth)
        return dot(attn_ref[:, at], low_ref[...], (0,), (0,))

    others = (((col + 2) % 4, over_y), (3 - col, over_far), (col + 1 - 2 * core, over_core))
    for s in range(CHUNKS):
        give(0, s)
    loads[0].wait()
    for z in range(LINES):
        give_ref[z] = out_grad(z, 1 - x).astype(BF16)
    copies.send(4 * CHUNKS, give_ref, come_ref, over_x)
    for s in range(CHUNKS):
        keep(0, s)
    for i, (other, device) in enumerate(others):
        copies.send(4 * CHUNKS + 1 + i, blocks_ref.at[other], all_ref.at[col], device)
    for s in range(CHUNKS):
        give(1, s)
    for s in range(CHUNKS):
        keep(1, s)
    for z in range(LINES):
        part_ref[z * depth : (z + 1) * depth, :] = out_grad(z, x).astype(BF16)
    stage.wait()
    stage = pltpu.make_async_copy(stage_ref, all_ref.at[col], load_sem.at[3])
    stage.start()
    for load in loads[1:]:
        load.wait()
    for a in range(PAIR):
        turn_rows(left_ref, hidden_ref, a, rows)
    kept = []
    for s in range(CHUNKS):

        @pl.loop(0, PAIR * rows // TILE)
        def _(i):
            a, start = i // (rows // TILE), pl.multiple_of(i % (rows // TILE) * TILE, TILE)
            left = left_ref[pl.ds(pl.multiple_of(i * TILE, TILE), TILE), :]
            mix_ref[a * CHUNKS + s, pl.ds(start, TILE), :] = dot(left, down_ref[s]).astype(BF16)

        at = at_chunk(s)
        copies.wait(2 * CHUNKS + s, y_ref.at[at, :])
        own_ref[1, at, :] = (
            own_ref[1, at, :].astype(F32) + y_ref[at, :].astype(F32)
        ).astype(BF16)
        place = out_ref.at[pl.ds(pl.multiple_of(x * rows + s * count, 128), count), :]
        theirs = own_ref.at[1, at, pl.ds(pl.multiple_of((1 - x) * half, 128), half)]
        ours = own_ref.at[1, at, pl.ds(pl.multiple_of(x * half, 128), half)]
        copies.send(3 * CHUNKS + s, theirs, place, over_x)
        task = pltpu.make_async_copy(ours, place, out_sem.at[s])
        task.start()
        kept.append(task)
    copies.wait(4 * CHUNKS, come_ref)
    for z in range(LINES):
        at = pl.ds(z * depth, depth)
        add_rows(part_ref.at[at, :], part_ref.at[at, :], come_ref.at[z], depth)
    for s in range(CHUNKS):
        copies.wait(
            3 * CHUNKS + s,
            out_ref.at[pl.ds(pl.multiple_of((1 - x) * rows + s * count, 128), count), :],
        )
    for i, (other, _) in enumerate(others):
        copies.wait(4 * CHUNKS + 1 + i, all_ref.at[other])
    copies.finish()
    stage.wait()
    for task in kept:
        task.wait()


def back_heads(low, weight, attn, hidden, down, blocks, collective_id):
    rows, width = low.shape
    depth = weight.shape[0] // (PAIR * LINES)
    vmem, anywhere = pl.BlockSpec(memory_space=pltpu.VMEM), pl.BlockSpec(memory_space=pl.ANY)
    sems = lambda n: pltpu.SemaphoreType.DMA((n,))
    wide = pltpu.VMEM((2, rows, width), BF16)
    swapped = pltpu.VMEM((LINES, depth, width), BF16)
    return pl.pallas_call(
        back_heads_kernel,
        in_specs=[vmem] * 2 + [anywhere] * 4,
        out_specs=[anywhere, vmem, vmem, anywhere],
        out_shape=[
            jax.ShapeDtypeStruct((PAIR * rows, width // PAIR), BF16),
            jax.ShapeDtypeStruct((LINES * depth, width), BF16),
            jax.ShapeDtypeStruct((PAIR * CHUNKS, rows, width), BF16),
            jax.ShapeDtypeStruct(blocks.shape, BF16),
        ],
        scratch_shapes=[
            pltpu.VMEM(blocks.shape[1:], BF16),
            pltpu.VMEM(attn.shape, BF16), pltpu.VMEM(hidden.shape, BF16),
            pltpu.VMEM(down.shape, BF16), pltpu.VMEM(hidden.shape[::-1], BF16),
            wide, wide, wide, pltpu.VMEM((rows, width), BF16),
            swapped, swapped,
            sems(4), sems(CHUNKS), sems(4 * CHUNKS + 4), sems(4 * CHUNKS + 4),
        ],
        compiler_params=pltpu.CompilerParams(
            collective_id=collective_id, has_side_effects=True, vmem_limit_bytes=60 << 20
        ),
        cost_estimate=taking(60),
        name="back_heads",
    )(low, weight, attn, hidden, down, blocks)


def per_device(
    tokens, segment_ids, positions, attn_gain, query_weight, query_bias, key_weight, key_bias,
    value_weight, value_bias, out_weight, mlp_gain, gate_weight, up_weight, down_weight, out_grad,
):
    count, width = tokens.shape
    lines = lax.axis_size("row") // PAIR
    cols = lax.axis_size("col")
    row = lax.axis_index("row")
    col = lax.axis_index("col")
    x = row % PAIR
    half = width // PAIR

    fast = cols == 4 and lines == LINES
    bias = jnp.concatenate(
        [pick(b, x, 0) for b in (query_bias, key_bias, value_bias)], axis=0
    )
    depth = out_weight.shape[0]
    hidden = down_weight.shape[0]
    down_line = gather_line(down_weight)
    if fast:
        tokens_all, grad_all, qkv_weight, out_all, ffn_part, gains, places_all = gather_first(
            tokens, out_grad, query_weight, key_weight, value_weight, out_weight,
            gate_weight, up_weight,
            jnp.pad(jnp.stack([attn_gain, mlp_gain]), ((0, 6), (0, 0))),
            jnp.pad(jnp.stack([positions, segment_ids]), ((0, 6), (0, 0))), 0,
        )
    else:
        qkv_weight = gather_line(
            jnp.concatenate(
                [own_columns(w, x) for w in (query_weight, key_weight, value_weight)], axis=1
            )
        )
        tokens_all = gather_plane(tokens, "gather_tokens", 0)
        grad_all = gather_plane(out_grad, "gather_cotangent", 1)
        out_line = gather_line(out_weight)
        full = (lines, 1, depth, width)
        out_all = in_order(
            x, out_line.reshape(full), swap_rows(out_line).reshape(full), 1
        ).reshape(-1, width)
        ffn_part = jnp.stack([own_units(w, x) for w in (gate_weight, up_weight)])[None]
        gains = lax.all_gather(jnp.stack([attn_gain, mlp_gain]), "col", axis=1, tiled=True)
        own_place = jnp.stack([positions, segment_ids])
        places_all = in_order(x, own_place, swap_rows(own_place), 1)
    cosine, sine = rotation_tables(places_all[0])
    plane_segments = places_all[1]
    down_blocks = after(down_line, tokens_all).reshape(lines, hidden, width)
    ffn_weight = gather_line(after(ffn_part, down_blocks))

    projections = (tokens_all, gains[0], qkv_weight, bias, cosine, sine)
    if fast:
        normed_first, queries, keys, values, stats_first, down_partly = project_heads(
            *projections, down_blocks, 1
        )
        attended, lse, down_all = attention_forward(
            queries, keys, values, plane_segments, down_blocks, down_partly, 8
        )
    else:
        normed_first, queries, keys, values, stats_first = project_heads(*projections)
        attended, lse = attention_forward(queries, keys, values, plane_segments)
        down_all = lax.all_to_all(down_blocks, "col", split_axis=0, concat_axis=0, tiled=True)
    if fast:
        attn_all, resid, resid_all = project_out(attended, out_all, tokens, 2)
    else:
        attn_all = gather_heads(attended, x)
        resid = tokens.astype(F32) + dot(attn_all, out_all)
        resid_all = gather_plane(resid.astype(BF16), "gather_residual", 3)

    normed_second, hidden_low, grad_gate, grad_up, stats_second = feed_forward(
        resid_all, gains[1], ffn_weight, grad_all, down_all
    )
    if fast:
        grad_ffn = weight_grads((grad_gate, grad_up), normed_second, width, "ffn_grads")
    else:
        grad_ffn = weight_grads((grad_gate, grad_up), normed_second, width, "ffn_grads")
    own_stats = pick(stats_second, x, 0)
    if fast:
        grad_resid, grad_resid_low, mlp_gain_part, down_blocks = back_second(
            after(grad_gate, grad_ffn), grad_up, ffn_weight, hidden_low, grad_all,
            resid, own_stats, mlp_gain, out_grad, 4,
        )
        mlp_gain_part = mlp_gain_part[0]
    else:
        grad_second = scatter_plane(
            back_project((grad_gate, grad_up), ffn_weight, "back_ffn"), "scatter_second", 4
        )
        mean_here, inv_here = own_stats[:, 0:1], own_stats[:, 1:2]
        grad_resid, mlp_gain_part = norm_backward(
            grad_second, (resid - mean_here) * inv_here, inv_here, mlp_gain
        )
        grad_resid = grad_resid + out_grad.astype(F32)
        grad_resid_low = grad_resid.astype(BF16)
    grad_ffn = scatter_line(grad_ffn)

    if fast:
        grad_attn, grad_out_weight, mixed, grad_down = back_heads(
            grad_resid_low, out_all, attn_all, hidden_low, down_all, down_blocks, 5
        )
        grad_qkv, bias_sums, mixed = attention_backward(
            queries, keys, values, grad_attn, lse, cosine, sine, plane_segments, mixed, resid, 9
        )
    else:
        grad_out_weight = dot(attn_all, grad_resid_low, (0,), (0,)).astype(BF16)
        grad_out_weight = grad_out_weight.reshape(lines, PAIR, depth, width)
        grad_out_weight = pick(grad_out_weight, x, 1) + swap_rows(pick(grad_out_weight, 1 - x, 1))
        grad_out_weight = scatter_line(grad_out_weight.reshape(lines * depth, width)).astype(F32)
        grad_attn = scatter_heads(dot(grad_resid_low, out_all, (1,), (1,)).astype(BF16), x)
        grad_qkv, bias_sums = attention_backward(
            queries, keys, values, grad_attn, lse, cosine, sine, plane_segments
        )
        grad_down = weight_grads((hidden_low,), grad_all, width, "down_grads")
        grad_down = lax.all_to_all(
            grad_down.reshape(cols, hidden, width), "col", split_axis=0, concat_axis=0, tiled=True
        )
    grad_qkv_weight = dot(normed_first, grad_qkv, (0,), (0,)).astype(BF16)
    grad_down = scatter_line(after(grad_down, grad_ffn).reshape(lines * hidden, width))
    grad_qkv_later = after(grad_qkv, grad_qkv_weight)
    own_stats = pick(stats_first, x, 0)
    bias_part = jnp.sum(bias_sums, axis=(0, 1)).reshape(3, half)
    bias_part = jnp.where(
        (jnp.arange(PAIR) == x)[None, :, None], bias_part[:, None, :], 0.0
    ).reshape(3, width)
    if fast:
        (
            tokens_grad, vectors, query_grad, key_grad, value_grad, gate_grad, up_grad,
            grad_out_weight,
        ) = back_first(
            grad_qkv_later, qkv_weight,
            tokens, own_stats, attn_gain, grad_resid, grad_qkv_weight, grad_ffn, grad_out_weight,
            jnp.concatenate(
                [bias_part, jnp.zeros((1, width), F32), mlp_gain_part[None], jnp.zeros((3, width), F32)]
            ),
            6,
        )
    else:
        kept, other = pick(grad_ffn[0], x, 2), swap_rows(pick(grad_ffn[0], 1 - x, 2))
        gate_grad, up_grad = (
            in_order(x, kept[i], other[i], 0).T.astype(F32) for i in range(2)
        )
        kept, other = own_rows(scatter_line(grad_qkv_weight), x)
        query_grad, key_grad, value_grad = (
            in_order(x, kept[:, at : at + half], other[:, at : at + half], 1).astype(F32)
            for at in (0, half, 2 * half)
        )
        grad_first = scatter_plane(
            dot(grad_qkv_later, qkv_weight, (1,), (1,)).astype(BF16), "scatter_first", 6
        )
        mean_here, inv_here = own_stats[:, 0:1], own_stats[:, 1:2]
        grad_input, attn_gain_part = norm_backward(
            grad_first, (tokens.astype(F32) - mean_here) * inv_here, inv_here, attn_gain
        )
        tokens_grad = grad_input + grad_resid
        vectors = lax.psum(
            jnp.concatenate([bias_part, attn_gain_part[None], mlp_gain_part[None]]), "row"
        )
        mixed = resid + scatter_plane(
            back_project((hidden_low,), down_all[:, None], "mix"), "scatter_mixed", 10
        )
        mixed = mixed.astype(BF16)

    return (
        mixed,
        tokens_grad,
        vectors[3],
        query_grad,
        vectors[0],
        key_grad,
        vectors[1],
        value_grad,
        vectors[2],
        grad_out_weight,
        vectors[4],
        gate_grad,
        up_grad,
        grad_down.astype(F32),
    )


def solution(mesh):
    grid, rows, cols = P("row", "col"), P("row"), P("col")
    in_specs = (
        grid, rows, rows, cols, grid, cols, grid, cols, grid, cols, grid, cols, grid, grid, grid, grid,
    )
    out_specs = (
        grid, grid, cols, grid, cols, grid, cols, grid, cols, grid, cols, grid, grid, grid,
    )
    return jax.shard_map(
        per_device, mesh=mesh, in_specs=in_specs, out_specs=out_specs, check_vma=False
    )
```

```python
import functools

import jax
import jax.numpy as jnp
from jax import lax
from jax.experimental import pallas as pl
from jax.experimental.pallas import tpu as pltpu
from jax.sharding import PartitionSpec as P

HEAD_DIM = 64
ROT = 16
SEQ = 1024
BASE = 10000.0
NEG = -1e30
F32 = jnp.float32
BF16 = jnp.bfloat16
SCALE = HEAD_DIM**-0.5
MESH = pl.DeviceIdType.MESH
QBLOCK = 256
PAIR = 2


def dot(left, right, left_dims=(1,), right_dims=(0,)):
    return lax.dot_general(
        left, right, ((left_dims, right_dims), ((), ())), preferred_element_type=F32
    )


def taking(microseconds):
    return pl.CostEstimate(
        flops=microseconds * 10**9, bytes_accessed=microseconds * 10**6, transcendentals=0
    )


def swap_pairs(values, lane):
    half = ROT // 2
    width = values.shape[1]
    ahead = pltpu.roll(values, width - half, 1)
    behind = pltpu.roll(values, half, 1)
    return jnp.where(lane < half, ahead, behind)


def attention_forward_kernel(
    q_ref, k_ref, v_ref, seg_col_ref, seg_row_ref, o_ref, lse_ref, acc_ref, lse_scratch
):
    width = q_ref.shape[1]
    heads = width // HEAD_DIM
    full_lane = lax.broadcasted_iota(jnp.int32, (1, width), 1)
    acc_ref[...] = jnp.zeros_like(acc_ref)
    lse_lane = lax.broadcasted_iota(jnp.int32, (1, lse_scratch.shape[1]), 1)

    @pl.loop(0, heads)
    def _(head):
        mask = full_lane // HEAD_DIM == head
        for start in range(0, SEQ, QBLOCK):
            keys = start + QBLOCK
            rows = slice(start, keys)
            queries = jnp.where(mask, q_ref[rows, :], jnp.zeros((), BF16))
            scores = dot(queries, k_ref[:keys, :], (1,), (1,))
            query_pos = start + lax.broadcasted_iota(jnp.int32, scores.shape, 0)
            key_pos = lax.broadcasted_iota(jnp.int32, scores.shape, 1)
            seen = (seg_col_ref[rows, :] == seg_row_ref[0, :, :keys]) & (key_pos <= query_pos)
            scores = jnp.where(seen, scores, NEG)
            peak = jnp.max(scores, axis=1, keepdims=True)
            weights = jnp.exp(scores - peak)
            total = jnp.sum(weights, axis=1, keepdims=True)
            probs = (weights * (1.0 / total)).astype(BF16)
            output = dot(probs, v_ref[:keys, :])
            acc_ref[rows, :] = jnp.where(mask, output, acc_ref[rows, :])
            lse_scratch[rows, :] = jnp.where(
                lse_lane == head, peak + jnp.log(total), lse_scratch[rows, :]
            )

    o_ref[...] = acc_ref[...].astype(BF16)
    lse_ref[0] = lse_scratch[...].T[: lse_ref.shape[1], :]


def attention_forward_exchange_kernel(*refs):
    ins, (blocks_ref, _), outs, all_ref = refs[:5], refs[5:7], refs[7:9], refs[9]
    scratch, sems = refs[10:12], refs[12:]
    exchange_beside(
        lambda: attention_forward_kernel(*ins, *outs, *scratch),
        blocks_ref, all_ref, (1, 3), None, *sems,
    )


def attention_forward(queries, keys, values, segments, blocks=None, partly=None, collective_id=None):
    rows, width = queries.shape
    seqs = rows // SEQ
    block = lambda columns: pl.BlockSpec((SEQ, columns), lambda s: (s, 0))
    in_specs = [block(width)] * 3 + [block(1), pl.BlockSpec((1, 1, SEQ), lambda s: (s, 0, 0))]
    out_specs = [block(width), pl.BlockSpec((1, 8, SEQ), lambda s: (s, 0, 0))]
    out_shape = [
        jax.ShapeDtypeStruct((rows, width), BF16), jax.ShapeDtypeStruct((seqs, 8, SEQ), F32)
    ]
    operands = [queries, keys, values, segments.reshape(rows, 1), segments.reshape(seqs, 1, SEQ)]
    scratch = [pltpu.VMEM((SEQ, width), F32), pltpu.VMEM((SEQ, 128), F32)]
    params, aliases, kernel = {}, {}, attention_forward_kernel
    if blocks is not None:
        anywhere = pl.BlockSpec(memory_space=pl.ANY)
        in_specs, out_specs = in_specs + [anywhere] * 2, out_specs + [anywhere]
        out_shape = out_shape + [jax.ShapeDtypeStruct(blocks.shape, BF16)]
        operands = operands + [blocks, partly]
        scratch = scratch + [pltpu.SemaphoreType.DMA((2,))] * 2
        params = dict(collective_id=collective_id, has_side_effects=True)
        aliases, kernel = {6: 2}, attention_forward_exchange_kernel
    return pl.pallas_call(
        kernel,
        grid=(seqs,),
        in_specs=in_specs,
        out_specs=out_specs,
        out_shape=out_shape,
        scratch_shapes=scratch,
        input_output_aliases=aliases,
        compiler_params=pltpu.CompilerParams(vmem_limit_bytes=56 << 20, **params),
        cost_estimate=taking(21),
        name="attention_forward",
    )(*operands)


def attention_backward_kernel(
    q_ref, k_ref, v_ref, do_ref, lse_ref, cos_ref, sin_ref, seg_col_ref, seg_row_ref,
    grad_ref, sums_ref, dq_ref, dk_ref, dv_ref, halfway=None,
):
    width = q_ref.shape[1]
    heads = width // HEAD_DIM
    full_lane = lax.broadcasted_iota(jnp.int32, (1, width), 1)
    in_head = full_lane % HEAD_DIM
    for ref in (dq_ref, dk_ref, dv_ref):
        ref[...] = jnp.zeros_like(ref)

    def one_head(head):
        mask = full_lane // HEAD_DIM == head
        nothing = jnp.zeros((), BF16)
        for start in range(0, SEQ, 2 * QBLOCK):
            keys = start + 2 * QBLOCK
            rows = slice(start, keys)
            queries = jnp.where(mask, q_ref[rows, :], nothing)
            grads = jnp.where(mask, do_ref[rows, :], nothing)
            scores = dot(k_ref[:keys, :], queries, (1,), (1,))
            key_pos = lax.broadcasted_iota(jnp.int32, scores.shape, 0)
            query_pos = start + lax.broadcasted_iota(jnp.int32, scores.shape, 1)
            seen = (seg_col_ref[:keys, :] == seg_row_ref[0, :, rows]) & (key_pos <= query_pos)
            probs = jnp.where(
                seen, jnp.exp(scores - lse_ref[0, pl.ds(head, 1), rows]), 0.0
            )
            dv_ref[:keys, :] += dot(probs.astype(BF16), grads)
            grad_probs = dot(v_ref[:keys, :], grads, (1,), (1,))
            delta = jnp.sum(probs * grad_probs, axis=0, keepdims=True)
            grad_scores = (probs * (grad_probs - delta)).astype(BF16)
            dk_ref[:keys, :] += dot(grad_scores, queries)
            masked_keys = jnp.where(mask, k_ref[:keys, :], nothing)
            dq_ref[rows, :] += dot(grad_scores, masked_keys, (0,), (0,))

    pl.loop(0, heads // 2)(one_head)
    if halfway is not None:
        halfway()
    pl.loop(heads // 2, heads)(one_head)

    cosine = jnp.tile(cos_ref[...], (1, width // cos_ref.shape[1]))
    sine = jnp.tile(sin_ref[...], (1, width // sin_ref.shape[1]))
    for part, (ref, scale) in enumerate(((dq_ref, SCALE), (dk_ref, 1.0), (dv_ref, None))):
        grad = ref[...]
        if scale is not None:
            grad = grad * scale
            grad = grad * cosine - swap_pairs(grad, in_head) * sine
        low = grad.astype(BF16)
        columns = slice(part * width, (part + 1) * width)
        grad_ref[:, columns] = low
        sums_ref[0, :, columns] = jnp.sum(low.astype(F32), axis=0, keepdims=True)


def attention_backward_sums_kernel(*refs):
    ins, parts_ref, resid_ref = refs[:9], refs[9], refs[10]
    outs, mixed_ref, scratch = refs[11:13], refs[13], refs[14:17]
    load_sem, send_sem, recv_sem, *blocks = refs[17:]
    devices = peers(lax.axis_index("row"), lax.axis_index("col"))
    copies = Copies(send_sem, recv_sem, devices[2])
    mixing = PartsScatter(copies, 0, parts_ref, load_sem, *blocks)
    step = pl.program_id(0)

    @pl.when(step == 0)
    def _():
        meet(devices)
        mixing.start()
        mixing.keep(0, 0)
        mixing.keep(0, 1)

    def halfway():
        @pl.when(step == 0)
        def _():
            for i, h in ((1, 0), (2, 0), (2, 1), (1, 1), (3, 0), (3, 1)):
                mixing.keep(i, h)

        @pl.when(step == 1)
        def _():
            mixing.second()

    attention_backward_kernel(*ins, *outs, *scratch, halfway=halfway)

    @pl.when(step == 1)
    def _():
        mixing.third()
        for start in range(0, mixed_ref.shape[0], STEP):
            at = pl.ds(start, STEP)
            mixed_ref[at, :] = (resid_ref[at, :] + mixing.result(start, STEP)).astype(BF16)
        mixing.drain()


def attention_backward(
    queries, keys, values, grad_out, lse, cosine, sine, segments,
    parts=None, resid=None, collective_id=None,
):
    rows, width = queries.shape
    seqs = rows // SEQ
    block = lambda columns: pl.BlockSpec((SEQ, columns), lambda s: (s, 0))
    in_specs = [block(width)] * 4 + [
        pl.BlockSpec((1, 8, SEQ), lambda s: (s, 0, 0)),
        block(cosine.shape[1]),
        block(cosine.shape[1]),
        block(1),
        pl.BlockSpec((1, 1, SEQ), lambda s: (s, 0, 0)),
    ]
    out_specs = [block(3 * width), pl.BlockSpec((1, 1, 3 * width), lambda s: (s, 0, 0))]
    out_shape = [
        jax.ShapeDtypeStruct((rows, 3 * width), BF16),
        jax.ShapeDtypeStruct((seqs, 1, 3 * width), F32),
    ]
    operands = [
        queries, keys, values, grad_out, lse, cosine, sine,
        segments.reshape(rows, 1), segments.reshape(seqs, 1, SEQ),
    ]
    scratch = [pltpu.VMEM((SEQ, width), F32)] * 3
    params, kernel = {}, attention_backward_kernel
    if parts is not None:
        in_specs = in_specs + [pl.BlockSpec(memory_space=pl.ANY), whole(resid.shape)]
        out_specs = out_specs + [whole(resid.shape)]
        out_shape = out_shape + [jax.ShapeDtypeStruct(resid.shape, BF16)]
        operands = operands + [parts, resid]
        sems = lambda n: pltpu.SemaphoreType.DMA((n,))
        scratch = scratch + [sems(4), sems(PlaneScatter.SEMS), sems(PlaneScatter.SEMS)]
        scratch = scratch + scatter_scratch(*resid.shape)[1:]
        params = dict(collective_id=collective_id, has_side_effects=True)
        kernel = attention_backward_sums_kernel
    return pl.pallas_call(
        kernel,
        grid=(seqs,),
        in_specs=in_specs,
        out_specs=out_specs,
        out_shape=out_shape,
        scratch_shapes=scratch,
        compiler_params=pltpu.CompilerParams(vmem_limit_bytes=60 << 20, **params),
        cost_estimate=taking(42),
        name="attention_backward",
    )(*operands)


def row_pairs():
    return [(r, r ^ 1) for r in range(lax.axis_size("row"))]


def row_lines():
    size = lax.axis_size("row")
    return [list(range(start, size, PAIR)) for start in range(PAIR)]


def neighbours():
    return [list(range(r, r + PAIR)) for r in range(0, lax.axis_size("row"), PAIR)]


def swap_rows(values):
    return lax.ppermute(values, "row", row_pairs())


def after(value, *others):
    return lax.optimization_barrier((value,) + others)[0]


def gather_line(values, axis=0):
    return lax.all_gather(values, "row", axis=axis, tiled=True, axis_index_groups=row_lines())


def scatter_line(values, axis=0):
    return lax.psum_scatter(
        values, "row", scatter_dimension=axis, tiled=True, axis_index_groups=row_lines()
    )


def pick(values, index, axis):
    size = values.shape[axis] // PAIR
    return lax.dynamic_slice_in_dim(values, index * size, size, axis)


def in_order(x, own, other, axis):
    return jnp.where(
        x == 0, jnp.concatenate([own, other], axis), jnp.concatenate([other, own], axis)
    )


def own_columns(weight, x):
    return in_order(x, pick(weight, x, 1), swap_rows(pick(weight, 1 - x, 1)), 0)


def own_units(weight, x):
    kept, sent = pick(weight, x, 1).T, pick(weight, 1 - x, 1).T
    return in_order(x, kept, swap_rows(sent), 1)


def own_rows(grad, x):
    return pick(grad, x, 0), swap_rows(pick(grad, 1 - x, 0))


def places():
    row, col = lax.axis_index("row"), lax.axis_index("col")
    return row % PAIR, col // 2, col % 2, row, col


def peers(row, col):
    x = row % PAIR
    over_x = (row + 1 - 2 * x, col)
    over_y = (row, (col + 2) % 4)
    over_core = (row, col + 1 - 2 * (col % 2))
    return over_x, over_y, over_core


def meet(devices):
    barrier = pltpu.get_barrier_semaphore()
    for device in devices:
        pl.semaphore_signal(barrier, inc=1, device_id=device, device_id_type=MESH)
    pl.semaphore_wait(barrier, len(devices))


def block_at(ref, a, col, rows, width, start, count):
    at = pl.multiple_of(a * rows + start, 128)
    return ref.at[pl.ds(at, count), pl.ds(pl.multiple_of(col * width, 128), width)]


CHUNKS = 4


class Copies:
    def __init__(self, send_sem, recv_sem, over_core):
        self.send_sem, self.recv_sem, self.any = send_sem, recv_sem, over_core
        self.sent = []

    def copy(self, index, source, place, device):
        return pltpu.make_async_remote_copy(
            source, place, self.send_sem.at[index], self.recv_sem.at[index],
            device_id=device, device_id_type=MESH,
        )

    def send(self, index, source, place, device):
        task = self.copy(index, source, place, device)
        task.start()
        self.sent.append(task)

    def wait(self, index, place):
        self.copy(index, place, place, self.any).wait_recv()

    def finish(self):
        for task in self.sent:
            task.wait_send()
        self.sent = []


class PlaneGather:
    def __init__(self, copies, base, src_ref, out_ref, local_sem, over_y=CHUNKS // 2):
        self.copies, self.base, self.src, self.out = copies, base, src_ref, out_ref
        self.local_sem = local_sem
        self.rows, self.width = src_ref.shape
        self.count = self.rows // CHUNKS
        self.x, self.y, self.core, self.row, self.col = places()
        self.over_x, self.over_y, self.over_core = peers(self.row, self.col)
        self.col_y = (self.col + 2) % 4
        self.col_core = self.col + 1 - 2 * self.core
        self.first = list(range(over_y))
        self.second = list(range(over_y, CHUNKS))

    def piece(self, a, c, s):
        return block_at(self.out, a, c, self.rows, self.width, s * self.count, self.count)

    def own(self, s):
        return self.src.at[pl.ds(s * self.count, self.count), :]

    def send(self, group, s, source, place, device):
        self.copies.send(self.base + group * CHUNKS + s, source, place, device)

    def pass_on(self, group, a, c, s, device):
        self.send(group, s, self.piece(a, c, s), self.piece(a, c, s), device)

    def wait(self, group, a, c, s):
        self.copies.wait(self.base + group * CHUNKS + s, self.piece(a, c, s))

    def start_x(self):
        for s in self.first + self.second:
            self.send(0, s, self.own(s), self.piece(self.x, self.col, s), self.over_x)

    def start_y(self):
        for s in self.second + self.first:
            self.send(1, s, self.own(s), self.piece(self.x, self.col, s), self.over_y)

    def start_chunk(self, s):
        self.send(0, s, self.own(s), self.piece(self.x, self.col, s), self.over_x)
        self.send(1, s, self.own(s), self.piece(self.x, self.col, s), self.over_y)
        self.send(4, s, self.own(s), self.piece(self.x, self.col, s), self.over_core)

    def near_in_order(self, s):
        x, col, col_y = self.x, self.col, self.col_y
        self.wait(0, 1 - x, col, s)
        if s in self.first:
            self.pass_on(2, 1 - x, col, s, self.over_y)
        self.pass_on(5, 1 - x, col, s, self.over_core)
        self.wait(1, x, col_y, s)
        if s in self.second:
            self.pass_on(2, x, col_y, s, self.over_x)
        self.pass_on(6, x, col_y, s, self.over_core)

    def keep_own(self):
        self.local = pltpu.make_async_copy(
            self.src, block_at(self.out, self.x, self.col, self.rows, self.width, 0, self.rows),
            self.local_sem,
        )
        self.local.start()

    def start_core(self):
        self.keep_own()
        for s in range(CHUNKS):
            self.send(4, s, self.own(s), self.piece(self.x, self.col, s), self.over_core)

    def near(self, i):
        s, t = (self.first + self.second)[i], (self.second + self.first)[i]
        x, col, col_y = self.x, self.col, self.col_y
        self.wait(0, 1 - x, col, s)
        if s in self.first:
            self.pass_on(2, 1 - x, col, s, self.over_y)
        self.pass_on(5, 1 - x, col, s, self.over_core)
        self.wait(1, x, col_y, t)
        if t in self.second:
            self.pass_on(2, x, col_y, t, self.over_x)
        self.pass_on(6, x, col_y, t, self.over_core)

    def far(self):
        for u in range(CHUNKS):
            self.wait(2, 1 - self.x, self.col_y, u)
            self.pass_on(7, 1 - self.x, self.col_y, u, self.over_core)

    def finish(self):
        other, corner = self.col_core, (self.col_core + 2) % 4
        for group, (a, c) in enumerate(
            ((self.x, other), (1 - self.x, other), (self.x, corner), (1 - self.x, corner))
        ):
            for s in range(CHUNKS):
                self.wait(4 + group, a, c, s)
        self.local.wait()


def gather_plane_kernel(src_ref, out_ref, local_sem, send_sem, recv_sem):
    _, _, _, row, col = places()
    devices = peers(row, col)
    meet(devices)
    copies = Copies(send_sem, recv_sem, devices[2])
    gather = PlaneGather(copies, 0, src_ref, out_ref, local_sem)
    gather.start_x()
    gather.start_y()
    gather.start_core()
    for i in range(CHUNKS):
        gather.near(i)
    gather.far()
    gather.finish()
    copies.finish()


LINES = 4


class LineGather:
    def __init__(self, up_send, up_recv, down_send, down_recv, block):
        self.up, self.down, self.block = (up_send, up_recv), (down_send, down_recv), block
        self.row, self.col = lax.axis_index("row"), lax.axis_index("col")
        self.z = self.row // PAIR

    def task(self, sems, step, source, device):
        send, recv = sems
        place = self.block(source)
        return pltpu.make_async_remote_copy(
            place, place, send.at[step], recv.at[step],
            device_id=(device, self.col), device_id_type=MESH,
        )

    def upward(self, step):
        source = jnp.maximum(self.z - step, 0)
        return self.task(self.up, step, source, jnp.minimum(self.row + PAIR, PAIR * LINES - 1))

    def downward(self, step):
        source = jnp.minimum(self.z + step, LINES - 1)
        return self.task(self.down, step, source, jnp.maximum(self.row - PAIR, 0))

    def start(self, step):
        @pl.when((self.z >= step) & (self.z < LINES - 1))
        def _():
            self.upward(step).start()

        @pl.when((self.z + step < LINES) & (self.z > 0))
        def _():
            self.downward(step).start()

    def receive(self, step):
        @pl.when(self.z >= step)
        def _():
            source = jnp.maximum(self.z - step, 0)
            self.task(self.up, step - 1, source, self.row).wait_recv()

        @pl.when(self.z + step < LINES)
        def _():
            source = jnp.minimum(self.z + step, LINES - 1)
            self.task(self.down, step - 1, source, self.row).wait_recv()

    def hop(self, step):
        self.receive(step)
        if step < LINES - 1:
            self.start(step)

    def finish(self):
        for step in range(LINES - 1):

            @pl.when((self.z >= step) & (self.z < LINES - 1))
            def _():
                self.upward(step).wait_send()

            @pl.when((self.z + step < LINES) & (self.z > 0))
            def _():
                self.downward(step).wait_send()


def gather_first_kernel(
    tokens_ref, grad_ref, query_ref, key_ref, value_ref, out_weight_ref, gate_ref, up_ref,
    gains_ref, places_ref,
    tokens_all_ref, grad_all_ref, qkv_ref, out_all_ref, ffn_ref, gains_all_ref, places_all_ref,
    turned_ref, local_sem, send_sem, recv_sem, swap_send, swap_recv, *line_sems,
):
    x, y, core, row, col = places()
    z = row // PAIR
    over_x, over_y, over_core = peers(row, col)
    over_far = (row, 3 - col)
    size = PAIR * LINES
    meet(
        (
            over_x, over_y, over_core, over_far,
            ((row + PAIR) % size, col), ((row + size - PAIR) % size, col),
        )
    )
    copies = Copies(send_sem, recv_sem, over_core)
    depth, width = out_weight_ref.shape
    half = width // PAIR
    units = ffn_ref.shape[2]
    base = 16 * CHUNKS
    local = []

    def keep(source, place):
        task = pltpu.make_async_copy(source, place, local_sem.at[2 + len(local)])
        task.start()
        local.append(task)

    def part(r, w):
        return qkv_ref.at[
            pl.ds(pl.multiple_of(r * depth, 128), depth), pl.ds(w * half, half)
        ]

    def out_block(z, x):
        return out_all_ref.at[pl.ds(pl.multiple_of((PAIR * z + x) * depth, 128), depth), :]

    def ffn_block(w, x):
        return ffn_ref.at[0, w, :, pl.ds(pl.multiple_of(x * depth, 128), depth)]

    def gains_block(c):
        return gains_all_ref.at[:, pl.ds(pl.multiple_of(c * width, 128), width)]

    def places_block(a):
        rows = places_ref.shape[1]
        return places_all_ref.at[:, pl.ds(pl.multiple_of(a * rows, 128), rows)]

    for w, ref in enumerate((query_ref, key_ref, value_ref)):
        theirs = ref.at[:, pl.ds(pl.multiple_of((1 - x) * half, 128), half)]
        copies.send(base + w, theirs, part(row, w), over_x)
        keep(ref.at[:, pl.ds(pl.multiple_of(x * half, 128), half)], part(row, w))
    keep(out_weight_ref, out_block(z, x))
    keep(gains_ref, gains_block(col))
    keep(places_ref, places_block(x))
    tokens = PlaneGather(copies, 0, tokens_ref, tokens_all_ref, local_sem.at[0], CHUNKS)
    grad = PlaneGather(copies, 8 * CHUNKS, grad_ref, grad_all_ref, local_sem.at[1], CHUNKS)
    tokens.start_y()
    tokens.start_core()
    copies.send(base + 5, places_ref, places_block(x), over_x)
    for i, device in enumerate((over_core, over_y, over_far)):
        copies.send(base + 6 + i, gains_ref, gains_block(col), device)
    for w in range(3):
        local[w].wait()
        copies.wait(base + w, part(row + 1 - 2 * x, w))
    heads = LineGather(
        *line_sems[:4],
        lambda at: qkv_ref.at[pl.ds(pl.multiple_of(at * PAIR * depth, 128), PAIR * depth), :],
    )
    outs = LineGather(*line_sems[4:], lambda at: out_block(at, x))

    def swap_out(z, x):
        block = out_block(z, x)
        return pltpu.make_async_remote_copy(
            block, block, swap_send.at[z], swap_recv.at[z], device_id=over_x, device_id_type=MESH
        )

    def swap_outs(step):
        @pl.when(z >= step)
        def _():
            swap_out(jnp.maximum(z - step, 0), x).start()

        @pl.when(z + step < LINES)
        def _():
            swap_out(jnp.minimum(z + step, LINES - 1), x).start()

    heads.start(0)
    tokens.start_x()
    for w, ref in enumerate((gate_ref, up_ref)):
        for j in range(PAIR * units // 128):
            turned_ref[w, j * 128 : (j + 1) * 128, :] = ref[:, j * 128 : (j + 1) * 128].T
    for i in range(CHUNKS - 1):
        tokens.near(i)
    local[3].wait()
    outs.start(0)
    heads.hop(1)
    tokens.near(CHUNKS - 1)
    for w in range(2):
        theirs = turned_ref.at[w, pl.ds(pl.multiple_of((1 - x) * units, 16), units), :]
        copies.send(base + 3 + w, theirs, ffn_block(w, x), over_x)
        keep(turned_ref.at[w, pl.ds(pl.multiple_of(x * units, 16), units), :], ffn_block(w, x))
    swap_out(z, x).start()
    grad.start_x()
    grad.start_y()
    grad.start_core()
    tokens.far()
    heads.hop(2)
    outs.hop(1)
    swap_outs(1)
    for i in range(CHUNKS - 1):
        grad.near(i)
    heads.hop(3)
    outs.hop(2)
    swap_outs(2)
    grad.near(CHUNKS - 1)
    grad.far()
    outs.hop(3)
    swap_outs(3)
    for at in range(LINES):
        swap_out(at, 1 - x).wait_recv()
    for w in range(2):
        copies.wait(base + 3 + w, ffn_block(w, 1 - x))
    copies.wait(base + 5, places_block(1 - x))
    for i, c in enumerate((col + 1 - 2 * core, (col + 2) % 4, 3 - col)):
        copies.wait(base + 6 + i, gains_block(c))
    for at in range(LINES):
        swap_out(at, x).wait_send()
    for task in local[3 + 1 :]:
        task.wait()
    tokens.finish()
    grad.finish()
    heads.finish()
    outs.finish()
    copies.finish()


def gather_first(
    tokens, grad, query, key, value, out_weight, gate, up, gains, places, collective_id
):
    rows, width = tokens.shape
    depth = out_weight.shape[0]
    units = gate.shape[1] // PAIR
    shape = lambda *dims: jax.ShapeDtypeStruct(dims, BF16)
    sems = lambda n: pltpu.SemaphoreType.DMA((n,))
    return pl.pallas_call(
        gather_first_kernel,
        in_specs=[pl.BlockSpec(memory_space=pltpu.VMEM)] * 10,
        out_specs=[pl.BlockSpec(memory_space=pl.ANY)] * 7,
        out_shape=[
            shape(PAIR * rows, 4 * width), shape(PAIR * rows, 4 * width),
            shape(PAIR * LINES * depth, 3 * width // PAIR), shape(PAIR * LINES * depth, width),
            shape(1, 2, units, PAIR * depth),
            jax.ShapeDtypeStruct((gains.shape[0], 4 * width), F32),
            jax.ShapeDtypeStruct((places.shape[0], PAIR * rows), jnp.int32),
        ],
        scratch_shapes=[
            pltpu.VMEM((2, PAIR * units, depth), BF16),
            sems(10), sems(16 * CHUNKS + 9), sems(16 * CHUNKS + 9), sems(4), sems(4),
        ]
        + [sems(3)] * 8,
        compiler_params=pltpu.CompilerParams(
            collective_id=collective_id, has_side_effects=True, vmem_limit_bytes=60 << 20
        ),
        cost_estimate=taking(110),
        name="gather_first",
    )(tokens, grad, query, key, value, out_weight, gate, up, gains, places)


def gather_plane(values, name, collective_id):
    cols = lax.axis_size("col")
    if cols != 4:
        across = lax.all_gather(values, "col", axis=1, tiled=True)
        return lax.all_gather(across, "row", axis=0, tiled=True, axis_index_groups=neighbours())
    rows, width = values.shape
    return pl.pallas_call(
        gather_plane_kernel,
        in_specs=[pl.BlockSpec(memory_space=pltpu.VMEM)],
        out_specs=pl.BlockSpec(memory_space=pl.ANY),
        out_shape=jax.ShapeDtypeStruct((PAIR * rows, cols * width), values.dtype),
        scratch_shapes=[
            pltpu.SemaphoreType.DMA,
            pltpu.SemaphoreType.DMA((8 * CHUNKS,)),
            pltpu.SemaphoreType.DMA((8 * CHUNKS,)),
        ],
        cost_estimate=taking(40),
        compiler_params=pltpu.CompilerParams(collective_id=collective_id, has_side_effects=True),
        name=name,
    )(values)


def add_rows(out_ref, left_ref, right_ref, rows, step=64):
    @pl.loop(0, rows // step)
    def _(i):
        at = pl.ds(pl.multiple_of(i * step, step), step)
        total = left_ref[at, :].astype(F32) + right_ref[at, :].astype(F32)
        out_ref[at, :] = total.astype(out_ref.dtype)


def scatter_plane_kernel(
    part_ref, out_ref, own_ref, core_ref, x_ref, y_ref, last_ref,
    load_sem, send_sem, recv_sem,
):
    rows, width = own_ref.shape[1:]
    half = rows // 2
    x, y, core, row, col = places()
    over_x, over_y, over_core = peers(row, col)
    meet((over_x, over_y, over_core))
    top, bottom = pl.ds(0, half), pl.ds(half, half)

    def copy(index, source, place, device):
        return pltpu.make_async_remote_copy(
            source, place, send_sem.at[index], recv_sem.at[index],
            device_id=device, device_id_type=MESH,
        )

    sent = []

    def send(index, source, place, device):
        task = copy(index, source, place, device)
        task.start()
        sent.append(task)

    def wait(index, place):
        copy(index, place, place, over_core).wait_recv()

    order = ((1 - x, 1 - y), (1 - x, y), (x, 1 - y), (x, y))
    loads = []
    for i, (a, b) in enumerate(order):
        slot = 2 * a + b
        send(
            i, block_at(part_ref, a, 2 * b + 1 - core, rows, width, 0, rows),
            core_ref.at[slot], over_core,
        )
        load = pltpu.make_async_copy(
            block_at(part_ref, a, 2 * b + core, rows, width, 0, rows),
            own_ref.at[slot], load_sem.at[i],
        )
        load.start()
        loads.append(load)
    for i, (a, b) in enumerate(order):
        slot = 2 * a + b
        loads[i].wait()
        wait(i, core_ref.at[slot])
        add_rows(own_ref.at[slot], own_ref.at[slot], core_ref.at[slot], rows)
        if i in (0, 1):
            send(4 + i, own_ref.at[slot, top, :], x_ref.at[i], over_x)
        if i in (0, 2):
            send(6 + i // 2, own_ref.at[slot, bottom, :], y_ref.at[i // 2], over_y)
    wait(4, x_ref.at[0])
    slot = 2 * x + 1 - y
    add_rows(own_ref.at[slot, top, :], own_ref.at[slot, top, :], x_ref.at[0], half)
    send(8, own_ref.at[slot, top, :], last_ref.at[0], over_y)
    wait(6, y_ref.at[0])
    slot = 2 * (1 - x) + y
    add_rows(own_ref.at[slot, bottom, :], own_ref.at[slot, bottom, :], y_ref.at[0], half)
    send(9, own_ref.at[slot, bottom, :], last_ref.at[1], over_x)
    slot = 2 * x + y
    wait(5, x_ref.at[1])
    add_rows(own_ref.at[slot, top, :], own_ref.at[slot, top, :], x_ref.at[1], half)
    wait(7, y_ref.at[1])
    add_rows(own_ref.at[slot, bottom, :], own_ref.at[slot, bottom, :], y_ref.at[1], half)
    wait(8, last_ref.at[0])
    add_rows(out_ref.at[top, :], own_ref.at[slot, top, :], last_ref.at[0], half)
    wait(9, last_ref.at[1])
    add_rows(out_ref.at[bottom, :], own_ref.at[slot, bottom, :], last_ref.at[1], half)
    for task in sent:
        task.wait_send()


def scatter_plane(values, name, collective_id):
    cols = lax.axis_size("col")
    if cols != 4:
        mine = lax.psum_scatter(
            values, "row", scatter_dimension=0, tiled=True, axis_index_groups=neighbours()
        )
        return lax.psum_scatter(mine, "col", scatter_dimension=1, tiled=True).astype(F32)
    rows, width = values.shape[0] // PAIR, values.shape[1] // cols
    return pl.pallas_call(
        scatter_plane_kernel,
        in_specs=[pl.BlockSpec(memory_space=pl.ANY)],
        out_specs=pl.BlockSpec(memory_space=pltpu.VMEM),
        out_shape=jax.ShapeDtypeStruct((rows, width), F32),
        scratch_shapes=[
            pltpu.VMEM((4, rows, width), BF16),
            pltpu.VMEM((4, rows, width), BF16),
            pltpu.VMEM((2, rows // 2, width), BF16),
            pltpu.VMEM((2, rows // 2, width), BF16),
            pltpu.VMEM((2, rows // 2, width), BF16),
            pltpu.SemaphoreType.DMA((4,)),
            pltpu.SemaphoreType.DMA((10,)),
            pltpu.SemaphoreType.DMA((10,)),
        ],
        cost_estimate=taking(40),
        compiler_params=pltpu.CompilerParams(
            collective_id=collective_id, has_side_effects=True, vmem_limit_bytes=40 << 20
        ),
        name=name,
    )(values)


def gather_heads(values, x):
    here = in_order(x, pick(values, x, 0), swap_rows(pick(values, 1 - x, 0)), 1)
    return lax.all_gather(here, "col", axis=1, tiled=True)


def scatter_heads(values, x):
    mine = lax.psum_scatter(values, "col", scatter_dimension=1, tiled=True)
    return in_order(x, pick(mine, x, 1), swap_rows(pick(mine, 1 - x, 1)), 0)


def project_out_kernel(
    heads_ref, weight_ref, tokens_ref, all_ref, resid_ref, resid_all_ref,
    joined_ref, low_ref, local_sem, send_sem, recv_sem,
):
    rows, width = resid_ref.shape
    part = heads_ref.shape[1]
    x, y, core, row, col = places()
    over_x, over_y, over_core = peers(row, col)
    count = rows // CHUNKS
    col_y, col_core = (col + 2) % 4, col + 1 - 2 * core
    corner = (col_core + 2) % 4
    meet((over_x, over_y, over_core))
    copies = Copies(send_sem, recv_sem, over_core)
    base = 8 * CHUNKS

    def piece(c, a, s):
        at = pl.multiple_of((PAIR * c + a) * part, 128)
        return joined_ref.at[pl.ds(s * count, count), pl.ds(at, part)]

    def mine(a, s):
        return heads_ref.at[pl.ds(pl.multiple_of(a * rows + s * count, 128), count), :]

    def send(group, s, source, place, device):
        copies.send(base + group * CHUNKS + s, source, place, device)

    def pass_on(group, s, place, device):
        send(group, s, place, place, device)

    def wait(group, s, place):
        copies.wait(base + group * CHUNKS + s, place)

    local = []
    for s in range(CHUNKS):
        send(0, s, mine(1 - x, s), piece(col, x, s), over_x)
        send(1, s, mine(x, s), piece(col, x, s), over_y)
        send(2, s, mine(x, s), piece(col, x, s), over_core)
        task = pltpu.make_async_copy(mine(x, s), piece(col, x, s), local_sem.at[s])
        task.start()
        local.append(task)
    gather = PlaneGather(copies, 0, low_ref, resid_all_ref, local_sem.at[CHUNKS])

    def relay(s):
        wait(0, s, piece(col, 1 - x, s))
        pass_on(3, s, piece(col, 1 - x, s), over_y)
        pass_on(4, s, piece(col, 1 - x, s), over_core)

    relay(0)
    for s in range(CHUNKS):
        if s + 1 < CHUNKS:
            relay(s + 1)
        wait(1, s, piece(col_y, x, s))
        pass_on(5, s, piece(col_y, x, s), over_core)
        wait(3, s, piece(col_y, 1 - x, s))
        pass_on(6, s, piece(col_y, 1 - x, s), over_core)
        wait(2, s, piece(col_core, x, s))
        wait(4, s, piece(col_core, 1 - x, s))
        wait(5, s, piece(corner, x, s))
        wait(6, s, piece(corner, 1 - x, s))
        local[s].wait()
        at = pl.ds(s * count, count)
        result = tokens_ref[at, :].astype(F32) + dot(joined_ref[at, :], weight_ref[...])
        resid_ref[at, :] = result
        low_ref[at, :] = result.astype(BF16)
        gather.start_chunk(s)
    store = pltpu.make_async_copy(joined_ref, all_ref, local_sem.at[CHUNKS + 1])
    store.start()
    gather.keep_own()
    for s in range(CHUNKS):
        gather.near_in_order(s)
    gather.far()
    gather.finish()
    copies.finish()
    store.wait()


def project_out(heads, weight, tokens, collective_id):
    rows, width = tokens.shape
    vmem, anywhere = pl.BlockSpec(memory_space=pltpu.VMEM), pl.BlockSpec(memory_space=pl.ANY)
    sems = lambda n: pltpu.SemaphoreType.DMA((n,))
    return pl.pallas_call(
        project_out_kernel,
        in_specs=[vmem] * 3,
        out_specs=[anywhere, vmem, anywhere],
        out_shape=[
            jax.ShapeDtypeStruct((rows, 4 * width), BF16),
            jax.ShapeDtypeStruct((rows, width), F32),
            jax.ShapeDtypeStruct((PAIR * rows, 4 * width), BF16),
        ],
        scratch_shapes=[
            pltpu.VMEM((rows, 4 * width), BF16), pltpu.VMEM((rows, width), BF16),
            sems(CHUNKS + 2), sems(15 * CHUNKS), sems(15 * CHUNKS),
        ],
        compiler_params=pltpu.CompilerParams(
            collective_id=collective_id, has_side_effects=True, vmem_limit_bytes=60 << 20
        ),
        cost_estimate=taking(66),
        name="project_out",
    )(heads, weight, tokens)


class RowSum:
    def __init__(self, copies, base, slots_ref):
        self.copies, self.base, self.slots = copies, base, slots_ref
        self.row, self.col = lax.axis_index("row"), lax.axis_index("col")
        self.size = slots_ref.shape[0]
        self.others = [((self.row + step) % self.size, self.col) for step in range(1, self.size)]

    def start(self):
        for step, device in enumerate(self.others, 1):
            self.copies.send(self.base + step - 1, self.slots.at[0], self.slots.at[step], device)

    def finish(self):
        for step in range(1, self.size):
            self.copies.wait(self.base + step - 1, self.slots.at[step])
        total = jnp.zeros(self.slots.shape[1:], F32)
        for r in range(self.size):
            total += self.slots[(self.row + self.size - r) % self.size]
        return total


def row_stats(values):
    mean = jnp.mean(values, axis=1, keepdims=True)
    var = jnp.mean(values * values, axis=1, keepdims=True) - mean * mean
    return mean, lax.rsqrt(var + 1e-05)


def norm_backward(grad_norm, unit_values, inv_std, norm_gain):
    full_width = grad_norm.shape[1] * lax.axis_size("col")
    grad_unit = grad_norm * norm_gain
    row_sums = lax.psum(
        (jnp.sum(grad_unit, axis=1), jnp.sum(grad_unit * unit_values, axis=1)), "col"
    )
    grad_in = inv_std * (
        grad_unit
        - row_sums[0][:, None] / full_width
        - unit_values * row_sums[1][:, None] / full_width
    )
    return grad_in, jnp.sum(grad_norm * unit_values, axis=0)


def rotation_tables(positions):
    half = ROT // 2
    inv_freq = BASE ** (-(jnp.arange(half, dtype=F32) * 2.0) / ROT)
    angles = positions.astype(F32)[:, None] * inv_freq[None, :]
    cosine, sine = jnp.cos(angles), jnp.sin(angles)
    rest = HEAD_DIM - ROT
    ones = jnp.ones((positions.shape[0], rest), F32)
    cosine = jnp.concatenate([cosine, cosine, ones], axis=1)
    sine = jnp.concatenate([-sine, sine, 0.0 * ones], axis=1)
    return jnp.tile(cosine, (1, 2)), jnp.tile(sine, (1, 2))


TILE = 256


def norm_tile(values_ref, gain_ref, row, stats_ref):
    values = values_ref[...].astype(F32)
    mean, inv_std = row_stats(values)
    gain = gain_ref[row : row + 1, :]
    lane = lax.broadcasted_iota(jnp.int32, stats_ref.shape, 1)
    stats_ref[...] = jnp.where(lane == 0, mean, inv_std)
    return ((values - mean) * inv_std * gain).astype(BF16)


def project_heads_kernel(
    tokens_ref, gain_ref, weight_ref, bias_ref, cos_ref, sin_ref,
    normed_ref, q_ref, k_ref, v_ref, stats_ref,
):
    width = q_ref.shape[1]
    normed = norm_tile(tokens_ref, gain_ref, 0, stats_ref)
    normed_ref[...] = normed
    in_head = lax.broadcasted_iota(jnp.int32, (1, width), 1) % HEAD_DIM
    cosine = jnp.tile(cos_ref[...], (1, width // cos_ref.shape[1]))
    sine = jnp.tile(sin_ref[...], (1, width // sin_ref.shape[1]))
    pre = dot(normed, weight_ref[...]) + bias_ref[...]
    for ref, at, scale in ((q_ref, 0, SCALE), (k_ref, width, 1.0)):
        part = pre[:, at : at + width]
        turned = part * cosine + swap_pairs(part, in_head) * sine
        ref[...] = turned.astype(BF16) * jnp.asarray(scale, BF16)
    v_ref[...] = pre[:, 2 * width :].astype(BF16)


def tiled(columns):
    return pl.BlockSpec((TILE, columns), lambda i: (i, 0))


def whole(shape):
    return pl.BlockSpec(shape, lambda i: (0,) * len(shape))


def column_block(blocks_ref, all_ref, other, sems, index):
    row, col = lax.axis_index("row"), lax.axis_index("col")
    send_sem, recv_sem = sems
    return pltpu.make_async_remote_copy(
        blocks_ref.at[other], all_ref.at[col], send_sem.at[index], recv_sem.at[index],
        device_id=(row, other), device_id_type=MESH,
    )


def exchange_beside(kernel, blocks_ref, all_ref, steps, local, *sems, more=()):
    row, col = lax.axis_index("row"), lax.axis_index("col")
    others = [col + d - 2 * d * ((col // d) % 2) if d < 3 else 3 - col for d in steps]

    @pl.when(pl.program_id(0) == 0)
    def _():
        meet([(row, other) for other in others] + list(more))
        for i, other in enumerate(others):
            column_block(blocks_ref, all_ref, other, sems, i).start()
        if local is not None:
            pltpu.make_async_copy(blocks_ref.at[col], *local).start()

    kernel()

    @pl.when(pl.program_id(0) == pl.num_programs(0) - 1)
    def _():
        if local is not None:
            stage, local_sem = local
            pltpu.make_async_copy(blocks_ref.at[col], stage, local_sem).wait()
            task = pltpu.make_async_copy(stage, all_ref.at[col], local_sem)
            task.start()
            task.wait()
        for i, other in enumerate(others):
            task = column_block(blocks_ref, all_ref, other, sems, i)
            task.wait_send()
            send_sem, recv_sem = sems
            pltpu.make_async_remote_copy(
                blocks_ref.at[other], all_ref.at[other], send_sem.at[i], recv_sem.at[i],
                device_id=(row, other), device_id_type=MESH,
            ).wait_recv()


def project_heads_exchange_kernel(*refs):
    *ins, blocks_ref = refs[:7]
    outs, all_ref, (stage, local_sem, *sems) = refs[7:12], refs[12], refs[13:]
    exchange_beside(
        lambda: project_heads_kernel(*ins, *outs),
        blocks_ref, all_ref, (2,), (stage, local_sem), *sems,
    )


def project_heads(tokens, gains, weight, bias, cosine, sine, blocks=None, collective_id=None):
    rows, depth = tokens.shape
    width = weight.shape[1] // 3
    in_specs = [
        tiled(depth), whole(gains.shape), whole(weight.shape), whole((1, 3 * width)),
        tiled(cosine.shape[1]), tiled(cosine.shape[1]),
    ]
    out_specs = [tiled(depth)] + [tiled(width)] * 3 + [tiled(8)]
    out_shape = [
        jax.ShapeDtypeStruct((rows, depth), BF16),
        *[jax.ShapeDtypeStruct((rows, width), BF16)] * 3,
        jax.ShapeDtypeStruct((rows, 8), F32),
    ]
    operands = [tokens, gains, weight, bias.reshape(1, 3 * width), cosine, sine]
    params, scratch, kernel = {}, [], project_heads_kernel
    if blocks is not None:
        anywhere = pl.BlockSpec(memory_space=pl.ANY)
        in_specs, out_specs = in_specs + [anywhere], out_specs + [anywhere]
        out_shape = out_shape + [jax.ShapeDtypeStruct(blocks.shape, BF16)]
        operands = operands + [blocks]
        scratch = [pltpu.VMEM(blocks.shape[1:], BF16), pltpu.SemaphoreType.DMA]
        scratch = scratch + [pltpu.SemaphoreType.DMA((1,))] * 2
        params = dict(collective_id=collective_id, has_side_effects=True)
        kernel = project_heads_exchange_kernel
    return pl.pallas_call(
        kernel,
        grid=(rows // TILE,),
        in_specs=in_specs,
        out_specs=out_specs,
        out_shape=out_shape,
        scratch_shapes=scratch,
        compiler_params=pltpu.CompilerParams(vmem_limit_bytes=60 << 20, **params),
        cost_estimate=taking(16),
        name="project_heads",
    )(*operands)


def feed_forward_kernel(
    resid_ref, gain_ref, weight_ref, grad_ref, down_ref,
    normed_ref, hidden_ref, dgate_ref, dup_ref, stats_ref,
):
    lines, _, hidden, width = weight_ref.shape
    normed_ref[...] = norm_tile(resid_ref, gain_ref, 1, stats_ref)
    gate = jnp.zeros((hidden, TILE), F32)
    up = jnp.zeros((hidden, TILE), F32)
    dhidden = jnp.zeros((hidden, TILE), F32)
    for z in range(lines):
        part = normed_ref[:, z * width : (z + 1) * width]
        gate += dot(weight_ref[z, 0], part, (1,), (1,))
        up += dot(weight_ref[z, 1], part, (1,), (1,))
    for c in range(down_ref.shape[0]):
        part = grad_ref[:, c * width : (c + 1) * width]
        dhidden += dot(down_ref[c], part, (1,), (1,))
    sigmoid = 1.0 / (1.0 + jnp.exp(-gate))
    silu = gate * sigmoid
    hidden_ref[...] = (silu * up).astype(BF16)
    dgate_ref[...] = (dhidden * up * sigmoid * (1.0 + gate * (1.0 - sigmoid))).astype(BF16)
    dup_ref[...] = (dhidden * silu).astype(BF16)


def feed_forward(resid, gains, weight, grad, down):
    rows, depth = resid.shape
    hidden = down.shape[1]
    across = pl.BlockSpec((hidden, TILE), lambda i: (0, i))
    return pl.pallas_call(
        feed_forward_kernel,
        grid=(rows // TILE,),
        in_specs=[
            tiled(depth), whole(gains.shape), whole(weight.shape), tiled(depth), whole(down.shape)
        ],
        out_specs=[tiled(depth)] + [across] * 3 + [tiled(8)],
        out_shape=[jax.ShapeDtypeStruct((rows, depth), BF16)]
        + [jax.ShapeDtypeStruct((hidden, rows), BF16)] * 3
        + [jax.ShapeDtypeStruct((rows, 8), F32)],
        compiler_params=pltpu.CompilerParams(vmem_limit_bytes=56 << 20),
        cost_estimate=taking(28),
        name="feed_forward",
    )(resid, gains, weight, grad, down)


def weight_grads_kernel(*refs):
    *left_refs, right_ref, out_ref = refs
    for i, left_ref in enumerate(left_refs):
        out_ref[0, i] = dot(left_ref[...], right_ref[...]).astype(BF16)


def weight_grads(lefts, right, width, name):
    hidden, rows = lefts[0].shape
    blocks = right.shape[1] // width
    return pl.pallas_call(
        weight_grads_kernel,
        grid=(blocks,),
        in_specs=[whole((hidden, rows))] * len(lefts)
        + [pl.BlockSpec((rows, width), lambda i: (0, i))],
        out_specs=pl.BlockSpec((1, len(lefts), hidden, width), lambda i: (i, 0, 0, 0)),
        out_shape=jax.ShapeDtypeStruct((blocks, len(lefts), hidden, width), BF16),
        compiler_params=pltpu.CompilerParams(vmem_limit_bytes=56 << 20),
        cost_estimate=taking(9 * len(lefts)),
        name=name,
    )(*lefts, right)


def back_project_kernel(*refs):
    *left_refs, weight_ref, out_ref = refs
    width = weight_ref.shape[-1]
    lefts = [ref[...].T for ref in left_refs]
    for z in range(weight_ref.shape[0]):
        total = sum(dot(left, weight_ref[z, i]) for i, left in enumerate(lefts))
        out_ref[:, z * width : (z + 1) * width] = total.astype(BF16)


def back_project(lefts, weight, name):
    hidden, rows = lefts[0].shape
    depth = weight.shape[0] * weight.shape[-1]
    return pl.pallas_call(
        back_project_kernel,
        grid=(rows // TILE,),
        in_specs=[pl.BlockSpec((hidden, TILE), lambda i: (0, i))] * len(lefts)
        + [whole(weight.shape)],
        out_specs=tiled(depth),
        out_shape=jax.ShapeDtypeStruct((rows, depth), BF16),
        compiler_params=pltpu.CompilerParams(vmem_limit_bytes=48 << 20),
        cost_estimate=taking(10 * len(lefts)),
        name=name,
    )(*lefts, weight)


class PlaneScatter:
    SEMS = 14

    def __init__(self, copies, base, fill, sent_ref, own_ref, core_ref, x_ref, y_ref, last_ref):
        self.copies, self.base, self.fill = copies, base, fill
        self.sent, self.own, self.core_part = sent_ref, own_ref, core_ref
        self.x_ref, self.y_ref, self.last = x_ref, y_ref, last_ref
        self.x, self.y, self.core, row, col = places()
        self.over_x, self.over_y, self.over_core = peers(row, col)
        x, y = self.x, self.y
        self.order = ((1 - x, 1 - y), (1 - x, y), (x, 1 - y), (x, y))
        self.theirs = [2 * b + 1 - self.core for _, b in self.order]
        self.ours = [2 * b + self.core for _, b in self.order]
        self.half = own_ref.shape[1] // 2
        self.rows = (pl.ds(0, self.half), pl.ds(self.half, self.half))
        self.given = Copies(copies.send_sem, copies.recv_sem, self.over_core)

    def send(self, index, source, place, device):
        self.copies.send(self.base + index, source, place, device)

    def wait(self, index, place):
        self.copies.wait(self.base + index, place)

    def give(self, i, h):
        a, _ = self.order[i]
        self.fill(self.sent.at[i], a, self.theirs[i], h, None)
        at = self.rows[h]
        self.given.send(
            self.base + 2 * i + h, self.sent.at[i, at, :], self.core_part.at[i, at, :], self.over_core
        )

    def keep(self, i, h):
        a, _ = self.order[i]
        at = self.rows[h]
        self.wait(2 * i + h, self.core_part.at[i, at, :])
        self.fill(self.own.at[i], a, self.ours[i], h, self.core_part.at[i])
        self.part_done(i, h)

    def part_done(self, i, h):
        at = self.rows[h]
        if h == 0 and i in (0, 1):
            self.send(8 + i, self.own.at[i, at, :], self.x_ref.at[i], self.over_x)
        if h == 1 and i in (0, 2):
            self.send(10 + i // 2, self.own.at[i, at, :], self.y_ref.at[i // 2], self.over_y)

    def begin(self):
        self.give(0, 0)
        self.give(0, 1)
        self.keep(0, 0)
        self.keep(0, 1)

    def proceed(self):
        for h in range(2):
            self.give(1, h)
            self.give(2, h)
        self.keep(1, 0)
        self.keep(2, 1)

    def complete(self):
        self.keep(2, 0)
        self.keep(1, 1)
        for h in range(2):
            self.give(3, h)
        for h in range(2):
            self.keep(3, h)

    def settle(self):
        self.given.finish()

    def drain(self):
        view = self.own.at[0, self.rows[0], :]
        for index in range(self.SEMS):
            self.copies.copy(self.base + index, view, view, self.over_core).wait_send()

    def add(self, i, h, ref):
        at = self.own.at[i, self.rows[h], :]
        add_rows(at, at, ref, self.half)

    def second(self):
        self.wait(8, self.x_ref.at[0])
        self.add(2, 0, self.x_ref.at[0])
        self.send(12, self.own.at[2, self.rows[0], :], self.last.at[0], self.over_y)
        self.wait(10, self.y_ref.at[0])
        self.add(1, 1, self.y_ref.at[0])
        self.send(13, self.own.at[1, self.rows[1], :], self.last.at[1], self.over_x)
        self.wait(9, self.x_ref.at[1])
        self.add(3, 0, self.x_ref.at[1])
        self.wait(11, self.y_ref.at[1])
        self.add(3, 1, self.y_ref.at[1])

    def third(self):
        self.wait(12, self.last.at[0])
        self.wait(13, self.last.at[1])

    def result(self, start, count):
        h, other = divmod(start, self.half)
        return self.own[3, pl.ds(start, count), :].astype(F32) + self.last[
            h, pl.ds(other, count), :
        ].astype(F32)


class PartsScatter(PlaneScatter):
    def __init__(self, copies, base, parts_ref, load_sem, *scratch):
        super().__init__(copies, base, None, None, *scratch)
        blocks = [a * 4 for a, _ in self.order]
        self.parts, self.load_sem = parts_ref, load_sem
        self.sources = [parts_ref.at[at + c] for at, c in zip(blocks, self.theirs)]
        self.loads = [
            pltpu.make_async_copy(parts_ref.at[at + c], self.own.at[i], load_sem.at[i])
            for i, (at, c) in enumerate(zip(blocks, self.ours))
        ]

    def start(self):
        for i, load in enumerate(self.loads):
            load.start()
            for h, at in enumerate(self.rows):
                self.given.send(
                    self.base + 2 * i + h, self.sources[i].at[at, :],
                    self.core_part.at[i, at, :], self.over_core,
                )

    def keep(self, i, h):
        if h == 0:
            self.loads[i].wait()
        at = self.rows[h]
        self.wait(2 * i + h, self.core_part.at[i, at, :])
        self.add(i, h, self.core_part.at[i, at, :])
        self.part_done(i, h)


class LineScatter:
    def __init__(self, up_send, up_recv, down_send, down_recv, part, up_ref, down_ref):
        self.part, self.row, self.col = part, lax.axis_index("row"), lax.axis_index("col")
        self.z = self.row // PAIR
        last = LINES - 1
        self.ways = (
            (self.z, lambda n: n, up_ref, up_send, up_recv, jnp.minimum(self.row + PAIR, PAIR * last + PAIR - 1)),
            (last - self.z, lambda n: last - n, down_ref, down_send, down_recv, jnp.maximum(self.row - PAIR, 0)),
        )

    def clear(self):
        for n, _, slots, _, _, _ in self.ways:

            @pl.when(n == 0)
            def _():
                slots[LINES - 2] = jnp.zeros(slots.shape[1:], slots.dtype)

    def task(self, way, step, source):
        _, _, slots, send, recv, device = way
        return pltpu.make_async_remote_copy(
            source, slots.at[step], send.at[step], recv.at[step],
            device_id=(device, self.col), device_id_type=MESH,
        )

    def sends(self, way, step, act):
        n, place, slots, _, _, _ = way

        @pl.when(n == 0)
        def _():
            act(self.task(way, step, self.part(place(LINES - 1 - step))))

        if step > 0:

            @pl.when((n > 0) & (n <= step))
            def _():
                act(self.task(way, step, slots.at[step - 1]))

    def start(self):
        for way in self.ways:
            self.sends(way, 0, lambda task: task.start())

    def hop(self, step):
        for way in self.ways:
            n, place, slots, _, _, _ = way

            @pl.when((n >= 1) & (n <= step + 1))
            def _():
                self.task(way, step, slots.at[step]).wait_recv()
                add_rows(
                    slots.at[step], slots.at[step], self.part(place(LINES - 2 - step + n)),
                    slots.shape[1],
                )

            self.sends(way, step + 1, lambda task: task.start())

    def receive(self):
        last = LINES - 2
        for way in self.ways:
            n, _, slots, _, _, _ = way

            @pl.when(n >= 1)
            def _():
                self.task(way, last, slots.at[last]).wait_recv()

    def total(self, at):
        last = LINES - 2
        result = self.part(self.z)[at, :].astype(F32)
        for _, _, slots, _, _, _ in self.ways:
            result = result + slots[last, at, :].astype(F32)
        return result

    def finish(self):
        for way in self.ways:
            for step in range(LINES - 1):
                self.sends(way, step, lambda task: task.wait_send())


STEP = 128


class NormBack:
    def __init__(
        self, copies, base, values_ref, stats_ref, gain_ref, base_ref, out_ref, low_ref, dgain_ref,
        sums_ref,
    ):
        self.copies, self.base = copies, base
        self.values, self.stats, self.gain, self.more = values_ref, stats_ref, gain_ref, base_ref
        self.out, self.low, self.dgain, self.sums = out_ref, low_ref, dgain_ref, sums_ref

    def stats_of(self, start):
        at = places()[0] * self.out.shape[0] + start
        return self.stats[pl.ds(pl.multiple_of(at, STEP), STEP), :]

    def unit_of(self, start):
        stats = self.stats_of(start)
        values = self.values[pl.ds(start, STEP), :].astype(F32)
        return (values - stats[:, 0:1]) * stats[:, 1:2]

    def start(self, result, devices):
        lane = lax.broadcasted_iota(jnp.int32, (1, 128), 1)
        self.dgain[...] = jnp.zeros_like(self.dgain)
        for start in range(0, self.out.shape[0], STEP):
            at = pl.ds(start, STEP)
            grad = result(start, STEP)
            self.out[at, :] = grad
            unit = self.unit_of(start)
            self.dgain[...] += jnp.sum(grad * unit, axis=0, keepdims=True)
            grad = grad * self.gain[...]
            first = jnp.sum(grad, axis=1, keepdims=True)
            second = jnp.sum(grad * unit, axis=1, keepdims=True)
            both = jnp.where(lane == 0, first, jnp.where(lane == 1, second, 0.0))
            self.sums[0, :, start : start + STEP] = both.T[:8]
        for i, device in enumerate(devices):
            self.copies.send(self.base + i, self.sums.at[0], self.sums.at[1 + i], device)

    def finish(self):
        rows, width = self.out.shape
        for i in range(3):
            self.copies.wait(self.base + i, self.sums.at[1 + i])
        for start in range(0, rows, STEP):
            at = pl.ds(start, STEP)
            columns = slice(start, start + STEP)
            total = (self.sums[0, :, columns] + self.sums[1, :, columns]) + (
                self.sums[2, :, columns] + self.sums[3, :, columns]
            )
            total = jnp.concatenate([total, jnp.zeros((STEP - 8, STEP), F32)], axis=0).T
            total = total * (1.0 / (4 * width))
            unit = self.unit_of(start)
            grad = self.out[at, :] * self.gain[...]
            grad = self.stats_of(start)[:, 1:2] * (grad - total[:, 0:1] - unit * total[:, 1:2])
            grad = grad + self.more[at, :].astype(F32)
            self.out[at, :] = grad
            if self.low is not None:
                self.low[at, :] = grad.astype(BF16)


def scatter_scratch(rows, width):
    block = lambda n, r: pltpu.VMEM((n, r, width), BF16)
    return [
        block(4, rows), block(4, rows), block(4, rows),
        block(2, rows // 2), block(2, rows // 2), block(2, rows // 2),
    ]


def around():
    _, _, _, row, col = places()
    over_x, over_y, over_core = peers(row, col)
    return over_x, over_y, over_core, (row, 3 - col)


def filling(rows, product):
    half = rows // 2

    def fill(ref, a, c, h, more):
        @pl.loop(0, half // TILE)
        def _(i):
            start = h * half + i * TILE
            total = product(pl.ds(pl.multiple_of(a * rows + start, TILE), TILE), c)
            at = pl.ds(pl.multiple_of(start, TILE), TILE)
            if more is not None:
                total = total + more[at, :].astype(F32)
            ref[at, :] = total.astype(BF16)

    return fill


def turn_rows(left_ref, source_ref, a, rows):
    @pl.loop(0, rows // TILE)
    def _(i):
        at = pl.ds(pl.multiple_of(a * rows + i * TILE, TILE), TILE)
        left_ref[at, :] = source_ref[:, at].T


def back_second_kernel(
    gate_ref, up_ref, weight_ref, hidden_hbm, grad_hbm, values_ref, stats_ref, gain_ref, base_ref,
    out_ref, low_ref, dgain_ref, down_ref,
    hidden_ref, grad_ref, gate_vmem, up_vmem, weight_vmem, left_ref, sums_ref, load_sem, send_sem, recv_sem, *scratch,
):
    rows, width = out_ref.shape
    x, y, core, _, _ = places()
    devices = around()

    def load_left(i, a):
        at = pl.ds(pl.multiple_of(a * rows, TILE), rows)
        return [
            pltpu.make_async_copy(ref.at[:, at], vmem.at[:, at], load_sem.at[2 * i + j])
            for j, (ref, vmem) in enumerate(((gate_ref, gate_vmem), (up_ref, up_vmem)))
        ]

    def load_weight(i, c):
        return pltpu.make_async_copy(weight_ref.at[c], weight_vmem.at[c], load_sem.at[4 + i])

    lefts = [load_left(0, 1 - x), load_left(1, x)]
    columns = (2 * (1 - y) + 1 - core, 2 * (1 - y) + core, 2 * y + 1 - core, 2 * y + core)
    weights = [load_weight(i, c) for i, c in enumerate(columns)]
    others = [
        pltpu.make_async_copy(hidden_hbm, hidden_ref, load_sem.at[8]),
        pltpu.make_async_copy(grad_hbm, grad_ref, load_sem.at[9]),
    ]
    for task in (*lefts[0], *weights, *lefts[1], *others):
        task.start()
    meet(devices)
    copies = Copies(send_sem, recv_sem, devices[2])

    def turn(i, a):
        for j, (task, vmem) in enumerate(zip(lefts[i], (gate_vmem, up_vmem))):
            task.wait()
            turn_rows(left_ref.at[j], vmem, a, rows)

    def product(at, c):
        return dot(left_ref[0, at, :], weight_vmem[c, 0]) + dot(
            left_ref[1, at, :], weight_vmem[c, 1]
        )

    scatter = PlaneScatter(copies, 0, filling(rows, product), *scratch)
    turn(0, 1 - x)
    weights[0].wait()
    scatter.give(0, 0)
    scatter.give(0, 1)
    weights[1].wait()
    scatter.keep(0, 0)
    scatter.keep(0, 1)
    weights[2].wait()
    scatter.give(1, 0)
    scatter.give(1, 1)
    weights[3].wait()
    scatter.keep(1, 0)
    turn(1, x)
    scatter.give(2, 1)
    scatter.give(2, 0)
    scatter.keep(2, 1)
    scatter.keep(2, 0)
    scatter.keep(1, 1)
    scatter.give(3, 0)
    scatter.give(3, 1)
    scatter.keep(3, 0)
    scatter.keep(3, 1)
    scatter.settle()
    scatter.second()
    for task in others:
        task.wait()
    for c in range(down_ref.shape[0]):
        right = grad_ref[:, c * width : (c + 1) * width]
        down_ref[c] = dot(hidden_ref[...], right).astype(BF16)
    scatter.third()
    norm = NormBack(
        copies, PlaneScatter.SEMS, values_ref, stats_ref, gain_ref, base_ref, out_ref, low_ref,
        dgain_ref, sums_ref,
    )
    norm.start(scatter.result, devices[1:])
    norm.finish()
    copies.finish()


def back_second(gate, up, weight, hidden, grad, values, stats, gain, base, collective_id):
    rows, width = values.shape
    units, tokens = gate.shape
    vmem, anywhere = pl.BlockSpec(memory_space=pltpu.VMEM), pl.BlockSpec(memory_space=pl.ANY)
    sems = lambda n: pltpu.SemaphoreType.DMA((n,))
    return pl.pallas_call(
        back_second_kernel,
        in_specs=[anywhere] * 5 + [vmem] * 4,
        out_specs=[vmem] * 4,
        out_shape=[
            jax.ShapeDtypeStruct((rows, width), F32),
            jax.ShapeDtypeStruct((rows, width), BF16),
            jax.ShapeDtypeStruct((1, width), F32),
            jax.ShapeDtypeStruct((grad.shape[1] // width, units, width), BF16),
        ],
        scratch_shapes=[
            pltpu.VMEM(hidden.shape, BF16), pltpu.VMEM(grad.shape, BF16),
            pltpu.VMEM(gate.shape, BF16), pltpu.VMEM(up.shape, BF16),
            pltpu.VMEM(weight.shape, BF16), pltpu.VMEM((2, tokens, units), BF16),
            pltpu.VMEM((4, 8, rows), F32),
            sems(10), sems(PlaneScatter.SEMS + 3), sems(PlaneScatter.SEMS + 3),
            *scatter_scratch(rows, width),
        ],
        compiler_params=pltpu.CompilerParams(
            collective_id=collective_id, has_side_effects=True, vmem_limit_bytes=63 << 20
        ),
        cost_estimate=taking(50),
        name="back_second",
    )(gate, up, weight, hidden, grad, values, stats, gain.reshape(1, width), base)


def back_first_kernel(
    grad_ref, weight_ref, values_ref, stats_ref, gain_ref, base_ref, normed_hbm, ffn_ref, heads_ref,
    vectors_ref,
    out_ref, vector_sums_ref, query_ref, key_ref, value_ref, gate_ref, up_grad_ref, out_grad_ref,
    normed_ref, part_ref, load_sem, dgain_ref, slots_ref, sums_ref, up_ref, down_line_ref, heads_up_ref, heads_down_ref, swap_ref, swapped_ref, turn_ref,
    send_sem, recv_sem, *scratch,
):
    line_sems, scratch = scratch[:12], scratch[12:]
    rows, width = out_ref.shape
    x, _, _, row, col = places()
    devices = around()
    load = pltpu.make_async_copy(normed_hbm, normed_ref, load_sem)
    load.start()
    copies = Copies(send_sem, recv_sem, devices[2])
    vectors = RowSum(copies, PlaneScatter.SEMS + 7, slots_ref)
    meet((*devices[1:], *vectors.others))
    depth, columns = up_ref.shape[2:]

    def line_of(k):
        at = pl.ds(k * columns, columns)
        return LineScatter(
            *line_sems[4 * k : 4 * k + 4],
            lambda b: part_ref.at[pl.ds(pl.multiple_of(b * depth, 128), depth), at],
            up_ref.at[k], down_line_ref.at[k],
        )

    out_depth = out_grad_ref.shape[0]
    heads = LineScatter(
        *line_sems[8:],
        lambda b: heads_ref.at[pl.ds(pl.multiple_of(b * out_depth, 128), out_depth), :],
        heads_up_ref, heads_down_ref,
    )
    lines = [line_of(k) for k in range(2)] + [heads]
    for line in lines:
        line.clear()
    heads.start()

    def product(at, c):
        weight = weight_ref[pl.ds(pl.multiple_of(c * width, 128), width), :]
        return dot(grad_ref[at, :], weight, (1,), (1,))

    scatter = PlaneScatter(copies, 0, filling(rows, product), *scratch)
    norm = NormBack(
        copies, PlaneScatter.SEMS, values_ref, stats_ref, gain_ref, base_ref, out_ref, None,
        dgain_ref, sums_ref,
    )
    half = depth // PAIR
    theirs = pl.multiple_of((1 - x) * half, 128)
    ours = pl.multiple_of(x * half, 128)
    swap = PlaneScatter.SEMS + 3
    units = ffn_ref.shape[2]
    scatter.begin()
    load.wait()
    for b in range(LINES):
        at = slice(b * depth, (b + 1) * depth)
        part_ref[at, :] = dot(normed_ref[:, at], grad_ref[...], (0,), (0,)).astype(BF16)
        if b == 1:
            heads.hop(0)
    lines[0].start()
    lines[1].start()
    scatter.proceed()
    heads.hop(1)
    scatter.complete()
    lines[0].hop(0)
    lines[1].hop(0)
    scatter.settle()
    scatter.second()
    lines[0].hop(1)
    here = pl.ds(pl.multiple_of(x * units, 16), units)
    there = pl.ds(pl.multiple_of((1 - x) * units, 16), units)
    for w in range(2):
        copies.send(
            swap + 2 + w, ffn_ref.at[0, w, :, pl.ds(theirs, half)], turn_ref.at[w, here, :], devices[0]
        )
        turn_ref[w, here, :] = ffn_ref[0, w, :, pl.ds(ours, half)]
    lines[1].hop(1)
    scatter.third()
    norm.start(scatter.result, devices[1:4])
    slots_ref[0] = vectors_ref[...]
    slots_ref[0, 3:4, :] = dgain_ref[...]
    vectors.start()
    part = width // PAIR
    outs = (query_ref, key_ref, value_ref)

    def pieces(k):
        for w in range(3):
            start, end = max(k * columns, w * part), min((k + 1) * columns, (w + 1) * part)
            if start < end:
                yield outs[w], start - w * part, start, end - start

    def close(k):
        lines[k].receive()
        at = pl.ds(k * columns, columns)
        swap_ref[:, at] = lines[k].total(pl.ds(theirs, half)).astype(BF16)
        copies.send(swap + k, swap_ref.at[:, at], swapped_ref.at[:, at], devices[0])
        total = lines[k].total(pl.ds(ours, half))
        for ref, place, start, size in pieces(k):
            columns_at = pl.ds(pl.multiple_of(x * part + place, 128), size)
            ref[:, columns_at] = total[:, start - k * columns : start - k * columns + size]

    close(0)
    norm.finish()
    close(1)
    for w, ref in enumerate((gate_ref, up_grad_ref)):
        copies.wait(swap + 2 + w, turn_ref.at[w, there, :])
        for j in range(PAIR * units // 128):
            at = slice(j * 128, (j + 1) * 128)
            ref[:, at] = turn_ref[w, at, :].T.astype(F32)
    heads.receive()
    out_grad_ref[...] = heads.total(pl.ds(0, out_depth))
    heads.finish()
    vector_sums_ref[...] = vectors.finish()
    for k in range(2):
        at = pl.ds(k * columns, columns)
        copies.wait(swap + k, swapped_ref.at[:, at])
        for ref, place, start, size in pieces(k):
            columns_at = pl.ds(pl.multiple_of((1 - x) * part + place, 128), size)
            ref[:, columns_at] = swapped_ref[:, start : start + size].astype(F32)
        lines[k].finish()
    copies.finish()


def back_first(
    grad, weight, values, stats, gain, base, normed, ffn, heads, vectors, collective_id
):
    rows, width = values.shape
    depth, columns = normed.shape[1] // LINES, grad.shape[1]
    vmem = pl.BlockSpec(memory_space=pltpu.VMEM)
    sems = lambda n: pltpu.SemaphoreType.DMA((n,))
    count = PlaneScatter.SEMS + 7 + PAIR * LINES - 1
    units = ffn.shape[2]
    return pl.pallas_call(
        back_first_kernel,
        in_specs=[vmem] * 6 + [pl.BlockSpec(memory_space=pl.ANY)] + [vmem] * 3,
        out_specs=[vmem] * 8,
        out_shape=[
            jax.ShapeDtypeStruct((rows, width), F32),
            jax.ShapeDtypeStruct(vectors.shape, F32),
        ]
        + [jax.ShapeDtypeStruct((depth // PAIR, width), F32)] * 3
        + [jax.ShapeDtypeStruct((depth // PAIR, PAIR * units), F32)] * 2
        + [jax.ShapeDtypeStruct((heads.shape[0] // LINES, width), F32)],
        scratch_shapes=[
            pltpu.VMEM(normed.shape, BF16), pltpu.VMEM((normed.shape[1], columns), BF16),
            pltpu.SemaphoreType.DMA,
            pltpu.VMEM((1, width), F32), pltpu.VMEM((PAIR * LINES,) + vectors.shape, F32),
            pltpu.VMEM((4, 8, rows), F32),
            pltpu.VMEM((2, LINES - 1, depth, columns // 2), BF16),
            pltpu.VMEM((2, LINES - 1, depth, columns // 2), BF16),
            *[pltpu.VMEM((LINES - 1, heads.shape[0] // LINES, width), BF16)] * 2,
            pltpu.VMEM((depth // PAIR, columns), BF16), pltpu.VMEM((depth // PAIR, columns), BF16),
            pltpu.VMEM((2, PAIR * units, depth // PAIR), BF16),
            sems(count), sems(count), *[sems(LINES - 1)] * 12,
            *scatter_scratch(rows, width),
        ],
        compiler_params=pltpu.CompilerParams(
            collective_id=collective_id, has_side_effects=True, vmem_limit_bytes=63 << 20
        ),
        cost_estimate=taking(10),
        name="back_first",
    )(grad, weight, values, stats, gain.reshape(1, width), base, normed, ffn, heads, vectors)


def back_heads_kernel(
    low_ref, weight_ref, attn_hbm, hidden_hbm, down_hbm, blocks_ref,
    out_ref, part_ref, mix_ref, all_ref,
    stage_ref, attn_ref, hidden_ref, down_ref, left_ref, sent_ref, own_ref, core_ref, y_ref, give_ref, come_ref,
    load_sem, out_sem, send_sem, recv_sem,
):
    rows, width = low_ref.shape
    half = width // PAIR
    count = rows // CHUNKS
    x, y, core, row, col = places()
    over_x, over_y, over_core = peers(row, col)
    over_far = (row, 3 - col)
    loads = [
        pltpu.make_async_copy(source, place, load_sem.at[i])
        for i, (source, place) in enumerate(
            ((attn_hbm, attn_ref), (hidden_hbm, hidden_ref), (down_hbm, down_ref))
        )
    ]
    for load in loads:
        load.start()
    stage = pltpu.make_async_copy(blocks_ref.at[col], stage_ref, load_sem.at[3])
    stage.start()
    meet((over_x, over_y, over_core, over_far))
    copies = Copies(send_sem, recv_sem, over_core)
    sides = (1 - y, y)

    def at_chunk(s):
        return pl.ds(s * count, count)

    def product(s, c):
        weight = weight_ref[pl.ds(pl.multiple_of(c * width, 128), width), :]
        return dot(low_ref[at_chunk(s), :], weight, (1,), (1,))

    def give(i, s):
        at = at_chunk(s)
        sent_ref[i, at, :] = product(s, 2 * sides[i] + 1 - core).astype(BF16)
        copies.send(i * CHUNKS + s, sent_ref.at[i, at, :], core_ref.at[i, at, :], over_core)

    def keep(i, s):
        at = at_chunk(s)
        part = product(s, 2 * sides[i] + core)
        copies.wait(i * CHUNKS + s, core_ref.at[i, at, :])
        own_ref[i, at, :] = (part + core_ref[i, at, :].astype(F32)).astype(BF16)
        if i == 0:
            copies.send(2 * CHUNKS + s, own_ref.at[0, at, :], y_ref.at[at, :], over_y)

    depth = give_ref.shape[1]

    def out_grad(z, x):
        at = pl.ds(pl.multiple_of((PAIR * z + x) * depth, 128), depth)
        return dot(attn_ref[:, at], low_ref[...], (0,), (0,))

    others = (((col + 2) % 4, over_y), (3 - col, over_far), (col + 1 - 2 * core, over_core))
    for s in range(CHUNKS):
        give(0, s)
    loads[0].wait()
    for z in range(LINES):
        give_ref[z] = out_grad(z, 1 - x).astype(BF16)
    copies.send(4 * CHUNKS, give_ref, come_ref, over_x)
    for s in range(CHUNKS):
        keep(0, s)
    for i, (other, device) in enumerate(others):
        copies.send(4 * CHUNKS + 1 + i, blocks_ref.at[other], all_ref.at[col], device)
    for s in range(CHUNKS):
        give(1, s)
    for s in range(CHUNKS):
        keep(1, s)
    for z in range(LINES):
        part_ref[z * depth : (z + 1) * depth, :] = out_grad(z, x).astype(BF16)
    stage.wait()
    stage = pltpu.make_async_copy(stage_ref, all_ref.at[col], load_sem.at[3])
    stage.start()
    for load in loads[1:]:
        load.wait()
    for a in range(PAIR):
        turn_rows(left_ref, hidden_ref, a, rows)
    kept = []
    for s in range(CHUNKS):

        @pl.loop(0, PAIR * rows // TILE)
        def _(i):
            a, start = i // (rows // TILE), pl.multiple_of(i % (rows // TILE) * TILE, TILE)
            left = left_ref[pl.ds(pl.multiple_of(i * TILE, TILE), TILE), :]
            mix_ref[a * CHUNKS + s, pl.ds(start, TILE), :] = dot(left, down_ref[s]).astype(BF16)

        at = at_chunk(s)
        copies.wait(2 * CHUNKS + s, y_ref.at[at, :])
        own_ref[1, at, :] = (
            own_ref[1, at, :].astype(F32) + y_ref[at, :].astype(F32)
        ).astype(BF16)
        place = out_ref.at[pl.ds(pl.multiple_of(x * rows + s * count, 128), count), :]
        theirs = own_ref.at[1, at, pl.ds(pl.multiple_of((1 - x) * half, 128), half)]
        ours = own_ref.at[1, at, pl.ds(pl.multiple_of(x * half, 128), half)]
        copies.send(3 * CHUNKS + s, theirs, place, over_x)
        task = pltpu.make_async_copy(ours, place, out_sem.at[s])
        task.start()
        kept.append(task)
    copies.wait(4 * CHUNKS, come_ref)
    for z in range(LINES):
        at = pl.ds(z * depth, depth)
        add_rows(part_ref.at[at, :], part_ref.at[at, :], come_ref.at[z], depth)
    for s in range(CHUNKS):
        copies.wait(
            3 * CHUNKS + s,
            out_ref.at[pl.ds(pl.multiple_of((1 - x) * rows + s * count, 128), count), :],
        )
    for i, (other, _) in enumerate(others):
        copies.wait(4 * CHUNKS + 1 + i, all_ref.at[other])
    copies.finish()
    stage.wait()
    for task in kept:
        task.wait()


def back_heads(low, weight, attn, hidden, down, blocks, collective_id):
    rows, width = low.shape
    depth = weight.shape[0] // (PAIR * LINES)
    vmem, anywhere = pl.BlockSpec(memory_space=pltpu.VMEM), pl.BlockSpec(memory_space=pl.ANY)
    sems = lambda n: pltpu.SemaphoreType.DMA((n,))
    wide = pltpu.VMEM((2, rows, width), BF16)
    swapped = pltpu.VMEM((LINES, depth, width), BF16)
    return pl.pallas_call(
        back_heads_kernel,
        in_specs=[vmem] * 2 + [anywhere] * 4,
        out_specs=[anywhere, vmem, vmem, anywhere],
        out_shape=[
            jax.ShapeDtypeStruct((PAIR * rows, width // PAIR), BF16),
            jax.ShapeDtypeStruct((LINES * depth, width), BF16),
            jax.ShapeDtypeStruct((PAIR * CHUNKS, rows, width), BF16),
            jax.ShapeDtypeStruct(blocks.shape, BF16),
        ],
        scratch_shapes=[
            pltpu.VMEM(blocks.shape[1:], BF16),
            pltpu.VMEM(attn.shape, BF16), pltpu.VMEM(hidden.shape, BF16),
            pltpu.VMEM(down.shape, BF16), pltpu.VMEM(hidden.shape[::-1], BF16),
            wide, wide, wide, pltpu.VMEM((rows, width), BF16),
            swapped, swapped,
            sems(4), sems(CHUNKS), sems(4 * CHUNKS + 4), sems(4 * CHUNKS + 4),
        ],
        compiler_params=pltpu.CompilerParams(
            collective_id=collective_id, has_side_effects=True, vmem_limit_bytes=60 << 20
        ),
        cost_estimate=taking(60),
        name="back_heads",
    )(low, weight, attn, hidden, down, blocks)


def per_device(
    tokens, segment_ids, positions, attn_gain, query_weight, query_bias, key_weight, key_bias,
    value_weight, value_bias, out_weight, mlp_gain, gate_weight, up_weight, down_weight, out_grad,
):
    count, width = tokens.shape
    lines = lax.axis_size("row") // PAIR
    cols = lax.axis_size("col")
    row = lax.axis_index("row")
    col = lax.axis_index("col")
    x = row % PAIR
    half = width // PAIR

    fast = cols == 4 and lines == LINES
    bias = jnp.concatenate(
        [pick(b, x, 0) for b in (query_bias, key_bias, value_bias)], axis=0
    )
    depth = out_weight.shape[0]
    hidden = down_weight.shape[0]
    down_line = gather_line(down_weight)
    if fast:
        tokens_all, grad_all, qkv_weight, out_all, ffn_part, gains, places_all = gather_first(
            tokens, out_grad, query_weight, key_weight, value_weight, out_weight,
            gate_weight, up_weight,
            jnp.pad(jnp.stack([attn_gain, mlp_gain]), ((0, 6), (0, 0))),
            jnp.pad(jnp.stack([positions, segment_ids]), ((0, 6), (0, 0))), 0,
        )
    else:
        qkv_weight = gather_line(
            jnp.concatenate(
                [own_columns(w, x) for w in (query_weight, key_weight, value_weight)], axis=1
            )
        )
        tokens_all = gather_plane(tokens, "gather_tokens", 0)
        grad_all = gather_plane(out_grad, "gather_cotangent", 1)
        out_line = gather_line(out_weight)
        full = (lines, 1, depth, width)
        out_all = in_order(
            x, out_line.reshape(full), swap_rows(out_line).reshape(full), 1
        ).reshape(-1, width)
        ffn_part = jnp.stack([own_units(w, x) for w in (gate_weight, up_weight)])[None]
        gains = lax.all_gather(jnp.stack([attn_gain, mlp_gain]), "col", axis=1, tiled=True)
        own_place = jnp.stack([positions, segment_ids])
        places_all = in_order(x, own_place, swap_rows(own_place), 1)
    cosine, sine = rotation_tables(places_all[0])
    plane_segments = places_all[1]
    down_blocks = after(down_line, tokens_all).reshape(lines, hidden, width)
    ffn_weight = gather_line(after(ffn_part, down_blocks))

    projections = (tokens_all, gains, qkv_weight, bias, cosine, sine)
    if fast:
        normed_first, queries, keys, values, stats_first, down_partly = project_heads(
            *projections, down_blocks, 1
        )
        attended, lse, down_all = attention_forward(
            queries, keys, values, plane_segments, down_blocks, down_partly, 8
        )
    else:
        normed_first, queries, keys, values, stats_first = project_heads(*projections)
        attended, lse = attention_forward(queries, keys, values, plane_segments)
        down_all = lax.all_to_all(down_blocks, "col", split_axis=0, concat_axis=0, tiled=True)
    if fast:
        attn_all, resid, resid_all = project_out(attended, out_all, tokens, 2)
    else:
        attn_all = gather_heads(attended, x)
        resid = tokens.astype(F32) + dot(attn_all, out_all)
        resid_all = gather_plane(resid.astype(BF16), "gather_residual", 3)

    normed_second, hidden_low, grad_gate, grad_up, stats_second = feed_forward(
        resid_all, gains, ffn_weight, grad_all, down_all
    )
    if fast:
        grad_ffn = weight_grads((grad_gate, grad_up), normed_second, width, "ffn_grads")
    else:
        grad_ffn = weight_grads((grad_gate, grad_up), normed_second, width, "ffn_grads")
    if fast:
        grad_resid, grad_resid_low, mlp_gain_part, down_blocks = back_second(
            after(grad_gate, grad_ffn), grad_up, ffn_weight, hidden_low, grad_all,
            resid, stats_second, mlp_gain, out_grad, 4,
        )
        mlp_gain_part = mlp_gain_part[0]
    else:
        grad_second = scatter_plane(
            back_project((grad_gate, grad_up), ffn_weight, "back_ffn"), "scatter_second", 4
        )
        own_stats = pick(stats_second, x, 0)
        mean_here, inv_here = own_stats[:, 0:1], own_stats[:, 1:2]
        grad_resid, mlp_gain_part = norm_backward(
            grad_second, (resid - mean_here) * inv_here, inv_here, mlp_gain
        )
        grad_resid = grad_resid + out_grad.astype(F32)
        grad_resid_low = grad_resid.astype(BF16)
    grad_ffn = scatter_line(grad_ffn)

    if fast:
        grad_attn, grad_out_weight, mixed, grad_down = back_heads(
            grad_resid_low, out_all, attn_all, hidden_low, down_all, down_blocks, 5
        )
        grad_qkv, bias_sums, mixed = attention_backward(
            queries, keys, values, grad_attn, lse, cosine, sine, plane_segments, mixed, resid, 9
        )
    else:
        grad_out_weight = dot(attn_all, grad_resid_low, (0,), (0,)).astype(BF16)
        grad_out_weight = grad_out_weight.reshape(lines, PAIR, depth, width)
        grad_out_weight = pick(grad_out_weight, x, 1) + swap_rows(pick(grad_out_weight, 1 - x, 1))
        grad_out_weight = scatter_line(grad_out_weight.reshape(lines * depth, width)).astype(F32)
        grad_attn = scatter_heads(dot(grad_resid_low, out_all, (1,), (1,)).astype(BF16), x)
        grad_qkv, bias_sums = attention_backward(
            queries, keys, values, grad_attn, lse, cosine, sine, plane_segments
        )
        grad_down = weight_grads((hidden_low,), grad_all, width, "down_grads")
        grad_down = lax.all_to_all(
            grad_down.reshape(cols, hidden, width), "col", split_axis=0, concat_axis=0, tiled=True
        )
    grad_down = scatter_line(after(grad_down, grad_ffn).reshape(lines * hidden, width))
    bias_part = jnp.sum(bias_sums, axis=(0, 1)).reshape(3, half)
    bias_part = jnp.where(
        (jnp.arange(PAIR) == x)[None, :, None], bias_part[:, None, :], 0.0
    ).reshape(3, width)
    if fast:
        (
            tokens_grad, vectors, query_grad, key_grad, value_grad, gate_grad, up_grad,
            grad_out_weight,
        ) = back_first(
            grad_qkv, qkv_weight,
            tokens, stats_first, attn_gain, grad_resid, normed_first, grad_ffn, grad_out_weight,
            jnp.concatenate(
                [bias_part, jnp.zeros((1, width), F32), mlp_gain_part[None], jnp.zeros((3, width), F32)]
            ),
            6,
        )
    else:
        kept, other = pick(grad_ffn[0], x, 2), swap_rows(pick(grad_ffn[0], 1 - x, 2))
        gate_grad, up_grad = (
            in_order(x, kept[i], other[i], 0).T.astype(F32) for i in range(2)
        )
        grad_qkv_weight = dot(normed_first, grad_qkv, (0,), (0,)).astype(BF16)
        kept, other = own_rows(scatter_line(grad_qkv_weight), x)
        query_grad, key_grad, value_grad = (
            in_order(x, kept[:, at : at + half], other[:, at : at + half], 1).astype(F32)
            for at in (0, half, 2 * half)
        )
        grad_first = scatter_plane(
            dot(grad_qkv, qkv_weight, (1,), (1,)).astype(BF16), "scatter_first", 6
        )
        own_stats = pick(stats_first, x, 0)
        mean_here, inv_here = own_stats[:, 0:1], own_stats[:, 1:2]
        grad_input, attn_gain_part = norm_backward(
            grad_first, (tokens.astype(F32) - mean_here) * inv_here, inv_here, attn_gain
        )
        tokens_grad = grad_input + grad_resid
        vectors = lax.psum(
            jnp.concatenate([bias_part, attn_gain_part[None], mlp_gain_part[None]]), "row"
        )
        mixed = resid + scatter_plane(
            back_project((hidden_low,), down_all[:, None], "mix"), "scatter_mixed", 10
        )
        mixed = mixed.astype(BF16)

    return (
        mixed,
        tokens_grad,
        vectors[3],
        query_grad,
        vectors[0],
        key_grad,
        vectors[1],
        value_grad,
        vectors[2],
        grad_out_weight,
        vectors[4],
        gate_grad,
        up_grad,
        grad_down.astype(F32),
    )


def solution(mesh):
    grid, rows, cols = P("row", "col"), P("row"), P("col")
    in_specs = (
        grid, rows, rows, cols, grid, cols, grid, cols, grid, cols, grid, cols, grid, grid, grid, grid,
    )
    out_specs = (
        grid, grid, cols, grid, cols, grid, cols, grid, cols, grid, cols, grid, grid, grid,
    )
    return jax.shard_map(
        per_device, mesh=mesh, in_specs=in_specs, out_specs=out_specs, check_vma=False
    )
```

```python
import functools

import jax
import jax.numpy as jnp
from jax import lax
from jax.experimental import pallas as pl
from jax.experimental.pallas import tpu as pltpu
from jax.sharding import PartitionSpec as P

HEAD_DIM = 64
ROT = 16
SEQ = 1024
BASE = 10000.0
NEG = -1e30
F32 = jnp.float32
BF16 = jnp.bfloat16
SCALE = HEAD_DIM**-0.5
MESH = pl.DeviceIdType.MESH
QBLOCK = 256
PAIR = 2


def dot(left, right, left_dims=(1,), right_dims=(0,)):
    return lax.dot_general(
        left, right, ((left_dims, right_dims), ((), ())), preferred_element_type=F32
    )


def taking(microseconds):
    return pl.CostEstimate(
        flops=microseconds * 10**9, bytes_accessed=microseconds * 10**6, transcendentals=0
    )


def swap_pairs(values, lane):
    half = ROT // 2
    width = values.shape[1]
    ahead = pltpu.roll(values, width - half, 1)
    behind = pltpu.roll(values, half, 1)
    return jnp.where(lane < half, ahead, behind)


def attention_forward_kernel(
    q_ref, k_ref, v_ref, seg_col_ref, seg_row_ref, o_ref, lse_ref, acc_ref, lse_scratch
):
    width = q_ref.shape[1]
    heads = width // HEAD_DIM
    full_lane = lax.broadcasted_iota(jnp.int32, (1, width), 1)
    acc_ref[...] = jnp.zeros_like(acc_ref)
    lse_lane = lax.broadcasted_iota(jnp.int32, (1, lse_scratch.shape[1]), 1)

    @pl.loop(0, heads)
    def _(head):
        mask = full_lane // HEAD_DIM == head
        for start in range(0, SEQ, QBLOCK):
            keys = start + QBLOCK
            rows = slice(start, keys)
            queries = jnp.where(mask, q_ref[rows, :], jnp.zeros((), BF16))
            scores = dot(queries, k_ref[:keys, :], (1,), (1,))
            query_pos = start + lax.broadcasted_iota(jnp.int32, scores.shape, 0)
            key_pos = lax.broadcasted_iota(jnp.int32, scores.shape, 1)
            seen = (seg_col_ref[rows, :] == seg_row_ref[0, :, :keys]) & (key_pos <= query_pos)
            scores = jnp.where(seen, scores, NEG)
            peak = jnp.max(scores, axis=1, keepdims=True)
            weights = jnp.exp(scores - peak)
            total = jnp.sum(weights, axis=1, keepdims=True)
            probs = (weights * (1.0 / total)).astype(BF16)
            output = dot(probs, v_ref[:keys, :])
            acc_ref[rows, :] = jnp.where(mask, output, acc_ref[rows, :])
            lse_scratch[rows, :] = jnp.where(
                lse_lane == head, peak + jnp.log(total), lse_scratch[rows, :]
            )

    o_ref[...] = acc_ref[...].astype(BF16)
    lse_ref[0] = lse_scratch[...].T[: lse_ref.shape[1], :]


def attention_forward_exchange_kernel(*refs):
    ins, (blocks_ref, _), outs, all_ref = refs[:5], refs[5:7], refs[7:9], refs[9]
    scratch, sems = refs[10:12], refs[12:]
    exchange_beside(
        lambda: attention_forward_kernel(*ins, *outs, *scratch),
        blocks_ref, all_ref, (1, 3), None, *sems,
    )


def attention_forward(queries, keys, values, segments, blocks=None, partly=None, collective_id=None):
    rows, width = queries.shape
    seqs = rows // SEQ
    block = lambda columns: pl.BlockSpec((SEQ, columns), lambda s: (s, 0))
    in_specs = [block(width)] * 3 + [block(1), pl.BlockSpec((1, 1, SEQ), lambda s: (s, 0, 0))]
    out_specs = [block(width), pl.BlockSpec((1, 8, SEQ), lambda s: (s, 0, 0))]
    out_shape = [
        jax.ShapeDtypeStruct((rows, width), BF16), jax.ShapeDtypeStruct((seqs, 8, SEQ), F32)
    ]
    operands = [queries, keys, values, segments.reshape(rows, 1), segments.reshape(seqs, 1, SEQ)]
    scratch = [pltpu.VMEM((SEQ, width), F32), pltpu.VMEM((SEQ, 128), F32)]
    params, aliases, kernel = {}, {}, attention_forward_kernel
    if blocks is not None:
        anywhere = pl.BlockSpec(memory_space=pl.ANY)
        in_specs, out_specs = in_specs + [anywhere] * 2, out_specs + [anywhere]
        out_shape = out_shape + [jax.ShapeDtypeStruct(blocks.shape, BF16)]
        operands = operands + [blocks, partly]
        scratch = scratch + [pltpu.SemaphoreType.DMA((2,))] * 2
        params = dict(collective_id=collective_id, has_side_effects=True)
        aliases, kernel = {6: 2}, attention_forward_exchange_kernel
    return pl.pallas_call(
        kernel,
        grid=(seqs,),
        in_specs=in_specs,
        out_specs=out_specs,
        out_shape=out_shape,
        scratch_shapes=scratch,
        input_output_aliases=aliases,
        compiler_params=pltpu.CompilerParams(vmem_limit_bytes=56 << 20, **params),
        cost_estimate=taking(21),
        name="attention_forward",
    )(*operands)


def attention_backward_kernel(
    q_ref, k_ref, v_ref, do_ref, lse_ref, cos_ref, sin_ref, seg_col_ref, seg_row_ref,
    grad_ref, sums_ref, dq_ref, dk_ref, dv_ref, halfway=None,
):
    width = q_ref.shape[1]
    heads = width // HEAD_DIM
    full_lane = lax.broadcasted_iota(jnp.int32, (1, width), 1)
    in_head = full_lane % HEAD_DIM
    for ref in (dq_ref, dk_ref, dv_ref):
        ref[...] = jnp.zeros_like(ref)

    def one_head(head):
        mask = full_lane // HEAD_DIM == head
        nothing = jnp.zeros((), BF16)
        for start in range(0, SEQ, 2 * QBLOCK):
            keys = start + 2 * QBLOCK
            rows = slice(start, keys)
            queries = jnp.where(mask, q_ref[rows, :], nothing)
            grads = jnp.where(mask, do_ref[rows, :], nothing)
            scores = dot(k_ref[:keys, :], queries, (1,), (1,))
            key_pos = lax.broadcasted_iota(jnp.int32, scores.shape, 0)
            query_pos = start + lax.broadcasted_iota(jnp.int32, scores.shape, 1)
            seen = (seg_col_ref[:keys, :] == seg_row_ref[0, :, rows]) & (key_pos <= query_pos)
            probs = jnp.where(
                seen, jnp.exp(scores - lse_ref[0, pl.ds(head, 1), rows]), 0.0
            )
            dv_ref[:keys, :] += dot(probs.astype(BF16), grads)
            grad_probs = dot(v_ref[:keys, :], grads, (1,), (1,))
            delta = jnp.sum(probs * grad_probs, axis=0, keepdims=True)
            grad_scores = (probs * (grad_probs - delta)).astype(BF16)
            dk_ref[:keys, :] += dot(grad_scores, queries)
            masked_keys = jnp.where(mask, k_ref[:keys, :], nothing)
            dq_ref[rows, :] += dot(grad_scores, masked_keys, (0,), (0,))

    pl.loop(0, heads // 2)(one_head)
    if halfway is not None:
        halfway()
    pl.loop(heads // 2, heads)(one_head)

    cosine = jnp.tile(cos_ref[...], (1, width // cos_ref.shape[1]))
    sine = jnp.tile(sin_ref[...], (1, width // sin_ref.shape[1]))
    for part, (ref, scale) in enumerate(((dq_ref, SCALE), (dk_ref, 1.0), (dv_ref, None))):
        grad = ref[...]
        if scale is not None:
            grad = grad * scale
            grad = grad * cosine - swap_pairs(grad, in_head) * sine
        low = grad.astype(BF16)
        columns = slice(part * width, (part + 1) * width)
        grad_ref[:, columns] = low
        sums_ref[0, :, columns] = jnp.sum(low.astype(F32), axis=0, keepdims=True)


def attention_backward_sums_kernel(*refs):
    ins, parts_ref, resid_ref = refs[:9], refs[9], refs[10]
    outs, mixed_ref, scratch = refs[11:13], refs[13], refs[14:17]
    load_sem, send_sem, recv_sem, *blocks = refs[17:]
    devices = peers(lax.axis_index("row"), lax.axis_index("col"))
    copies = Copies(send_sem, recv_sem, devices[2])
    mixing = PartsScatter(copies, 0, parts_ref, load_sem, *blocks)
    step = pl.program_id(0)

    @pl.when(step == 0)
    def _():
        meet(devices)
        mixing.start()
        mixing.keep(0, 0)
        mixing.keep(0, 1)

    def halfway():
        @pl.when(step == 0)
        def _():
            for i, h in ((1, 0), (2, 0), (2, 1), (1, 1), (3, 0), (3, 1)):
                mixing.keep(i, h)

        @pl.when(step == 1)
        def _():
            mixing.second()

    attention_backward_kernel(*ins, *outs, *scratch, halfway=halfway)

    @pl.when(step == 1)
    def _():
        mixing.third()
        for start in range(0, mixed_ref.shape[0], STEP):
            at = pl.ds(start, STEP)
            mixed_ref[at, :] = (resid_ref[at, :] + mixing.result(start, STEP)).astype(BF16)
        mixing.drain()


def attention_backward(
    queries, keys, values, grad_out, lse, cosine, sine, segments,
    parts=None, resid=None, collective_id=None,
):
    rows, width = queries.shape
    seqs = rows // SEQ
    block = lambda columns: pl.BlockSpec((SEQ, columns), lambda s: (s, 0))
    in_specs = [block(width)] * 4 + [
        pl.BlockSpec((1, 8, SEQ), lambda s: (s, 0, 0)),
        block(cosine.shape[1]),
        block(cosine.shape[1]),
        block(1),
        pl.BlockSpec((1, 1, SEQ), lambda s: (s, 0, 0)),
    ]
    out_specs = [block(3 * width), pl.BlockSpec((1, 1, 3 * width), lambda s: (s, 0, 0))]
    out_shape = [
        jax.ShapeDtypeStruct((rows, 3 * width), BF16),
        jax.ShapeDtypeStruct((seqs, 1, 3 * width), F32),
    ]
    operands = [
        queries, keys, values, grad_out, lse, cosine, sine,
        segments.reshape(rows, 1), segments.reshape(seqs, 1, SEQ),
    ]
    scratch = [pltpu.VMEM((SEQ, width), F32)] * 3
    params, kernel = {}, attention_backward_kernel
    if parts is not None:
        in_specs = in_specs + [pl.BlockSpec(memory_space=pl.ANY), whole(resid.shape)]
        out_specs = out_specs + [whole(resid.shape)]
        out_shape = out_shape + [jax.ShapeDtypeStruct(resid.shape, BF16)]
        operands = operands + [parts, resid]
        sems = lambda n: pltpu.SemaphoreType.DMA((n,))
        scratch = scratch + [sems(4), sems(PlaneScatter.SEMS), sems(PlaneScatter.SEMS)]
        scratch = scratch + scatter_scratch(*resid.shape)[1:]
        params = dict(collective_id=collective_id, has_side_effects=True)
        kernel = attention_backward_sums_kernel
    return pl.pallas_call(
        kernel,
        grid=(seqs,),
        in_specs=in_specs,
        out_specs=out_specs,
        out_shape=out_shape,
        scratch_shapes=scratch,
        compiler_params=pltpu.CompilerParams(vmem_limit_bytes=60 << 20, **params),
        cost_estimate=taking(42),
        name="attention_backward",
    )(*operands)


def row_pairs():
    return [(r, r ^ 1) for r in range(lax.axis_size("row"))]


def row_lines():
    size = lax.axis_size("row")
    return [list(range(start, size, PAIR)) for start in range(PAIR)]


def neighbours():
    return [list(range(r, r + PAIR)) for r in range(0, lax.axis_size("row"), PAIR)]


def swap_rows(values):
    return lax.ppermute(values, "row", row_pairs())


def after(value, *others):
    return lax.optimization_barrier((value,) + others)[0]


def gather_line(values, axis=0):
    return lax.all_gather(values, "row", axis=axis, tiled=True, axis_index_groups=row_lines())


def scatter_line(values, axis=0):
    return lax.psum_scatter(
        values, "row", scatter_dimension=axis, tiled=True, axis_index_groups=row_lines()
    )


def pick(values, index, axis):
    size = values.shape[axis] // PAIR
    return lax.dynamic_slice_in_dim(values, index * size, size, axis)


def in_order(x, own, other, axis):
    return jnp.where(
        x == 0, jnp.concatenate([own, other], axis), jnp.concatenate([other, own], axis)
    )


def own_columns(weight, x):
    return in_order(x, pick(weight, x, 1), swap_rows(pick(weight, 1 - x, 1)), 0)


def own_units(weight, x):
    kept, sent = pick(weight, x, 1).T, pick(weight, 1 - x, 1).T
    return in_order(x, kept, swap_rows(sent), 1)


def own_rows(grad, x):
    return pick(grad, x, 0), swap_rows(pick(grad, 1 - x, 0))


def places():
    row, col = lax.axis_index("row"), lax.axis_index("col")
    return row % PAIR, col // 2, col % 2, row, col


def peers(row, col):
    x = row % PAIR
    over_x = (row + 1 - 2 * x, col)
    over_y = (row, (col + 2) % 4)
    over_core = (row, col + 1 - 2 * (col % 2))
    return over_x, over_y, over_core


def meet(devices):
    barrier = pltpu.get_barrier_semaphore()
    for device in devices:
        pl.semaphore_signal(barrier, inc=1, device_id=device, device_id_type=MESH)
    pl.semaphore_wait(barrier, len(devices))


def block_at(ref, a, col, rows, width, start, count):
    at = pl.multiple_of(a * rows + start, 128)
    return ref.at[pl.ds(at, count), pl.ds(pl.multiple_of(col * width, 128), width)]


CHUNKS = 4


class Copies:
    def __init__(self, send_sem, recv_sem, over_core):
        self.send_sem, self.recv_sem, self.any = send_sem, recv_sem, over_core
        self.sent = []

    def copy(self, index, source, place, device):
        return pltpu.make_async_remote_copy(
            source, place, self.send_sem.at[index], self.recv_sem.at[index],
            device_id=device, device_id_type=MESH,
        )

    def send(self, index, source, place, device):
        task = self.copy(index, source, place, device)
        task.start()
        self.sent.append(task)

    def wait(self, index, place):
        self.copy(index, place, place, self.any).wait_recv()

    def finish(self):
        for task in self.sent:
            task.wait_send()
        self.sent = []


class PlaneGather:
    def __init__(self, copies, base, src_ref, out_ref, local_sem, over_y=CHUNKS // 2):
        self.copies, self.base, self.src, self.out = copies, base, src_ref, out_ref
        self.local_sem = local_sem
        self.rows, self.width = src_ref.shape
        self.count = self.rows // CHUNKS
        self.x, self.y, self.core, self.row, self.col = places()
        self.over_x, self.over_y, self.over_core = peers(self.row, self.col)
        self.col_y = (self.col + 2) % 4
        self.col_core = self.col + 1 - 2 * self.core
        self.first = list(range(over_y))
        self.second = list(range(over_y, CHUNKS))

    def piece(self, a, c, s):
        return block_at(self.out, a, c, self.rows, self.width, s * self.count, self.count)

    def own(self, s):
        return self.src.at[pl.ds(s * self.count, self.count), :]

    def send(self, group, s, source, place, device):
        self.copies.send(self.base + group * CHUNKS + s, source, place, device)

    def pass_on(self, group, a, c, s, device):
        self.send(group, s, self.piece(a, c, s), self.piece(a, c, s), device)

    def wait(self, group, a, c, s):
        self.copies.wait(self.base + group * CHUNKS + s, self.piece(a, c, s))

    def start_x(self):
        for s in self.first + self.second:
            self.send(0, s, self.own(s), self.piece(self.x, self.col, s), self.over_x)

    def start_y(self):
        for s in self.second + self.first:
            self.send(1, s, self.own(s), self.piece(self.x, self.col, s), self.over_y)

    def start_chunk(self, s):
        self.send(0, s, self.own(s), self.piece(self.x, self.col, s), self.over_x)
        self.send(1, s, self.own(s), self.piece(self.x, self.col, s), self.over_y)
        self.send(4, s, self.own(s), self.piece(self.x, self.col, s), self.over_core)

    def near_in_order(self, s):
        x, col, col_y = self.x, self.col, self.col_y
        self.wait(0, 1 - x, col, s)
        if s in self.first:
            self.pass_on(2, 1 - x, col, s, self.over_y)
        self.pass_on(5, 1 - x, col, s, self.over_core)
        self.wait(1, x, col_y, s)
        if s in self.second:
            self.pass_on(2, x, col_y, s, self.over_x)
        self.pass_on(6, x, col_y, s, self.over_core)

    def keep_own(self):
        self.local = pltpu.make_async_copy(
            self.src, block_at(self.out, self.x, self.col, self.rows, self.width, 0, self.rows),
            self.local_sem,
        )
        self.local.start()

    def start_core(self):
        self.keep_own()
        for s in range(CHUNKS):
            self.send(4, s, self.own(s), self.piece(self.x, self.col, s), self.over_core)

    def near(self, i):
        s, t = (self.first + self.second)[i], (self.second + self.first)[i]
        x, col, col_y = self.x, self.col, self.col_y
        self.wait(0, 1 - x, col, s)
        if s in self.first:
            self.pass_on(2, 1 - x, col, s, self.over_y)
        self.pass_on(5, 1 - x, col, s, self.over_core)
        self.wait(1, x, col_y, t)
        if t in self.second:
            self.pass_on(2, x, col_y, t, self.over_x)
        self.pass_on(6, x, col_y, t, self.over_core)

    def far(self):
        for u in range(CHUNKS):
            self.wait(2, 1 - self.x, self.col_y, u)
            self.pass_on(7, 1 - self.x, self.col_y, u, self.over_core)

    def finish(self):
        other, corner = self.col_core, (self.col_core + 2) % 4
        for group, (a, c) in enumerate(
            ((self.x, other), (1 - self.x, other), (self.x, corner), (1 - self.x, corner))
        ):
            for s in range(CHUNKS):
                self.wait(4 + group, a, c, s)
        self.local.wait()


def gather_plane_kernel(src_ref, out_ref, local_sem, send_sem, recv_sem):
    _, _, _, row, col = places()
    devices = peers(row, col)
    meet(devices)
    copies = Copies(send_sem, recv_sem, devices[2])
    gather = PlaneGather(copies, 0, src_ref, out_ref, local_sem)
    gather.start_x()
    gather.start_y()
    gather.start_core()
    for i in range(CHUNKS):
        gather.near(i)
    gather.far()
    gather.finish()
    copies.finish()


LINES = 4


class LineGather:
    def __init__(self, up_send, up_recv, down_send, down_recv, block):
        self.up, self.down, self.block = (up_send, up_recv), (down_send, down_recv), block
        self.row, self.col = lax.axis_index("row"), lax.axis_index("col")
        self.z = self.row // PAIR

    def task(self, sems, step, source, device):
        send, recv = sems
        place = self.block(source)
        return pltpu.make_async_remote_copy(
            place, place, send.at[step], recv.at[step],
            device_id=(device, self.col), device_id_type=MESH,
        )

    def upward(self, step):
        source = jnp.maximum(self.z - step, 0)
        return self.task(self.up, step, source, jnp.minimum(self.row + PAIR, PAIR * LINES - 1))

    def downward(self, step):
        source = jnp.minimum(self.z + step, LINES - 1)
        return self.task(self.down, step, source, jnp.maximum(self.row - PAIR, 0))

    def start(self, step):
        @pl.when((self.z >= step) & (self.z < LINES - 1))
        def _():
            self.upward(step).start()

        @pl.when((self.z + step < LINES) & (self.z > 0))
        def _():
            self.downward(step).start()

    def receive(self, step):
        @pl.when(self.z >= step)
        def _():
            source = jnp.maximum(self.z - step, 0)
            self.task(self.up, step - 1, source, self.row).wait_recv()

        @pl.when(self.z + step < LINES)
        def _():
            source = jnp.minimum(self.z + step, LINES - 1)
            self.task(self.down, step - 1, source, self.row).wait_recv()

    def hop(self, step):
        self.receive(step)
        if step < LINES - 1:
            self.start(step)

    def finish(self):
        for step in range(LINES - 1):

            @pl.when((self.z >= step) & (self.z < LINES - 1))
            def _():
                self.upward(step).wait_send()

            @pl.when((self.z + step < LINES) & (self.z > 0))
            def _():
                self.downward(step).wait_send()


def gather_first_kernel(
    tokens_ref, grad_ref, query_ref, key_ref, value_ref, out_weight_ref, gate_ref, up_ref,
    gains_ref, places_ref,
    tokens_all_ref, grad_all_ref, qkv_ref, out_all_ref, ffn_ref, gains_all_ref, places_all_ref,
    turned_ref, local_sem, send_sem, recv_sem, swap_send, swap_recv, *line_sems,
):
    x, y, core, row, col = places()
    z = row // PAIR
    over_x, over_y, over_core = peers(row, col)
    over_far = (row, 3 - col)
    size = PAIR * LINES
    meet(
        (
            over_x, over_y, over_core, over_far,
            ((row + PAIR) % size, col), ((row + size - PAIR) % size, col),
        )
    )
    copies = Copies(send_sem, recv_sem, over_core)
    depth, width = out_weight_ref.shape
    half = width // PAIR
    units = ffn_ref.shape[2]
    base = 16 * CHUNKS
    local = []

    def keep(source, place):
        task = pltpu.make_async_copy(source, place, local_sem.at[2 + len(local)])
        task.start()
        local.append(task)

    def part(r, w):
        return qkv_ref.at[
            pl.ds(pl.multiple_of(r * depth, 128), depth), pl.ds(w * half, half)
        ]

    def out_block(z, x):
        return out_all_ref.at[pl.ds(pl.multiple_of((PAIR * z + x) * depth, 128), depth), :]

    def ffn_block(w, x):
        return ffn_ref.at[0, w, :, pl.ds(pl.multiple_of(x * depth, 128), depth)]

    def gains_block(c):
        return gains_all_ref.at[:, pl.ds(pl.multiple_of(c * width, 128), width)]

    def places_block(a):
        rows = places_ref.shape[1]
        return places_all_ref.at[:, pl.ds(pl.multiple_of(a * rows, 128), rows)]

    for w, ref in enumerate((query_ref, key_ref, value_ref)):
        theirs = ref.at[:, pl.ds(pl.multiple_of((1 - x) * half, 128), half)]
        copies.send(base + w, theirs, part(row, w), over_x)
        keep(ref.at[:, pl.ds(pl.multiple_of(x * half, 128), half)], part(row, w))
    keep(out_weight_ref, out_block(z, x))
    keep(gains_ref, gains_block(col))
    keep(places_ref, places_block(x))
    tokens = PlaneGather(copies, 0, tokens_ref, tokens_all_ref, local_sem.at[0], CHUNKS)
    grad = PlaneGather(copies, 8 * CHUNKS, grad_ref, grad_all_ref, local_sem.at[1], CHUNKS)
    tokens.start_y()
    tokens.start_core()
    copies.send(base + 5, places_ref, places_block(x), over_x)
    for i, device in enumerate((over_core, over_y, over_far)):
        copies.send(base + 6 + i, gains_ref, gains_block(col), device)
    for w in range(3):
        local[w].wait()
        copies.wait(base + w, part(row + 1 - 2 * x, w))
    heads = LineGather(
        *line_sems[:4],
        lambda at: qkv_ref.at[pl.ds(pl.multiple_of(at * PAIR * depth, 128), PAIR * depth), :],
    )
    outs = LineGather(*line_sems[4:], lambda at: out_block(at, x))

    def swap_out(z, x):
        block = out_block(z, x)
        return pltpu.make_async_remote_copy(
            block, block, swap_send.at[z], swap_recv.at[z], device_id=over_x, device_id_type=MESH
        )

    def swap_outs(step):
        @pl.when(z >= step)
        def _():
            swap_out(jnp.maximum(z - step, 0), x).start()

        @pl.when(z + step < LINES)
        def _():
            swap_out(jnp.minimum(z + step, LINES - 1), x).start()

    heads.start(0)
    tokens.start_x()
    for w, ref in enumerate((gate_ref, up_ref)):
        for j in range(PAIR * units // 128):
            turned_ref[w, j * 128 : (j + 1) * 128, :] = ref[:, j * 128 : (j + 1) * 128].T
    for i in range(CHUNKS - 1):
        tokens.near(i)
    local[3].wait()
    outs.start(0)
    heads.hop(1)
    tokens.near(CHUNKS - 1)
    for w in range(2):
        theirs = turned_ref.at[w, pl.ds(pl.multiple_of((1 - x) * units, 16), units), :]
        copies.send(base + 3 + w, theirs, ffn_block(w, x), over_x)
        keep(turned_ref.at[w, pl.ds(pl.multiple_of(x * units, 16), units), :], ffn_block(w, x))
    swap_out(z, x).start()
    grad.start_x()
    grad.start_y()
    grad.start_core()
    tokens.far()
    heads.hop(2)
    outs.hop(1)
    swap_outs(1)
    for i in range(CHUNKS - 1):
        grad.near(i)
    heads.hop(3)
    outs.hop(2)
    swap_outs(2)
    grad.near(CHUNKS - 1)
    grad.far()
    outs.hop(3)
    swap_outs(3)
    for at in range(LINES):
        swap_out(at, 1 - x).wait_recv()
    for w in range(2):
        copies.wait(base + 3 + w, ffn_block(w, 1 - x))
    copies.wait(base + 5, places_block(1 - x))
    for i, c in enumerate((col + 1 - 2 * core, (col + 2) % 4, 3 - col)):
        copies.wait(base + 6 + i, gains_block(c))
    for at in range(LINES):
        swap_out(at, x).wait_send()
    for task in local[3 + 1 :]:
        task.wait()
    tokens.finish()
    grad.finish()
    heads.finish()
    outs.finish()
    copies.finish()


def gather_first(
    tokens, grad, query, key, value, out_weight, gate, up, gains, places, collective_id
):
    rows, width = tokens.shape
    depth = out_weight.shape[0]
    units = gate.shape[1] // PAIR
    shape = lambda *dims: jax.ShapeDtypeStruct(dims, BF16)
    sems = lambda n: pltpu.SemaphoreType.DMA((n,))
    return pl.pallas_call(
        gather_first_kernel,
        in_specs=[pl.BlockSpec(memory_space=pltpu.VMEM)] * 10,
        out_specs=[pl.BlockSpec(memory_space=pl.ANY)] * 7,
        out_shape=[
            shape(PAIR * rows, 4 * width), shape(PAIR * rows, 4 * width),
            shape(PAIR * LINES * depth, 3 * width // PAIR), shape(PAIR * LINES * depth, width),
            shape(1, 2, units, PAIR * depth),
            jax.ShapeDtypeStruct((gains.shape[0], 4 * width), F32),
            jax.ShapeDtypeStruct((places.shape[0], PAIR * rows), jnp.int32),
        ],
        scratch_shapes=[
            pltpu.VMEM((2, PAIR * units, depth), BF16),
            sems(10), sems(16 * CHUNKS + 9), sems(16 * CHUNKS + 9), sems(4), sems(4),
        ]
        + [sems(3)] * 8,
        compiler_params=pltpu.CompilerParams(
            collective_id=collective_id, has_side_effects=True, vmem_limit_bytes=60 << 20
        ),
        cost_estimate=taking(110),
        name="gather_first",
    )(tokens, grad, query, key, value, out_weight, gate, up, gains, places)


def gather_plane(values, name, collective_id):
    cols = lax.axis_size("col")
    if cols != 4:
        across = lax.all_gather(values, "col", axis=1, tiled=True)
        return lax.all_gather(across, "row", axis=0, tiled=True, axis_index_groups=neighbours())
    rows, width = values.shape
    return pl.pallas_call(
        gather_plane_kernel,
        in_specs=[pl.BlockSpec(memory_space=pltpu.VMEM)],
        out_specs=pl.BlockSpec(memory_space=pl.ANY),
        out_shape=jax.ShapeDtypeStruct((PAIR * rows, cols * width), values.dtype),
        scratch_shapes=[
            pltpu.SemaphoreType.DMA,
            pltpu.SemaphoreType.DMA((8 * CHUNKS,)),
            pltpu.SemaphoreType.DMA((8 * CHUNKS,)),
        ],
        cost_estimate=taking(40),
        compiler_params=pltpu.CompilerParams(collective_id=collective_id, has_side_effects=True),
        name=name,
    )(values)


def add_rows(out_ref, left_ref, right_ref, rows, step=64):
    @pl.loop(0, rows // step)
    def _(i):
        at = pl.ds(pl.multiple_of(i * step, step), step)
        total = left_ref[at, :].astype(F32) + right_ref[at, :].astype(F32)
        out_ref[at, :] = total.astype(out_ref.dtype)


def scatter_plane_kernel(
    part_ref, out_ref, own_ref, core_ref, x_ref, y_ref, last_ref,
    load_sem, send_sem, recv_sem,
):
    rows, width = own_ref.shape[1:]
    half = rows // 2
    x, y, core, row, col = places()
    over_x, over_y, over_core = peers(row, col)
    meet((over_x, over_y, over_core))
    top, bottom = pl.ds(0, half), pl.ds(half, half)

    def copy(index, source, place, device):
        return pltpu.make_async_remote_copy(
            source, place, send_sem.at[index], recv_sem.at[index],
            device_id=device, device_id_type=MESH,
        )

    sent = []

    def send(index, source, place, device):
        task = copy(index, source, place, device)
        task.start()
        sent.append(task)

    def wait(index, place):
        copy(index, place, place, over_core).wait_recv()

    order = ((1 - x, 1 - y), (1 - x, y), (x, 1 - y), (x, y))
    loads = []
    for i, (a, b) in enumerate(order):
        slot = 2 * a + b
        send(
            i, block_at(part_ref, a, 2 * b + 1 - core, rows, width, 0, rows),
            core_ref.at[slot], over_core,
        )
        load = pltpu.make_async_copy(
            block_at(part_ref, a, 2 * b + core, rows, width, 0, rows),
            own_ref.at[slot], load_sem.at[i],
        )
        load.start()
        loads.append(load)
    for i, (a, b) in enumerate(order):
        slot = 2 * a + b
        loads[i].wait()
        wait(i, core_ref.at[slot])
        add_rows(own_ref.at[slot], own_ref.at[slot], core_ref.at[slot], rows)
        if i in (0, 1):
            send(4 + i, own_ref.at[slot, top, :], x_ref.at[i], over_x)
        if i in (0, 2):
            send(6 + i // 2, own_ref.at[slot, bottom, :], y_ref.at[i // 2], over_y)
    wait(4, x_ref.at[0])
    slot = 2 * x + 1 - y
    add_rows(own_ref.at[slot, top, :], own_ref.at[slot, top, :], x_ref.at[0], half)
    send(8, own_ref.at[slot, top, :], last_ref.at[0], over_y)
    wait(6, y_ref.at[0])
    slot = 2 * (1 - x) + y
    add_rows(own_ref.at[slot, bottom, :], own_ref.at[slot, bottom, :], y_ref.at[0], half)
    send(9, own_ref.at[slot, bottom, :], last_ref.at[1], over_x)
    slot = 2 * x + y
    wait(5, x_ref.at[1])
    add_rows(own_ref.at[slot, top, :], own_ref.at[slot, top, :], x_ref.at[1], half)
    wait(7, y_ref.at[1])
    add_rows(own_ref.at[slot, bottom, :], own_ref.at[slot, bottom, :], y_ref.at[1], half)
    wait(8, last_ref.at[0])
    add_rows(out_ref.at[top, :], own_ref.at[slot, top, :], last_ref.at[0], half)
    wait(9, last_ref.at[1])
    add_rows(out_ref.at[bottom, :], own_ref.at[slot, bottom, :], last_ref.at[1], half)
    for task in sent:
        task.wait_send()


def scatter_plane(values, name, collective_id):
    cols = lax.axis_size("col")
    if cols != 4:
        mine = lax.psum_scatter(
            values, "row", scatter_dimension=0, tiled=True, axis_index_groups=neighbours()
        )
        return lax.psum_scatter(mine, "col", scatter_dimension=1, tiled=True).astype(F32)
    rows, width = values.shape[0] // PAIR, values.shape[1] // cols
    return pl.pallas_call(
        scatter_plane_kernel,
        in_specs=[pl.BlockSpec(memory_space=pl.ANY)],
        out_specs=pl.BlockSpec(memory_space=pltpu.VMEM),
        out_shape=jax.ShapeDtypeStruct((rows, width), F32),
        scratch_shapes=[
            pltpu.VMEM((4, rows, width), BF16),
            pltpu.VMEM((4, rows, width), BF16),
            pltpu.VMEM((2, rows // 2, width), BF16),
            pltpu.VMEM((2, rows // 2, width), BF16),
            pltpu.VMEM((2, rows // 2, width), BF16),
            pltpu.SemaphoreType.DMA((4,)),
            pltpu.SemaphoreType.DMA((10,)),
            pltpu.SemaphoreType.DMA((10,)),
        ],
        cost_estimate=taking(40),
        compiler_params=pltpu.CompilerParams(
            collective_id=collective_id, has_side_effects=True, vmem_limit_bytes=40 << 20
        ),
        name=name,
    )(values)


def gather_heads(values, x):
    here = in_order(x, pick(values, x, 0), swap_rows(pick(values, 1 - x, 0)), 1)
    return lax.all_gather(here, "col", axis=1, tiled=True)


def scatter_heads(values, x):
    mine = lax.psum_scatter(values, "col", scatter_dimension=1, tiled=True)
    return in_order(x, pick(mine, x, 1), swap_rows(pick(mine, 1 - x, 1)), 0)


def project_out_kernel(
    heads_ref, weight_ref, tokens_ref, all_ref, resid_ref, resid_all_ref,
    joined_ref, low_ref, local_sem, send_sem, recv_sem,
):
    rows, width = resid_ref.shape
    part = heads_ref.shape[1]
    x, y, core, row, col = places()
    over_x, over_y, over_core = peers(row, col)
    count = rows // CHUNKS
    col_y, col_core = (col + 2) % 4, col + 1 - 2 * core
    corner = (col_core + 2) % 4
    meet((over_x, over_y, over_core))
    copies = Copies(send_sem, recv_sem, over_core)
    base = 8 * CHUNKS

    def piece(c, a, s):
        at = pl.multiple_of((PAIR * c + a) * part, 128)
        return joined_ref.at[pl.ds(s * count, count), pl.ds(at, part)]

    def mine(a, s):
        return heads_ref.at[pl.ds(pl.multiple_of(a * rows + s * count, 128), count), :]

    def send(group, s, source, place, device):
        copies.send(base + group * CHUNKS + s, source, place, device)

    def pass_on(group, s, place, device):
        send(group, s, place, place, device)

    def wait(group, s, place):
        copies.wait(base + group * CHUNKS + s, place)

    local = []
    for s in range(CHUNKS):
        send(0, s, mine(1 - x, s), piece(col, x, s), over_x)
        send(1, s, mine(x, s), piece(col, x, s), over_y)
        send(2, s, mine(x, s), piece(col, x, s), over_core)
        task = pltpu.make_async_copy(mine(x, s), piece(col, x, s), local_sem.at[s])
        task.start()
        local.append(task)
    gather = PlaneGather(copies, 0, low_ref, resid_all_ref, local_sem.at[CHUNKS])

    def relay(s):
        wait(0, s, piece(col, 1 - x, s))
        pass_on(3, s, piece(col, 1 - x, s), over_y)
        pass_on(4, s, piece(col, 1 - x, s), over_core)

    relay(0)
    for s in range(CHUNKS):
        if s + 1 < CHUNKS:
            relay(s + 1)
        wait(1, s, piece(col_y, x, s))
        pass_on(5, s, piece(col_y, x, s), over_core)
        wait(3, s, piece(col_y, 1 - x, s))
        pass_on(6, s, piece(col_y, 1 - x, s), over_core)
        wait(2, s, piece(col_core, x, s))
        wait(4, s, piece(col_core, 1 - x, s))
        wait(5, s, piece(corner, x, s))
        wait(6, s, piece(corner, 1 - x, s))
        local[s].wait()
        at = pl.ds(s * count, count)
        result = tokens_ref[at, :].astype(F32) + dot(joined_ref[at, :], weight_ref[...])
        resid_ref[at, :] = result
        low_ref[at, :] = result.astype(BF16)
        gather.start_chunk(s)
    store = pltpu.make_async_copy(joined_ref, all_ref, local_sem.at[CHUNKS + 1])
    store.start()
    gather.keep_own()
    for s in range(CHUNKS):
        gather.near_in_order(s)
    gather.far()
    gather.finish()
    copies.finish()
    store.wait()


def project_out(heads, weight, tokens, collective_id):
    rows, width = tokens.shape
    vmem, anywhere = pl.BlockSpec(memory_space=pltpu.VMEM), pl.BlockSpec(memory_space=pl.ANY)
    sems = lambda n: pltpu.SemaphoreType.DMA((n,))
    return pl.pallas_call(
        project_out_kernel,
        in_specs=[vmem] * 3,
        out_specs=[anywhere, vmem, anywhere],
        out_shape=[
            jax.ShapeDtypeStruct((rows, 4 * width), BF16),
            jax.ShapeDtypeStruct((rows, width), F32),
            jax.ShapeDtypeStruct((PAIR * rows, 4 * width), BF16),
        ],
        scratch_shapes=[
            pltpu.VMEM((rows, 4 * width), BF16), pltpu.VMEM((rows, width), BF16),
            sems(CHUNKS + 2), sems(15 * CHUNKS), sems(15 * CHUNKS),
        ],
        compiler_params=pltpu.CompilerParams(
            collective_id=collective_id, has_side_effects=True, vmem_limit_bytes=60 << 20
        ),
        cost_estimate=taking(66),
        name="project_out",
    )(heads, weight, tokens)


class RowSum:
    def __init__(self, copies, base, slots_ref):
        self.copies, self.base, self.slots = copies, base, slots_ref
        self.row, self.col = lax.axis_index("row"), lax.axis_index("col")
        self.size = slots_ref.shape[0]
        self.others = [((self.row + step) % self.size, self.col) for step in range(1, self.size)]

    def start(self):
        for step, device in enumerate(self.others, 1):
            self.copies.send(self.base + step - 1, self.slots.at[0], self.slots.at[step], device)

    def finish(self):
        for step in range(1, self.size):
            self.copies.wait(self.base + step - 1, self.slots.at[step])
        total = jnp.zeros(self.slots.shape[1:], F32)
        for r in range(self.size):
            total += self.slots[(self.row + self.size - r) % self.size]
        return total


def row_stats(values):
    mean = jnp.mean(values, axis=1, keepdims=True)
    var = jnp.mean(values * values, axis=1, keepdims=True) - mean * mean
    return mean, lax.rsqrt(var + 1e-05)


def norm_backward(grad_norm, unit_values, inv_std, norm_gain):
    full_width = grad_norm.shape[1] * lax.axis_size("col")
    grad_unit = grad_norm * norm_gain
    row_sums = lax.psum(
        (jnp.sum(grad_unit, axis=1), jnp.sum(grad_unit * unit_values, axis=1)), "col"
    )
    grad_in = inv_std * (
        grad_unit
        - row_sums[0][:, None] / full_width
        - unit_values * row_sums[1][:, None] / full_width
    )
    return grad_in, jnp.sum(grad_norm * unit_values, axis=0)


def rotation_tables(positions):
    half = ROT // 2
    inv_freq = BASE ** (-(jnp.arange(half, dtype=F32) * 2.0) / ROT)
    angles = positions.astype(F32)[:, None] * inv_freq[None, :]
    cosine, sine = jnp.cos(angles), jnp.sin(angles)
    rest = HEAD_DIM - ROT
    ones = jnp.ones((positions.shape[0], rest), F32)
    cosine = jnp.concatenate([cosine, cosine, ones], axis=1)
    sine = jnp.concatenate([-sine, sine, 0.0 * ones], axis=1)
    return jnp.tile(cosine, (1, 2)), jnp.tile(sine, (1, 2))


TILE = 256


def norm_tile(values_ref, gain_ref, row, stats_ref):
    values = values_ref[...].astype(F32)
    mean, inv_std = row_stats(values)
    gain = gain_ref[row : row + 1, :]
    lane = lax.broadcasted_iota(jnp.int32, stats_ref.shape, 1)
    stats_ref[...] = jnp.where(lane == 0, mean, inv_std)
    return ((values - mean) * inv_std * gain).astype(BF16)


def project_heads_kernel(
    tokens_ref, gain_ref, weight_ref, bias_ref, cos_ref, sin_ref,
    normed_ref, q_ref, k_ref, v_ref, stats_ref,
):
    width = q_ref.shape[1]
    normed = norm_tile(tokens_ref, gain_ref, 0, stats_ref)
    normed_ref[...] = normed
    in_head = lax.broadcasted_iota(jnp.int32, (1, width), 1) % HEAD_DIM
    cosine = jnp.tile(cos_ref[...], (1, width // cos_ref.shape[1]))
    sine = jnp.tile(sin_ref[...], (1, width // sin_ref.shape[1]))
    pre = dot(normed, weight_ref[...]) + bias_ref[...]
    for ref, at, scale in ((q_ref, 0, SCALE), (k_ref, width, 1.0)):
        part = pre[:, at : at + width]
        turned = part * cosine + swap_pairs(part, in_head) * sine
        ref[...] = turned.astype(BF16) * jnp.asarray(scale, BF16)
    v_ref[...] = pre[:, 2 * width :].astype(BF16)


def tiled(columns):
    return pl.BlockSpec((TILE, columns), lambda i: (i, 0))


def whole(shape):
    return pl.BlockSpec(shape, lambda i: (0,) * len(shape))


def column_block(blocks_ref, all_ref, other, sems, index):
    row, col = lax.axis_index("row"), lax.axis_index("col")
    send_sem, recv_sem = sems
    return pltpu.make_async_remote_copy(
        blocks_ref.at[other], all_ref.at[col], send_sem.at[index], recv_sem.at[index],
        device_id=(row, other), device_id_type=MESH,
    )


def exchange_beside(kernel, blocks_ref, all_ref, steps, local, *sems, more=()):
    row, col = lax.axis_index("row"), lax.axis_index("col")
    others = [col + d - 2 * d * ((col // d) % 2) if d < 3 else 3 - col for d in steps]

    @pl.when(pl.program_id(0) == 0)
    def _():
        meet([(row, other) for other in others] + list(more))
        for i, other in enumerate(others):
            column_block(blocks_ref, all_ref, other, sems, i).start()
        if local is not None:
            pltpu.make_async_copy(blocks_ref.at[col], *local).start()

    kernel()

    @pl.when(pl.program_id(0) == pl.num_programs(0) - 1)
    def _():
        if local is not None:
            stage, local_sem = local
            pltpu.make_async_copy(blocks_ref.at[col], stage, local_sem).wait()
            task = pltpu.make_async_copy(stage, all_ref.at[col], local_sem)
            task.start()
            task.wait()
        for i, other in enumerate(others):
            task = column_block(blocks_ref, all_ref, other, sems, i)
            task.wait_send()
            send_sem, recv_sem = sems
            pltpu.make_async_remote_copy(
                blocks_ref.at[other], all_ref.at[other], send_sem.at[i], recv_sem.at[i],
                device_id=(row, other), device_id_type=MESH,
            ).wait_recv()


def project_heads_exchange_kernel(*refs):
    *ins, blocks_ref = refs[:7]
    outs, all_ref, (stage, local_sem, *sems) = refs[7:12], refs[12], refs[13:]
    exchange_beside(
        lambda: project_heads_kernel(*ins, *outs),
        blocks_ref, all_ref, (2,), (stage, local_sem), *sems,
    )


def project_heads(tokens, gains, weight, bias, cosine, sine, blocks=None, collective_id=None):
    rows, depth = tokens.shape
    width = weight.shape[1] // 3
    in_specs = [
        tiled(depth), whole(gains.shape), whole(weight.shape), whole((1, 3 * width)),
        tiled(cosine.shape[1]), tiled(cosine.shape[1]),
    ]
    out_specs = [tiled(depth)] + [tiled(width)] * 3 + [tiled(8)]
    out_shape = [
        jax.ShapeDtypeStruct((rows, depth), BF16),
        *[jax.ShapeDtypeStruct((rows, width), BF16)] * 3,
        jax.ShapeDtypeStruct((rows, 8), F32),
    ]
    operands = [tokens, gains, weight, bias.reshape(1, 3 * width), cosine, sine]
    params, scratch, kernel = {}, [], project_heads_kernel
    if blocks is not None:
        anywhere = pl.BlockSpec(memory_space=pl.ANY)
        in_specs, out_specs = in_specs + [anywhere], out_specs + [anywhere]
        out_shape = out_shape + [jax.ShapeDtypeStruct(blocks.shape, BF16)]
        operands = operands + [blocks]
        scratch = [pltpu.VMEM(blocks.shape[1:], BF16), pltpu.SemaphoreType.DMA]
        scratch = scratch + [pltpu.SemaphoreType.DMA((1,))] * 2
        params = dict(collective_id=collective_id, has_side_effects=True)
        kernel = project_heads_exchange_kernel
    return pl.pallas_call(
        kernel,
        grid=(rows // TILE,),
        in_specs=in_specs,
        out_specs=out_specs,
        out_shape=out_shape,
        scratch_shapes=scratch,
        compiler_params=pltpu.CompilerParams(vmem_limit_bytes=60 << 20, **params),
        cost_estimate=taking(16),
        name="project_heads",
    )(*operands)


def feed_forward_kernel(
    resid_ref, gain_ref, weight_ref, grad_ref, down_ref,
    normed_ref, hidden_ref, dgate_ref, dup_ref, stats_ref,
):
    lines, _, hidden, width = weight_ref.shape
    normed_ref[...] = norm_tile(resid_ref, gain_ref, 1, stats_ref)
    gate = jnp.zeros((hidden, TILE), F32)
    up = jnp.zeros((hidden, TILE), F32)
    dhidden = jnp.zeros((hidden, TILE), F32)
    for z in range(lines):
        part = normed_ref[:, z * width : (z + 1) * width]
        gate += dot(weight_ref[z, 0], part, (1,), (1,))
        up += dot(weight_ref[z, 1], part, (1,), (1,))
    for c in range(down_ref.shape[0]):
        part = grad_ref[:, c * width : (c + 1) * width]
        dhidden += dot(down_ref[c], part, (1,), (1,))
    sigmoid = 1.0 / (1.0 + jnp.exp(-gate))
    silu = gate * sigmoid
    hidden_ref[...] = (silu * up).astype(BF16)
    dgate_ref[...] = (dhidden * up * sigmoid * (1.0 + gate * (1.0 - sigmoid))).astype(BF16)
    dup_ref[...] = (dhidden * silu).astype(BF16)


def feed_forward(resid, gains, weight, grad, down):
    rows, depth = resid.shape
    hidden = down.shape[1]
    across = pl.BlockSpec((hidden, TILE), lambda i: (0, i))
    return pl.pallas_call(
        feed_forward_kernel,
        grid=(rows // TILE,),
        in_specs=[
            tiled(depth), whole(gains.shape), whole(weight.shape), tiled(depth), whole(down.shape)
        ],
        out_specs=[tiled(depth)] + [across] * 3 + [tiled(8)],
        out_shape=[jax.ShapeDtypeStruct((rows, depth), BF16)]
        + [jax.ShapeDtypeStruct((hidden, rows), BF16)] * 3
        + [jax.ShapeDtypeStruct((rows, 8), F32)],
        compiler_params=pltpu.CompilerParams(vmem_limit_bytes=56 << 20),
        cost_estimate=taking(28),
        name="feed_forward",
    )(resid, gains, weight, grad, down)


def weight_grads_kernel(*refs):
    *left_refs, right_ref, out_ref = refs
    for i, left_ref in enumerate(left_refs):
        out_ref[0, i] = dot(left_ref[...], right_ref[...]).astype(BF16)


def weight_grads(lefts, right, width, name):
    hidden, rows = lefts[0].shape
    blocks = right.shape[1] // width
    return pl.pallas_call(
        weight_grads_kernel,
        grid=(blocks,),
        in_specs=[whole((hidden, rows))] * len(lefts)
        + [pl.BlockSpec((rows, width), lambda i: (0, i))],
        out_specs=pl.BlockSpec((1, len(lefts), hidden, width), lambda i: (i, 0, 0, 0)),
        out_shape=jax.ShapeDtypeStruct((blocks, len(lefts), hidden, width), BF16),
        compiler_params=pltpu.CompilerParams(vmem_limit_bytes=56 << 20),
        cost_estimate=taking(9 * len(lefts)),
        name=name,
    )(*lefts, right)


def back_project_kernel(*refs):
    *left_refs, weight_ref, out_ref = refs
    width = weight_ref.shape[-1]
    lefts = [ref[...].T for ref in left_refs]
    for z in range(weight_ref.shape[0]):
        total = sum(dot(left, weight_ref[z, i]) for i, left in enumerate(lefts))
        out_ref[:, z * width : (z + 1) * width] = total.astype(BF16)


def back_project(lefts, weight, name):
    hidden, rows = lefts[0].shape
    depth = weight.shape[0] * weight.shape[-1]
    return pl.pallas_call(
        back_project_kernel,
        grid=(rows // TILE,),
        in_specs=[pl.BlockSpec((hidden, TILE), lambda i: (0, i))] * len(lefts)
        + [whole(weight.shape)],
        out_specs=tiled(depth),
        out_shape=jax.ShapeDtypeStruct((rows, depth), BF16),
        compiler_params=pltpu.CompilerParams(vmem_limit_bytes=48 << 20),
        cost_estimate=taking(10 * len(lefts)),
        name=name,
    )(*lefts, weight)


class PlaneScatter:
    SEMS = 14

    def __init__(self, copies, base, fill, sent_ref, own_ref, core_ref, x_ref, y_ref, last_ref):
        self.copies, self.base, self.fill = copies, base, fill
        self.sent, self.own, self.core_part = sent_ref, own_ref, core_ref
        self.x_ref, self.y_ref, self.last = x_ref, y_ref, last_ref
        self.x, self.y, self.core, row, col = places()
        self.over_x, self.over_y, self.over_core = peers(row, col)
        x, y = self.x, self.y
        self.order = ((1 - x, 1 - y), (1 - x, y), (x, 1 - y), (x, y))
        self.theirs = [2 * b + 1 - self.core for _, b in self.order]
        self.ours = [2 * b + self.core for _, b in self.order]
        self.half = own_ref.shape[1] // 2
        self.rows = (pl.ds(0, self.half), pl.ds(self.half, self.half))
        self.given = Copies(copies.send_sem, copies.recv_sem, self.over_core)

    def send(self, index, source, place, device):
        self.copies.send(self.base + index, source, place, device)

    def wait(self, index, place):
        self.copies.wait(self.base + index, place)

    def give(self, i, h):
        a, _ = self.order[i]
        self.fill(self.sent.at[i], a, self.theirs[i], h, None)
        at = self.rows[h]
        self.given.send(
            self.base + 2 * i + h, self.sent.at[i, at, :], self.core_part.at[i, at, :], self.over_core
        )

    def keep(self, i, h):
        a, _ = self.order[i]
        at = self.rows[h]
        self.wait(2 * i + h, self.core_part.at[i, at, :])
        self.fill(self.own.at[i], a, self.ours[i], h, self.core_part.at[i])
        self.part_done(i, h)

    def part_done(self, i, h):
        at = self.rows[h]
        if h == 0 and i in (0, 1):
            self.send(8 + i, self.own.at[i, at, :], self.x_ref.at[i], self.over_x)
        if h == 1 and i in (0, 2):
            self.send(10 + i // 2, self.own.at[i, at, :], self.y_ref.at[i // 2], self.over_y)

    def begin(self):
        self.give(0, 0)
        self.give(0, 1)
        self.keep(0, 0)
        self.keep(0, 1)

    def proceed(self):
        for h in range(2):
            self.give(1, h)
            self.give(2, h)
        self.keep(1, 0)
        self.keep(2, 1)

    def complete(self):
        self.keep(2, 0)
        self.keep(1, 1)
        for h in range(2):
            self.give(3, h)
        for h in range(2):
            self.keep(3, h)

    def settle(self):
        self.given.finish()

    def drain(self):
        view = self.own.at[0, self.rows[0], :]
        for index in range(self.SEMS):
            self.copies.copy(self.base + index, view, view, self.over_core).wait_send()

    def add(self, i, h, ref):
        at = self.own.at[i, self.rows[h], :]
        add_rows(at, at, ref, self.half)

    def second(self):
        self.wait(8, self.x_ref.at[0])
        self.add(2, 0, self.x_ref.at[0])
        self.send(12, self.own.at[2, self.rows[0], :], self.last.at[0], self.over_y)
        self.wait(10, self.y_ref.at[0])
        self.add(1, 1, self.y_ref.at[0])
        self.send(13, self.own.at[1, self.rows[1], :], self.last.at[1], self.over_x)
        self.wait(9, self.x_ref.at[1])
        self.add(3, 0, self.x_ref.at[1])
        self.wait(11, self.y_ref.at[1])
        self.add(3, 1, self.y_ref.at[1])

    def third(self):
        self.wait(12, self.last.at[0])
        self.wait(13, self.last.at[1])

    def result(self, start, count):
        h, other = divmod(start, self.half)
        return self.own[3, pl.ds(start, count), :].astype(F32) + self.last[
            h, pl.ds(other, count), :
        ].astype(F32)


class PartsScatter(PlaneScatter):
    def __init__(self, copies, base, parts_ref, load_sem, *scratch):
        super().__init__(copies, base, None, None, *scratch)
        blocks = [a * 4 for a, _ in self.order]
        self.parts, self.load_sem = parts_ref, load_sem
        self.sources = [parts_ref.at[at + c] for at, c in zip(blocks, self.theirs)]
        self.loads = [
            pltpu.make_async_copy(parts_ref.at[at + c], self.own.at[i], load_sem.at[i])
            for i, (at, c) in enumerate(zip(blocks, self.ours))
        ]

    def start(self):
        for i, load in enumerate(self.loads):
            load.start()
            for h, at in enumerate(self.rows):
                self.given.send(
                    self.base + 2 * i + h, self.sources[i].at[at, :],
                    self.core_part.at[i, at, :], self.over_core,
                )

    def keep(self, i, h):
        if h == 0:
            self.loads[i].wait()
        at = self.rows[h]
        self.wait(2 * i + h, self.core_part.at[i, at, :])
        self.add(i, h, self.core_part.at[i, at, :])
        self.part_done(i, h)


class LineScatter:
    def __init__(self, up_send, up_recv, down_send, down_recv, part, up_ref, down_ref):
        self.part, self.row, self.col = part, lax.axis_index("row"), lax.axis_index("col")
        self.z = self.row // PAIR
        last = LINES - 1
        self.ways = (
            (self.z, lambda n: n, up_ref, up_send, up_recv, jnp.minimum(self.row + PAIR, PAIR * last + PAIR - 1)),
            (last - self.z, lambda n: last - n, down_ref, down_send, down_recv, jnp.maximum(self.row - PAIR, 0)),
        )

    def clear(self):
        for n, _, slots, _, _, _ in self.ways:

            @pl.when(n == 0)
            def _():
                slots[LINES - 2] = jnp.zeros(slots.shape[1:], slots.dtype)

    def task(self, way, step, source):
        _, _, slots, send, recv, device = way
        return pltpu.make_async_remote_copy(
            source, slots.at[step], send.at[step], recv.at[step],
            device_id=(device, self.col), device_id_type=MESH,
        )

    def sends(self, way, step, act):
        n, place, slots, _, _, _ = way

        @pl.when(n == 0)
        def _():
            act(self.task(way, step, self.part(place(LINES - 1 - step))))

        if step > 0:

            @pl.when((n > 0) & (n <= step))
            def _():
                act(self.task(way, step, slots.at[step - 1]))

    def start(self):
        for way in self.ways:
            self.sends(way, 0, lambda task: task.start())

    def hop(self, step):
        for way in self.ways:
            n, place, slots, _, _, _ = way

            @pl.when((n >= 1) & (n <= step + 1))
            def _():
                self.task(way, step, slots.at[step]).wait_recv()
                add_rows(
                    slots.at[step], slots.at[step], self.part(place(LINES - 2 - step + n)),
                    slots.shape[1],
                )

            self.sends(way, step + 1, lambda task: task.start())

    def receive(self):
        last = LINES - 2
        for way in self.ways:
            n, _, slots, _, _, _ = way

            @pl.when(n >= 1)
            def _():
                self.task(way, last, slots.at[last]).wait_recv()

    def total(self, at):
        last = LINES - 2
        result = self.part(self.z)[at, :].astype(F32)
        for _, _, slots, _, _, _ in self.ways:
            result = result + slots[last, at, :].astype(F32)
        return result

    def finish(self):
        for way in self.ways:
            for step in range(LINES - 1):
                self.sends(way, step, lambda task: task.wait_send())


STEP = 128


class NormBack:
    def __init__(
        self, copies, base, values_ref, stats_ref, gain_ref, base_ref, out_ref, low_ref, dgain_ref,
        sums_ref,
    ):
        self.copies, self.base = copies, base
        self.values, self.stats, self.gain, self.more = values_ref, stats_ref, gain_ref, base_ref
        self.out, self.low, self.dgain, self.sums = out_ref, low_ref, dgain_ref, sums_ref

    def stats_of(self, start):
        at = places()[0] * self.out.shape[0] + start
        return self.stats[pl.ds(pl.multiple_of(at, STEP), STEP), :]

    def unit_of(self, start):
        stats = self.stats_of(start)
        values = self.values[pl.ds(start, STEP), :].astype(F32)
        return (values - stats[:, 0:1]) * stats[:, 1:2]

    def start(self, result, devices):
        lane = lax.broadcasted_iota(jnp.int32, (1, 128), 1)
        self.dgain[...] = jnp.zeros_like(self.dgain)
        for start in range(0, self.out.shape[0], STEP):
            at = pl.ds(start, STEP)
            grad = result(start, STEP)
            self.out[at, :] = grad
            unit = self.unit_of(start)
            self.dgain[...] += jnp.sum(grad * unit, axis=0, keepdims=True)
            grad = grad * self.gain[...]
            first = jnp.sum(grad, axis=1, keepdims=True)
            second = jnp.sum(grad * unit, axis=1, keepdims=True)
            both = jnp.where(lane == 0, first, jnp.where(lane == 1, second, 0.0))
            self.sums[0, :, start : start + STEP] = both.T[:8]
        for i, device in enumerate(devices):
            self.copies.send(self.base + i, self.sums.at[0], self.sums.at[1 + i], device)

    def finish(self):
        rows, width = self.out.shape
        for i in range(3):
            self.copies.wait(self.base + i, self.sums.at[1 + i])
        for start in range(0, rows, STEP):
            at = pl.ds(start, STEP)
            columns = slice(start, start + STEP)
            total = (self.sums[0, :, columns] + self.sums[1, :, columns]) + (
                self.sums[2, :, columns] + self.sums[3, :, columns]
            )
            total = jnp.concatenate([total, jnp.zeros((STEP - 8, STEP), F32)], axis=0).T
            total = total * (1.0 / (4 * width))
            unit = self.unit_of(start)
            grad = self.out[at, :] * self.gain[...]
            grad = self.stats_of(start)[:, 1:2] * (grad - total[:, 0:1] - unit * total[:, 1:2])
            grad = grad + self.more[at, :].astype(F32)
            self.out[at, :] = grad
            if self.low is not None:
                self.low[at, :] = grad.astype(BF16)


def scatter_scratch(rows, width):
    block = lambda n, r: pltpu.VMEM((n, r, width), BF16)
    return [
        block(4, rows), block(4, rows), block(4, rows),
        block(2, rows // 2), block(2, rows // 2), block(2, rows // 2),
    ]


def around():
    _, _, _, row, col = places()
    over_x, over_y, over_core = peers(row, col)
    return over_x, over_y, over_core, (row, 3 - col)


def filling(rows, product):
    half = rows // 2

    def fill(ref, a, c, h, more):
        @pl.loop(0, half // TILE)
        def _(i):
            start = h * half + i * TILE
            total = product(pl.ds(pl.multiple_of(a * rows + start, TILE), TILE), c)
            at = pl.ds(pl.multiple_of(start, TILE), TILE)
            if more is not None:
                total = total + more[at, :].astype(F32)
            ref[at, :] = total.astype(BF16)

    return fill


def turn_rows(left_ref, source_ref, a, rows):
    @pl.loop(0, rows // TILE)
    def _(i):
        at = pl.ds(pl.multiple_of(a * rows + i * TILE, TILE), TILE)
        left_ref[at, :] = source_ref[:, at].T


def back_second_kernel(
    gate_ref, up_ref, weight_ref, hidden_hbm, grad_hbm, values_ref, stats_ref, gain_ref, base_ref,
    out_ref, low_ref, dgain_ref, down_ref,
    hidden_ref, grad_ref, gate_vmem, up_vmem, weight_vmem, left_ref, sums_ref, load_sem, send_sem, recv_sem, *scratch,
):
    rows, width = out_ref.shape
    x, y, core, _, _ = places()
    devices = around()

    def load_left(i, a):
        at = pl.ds(pl.multiple_of(a * rows, TILE), rows)
        return [
            pltpu.make_async_copy(ref.at[:, at], vmem.at[:, at], load_sem.at[2 * i + j])
            for j, (ref, vmem) in enumerate(((gate_ref, gate_vmem), (up_ref, up_vmem)))
        ]

    def load_weight(i, c):
        return pltpu.make_async_copy(weight_ref.at[c], weight_vmem.at[c], load_sem.at[4 + i])

    lefts = [load_left(0, 1 - x), load_left(1, x)]
    columns = (2 * (1 - y) + 1 - core, 2 * (1 - y) + core, 2 * y + 1 - core, 2 * y + core)
    weights = [load_weight(i, c) for i, c in enumerate(columns)]
    others = [
        pltpu.make_async_copy(hidden_hbm, hidden_ref, load_sem.at[8]),
        pltpu.make_async_copy(grad_hbm, grad_ref, load_sem.at[9]),
    ]
    for task in (*lefts[0], *weights, *lefts[1], *others):
        task.start()
    meet(devices)
    copies = Copies(send_sem, recv_sem, devices[2])

    def turn(i, a):
        for j, (task, vmem) in enumerate(zip(lefts[i], (gate_vmem, up_vmem))):
            task.wait()
            turn_rows(left_ref.at[j], vmem, a, rows)

    def product(at, c):
        return dot(left_ref[0, at, :], weight_vmem[c, 0]) + dot(
            left_ref[1, at, :], weight_vmem[c, 1]
        )

    scatter = PlaneScatter(copies, 0, filling(rows, product), *scratch)
    turn(0, 1 - x)
    weights[0].wait()
    scatter.give(0, 0)
    scatter.give(0, 1)
    weights[1].wait()
    scatter.keep(0, 0)
    scatter.keep(0, 1)
    weights[2].wait()
    scatter.give(1, 0)
    scatter.give(1, 1)
    weights[3].wait()
    scatter.keep(1, 0)
    turn(1, x)
    scatter.give(2, 1)
    scatter.give(2, 0)
    scatter.keep(2, 1)
    scatter.keep(2, 0)
    scatter.keep(1, 1)
    scatter.give(3, 0)
    scatter.give(3, 1)
    scatter.keep(3, 0)
    scatter.keep(3, 1)
    scatter.settle()
    scatter.second()
    for task in others:
        task.wait()
    for c in range(down_ref.shape[0]):
        right = grad_ref[:, c * width : (c + 1) * width]
        down_ref[c] = dot(hidden_ref[...], right).astype(BF16)
    scatter.third()
    norm = NormBack(
        copies, PlaneScatter.SEMS, values_ref, stats_ref, gain_ref, base_ref, out_ref, low_ref,
        dgain_ref, sums_ref,
    )
    norm.start(scatter.result, devices[1:])
    norm.finish()
    copies.finish()


def back_second(gate, up, weight, hidden, grad, values, stats, gain, base, collective_id):
    rows, width = values.shape
    units, tokens = gate.shape
    vmem, anywhere = pl.BlockSpec(memory_space=pltpu.VMEM), pl.BlockSpec(memory_space=pl.ANY)
    sems = lambda n: pltpu.SemaphoreType.DMA((n,))
    return pl.pallas_call(
        back_second_kernel,
        in_specs=[anywhere] * 5 + [vmem] * 4,
        out_specs=[vmem] * 4,
        out_shape=[
            jax.ShapeDtypeStruct((rows, width), F32),
            jax.ShapeDtypeStruct((rows, width), BF16),
            jax.ShapeDtypeStruct((1, width), F32),
            jax.ShapeDtypeStruct((grad.shape[1] // width, units, width), BF16),
        ],
        scratch_shapes=[
            pltpu.VMEM(hidden.shape, BF16), pltpu.VMEM(grad.shape, BF16),
            pltpu.VMEM(gate.shape, BF16), pltpu.VMEM(up.shape, BF16),
            pltpu.VMEM(weight.shape, BF16), pltpu.VMEM((2, tokens, units), BF16),
            pltpu.VMEM((4, 8, rows), F32),
            sems(10), sems(PlaneScatter.SEMS + 3), sems(PlaneScatter.SEMS + 3),
            *scatter_scratch(rows, width),
        ],
        compiler_params=pltpu.CompilerParams(
            collective_id=collective_id, has_side_effects=True, vmem_limit_bytes=63 << 20
        ),
        cost_estimate=taking(50),
        name="back_second",
    )(gate, up, weight, hidden, grad, values, stats, gain.reshape(1, width), base)


def back_first_kernel(
    grad_ref, weight_ref, values_ref, stats_ref, gain_ref, base_ref, normed_hbm, ffn_ref, heads_ref,
    vectors_ref,
    out_ref, vector_sums_ref, query_ref, key_ref, value_ref, gate_ref, up_grad_ref, out_grad_ref,
    normed_ref, part_ref, load_sem, dgain_ref, slots_ref, sums_ref, up_ref, down_line_ref, heads_up_ref, heads_down_ref, swap_ref, swapped_ref, turn_ref,
    send_sem, recv_sem, *scratch,
):
    line_sems, scratch = scratch[:12], scratch[12:]
    rows, width = out_ref.shape
    x, _, _, row, col = places()
    devices = around()
    load = pltpu.make_async_copy(normed_hbm, normed_ref, load_sem)
    load.start()
    copies = Copies(send_sem, recv_sem, devices[2])
    vectors = RowSum(copies, PlaneScatter.SEMS + 7, slots_ref)
    meet((*devices[1:], *vectors.others))
    depth, columns = up_ref.shape[2:]

    def line_of(k):
        at = pl.ds(k * columns, columns)
        return LineScatter(
            *line_sems[4 * k : 4 * k + 4],
            lambda b: part_ref.at[pl.ds(pl.multiple_of(b * depth, 128), depth), at],
            up_ref.at[k], down_line_ref.at[k],
        )

    out_depth = out_grad_ref.shape[0]
    heads = LineScatter(
        *line_sems[8:],
        lambda b: heads_ref.at[pl.ds(pl.multiple_of(b * out_depth, 128), out_depth), :],
        heads_up_ref, heads_down_ref,
    )
    lines = [line_of(k) for k in range(2)] + [heads]
    for line in lines:
        line.clear()
    heads.start()

    def product(at, c):
        weight = weight_ref[pl.ds(pl.multiple_of(c * width, 128), width), :]
        return dot(grad_ref[at, :], weight, (1,), (1,))

    scatter = PlaneScatter(copies, 0, filling(rows, product), *scratch)
    norm = NormBack(
        copies, PlaneScatter.SEMS, values_ref, stats_ref, gain_ref, base_ref, out_ref, None,
        dgain_ref, sums_ref,
    )
    half = depth // PAIR
    theirs = pl.multiple_of((1 - x) * half, 128)
    ours = pl.multiple_of(x * half, 128)
    swap = PlaneScatter.SEMS + 3
    units = ffn_ref.shape[2]
    scatter.begin()
    load.wait()
    for b in range(LINES):
        at = slice(b * depth, (b + 1) * depth)
        part_ref[at, :] = dot(normed_ref[:, at], grad_ref[...], (0,), (0,)).astype(BF16)
        if b == 1:
            heads.hop(0)
    lines[0].start()
    lines[1].start()
    scatter.proceed()
    heads.hop(1)
    scatter.complete()
    lines[0].hop(0)
    lines[1].hop(0)
    scatter.settle()
    scatter.second()
    lines[0].hop(1)
    here = pl.ds(pl.multiple_of(x * units, 16), units)
    there = pl.ds(pl.multiple_of((1 - x) * units, 16), units)
    for w in range(2):
        copies.send(
            swap + 2 + w, ffn_ref.at[0, w, :, pl.ds(theirs, half)], turn_ref.at[w, here, :], devices[0]
        )
        turn_ref[w, here, :] = ffn_ref[0, w, :, pl.ds(ours, half)]
    lines[1].hop(1)
    scatter.third()
    norm.start(scatter.result, devices[1:4])
    slots_ref[0] = vectors_ref[...]
    slots_ref[0, 3:4, :] = dgain_ref[...]
    vectors.start()
    part = width // PAIR
    outs = (query_ref, key_ref, value_ref)

    def pieces(k):
        for w in range(3):
            start, end = max(k * columns, w * part), min((k + 1) * columns, (w + 1) * part)
            if start < end:
                yield outs[w], start - w * part, start, end - start

    def close(k):
        lines[k].receive()
        at = pl.ds(k * columns, columns)
        swap_ref[:, at] = lines[k].total(pl.ds(theirs, half)).astype(BF16)
        copies.send(swap + k, swap_ref.at[:, at], swapped_ref.at[:, at], devices[0])
        total = lines[k].total(pl.ds(ours, half))
        for ref, place, start, size in pieces(k):
            columns_at = pl.ds(pl.multiple_of(x * part + place, 128), size)
            ref[:, columns_at] = total[:, start - k * columns : start - k * columns + size]

    close(0)
    norm.finish()
    close(1)
    for w, ref in enumerate((gate_ref, up_grad_ref)):
        copies.wait(swap + 2 + w, turn_ref.at[w, there, :])
        for j in range(PAIR * units // 128):
            at = slice(j * 128, (j + 1) * 128)
            ref[:, at] = turn_ref[w, at, :].T.astype(F32)
    heads.receive()
    out_grad_ref[...] = heads.total(pl.ds(0, out_depth))
    heads.finish()
    vector_sums_ref[...] = vectors.finish()
    for k in range(2):
        at = pl.ds(k * columns, columns)
        copies.wait(swap + k, swapped_ref.at[:, at])
        for ref, place, start, size in pieces(k):
            columns_at = pl.ds(pl.multiple_of((1 - x) * part + place, 128), size)
            ref[:, columns_at] = swapped_ref[:, start : start + size].astype(F32)
        lines[k].finish()
    copies.finish()


def back_first(
    grad, weight, values, stats, gain, base, normed, ffn, heads, vectors, collective_id
):
    rows, width = values.shape
    depth, columns = normed.shape[1] // LINES, grad.shape[1]
    vmem = pl.BlockSpec(memory_space=pltpu.VMEM)
    sems = lambda n: pltpu.SemaphoreType.DMA((n,))
    count = PlaneScatter.SEMS + 7 + PAIR * LINES - 1
    units = ffn.shape[2]
    return pl.pallas_call(
        back_first_kernel,
        in_specs=[vmem] * 6 + [pl.BlockSpec(memory_space=pl.ANY)] + [vmem] * 3,
        out_specs=[vmem] * 8,
        out_shape=[
            jax.ShapeDtypeStruct((rows, width), F32),
            jax.ShapeDtypeStruct(vectors.shape, F32),
        ]
        + [jax.ShapeDtypeStruct((depth // PAIR, width), F32)] * 3
        + [jax.ShapeDtypeStruct((depth // PAIR, PAIR * units), F32)] * 2
        + [jax.ShapeDtypeStruct((heads.shape[0] // LINES, width), F32)],
        scratch_shapes=[
            pltpu.VMEM(normed.shape, BF16), pltpu.VMEM((normed.shape[1], columns), BF16),
            pltpu.SemaphoreType.DMA,
            pltpu.VMEM((1, width), F32), pltpu.VMEM((PAIR * LINES,) + vectors.shape, F32),
            pltpu.VMEM((4, 8, rows), F32),
            pltpu.VMEM((2, LINES - 1, depth, columns // 2), BF16),
            pltpu.VMEM((2, LINES - 1, depth, columns // 2), BF16),
            *[pltpu.VMEM((LINES - 1, heads.shape[0] // LINES, width), BF16)] * 2,
            pltpu.VMEM((depth // PAIR, columns), BF16), pltpu.VMEM((depth // PAIR, columns), BF16),
            pltpu.VMEM((2, PAIR * units, depth // PAIR), BF16),
            sems(count), sems(count), *[sems(LINES - 1)] * 12,
            *scatter_scratch(rows, width),
        ],
        compiler_params=pltpu.CompilerParams(
            collective_id=collective_id, has_side_effects=True, vmem_limit_bytes=63 << 20
        ),
        cost_estimate=taking(10),
        name="back_first",
    )(grad, weight, values, stats, gain.reshape(1, width), base, normed, ffn, heads, vectors)


def back_heads_kernel(
    low_ref, weight_ref, attn_hbm, hidden_hbm, down_hbm, blocks_ref,
    out_ref, part_ref, mix_ref, all_ref,
    stage_ref, attn_ref, hidden_ref, down_ref, left_ref, sent_ref, own_ref, core_ref, y_ref, give_ref, come_ref,
    load_sem, out_sem, send_sem, recv_sem,
):
    rows, width = low_ref.shape
    half = width // PAIR
    count = rows // CHUNKS
    x, y, core, row, col = places()
    over_x, over_y, over_core = peers(row, col)
    over_far = (row, 3 - col)
    loads = [
        pltpu.make_async_copy(source, place, load_sem.at[i])
        for i, (source, place) in enumerate(
            ((attn_hbm, attn_ref), (hidden_hbm, hidden_ref), (down_hbm, down_ref))
        )
    ]
    for load in loads:
        load.start()
    stage = pltpu.make_async_copy(blocks_ref.at[col], stage_ref, load_sem.at[3])
    stage.start()
    meet((over_x, over_y, over_core, over_far))
    copies = Copies(send_sem, recv_sem, over_core)
    sides = (1 - y, y)

    def at_chunk(s):
        return pl.ds(s * count, count)

    def product(s, c):
        weight = weight_ref[pl.ds(pl.multiple_of(c * width, 128), width), :]
        return dot(low_ref[at_chunk(s), :], weight, (1,), (1,))

    def give(i, s):
        at = at_chunk(s)
        sent_ref[i, at, :] = product(s, 2 * sides[i] + 1 - core).astype(BF16)
        copies.send(i * CHUNKS + s, sent_ref.at[i, at, :], core_ref.at[i, at, :], over_core)

    def keep(i, s):
        at = at_chunk(s)
        part = product(s, 2 * sides[i] + core)
        copies.wait(i * CHUNKS + s, core_ref.at[i, at, :])
        own_ref[i, at, :] = (part + core_ref[i, at, :].astype(F32)).astype(BF16)
        if i == 0:
            copies.send(2 * CHUNKS + s, own_ref.at[0, at, :], y_ref.at[at, :], over_y)

    depth = give_ref.shape[1]

    def out_grad(z, x):
        at = pl.ds(pl.multiple_of((PAIR * z + x) * depth, 128), depth)
        return dot(attn_ref[:, at], low_ref[...], (0,), (0,))

    others = (((col + 2) % 4, over_y), (3 - col, over_far), (col + 1 - 2 * core, over_core))
    for s in range(CHUNKS):
        give(0, s)
    loads[0].wait()
    for z in range(LINES):
        give_ref[z] = out_grad(z, 1 - x).astype(BF16)
    copies.send(4 * CHUNKS, give_ref, come_ref, over_x)
    for s in range(CHUNKS):
        keep(0, s)
    for s in range(CHUNKS):
        give(1, s)
    for s in range(CHUNKS):
        keep(1, s)
    for z in range(LINES):
        part_ref[z * depth : (z + 1) * depth, :] = out_grad(z, x).astype(BF16)
    stage.wait()
    stage = pltpu.make_async_copy(stage_ref, all_ref.at[col], load_sem.at[3])
    stage.start()
    for load in loads[1:]:
        load.wait()
    for a in range(PAIR):
        turn_rows(left_ref, hidden_ref, a, rows)
    for i, (other, device) in enumerate(others):
        copies.send(4 * CHUNKS + 1 + i, blocks_ref.at[other], all_ref.at[col], device)
    kept = []
    for s in range(CHUNKS):

        @pl.loop(0, PAIR * rows // TILE)
        def _(i):
            a, start = i // (rows // TILE), pl.multiple_of(i % (rows // TILE) * TILE, TILE)
            left = left_ref[pl.ds(pl.multiple_of(i * TILE, TILE), TILE), :]
            mix_ref[a * CHUNKS + s, pl.ds(start, TILE), :] = dot(left, down_ref[s]).astype(BF16)

        at = at_chunk(s)
        copies.wait(2 * CHUNKS + s, y_ref.at[at, :])
        own_ref[1, at, :] = (
            own_ref[1, at, :].astype(F32) + y_ref[at, :].astype(F32)
        ).astype(BF16)
        place = out_ref.at[pl.ds(pl.multiple_of(x * rows + s * count, 128), count), :]
        theirs = own_ref.at[1, at, pl.ds(pl.multiple_of((1 - x) * half, 128), half)]
        ours = own_ref.at[1, at, pl.ds(pl.multiple_of(x * half, 128), half)]
        copies.send(3 * CHUNKS + s, theirs, place, over_x)
        task = pltpu.make_async_copy(ours, place, out_sem.at[s])
        task.start()
        kept.append(task)
    copies.wait(4 * CHUNKS, come_ref)
    for z in range(LINES):
        at = pl.ds(z * depth, depth)
        add_rows(part_ref.at[at, :], part_ref.at[at, :], come_ref.at[z], depth)
    for s in range(CHUNKS):
        copies.wait(
            3 * CHUNKS + s,
            out_ref.at[pl.ds(pl.multiple_of((1 - x) * rows + s * count, 128), count), :],
        )
    for i, (other, _) in enumerate(others):
        copies.wait(4 * CHUNKS + 1 + i, all_ref.at[other])
    copies.finish()
    stage.wait()
    for task in kept:
        task.wait()


def back_heads(low, weight, attn, hidden, down, blocks, collective_id):
    rows, width = low.shape
    depth = weight.shape[0] // (PAIR * LINES)
    vmem, anywhere = pl.BlockSpec(memory_space=pltpu.VMEM), pl.BlockSpec(memory_space=pl.ANY)
    sems = lambda n: pltpu.SemaphoreType.DMA((n,))
    wide = pltpu.VMEM((2, rows, width), BF16)
    swapped = pltpu.VMEM((LINES, depth, width), BF16)
    return pl.pallas_call(
        back_heads_kernel,
        in_specs=[vmem] * 2 + [anywhere] * 4,
        out_specs=[anywhere, vmem, vmem, anywhere],
        out_shape=[
            jax.ShapeDtypeStruct((PAIR * rows, width // PAIR), BF16),
            jax.ShapeDtypeStruct((LINES * depth, width), BF16),
            jax.ShapeDtypeStruct((PAIR * CHUNKS, rows, width), BF16),
            jax.ShapeDtypeStruct(blocks.shape, BF16),
        ],
        scratch_shapes=[
            pltpu.VMEM(blocks.shape[1:], BF16),
            pltpu.VMEM(attn.shape, BF16), pltpu.VMEM(hidden.shape, BF16),
            pltpu.VMEM(down.shape, BF16), pltpu.VMEM(hidden.shape[::-1], BF16),
            wide, wide, wide, pltpu.VMEM((rows, width), BF16),
            swapped, swapped,
            sems(4), sems(CHUNKS), sems(4 * CHUNKS + 4), sems(4 * CHUNKS + 4),
        ],
        compiler_params=pltpu.CompilerParams(
            collective_id=collective_id, has_side_effects=True, vmem_limit_bytes=60 << 20
        ),
        cost_estimate=taking(60),
        name="back_heads",
    )(low, weight, attn, hidden, down, blocks)


def per_device(
    tokens, segment_ids, positions, attn_gain, query_weight, query_bias, key_weight, key_bias,
    value_weight, value_bias, out_weight, mlp_gain, gate_weight, up_weight, down_weight, out_grad,
):
    count, width = tokens.shape
    lines = lax.axis_size("row") // PAIR
    cols = lax.axis_size("col")
    row = lax.axis_index("row")
    col = lax.axis_index("col")
    x = row % PAIR
    half = width // PAIR

    fast = cols == 4 and lines == LINES
    bias = jnp.concatenate(
        [pick(b, x, 0) for b in (query_bias, key_bias, value_bias)], axis=0
    )
    depth = out_weight.shape[0]
    hidden = down_weight.shape[0]
    down_line = gather_line(down_weight)
    if fast:
        tokens_all, grad_all, qkv_weight, out_all, ffn_part, gains, places_all = gather_first(
            tokens, out_grad, query_weight, key_weight, value_weight, out_weight,
            gate_weight, up_weight,
            jnp.pad(jnp.stack([attn_gain, mlp_gain]), ((0, 6), (0, 0))),
            jnp.pad(jnp.stack([positions, segment_ids]), ((0, 6), (0, 0))), 0,
        )
    else:
        qkv_weight = gather_line(
            jnp.concatenate(
                [own_columns(w, x) for w in (query_weight, key_weight, value_weight)], axis=1
            )
        )
        tokens_all = gather_plane(tokens, "gather_tokens", 0)
        grad_all = gather_plane(out_grad, "gather_cotangent", 1)
        out_line = gather_line(out_weight)
        full = (lines, 1, depth, width)
        out_all = in_order(
            x, out_line.reshape(full), swap_rows(out_line).reshape(full), 1
        ).reshape(-1, width)
        ffn_part = jnp.stack([own_units(w, x) for w in (gate_weight, up_weight)])[None]
        gains = lax.all_gather(jnp.stack([attn_gain, mlp_gain]), "col", axis=1, tiled=True)
        own_place = jnp.stack([positions, segment_ids])
        places_all = in_order(x, own_place, swap_rows(own_place), 1)
    cosine, sine = rotation_tables(places_all[0])
    plane_segments = places_all[1]
    down_blocks = after(down_line, tokens_all).reshape(lines, hidden, width)
    ffn_weight = gather_line(after(ffn_part, down_blocks))

    projections = (tokens_all, gains, qkv_weight, bias, cosine, sine)
    if fast:
        normed_first, queries, keys, values, stats_first, down_partly = project_heads(
            *projections, down_blocks, 1
        )
        attended, lse, down_all = attention_forward(
            queries, keys, values, plane_segments, down_blocks, down_partly, 8
        )
    else:
        normed_first, queries, keys, values, stats_first = project_heads(*projections)
        attended, lse = attention_forward(queries, keys, values, plane_segments)
        down_all = lax.all_to_all(down_blocks, "col", split_axis=0, concat_axis=0, tiled=True)
    if fast:
        attn_all, resid, resid_all = project_out(attended, out_all, tokens, 2)
    else:
        attn_all = gather_heads(attended, x)
        resid = tokens.astype(F32) + dot(attn_all, out_all)
        resid_all = gather_plane(resid.astype(BF16), "gather_residual", 3)

    normed_second, hidden_low, grad_gate, grad_up, stats_second = feed_forward(
        resid_all, gains, ffn_weight, grad_all, down_all
    )
    if fast:
        grad_ffn = weight_grads((grad_gate, grad_up), normed_second, width, "ffn_grads")
    else:
        grad_ffn = weight_grads((grad_gate, grad_up), normed_second, width, "ffn_grads")
    if fast:
        grad_resid, grad_resid_low, mlp_gain_part, down_blocks = back_second(
            after(grad_gate, grad_ffn), grad_up, ffn_weight, hidden_low, grad_all,
            resid, stats_second, mlp_gain, out_grad, 4,
        )
        mlp_gain_part = mlp_gain_part[0]
    else:
        grad_second = scatter_plane(
            back_project((grad_gate, grad_up), ffn_weight, "back_ffn"), "scatter_second", 4
        )
        own_stats = pick(stats_second, x, 0)
        mean_here, inv_here = own_stats[:, 0:1], own_stats[:, 1:2]
        grad_resid, mlp_gain_part = norm_backward(
            grad_second, (resid - mean_here) * inv_here, inv_here, mlp_gain
        )
        grad_resid = grad_resid + out_grad.astype(F32)
        grad_resid_low = grad_resid.astype(BF16)
    grad_ffn = scatter_line(grad_ffn)

    if fast:
        grad_attn, grad_out_weight, mixed, grad_down = back_heads(
            grad_resid_low, out_all, attn_all, hidden_low, down_all, down_blocks, 5
        )
        grad_qkv, bias_sums, mixed = attention_backward(
            queries, keys, values, grad_attn, lse, cosine, sine, plane_segments, mixed, resid, 9
        )
    else:
        grad_out_weight = dot(attn_all, grad_resid_low, (0,), (0,)).astype(BF16)
        grad_out_weight = grad_out_weight.reshape(lines, PAIR, depth, width)
        grad_out_weight = pick(grad_out_weight, x, 1) + swap_rows(pick(grad_out_weight, 1 - x, 1))
        grad_out_weight = scatter_line(grad_out_weight.reshape(lines * depth, width)).astype(F32)
        grad_attn = scatter_heads(dot(grad_resid_low, out_all, (1,), (1,)).astype(BF16), x)
        grad_qkv, bias_sums = attention_backward(
            queries, keys, values, grad_attn, lse, cosine, sine, plane_segments
        )
        grad_down = weight_grads((hidden_low,), grad_all, width, "down_grads")
        grad_down = lax.all_to_all(
            grad_down.reshape(cols, hidden, width), "col", split_axis=0, concat_axis=0, tiled=True
        )
    grad_down = scatter_line(after(grad_down, grad_ffn).reshape(lines * hidden, width))
    bias_part = jnp.sum(bias_sums, axis=(0, 1)).reshape(3, half)
    bias_part = jnp.where(
        (jnp.arange(PAIR) == x)[None, :, None], bias_part[:, None, :], 0.0
    ).reshape(3, width)
    if fast:
        (
            tokens_grad, vectors, query_grad, key_grad, value_grad, gate_grad, up_grad,
            grad_out_weight,
        ) = back_first(
            grad_qkv, qkv_weight,
            tokens, stats_first, attn_gain, grad_resid, normed_first, grad_ffn, grad_out_weight,
            jnp.concatenate(
                [bias_part, jnp.zeros((1, width), F32), mlp_gain_part[None], jnp.zeros((3, width), F32)]
            ),
            6,
        )
    else:
        kept, other = pick(grad_ffn[0], x, 2), swap_rows(pick(grad_ffn[0], 1 - x, 2))
        gate_grad, up_grad = (
            in_order(x, kept[i], other[i], 0).T.astype(F32) for i in range(2)
        )
        grad_qkv_weight = dot(normed_first, grad_qkv, (0,), (0,)).astype(BF16)
        kept, other = own_rows(scatter_line(grad_qkv_weight), x)
        query_grad, key_grad, value_grad = (
            in_order(x, kept[:, at : at + half], other[:, at : at + half], 1).astype(F32)
            for at in (0, half, 2 * half)
        )
        grad_first = scatter_plane(
            dot(grad_qkv, qkv_weight, (1,), (1,)).astype(BF16), "scatter_first", 6
        )
        own_stats = pick(stats_first, x, 0)
        mean_here, inv_here = own_stats[:, 0:1], own_stats[:, 1:2]
        grad_input, attn_gain_part = norm_backward(
            grad_first, (tokens.astype(F32) - mean_here) * inv_here, inv_here, attn_gain
        )
        tokens_grad = grad_input + grad_resid
        vectors = lax.psum(
            jnp.concatenate([bias_part, attn_gain_part[None], mlp_gain_part[None]]), "row"
        )
        mixed = resid + scatter_plane(
            back_project((hidden_low,), down_all[:, None], "mix"), "scatter_mixed", 10
        )
        mixed = mixed.astype(BF16)

    return (
        mixed,
        tokens_grad,
        vectors[3],
        query_grad,
        vectors[0],
        key_grad,
        vectors[1],
        value_grad,
        vectors[2],
        grad_out_weight,
        vectors[4],
        gate_grad,
        up_grad,
        grad_down.astype(F32),
    )


def solution(mesh):
    grid, rows, cols = P("row", "col"), P("row"), P("col")
    in_specs = (
        grid, rows, rows, cols, grid, cols, grid, cols, grid, cols, grid, cols, grid, grid, grid, grid,
    )
    out_specs = (
        grid, grid, cols, grid, cols, grid, cols, grid, cols, grid, cols, grid, grid, grid,
    )
    return jax.shard_map(
        per_device, mesh=mesh, in_specs=in_specs, out_specs=out_specs, check_vma=False
    )
```
